32 devices in a mesh: dp: 2 (over x), expert: 16 (over z, y, core).
Axes of the slice: x: 2, y: 2, z: 4, core: 2. Of those that a mesh axis runs over, the one named last changes fastest.
Arguments:
- tokens: bfloat16 [32, 576, 768], P(('dp', 'expert')), may hold values from -6 to 6
- cotangent: bfloat16 [32, 576, 768], P(('dp', 'expert')), may hold values from -6 to 6
- expert_choice: int32 [32, 576, 2], P(('dp', 'expert')), may hold values from 0 to 15, all different within a row
- priority: int32 [32, 576], P(('dp', 'expert')), may hold values from 0 to 575, each once within a row
- projection: float32 [768, 2304], P(('dp', 'expert')), may hold values from -1 to 1
- projection_first: float32 [768, 2304], P(('dp', 'expert'))
- projection_second: float32 [768, 2304], P(('dp', 'expert'))
- output_weight: float32 [768, 768], P(('dp', 'expert')), may hold values from -2.5 to 2.5
- output_first: float32 [768, 768], P(('dp', 'expert'))
- output_second: float32 [768, 768], P(('dp', 'expert'))
- router_weight: float32 [768, 16], P(('dp', 'expert')), may hold values from -0.125 to 0.125
- router_first: float32 [768, 16], P(('dp', 'expert'))
- router_second: float32 [768, 16], P(('dp', 'expert'))
- vectors: float32 [7, 768], P(None, ('dp', 'expert')), may hold values from -0.4 to 2.5
- vectors_first: float32 [7, 768], P(None, ('dp', 'expert'))
- vectors_second: float32 [7, 768], P(None, ('dp', 'expert'))
- expert_inner: float32 [16, 768, 3072], P('expert', None, 'dp'), may hold values from -0.21875 to 0.21875
- inner_first: float32 [16, 768, 3072], P('expert', None, 'dp')
- inner_second: float32 [16, 768, 3072], P('expert', None, 'dp')
- hidden_bias: float32 [16, 3072], P('expert', 'dp'), may hold values from -0.6 to 0.6
- hidden_first: float32 [16, 3072], P('expert', 'dp')
- hidden_second: float32 [16, 3072], P('expert', 'dp')
- expert_outer: float32 [16, 3072, 768], P('expert', 'dp'), may hold values from -1.75 to 1.75
- outer_first: float32 [16, 3072, 768], P('expert', 'dp')
- outer_second: float32 [16, 3072, 768], P('expert', 'dp')
- return_bias: float32 [16, 768], P('expert', 'dp'), may hold values from -6 to 6
- return_first: float32 [16, 768], P('expert', 'dp')
- return_second: float32 [16, 768], P('expert', 'dp')
Outputs:
- block_output: bfloat16 [32, 576, 768], P(('dp', 'expert'))
- input_grad: float32 [32, 576, 768], P(('dp', 'expert'))
- grad_norm: float32 [], replicated
- projection_next: float32 [768, 2304], P(('dp', 'expert'))
- projection_moment: float32 [768, 2304], P(('dp', 'expert'))
- projection_square: float32 [768, 2304], P(('dp', 'expert'))
- output_next: float32 [768, 768], P(('dp', 'expert'))
- output_moment: float32 [768, 768], P(('dp', 'expert'))
- output_square: float32 [768, 768], P(('dp', 'expert'))
- router_next: float32 [768, 16], P(('dp', 'expert'))
- router_moment: float32 [768, 16], P(('dp', 'expert'))
- router_square: float32 [768, 16], P(('dp', 'expert'))
- vectors_next: float32 [7, 768], P(None, ('dp', 'expert'))
- vectors_moment: float32 [7, 768], P(None, ('dp', 'expert'))
- vectors_square: float32 [7, 768], P(None, ('dp', 'expert'))
- inner_next: float32 [16, 768, 3072], P('expert', None, 'dp')
- inner_moment: float32 [16, 768, 3072], P('expert', None, 'dp')
- inner_square: float32 [16, 768, 3072], P('expert', None, 'dp')
- hidden_next: float32 [16, 3072], P('expert', 'dp')
- hidden_moment: float32 [16, 3072], P('expert', 'dp')
- hidden_square: float32 [16, 3072], P('expert', 'dp')
- outer_next: float32 [16, 3072, 768], P('expert', 'dp')
- outer_moment: float32 [16, 3072, 768], P('expert', 'dp')
- outer_square: float32 [16, 3072, 768], P('expert', 'dp')
- return_next: float32 [16, 768], P('expert', 'dp')
- return_moment: float32 [16, 768], P('expert', 'dp')
- return_square: float32 [16, 768], P('expert', 'dp')
The draws below stay inside these ranges and needn't reach their ends.
Inputs may be any that keep to these rules, and one draw needn't show every extreme that they name: `expert_choice`: the 2 experts of a patch are all different. `priority`: in each image every number from 0 to 575 stands once; a lower number claims expert slots earlier.
All inputs are finite; a program needn't handle non-finite values.
Results may differ from the reference program's by a relative error of at most 0.025.
Values may be sent and summed in bfloat16 or wider, within the bound.
A program may use at most 256 MiB of HBM per device.

```python
import math
from functools import partial
import jax
import jax.numpy as jnp
from jax import lax

D = 768
HEADS = 12
HEAD_DIM = 64
FF = 3072
TOP = 2
STEP = 10
PATCHES = 576
EXPERTS = 16
IMAGES = 32
TOKENS = 18432
CAP = 36
DP_ROWS = 384


def clipped_scales():
    routed = IMAGES * CAP
    square_guess = TOKENS * (11.8 * D * D + 47.0 * D + 9.0 * D * D / PATCHES) + routed * (0.13 * EXPERTS * D * FF + 0.09 * EXPERTS * FF + 0.64 * D * FF / EXPERTS + D / EXPERTS)
    norm_guess = math.sqrt(square_guess)
    dense_root = math.sqrt(TOKENS)
    expert_root = math.sqrt(routed)
    return (1.8 * dense_root / norm_guess, 3.0 * math.sqrt(TOKENS / PATCHES) / norm_guess, 1.44 * math.sqrt(D / EXPERTS) * dense_root / norm_guess, 2.6 * dense_root / norm_guess, 0.36 * expert_root / norm_guess, 0.3 * expert_root / norm_guess, 0.8 * expert_root / EXPERTS / norm_guess, expert_root / EXPERTS / norm_guess)


def first_moment(key, array_shape, kind_index):
    entry_scale = clipped_scales()[kind_index] * (1.0 - 0.9) / 0.9
    return entry_scale * jax.random.truncated_normal(key, -3.0, 3.0, array_shape, jnp.float32)


def second_moment(key, array_shape, kind_index):
    entry_scale = clipped_scales()[kind_index]
    spread = jnp.exp(jax.random.uniform(key, array_shape, jnp.float32, 0.0, math.log(4.0)))
    return spread * (entry_scale * entry_scale * (1.0 - 0.999) / 0.999)


def draw_projection(key, part):
    key = jax.random.fold_in(key, 20)
    subkeys = jax.random.split(key, 2)
    entries = jax.random.truncated_normal(subkeys[0], -3.0, 3.0, (D, 3 * D), jnp.float32)
    common_row = jax.random.truncated_normal(subkeys[1], -3.0, 3.0, (3 * D,), jnp.float32)
    return (entries + 0.5 * common_row[None, :]) * (1.0 / math.sqrt(D))


def draw_vectors(key, part):
    key = jax.random.fold_in(key, 11)
    subkeys = jax.random.split(key, 2)
    outer_place = jnp.arange(D, dtype=jnp.int32).astype(jnp.float32) / D
    inner_place = (jnp.arange(D, dtype=jnp.int32) % DP_ROWS).astype(jnp.float32) / DP_ROWS
    profile = (0.75 + 0.5 * outer_place) * (0.8 + 0.6 * inner_place)
    gain_rows = profile[None, :] * jax.random.uniform(subkeys[0], (2, D), jnp.float32, 0.85, 1.15)
    biases = 0.1 * jax.random.truncated_normal(subkeys[1], -3.0, 3.0, (5, D), jnp.float32)
    return jnp.stack([gain_rows[0], biases[0], biases[1], biases[2], biases[3], gain_rows[1], biases[4]])


def draw_projection_first(key, part):
    key = jax.random.fold_in(key, 21)
    return first_moment(key, (D, 3 * D), 0)


def draw_projection_second(key, part):
    key = jax.random.fold_in(key, 22)
    return second_moment(key, (D, 3 * D), 0)


def draw_output_first(key, part):
    key = jax.random.fold_in(key, 23)
    return first_moment(key, (D, D), 1)


def draw_output_second(key, part):
    key = jax.random.fold_in(key, 24)
    return second_moment(key, (D, D), 1)


def draw_router_first(key, part):
    key = jax.random.fold_in(key, 25)
    return first_moment(key, (D, EXPERTS), 2)


def draw_router_second(key, part):
    key = jax.random.fold_in(key, 26)
    return second_moment(key, (D, EXPERTS), 2)


def draw_vectors_first(key, part):
    key = jax.random.fold_in(key, 27)
    return first_moment(key, (7, D), 3)


def draw_vectors_second(key, part):
    key = jax.random.fold_in(key, 28)
    return second_moment(key, (7, D), 3)


def draw_inner_first(key, part):
    key = jax.random.fold_in(key, 29)
    return first_moment(key, (EXPERTS, D, FF), 4)


def draw_inner_second(key, part):
    key = jax.random.fold_in(key, 30)
    return second_moment(key, (EXPERTS, D, FF), 4)


def draw_hidden_first(key, part):
    key = jax.random.fold_in(key, 31)
    return first_moment(key, (EXPERTS, FF), 5)


def draw_hidden_second(key, part):
    key = jax.random.fold_in(key, 32)
    return second_moment(key, (EXPERTS, FF), 5)


def draw_outer_first(key, part):
    key = jax.random.fold_in(key, 33)
    return first_moment(key, (EXPERTS, FF, D), 6)


def draw_outer_second(key, part):
    key = jax.random.fold_in(key, 34)
    return second_moment(key, (EXPERTS, FF, D), 6)


def draw_return_first(key, part):
    key = jax.random.fold_in(key, 35)
    return first_moment(key, (EXPERTS, D), 7)


def draw_return_second(key, part):
    key = jax.random.fold_in(key, 36)
    return second_moment(key, (EXPERTS, D), 7)


def block_scale(rng, dims, pieces, low, high):
    factor_of = 1.0
    for dim, shards_of in pieces:
        draws = jax.random.uniform(jax.random.fold_in(jax.random.fold_in(rng, 6), dim), (shards_of,), jnp.float32, low / len(pieces), high / len(pieces))
        factor_of = factor_of * jnp.repeat(jnp.exp(draws), dims[dim] // shards_of).reshape((-1,) + (1,) * (len(dims) - 1 - dim))
    return factor_of


def picks_of(stream_key, rows, count, top, lift):
    order = jax.random.permutation(jax.random.fold_in(stream_key, 1), count)
    pull = order
    for power in range(3):
        pull = pull * pull // count
    pull = pull * lift // count
    lots = jax.random.randint(jax.random.fold_in(stream_key, 2), (rows, count), 0, 4096) + pull
    holders = jax.random.permutation(jax.random.fold_in(stream_key, 3), rows)[jnp.arange(count) % rows]
    lots = jnp.where(jnp.arange(rows)[:, None] == holders[None, :], 1 << 14, lots)
    merit = lots * count + jnp.arange(count)
    return lax.top_k(merit.astype(jnp.int32), top)[1].astype(jnp.int32)


def gaussian(rng, shape, deviation, bound, cuts=(), held_as=jnp.bfloat16):
    loudness = block_scale(rng, shape, cuts, -0.22, 0.18) if cuts else 1.0
    values = jax.random.normal(rng, shape, jnp.float32) * deviation * loudness
    return jnp.minimum(jnp.maximum(values, -bound), bound).astype(held_as)


def setup_inputs(seed: int = 0) -> dict:
    streams_of = jax.random.split(jax.random.key(seed), 29)
    tokens = gaussian(streams_of[0], (IMAGES, PATCHES, D), 1.0, 6.0, ((0, 32),))
    cotangent = gaussian(streams_of[1], (IMAGES, PATCHES, D), 1.0, 6.0, ((0, 32),))
    expert_choice = picks_of(streams_of[2], IMAGES * PATCHES, EXPERTS, TOP, 1024).reshape((IMAGES, PATCHES, TOP))
    priority = jax.vmap(lambda own: jax.random.permutation(own, PATCHES))(jax.random.split(streams_of[3], IMAGES)).reshape((IMAGES, PATCHES)).astype(jnp.int32)
    projection = draw_projection(jax.random.fold_in(streams_of[28], 71), 0)
    projection_first = draw_projection_first(jax.random.fold_in(streams_of[28], 71), 0)
    projection_second = draw_projection_second(jax.random.fold_in(streams_of[28], 71), 0)
    output_weight = gaussian(streams_of[7], (D, D), (4 * D // PATCHES) ** -0.5, 2.5, ((0, 32),), jnp.float32)
    output_first = draw_output_first(jax.random.fold_in(streams_of[28], 71), 0)
    output_second = draw_output_second(jax.random.fold_in(streams_of[28], 71), 0)
    router_weight = gaussian(streams_of[10], (D, EXPERTS), (3 * D) ** -0.5, 0.125, ((0, 32),), jnp.float32)
    router_first = draw_router_first(jax.random.fold_in(streams_of[28], 71), 0)
    router_second = draw_router_second(jax.random.fold_in(streams_of[28], 71), 0)
    vectors = draw_vectors(jax.random.fold_in(streams_of[28], 71), 0)
    vectors_first = draw_vectors_first(jax.random.fold_in(streams_of[28], 71), 0)
    vectors_second = draw_vectors_second(jax.random.fold_in(streams_of[28], 71), 0)
    expert_inner = gaussian(streams_of[16], (EXPERTS, D, FF), D ** -0.5, 0.21875, ((0, 16), (2, 2)), jnp.float32)
    inner_first = draw_inner_first(jax.random.fold_in(streams_of[28], 71), 0)
    inner_second = draw_inner_second(jax.random.fold_in(streams_of[28], 71), 0)
    hidden_bias = gaussian(streams_of[19], (EXPERTS, FF), 0.1, 0.6, ((0, 16), (1, 2)), jnp.float32)
    hidden_first = draw_hidden_first(jax.random.fold_in(streams_of[28], 71), 0)
    hidden_second = draw_hidden_second(jax.random.fold_in(streams_of[28], 71), 0)
    expert_outer = gaussian(streams_of[22], (EXPERTS, FF, D), (max(1, FF // (EXPERTS * EXPERTS))) ** -0.5, 1.75, ((0, 16), (1, 2)), jnp.float32)
    outer_first = draw_outer_first(jax.random.fold_in(streams_of[28], 71), 0)
    outer_second = draw_outer_second(jax.random.fold_in(streams_of[28], 71), 0)
    return_bias = gaussian(streams_of[25], (EXPERTS, D), (EXPERTS // 16), 6.0, ((0, 16), (1, 2)), jnp.float32)
    return_first = draw_return_first(jax.random.fold_in(streams_of[28], 71), 0)
    return_second = draw_return_second(jax.random.fold_in(streams_of[28], 71), 0)
    return dict(tokens=tokens, cotangent=cotangent, expert_choice=expert_choice, priority=priority, projection=projection, projection_first=projection_first, projection_second=projection_second, output_weight=output_weight, output_first=output_first, output_second=output_second, router_weight=router_weight, router_first=router_first, router_second=router_second, vectors=vectors, vectors_first=vectors_first, vectors_second=vectors_second, expert_inner=expert_inner, inner_first=inner_first, inner_second=inner_second, hidden_bias=hidden_bias, hidden_first=hidden_first, hidden_second=hidden_second, expert_outer=expert_outer, outer_first=outer_first, outer_second=outer_second, return_bias=return_bias, return_first=return_first, return_second=return_second)


NORM_EPS = 1e-06
ADAM_EPS = 1e-08
BETA_ONE = 0.9
BETA_TWO = 0.999
DECAY = 0.1
THRESHOLD = 1.0
RATE_PROJECTION = 0.1
RATE_OUTPUT = 1.0
RATE_ROUTER = 0.05
RATE_VECTORS = 0.5
RATE_INNER = 0.1
RATE_HIDDEN = 0.25
RATE_OUTER = 1.5
RATE_RETURN = 2.0

@jax.custom_vjp
def low(v):
    return lax.optimization_barrier(v.astype(jnp.bfloat16)).astype(jnp.float32)

@jax.custom_vjp
def low_back(v):
    return v

def low_keep(v):
    return (low(v), None)

def low_pass(kept, grad):
    return (grad,)

def back_keep(v):
    return (v, None)

def back_low(kept, grad):
    return (low(grad),)
low.defvjp(low_keep, low_pass)
low_back.defvjp(back_keep, back_low)

def exact_dot(left, right):
    return jnp.dot(left, right, precision=lax.Precision.HIGHEST, preferred_element_type=jnp.float32)

def layer_norm(values, norm_gain, norm_bias):
    center = values - lax.optimization_barrier(jnp.mean(values, axis=-1, keepdims=True))
    spread = lax.optimization_barrier(jnp.mean(center * center, axis=-1, keepdims=True))
    return center * lax.rsqrt(spread + NORM_EPS) * norm_gain + norm_bias

def smooth_gate(values):
    return jax.nn.gelu(values, approximate=True)

def assign_slots(chosen, claim_order, expert_count, capacity):
    patches = chosen.shape[0]
    top_count = chosen.shape[1]
    claim_rank = (jnp.arange(top_count, dtype=jnp.int32)[None, :] * patches + claim_order[:, None]).T.reshape(-1)
    flat_choice = chosen.T.reshape(-1)
    onehot = (flat_choice[:, None] == jnp.arange(expert_count, dtype=jnp.int32)[None, :]).astype(jnp.float32)
    earlier = (claim_rank[None, :] < claim_rank[:, None]).astype(jnp.float32)
    counts = jnp.dot(earlier, onehot, precision=lax.Precision.HIGHEST, preferred_element_type=jnp.float32)
    position = lax.optimization_barrier(jnp.sum(counts * onehot, axis=1)).astype(jnp.int32).reshape(top_count, patches).T
    kept_mask = position < capacity
    flat_slot = chosen * capacity + jnp.minimum(position, capacity - 1)
    return (flat_slot, kept_mask)

def slot_matches(flat_slot, kept_mask, slot_count):
    slot_ids = jnp.arange(slot_count, dtype=jnp.int32)
    return (flat_slot[None, :, :] == slot_ids[:, None, None]) & kept_mask[None, :, :]

def attend_image(projection_low, output_low, router_low, vector_rows, image_rows, chosen, flat_slot, kept_mask):
    normed = low(layer_norm(image_rows, vector_rows[0], vector_rows[1]))
    projected = exact_dot(normed, projection_low)
    queries = low_back(low(projected[:, :D] + vector_rows[2])).reshape(PATCHES, HEADS, HEAD_DIM)
    key_rows = low_back(low(projected[:, D:2 * D])).reshape(PATCHES, HEADS, HEAD_DIM)
    value_rows = low_back(low(projected[:, 2 * D:] + vector_rows[3])).reshape(PATCHES, HEADS, HEAD_DIM)
    scores = low_back(jnp.einsum('qhd,khd->hqk', queries, key_rows, precision=lax.Precision.HIGHEST) * HEAD_DIM ** (-0.5))
    attention = jax.nn.softmax(scores, axis=-1)
    context = jnp.einsum('hqk,khd->qhd', low(attention), value_rows, precision=lax.Precision.HIGHEST).reshape(PATCHES, D)
    context = low_back(low(context))
    branch = low_back(exact_dot(context, output_low) + vector_rows[4])
    middle = image_rows + branch
    normed_two = low(layer_norm(middle, vector_rows[5], vector_rows[6]))
    logits = low_back(exact_dot(normed_two, router_low))
    gate_values = jnp.take_along_axis(jax.nn.softmax(logits, axis=-1), chosen, axis=1)
    slot_table = jnp.any(slot_matches(flat_slot, kept_mask, EXPERTS * CAP), axis=2).astype(jnp.float32)
    dispatched = low_back(exact_dot(slot_table, normed_two))
    return (middle, gate_values, dispatched)

def expert_apply(operands):
    slot_rows, inner_low, hidden_low, outer_low, shift_low = operands
    pre_act = low_back(exact_dot(slot_rows, inner_low) + hidden_low)
    activated = low(smooth_gate(pre_act))
    return low_back(low(exact_dot(activated, outer_low) + shift_low))

def combine_image(middle, gate_values, returned, flat_slot, kept_mask):
    picked = returned[flat_slot]
    weighted = jnp.where(kept_mask, gate_values, 0.0)
    return middle + lax.optimization_barrier(jnp.sum(weighted[:, :, None] * picked, axis=1))

def adam_update(weight, first_state, second, gradient, clip_factor, step_rate, decay_rate):
    scaled = gradient * clip_factor
    first_new = BETA_ONE * first_state + (1.0 - BETA_ONE) * scaled
    second_new = BETA_TWO * second + (1.0 - BETA_TWO) * scaled * scaled
    first_hat = first_new / (1.0 - BETA_ONE ** STEP)
    second_hat = second_new / (1.0 - BETA_TWO ** STEP)
    weight_new = weight - step_rate * (first_hat / (jnp.sqrt(second_hat) + ADAM_EPS) + decay_rate * weight)
    return (weight_new, first_new, second_new)

def reference(tokens, cotangent, expert_choice, priority, projection, projection_first, projection_second, output_weight, output_first, output_second, router_weight, router_first, router_second, vectors, vectors_first, vectors_second, expert_inner, inner_first, inner_second, hidden_bias, hidden_first, hidden_second, expert_outer, outer_first, outer_second, return_bias, return_first, return_second):

    def route_image(operands):
        return assign_slots(operands[0], operands[1], EXPERTS, CAP)
    flat_slot, kept_mask = lax.map(route_image, (expert_choice, priority))
    group_size = 1
    while group_size * 2 * PATCHES <= 4096 and IMAGES % (group_size * 2) == 0:
        group_size = group_size * 2
    group_count = IMAGES // group_size

    def grouped(array):
        return array.reshape((group_count, group_size) + array.shape[1:])

    def forward(given_tokens, given_projection, given_output, given_router, given_vectors, given_inner, given_hidden, given_outer, given_return):
        vector_rows = low(given_vectors)
        projection_low = low(given_projection)
        output_low = low(given_output)
        router_low = low(given_router)

        def attend_group(operands):
            image_group, chosen_group, slot_group, kept_group = operands
            return jax.vmap(partial(attend_image, projection_low, output_low, router_low, vector_rows))(image_group, chosen_group, slot_group, kept_group)
        middle, gate_values, dispatched = lax.map(jax.checkpoint(attend_group), (grouped(given_tokens), grouped(expert_choice), grouped(flat_slot), grouped(kept_mask)))
        middle = middle.reshape(IMAGES, PATCHES, D)
        gate_values = gate_values.reshape(IMAGES, PATCHES, TOP)
        per_expert = dispatched.reshape(IMAGES, EXPERTS, CAP, D).transpose(1, 0, 2, 3).reshape(EXPERTS, IMAGES * CAP, D)
        outputs = lax.map(jax.checkpoint(expert_apply), (per_expert, low(given_inner), low(given_hidden), low(given_outer), low(given_return)))
        returned = outputs.reshape(EXPERTS, IMAGES, CAP, D).transpose(1, 0, 2, 3).reshape(IMAGES, EXPERTS * CAP, D)

        def combine_group(operands):
            return jax.vmap(combine_image)(operands[0], operands[1], operands[2], operands[3], operands[4])
        final = lax.map(jax.checkpoint(combine_group), (grouped(middle), grouped(gate_values), grouped(returned), grouped(flat_slot), grouped(kept_mask)))
        return final.reshape(IMAGES, PATCHES, D)
    final, pullback = jax.vjp(forward, tokens.astype(jnp.float32), projection, output_weight, router_weight, vectors, expert_inner, hidden_bias, expert_outer, return_bias)
    gradients = pullback(cotangent.astype(jnp.float32))
    square_sum = jnp.sum(gradients[1] * gradients[1])
    for gradient in gradients[2:]:
        square_sum = square_sum + jnp.sum(gradient * gradient)
    grad_norm = jnp.sqrt(square_sum)
    clip_factor = THRESHOLD / jnp.maximum(grad_norm, THRESHOLD)
    projection_next, projection_moment, projection_square = adam_update(projection, projection_first, projection_second, gradients[1], clip_factor, RATE_PROJECTION, DECAY)
    output_next, output_moment, output_square = adam_update(output_weight, output_first, output_second, gradients[2], clip_factor, RATE_OUTPUT, DECAY)
    router_next, router_moment, router_square = adam_update(router_weight, router_first, router_second, gradients[3], clip_factor, RATE_ROUTER, DECAY)
    vectors_next, vectors_moment, vectors_square = adam_update(vectors, vectors_first, vectors_second, gradients[4], clip_factor, RATE_VECTORS, 0.0)
    inner_next, inner_moment, inner_square = adam_update(expert_inner, inner_first, inner_second, gradients[5], clip_factor, RATE_INNER, DECAY)
    hidden_next, hidden_moment, hidden_square = adam_update(hidden_bias, hidden_first, hidden_second, gradients[6], clip_factor, RATE_HIDDEN, 0.0)
    outer_next, outer_moment, outer_square = adam_update(expert_outer, outer_first, outer_second, gradients[7], clip_factor, RATE_OUTER, DECAY)
    return_next, return_moment, return_square = adam_update(return_bias, return_first, return_second, gradients[8], clip_factor, RATE_RETURN, 0.0)
    return (final.astype(jnp.bfloat16), gradients[0], grad_norm, projection_next, projection_moment, projection_square, output_next, output_moment, output_square, router_next, router_moment, router_square, vectors_next, vectors_moment, vectors_square, inner_next, inner_moment, inner_square, hidden_next, hidden_moment, hidden_square, outer_next, outer_moment, outer_square, return_next, return_moment, return_square)
```

```python
import functools

import jax
import jax.numpy as jnp
from jax import lax
from jax.experimental import pallas as pl
from jax.experimental.pallas import tpu as pltpu
from jax.sharding import PartitionSpec as P

HEADS = 12
HEAD_DIM = 64
STEP = 10


NORM_EPS = 1e-06
ADAM_EPS = 1e-08
BETA_ONE = 0.9
BETA_TWO = 0.999
DECAY = 0.1
THRESHOLD = 1.0
RATE_PROJECTION = 0.1
RATE_OUTPUT = 1.0
RATE_ROUTER = 0.05
RATE_VECTORS = 0.5
RATE_INNER = 0.1
RATE_HIDDEN = 0.25
RATE_OUTER = 1.5
RATE_RETURN = 2.0


def layer_norm(values, norm_gain, norm_bias):
    center = values - jnp.mean(values, axis=-1, keepdims=True)
    spread = jnp.mean(center * center, axis=-1, keepdims=True)
    return center * lax.rsqrt(spread + NORM_EPS) * norm_gain + norm_bias


def smooth_gate(values):
    return jax.nn.gelu(values, approximate=True)


def mixed_dot(left, right):
    return jnp.dot(left, right, preferred_element_type=jnp.float32)


def rows_product(left, right):
    return lax.dot_general(
        left, right, (((0,), (0,)), ((), ())), preferred_element_type=jnp.float32
    )


def columns_product(left, right):
    return lax.dot_general(
        left, right, (((1,), (1,)), ((), ())), preferred_element_type=jnp.float32
    )


def assign_slots(chosen, claim_order, expert_count, capacity):
    patches = chosen.shape[0]
    top_count = chosen.shape[1]
    claim_rank = (
        jnp.arange(top_count, dtype=jnp.int32)[None, :] * patches + claim_order[:, None]
    ).T.reshape(-1)
    flat_choice = chosen.T.reshape(-1)
    onehot = (flat_choice[:, None] == jnp.arange(expert_count, dtype=jnp.int32)[None, :]).astype(
        jnp.float32
    )
    earlier = (claim_rank[None, :] < claim_rank[:, None]).astype(jnp.float32)
    counts = jnp.dot(
        earlier, onehot, precision=lax.Precision.HIGHEST, preferred_element_type=jnp.float32
    )
    position = jnp.sum(counts * onehot, axis=1).astype(jnp.int32).reshape(top_count, patches).T
    kept_mask = position < capacity
    flat_slot = chosen * capacity + jnp.minimum(position, capacity - 1)
    return (flat_slot, kept_mask)


def slot_matches(flat_slot, kept_mask, slot_count):
    slot_ids = jnp.arange(slot_count, dtype=jnp.int32)
    return (flat_slot[None, :, :] == slot_ids[:, None, None]) & kept_mask[None, :, :]


def select_gates(logits, chosen, expert_count):
    router_probs = jax.nn.softmax(logits, axis=-1)
    onehot = chosen[:, :, None] == jnp.arange(expert_count, dtype=jnp.int32)[None, None, :]
    return jnp.sum(jnp.where(onehot, router_probs[:, None, :], 0.0), axis=2)


def adam_update(weight, first_state, second, gradient, clip_factor, step_rate, decay_rate):
    scaled = gradient * clip_factor
    first_new = BETA_ONE * first_state + (1.0 - BETA_ONE) * scaled
    second_new = BETA_TWO * second + (1.0 - BETA_TWO) * scaled * scaled
    first_hat = first_new / (1.0 - BETA_ONE**STEP)
    second_hat = second_new / (1.0 - BETA_TWO**STEP)
    weight_new = weight - step_rate * (
        first_hat / (jnp.sqrt(second_hat) + ADAM_EPS) + decay_rate * weight
    )
    return (weight_new, first_new, second_new)


def shards(
    tokens,
    cotangent,
    expert_choice,
    priority,
    projection,
    projection_first,
    projection_second,
    output_weight,
    output_first,
    output_second,
    router_weight,
    router_first,
    router_second,
    vectors,
    vectors_first,
    vectors_second,
    expert_inner,
    inner_first,
    inner_second,
    hidden_bias,
    hidden_first,
    hidden_second,
    expert_outer,
    outer_first,
    outer_second,
    return_bias,
    return_first,
    return_second,
):
    model_width = tokens.shape[2]
    patches = tokens.shape[1]
    experts = lax.axis_size("expert")
    capacity = max(2, patches // experts)
    slot_count = experts * capacity
    score_scale = HEAD_DIM ** (-0.5)
    dense_shards = (
        projection.astype(jnp.bfloat16),
        output_weight.astype(jnp.bfloat16),
        router_weight.astype(jnp.bfloat16),
        vectors.astype(jnp.bfloat16),
    )
    partial_shards = (
        lax.all_gather(dense_shards[0], "expert", axis=0, tiled=True),
        lax.all_gather(dense_shards[1], "expert", axis=0, tiled=True),
        lax.all_gather(dense_shards[2], "expert", axis=0, tiled=True),
        lax.all_gather(dense_shards[3], "expert", axis=1, tiled=True),
    )
    whole_projection, whole_output, whole_router, whole_vectors = (
        lax.all_gather(partial_shards[0], "dp", axis=0, tiled=True),
        lax.all_gather(partial_shards[1], "dp", axis=0, tiled=True),
        lax.all_gather(partial_shards[2], "dp", axis=0, tiled=True),
        lax.all_gather(partial_shards[3], "dp", axis=1, tiled=True),
    )
    inner_low = expert_inner.astype(jnp.bfloat16)
    hidden_low = hidden_bias.astype(jnp.bfloat16)
    outer_low = expert_outer.astype(jnp.bfloat16)
    return_low = return_bias.astype(jnp.bfloat16)
    inner_all, hidden_all, outer_all, return_all = (
        lax.all_gather(inner_low, "dp", axis=2, tiled=True),
        lax.all_gather(hidden_low, "dp", axis=1, tiled=True),
        lax.all_gather(outer_low, "dp", axis=1, tiled=True),
        lax.all_gather(return_low, "dp", axis=1, tiled=True),
    )
    vector_rows = whole_vectors.astype(jnp.float32)
    image_rows = tokens[0].astype(jnp.float32)
    normed_one, norm_back_one = jax.vjp(layer_norm, image_rows, vector_rows[0], vector_rows[1])
    normed_low = normed_one.astype(jnp.bfloat16)
    projected = mixed_dot(normed_low, whole_projection)
    queries = (
        (projected[:, :model_width] + vector_rows[2])
        .astype(jnp.bfloat16)
        .reshape(patches, HEADS, HEAD_DIM)
    )
    key_rows = (
        projected[:, model_width : 2 * model_width]
        .astype(jnp.bfloat16)
        .reshape(patches, HEADS, HEAD_DIM)
    )
    value_rows = (
        (projected[:, 2 * model_width :] + vector_rows[3])
        .astype(jnp.bfloat16)
        .reshape(patches, HEADS, HEAD_DIM)
    )
    scores = (
        jnp.einsum("qhd,khd->hqk", queries, key_rows, preferred_element_type=jnp.float32)
        * score_scale
    )
    score_top = jnp.max(scores, axis=-1, keepdims=True)
    raised = jnp.exp(scores - score_top)
    totals = jnp.sum(raised, axis=-1, keepdims=True)
    attention = raised / totals
    log_total = score_top + jnp.log(totals)
    context = (
        jnp.einsum(
            "hqk,khd->qhd",
            attention.astype(jnp.bfloat16),
            value_rows,
            preferred_element_type=jnp.float32,
        )
        .reshape(patches, model_width)
        .astype(jnp.bfloat16)
    )
    middle = image_rows + (mixed_dot(context, whole_output) + vector_rows[4])
    normed_two, norm_back_two = jax.vjp(layer_norm, middle, vector_rows[5], vector_rows[6])
    second_low = normed_two.astype(jnp.bfloat16)
    logits = mixed_dot(second_low, whole_router)
    chosen = expert_choice[0]

    def gate_choice(values):
        return select_gates(values, chosen, experts)

    gate_values, gate_back = jax.vjp(gate_choice, logits)
    flat_slot, kept_mask = assign_slots(chosen, priority[0], experts, capacity)
    matches = slot_matches(flat_slot, kept_mask, slot_count)
    slot_table = jnp.any(matches, axis=2).astype(jnp.bfloat16)
    dispatched = (
        mixed_dot(slot_table, second_low)
        .astype(jnp.bfloat16)
        .reshape(experts, capacity, model_width)
    )
    arrived = lax.all_to_all(dispatched, "expert", split_axis=0, concat_axis=0, tiled=True).reshape(
        slot_count, model_width
    )
    pre_act = mixed_dot(arrived, inner_all[0]) + hidden_all[0].astype(jnp.float32)
    activated, gelu_back = jax.vjp(smooth_gate, pre_act)
    active_low = activated.astype(jnp.bfloat16)
    expert_out = (mixed_dot(active_low, outer_all[0]) + return_all[0].astype(jnp.float32)).astype(
        jnp.bfloat16
    )
    returned = lax.all_to_all(
        expert_out.reshape(experts, capacity, model_width),
        "expert",
        split_axis=0,
        concat_axis=0,
        tiled=True,
    ).reshape(slot_count, model_width)
    picked = returned[flat_slot].astype(jnp.float32)
    weighted = jnp.where(kept_mask, gate_values, 0.0)
    final = middle + jnp.sum(weighted[:, :, None] * picked, axis=1)
    block_output = final.astype(jnp.bfloat16)[None]
    upstream = cotangent[0].astype(jnp.float32)
    gate_grad = jnp.where(kept_mask, jnp.sum(upstream[:, None, :] * picked, axis=2), 0.0)
    slot_gate = jnp.sum(jnp.where(matches, weighted[None, :, :], 0.0), axis=(1, 2))
    slot_grad = (mixed_dot(slot_table, cotangent[0]) * slot_gate[:, None]).astype(jnp.bfloat16)
    sent_grad = lax.all_to_all(
        slot_grad.reshape(experts, capacity, model_width),
        "expert",
        split_axis=0,
        concat_axis=0,
        tiled=True,
    ).reshape(slot_count, model_width)
    outer_grad = rows_product(active_low, sent_grad)
    return_grad = jnp.sum(sent_grad, axis=0, dtype=jnp.float32)
    active_grad = columns_product(sent_grad, outer_all[0])
    (pre_grad,) = gelu_back(active_grad)
    pre_low = pre_grad.astype(jnp.bfloat16)
    inner_grad = rows_product(arrived, pre_low)
    hidden_grad = jnp.sum(pre_low, axis=0, dtype=jnp.float32)
    row_grad = columns_product(pre_low, inner_all[0]).astype(jnp.bfloat16)
    expert_grads = (
        lax.psum_scatter(
            inner_grad[None].astype(jnp.bfloat16), "dp", scatter_dimension=2, tiled=True
        ).astype(jnp.float32),
        lax.psum_scatter(
            hidden_grad[None].astype(jnp.bfloat16), "dp", scatter_dimension=1, tiled=True
        ).astype(jnp.float32),
        lax.psum_scatter(
            outer_grad[None].astype(jnp.bfloat16), "dp", scatter_dimension=1, tiled=True
        ).astype(jnp.float32),
        lax.psum_scatter(
            return_grad[None].astype(jnp.bfloat16), "dp", scatter_dimension=1, tiled=True
        ).astype(jnp.float32),
    )
    back_rows = lax.all_to_all(
        row_grad.reshape(experts, capacity, model_width),
        "expert",
        split_axis=0,
        concat_axis=0,
        tiled=True,
    ).reshape(slot_count, model_width)
    (logit_grad,) = gate_back(gate_grad)
    logit_low = logit_grad.astype(jnp.bfloat16)
    router_grad = rows_product(second_low, logit_low)
    second_grad = rows_product(slot_table, back_rows) + columns_product(logit_low, whole_router)
    middle_part, gain_two_grad, bias_two_grad = norm_back_two(second_grad)
    middle_grad = upstream + middle_part
    branch_low = middle_grad.astype(jnp.bfloat16)
    output_grad = rows_product(context, branch_low)
    out_bias_grad = jnp.sum(branch_low, axis=0, dtype=jnp.float32)
    context_grad = (
        columns_product(branch_low, whole_output)
        .astype(jnp.bfloat16)
        .reshape(patches, HEADS, HEAD_DIM)
    )
    scores = (
        jnp.einsum("qhd,khd->hqk", queries, key_rows, preferred_element_type=jnp.float32)
        * score_scale
    )
    attention = jnp.exp(scores - log_total)
    attention_grad = jnp.einsum(
        "qhd,khd->hqk", context_grad, value_rows, preferred_element_type=jnp.float32
    )
    value_grad = jnp.einsum(
        "hqk,qhd->khd",
        attention.astype(jnp.bfloat16),
        context_grad,
        preferred_element_type=jnp.float32,
    ).astype(jnp.bfloat16)
    centered = jnp.sum(attention * attention_grad, axis=-1, keepdims=True)
    score_grad = (attention * (attention_grad - centered)).astype(jnp.bfloat16)
    query_grad = (
        (
            jnp.einsum("hqk,khd->qhd", score_grad, key_rows, preferred_element_type=jnp.float32)
            * score_scale
        )
        .astype(jnp.bfloat16)
        .reshape(patches, model_width)
    )
    key_grad = (
        (
            jnp.einsum("hqk,qhd->khd", score_grad, queries, preferred_element_type=jnp.float32)
            * score_scale
        )
        .astype(jnp.bfloat16)
        .reshape(patches, model_width)
    )
    value_flat = value_grad.reshape(patches, model_width)
    joined_grad = jnp.concatenate([query_grad, key_grad, value_flat], axis=1)
    projection_grad = rows_product(normed_low, joined_grad)
    normed_grad = columns_product(joined_grad, whole_projection)
    input_part, gain_one_grad, bias_one_grad = norm_back_one(normed_grad)
    input_grad = (middle_grad + input_part)[None]
    vector_grad = jnp.stack(
        [
            gain_one_grad,
            bias_one_grad,
            jnp.sum(query_grad, axis=0, dtype=jnp.float32),
            jnp.sum(value_flat, axis=0, dtype=jnp.float32),
            out_bias_grad,
            gain_two_grad,
            bias_two_grad,
        ]
    )
    local_grads = (projection_grad, output_grad, router_grad, vector_grad)
    partial_grads = (
        lax.psum_scatter(
            local_grads[0].astype(jnp.bfloat16), "dp", scatter_dimension=0, tiled=True
        ).astype(jnp.float32),
        lax.psum_scatter(
            local_grads[1].astype(jnp.bfloat16), "dp", scatter_dimension=0, tiled=True
        ).astype(jnp.float32),
        lax.psum_scatter(
            local_grads[2].astype(jnp.bfloat16), "dp", scatter_dimension=0, tiled=True
        ).astype(jnp.float32),
        lax.psum_scatter(
            local_grads[3].astype(jnp.bfloat16), "dp", scatter_dimension=1, tiled=True
        ).astype(jnp.float32),
    )
    dense_grads = (
        lax.psum_scatter(
            partial_grads[0].astype(jnp.bfloat16), "expert", scatter_dimension=0, tiled=True
        ).astype(jnp.float32),
        lax.psum_scatter(
            partial_grads[1].astype(jnp.bfloat16), "expert", scatter_dimension=0, tiled=True
        ).astype(jnp.float32),
        lax.psum_scatter(
            partial_grads[2].astype(jnp.bfloat16), "expert", scatter_dimension=0, tiled=True
        ).astype(jnp.float32),
        lax.psum_scatter(
            partial_grads[3].astype(jnp.bfloat16), "expert", scatter_dimension=1, tiled=True
        ).astype(jnp.float32),
    )
    all_grads = tuple(dense_grads) + tuple(expert_grads)
    local_square = jnp.sum(all_grads[0] * all_grads[0])
    for gradient in all_grads[1:]:
        local_square = local_square + jnp.sum(gradient * gradient)
    square_total = lax.psum(local_square, ("dp", "expert"))
    grad_norm = jnp.sqrt(square_total)
    clip_factor = THRESHOLD / jnp.maximum(grad_norm, THRESHOLD)
    projection_next, projection_moment, projection_square = adam_update(
        projection,
        projection_first,
        projection_second,
        all_grads[0],
        clip_factor,
        RATE_PROJECTION,
        DECAY,
    )
    output_next, output_moment, output_square = adam_update(
        output_weight, output_first, output_second, all_grads[1], clip_factor, RATE_OUTPUT, DECAY
    )
    router_next, router_moment, router_square = adam_update(
        router_weight, router_first, router_second, all_grads[2], clip_factor, RATE_ROUTER, DECAY
    )
    vectors_next, vectors_moment, vectors_square = adam_update(
        vectors, vectors_first, vectors_second, all_grads[3], clip_factor, RATE_VECTORS, 0.0
    )
    inner_next, inner_moment, inner_square = adam_update(
        expert_inner, inner_first, inner_second, all_grads[4], clip_factor, RATE_INNER, DECAY
    )
    hidden_next, hidden_moment, hidden_square = adam_update(
        hidden_bias, hidden_first, hidden_second, all_grads[5], clip_factor, RATE_HIDDEN, 0.0
    )
    outer_next, outer_moment, outer_square = adam_update(
        expert_outer, outer_first, outer_second, all_grads[6], clip_factor, RATE_OUTER, DECAY
    )
    return_next, return_moment, return_square = adam_update(
        return_bias, return_first, return_second, all_grads[7], clip_factor, RATE_RETURN, 0.0
    )
    return (
        block_output,
        input_grad,
        grad_norm,
        projection_next,
        projection_moment,
        projection_square,
        output_next,
        output_moment,
        output_square,
        router_next,
        router_moment,
        router_square,
        vectors_next,
        vectors_moment,
        vectors_square,
        inner_next,
        inner_moment,
        inner_square,
        hidden_next,
        hidden_moment,
        hidden_square,
        outer_next,
        outer_moment,
        outer_square,
        return_next,
        return_moment,
        return_square,
    )


MESH = pl.DeviceIdType.MESH
ANY = pl.BlockSpec(memory_space=pl.ANY)
VMEM = pl.BlockSpec(memory_space=pltpu.VMEM)


class Place:
    def __init__(self, dp, experts):
        self.dp, self.experts = dp, experts
        self.ys = 2
        self.zs = experts // 4
        self.a = lax.axis_index("dp")
        self.e = lax.axis_index("expert")
        self.core = lax.rem(self.e, 2)
        self.y = lax.rem(lax.div(self.e, 2), self.ys)
        self.z = lax.div(self.e, 2 * self.ys)

    def chip_of(self, core, dz, s2, s3):
        zz = lax.rem(self.z + dz, self.zs)
        if s2 == s3:
            fa = fy = s2
        elif s2:
            fa, fy = core, 1 - core
        else:
            fa, fy = 1 - core, core
        aa = lax.rem(self.a + fa, 2)
        yy = lax.rem(self.y + fy, 2)
        return aa, zz, yy

    def device(self, core, dz, s2, s3, own_core=None):
        aa, zz, yy = self.chip_of(core, dz, s2, s3)
        c = core if own_core is None else own_core
        return (aa, (zz * self.ys + yy) * 2 + c)

    def flat(self, dev):
        return dev[0] * self.experts + dev[1]

    def chip(self, core, dz, s2, s3):
        aa, zz, yy = self.chip_of(core, dz, s2, s3)
        return (aa * self.zs + zz) * self.ys + yy


def remote(src, dst, send, recv, dev):
    return pltpu.make_async_remote_copy(src_ref=src, dst_ref=dst, send_sem=send, recv_sem=recv, device_id=dev, device_id_type=MESH)


def greet(devices):
    barrier = pltpu.get_barrier_semaphore()
    for dev in devices:
        pl.semaphore_signal(barrier, inc=1, device_id=dev, device_id_type=MESH)
    pl.semaphore_wait(barrier, len(devices))


def split_index(k, zs):
    return k % zs, (k // zs) % 2, k // (2 * zs)


def gather_kernel(dp, experts, in_ref, out_ref, send, recv, csend, crecv, own):
    p = Place(dp, experts)
    zs = p.zs
    c = p.core
    n = 4 * zs
    partner = (p.a, p.e + 1 - 2 * c)
    peers = [p.device(c, dz, 0, 0) for dz in range(1, zs)]
    second = p.device(c, 0, 1, 0)
    third = p.device(c, 0, 0, 1)
    me = p.flat((p.a, p.e))
    mine = pltpu.make_async_copy(in_ref, out_ref.at[me], own)
    mine.start()
    greet(peers + [second, third, partner])
    pending = []

    def block(k):
        if k == 0:
            return me, in_ref
        dz, s2, s3 = split_index(k, zs)
        at = p.flat(p.device(c, (zs - dz) % zs, s2, s3))
        return at, out_ref.at[at]

    def push(k, slot, dev):
        at, src = block(k)
        cp = remote(src, out_ref.at[at], send.at[slot], recv.at[slot], dev)
        cp.start()
        pending.append(cp)

    def hand(k):
        at, src = block(k)
        cp = remote(src, out_ref.at[at], csend.at[k], crecv.at[k], partner)
        cp.start()
        pending.append(cp)

    def arrived(k):
        at, _ = block(k)
        remote(in_ref, out_ref.at[at], send.at[k], recv.at[k], partner).wait_recv()

    for dz in range(1, zs):
        push(0, dz, peers[dz - 1])
    push(0, zs, second)
    push(0, 2 * zs, third)
    hand(0)
    for k in range(1, zs):
        arrived(k)
        push(k, zs + k, second)
        push(k, 2 * zs + k, third)
        hand(k)
    for k in range(zs, 2 * zs):
        arrived(k)
        push(k, 2 * zs + k, third)
        hand(k)
    for k in range(2 * zs, 4 * zs):
        arrived(k)
        hand(k)
    for k in range(n):
        dz, s2, s3 = split_index(k, zs)
        at = p.flat(p.device(1 - c, (zs - dz) % zs, s2, s3))
        remote(in_ref, out_ref.at[at], csend.at[k], crecv.at[k], partner).wait_recv()
    for cp in pending:
        cp.wait_send()
    mine.wait()


def gather_blocks(block, dp, experts, cid):
    n = dp * experts
    return pl.pallas_call(
        functools.partial(gather_kernel, dp, experts),
        out_shape=jax.ShapeDtypeStruct((n,) + block.shape, block.dtype),
        in_specs=[ANY],
        out_specs=ANY,
        scratch_shapes=[
            pltpu.SemaphoreType.DMA((n // 2,)),
            pltpu.SemaphoreType.DMA((n // 2,)),
            pltpu.SemaphoreType.DMA((n // 2,)),
            pltpu.SemaphoreType.DMA((n // 2,)),
            pltpu.SemaphoreType.DMA,
        ],
        compiler_params=pltpu.CompilerParams(collective_id=cid, has_side_effects=True),
        name="gather_dense",
    )(block)


def dispatch_kernel(dp, experts, *refs):
    m = (len(refs) - 5) // 2
    ins, outs = refs[:m], refs[m : 2 * m]
    send, recv, xsend, xrecv, own = refs[2 * m :]
    a = lax.axis_index("dp")
    e = lax.axis_index("expert")
    across = (1 - a, e)
    others = [(a, lax.rem(e + j, experts)) for j in range(1, experts)]
    locals_ = []
    for i in range(m):
        cp = pltpu.make_async_copy(ins[i].at[e], outs[i].at[a, e], own.at[i])
        cp.start()
        locals_.append(cp)
    greet(others + [across])
    pending = []
    for i in range(m):
        cp = remote(ins[i].at[e], outs[i].at[a, e], xsend.at[i, 0], xrecv.at[i, 0], across)
        cp.start()
        pending.append(cp)
        for j in range(1, experts):
            dev = others[j - 1]
            cp = remote(ins[i].at[dev[1]], outs[i].at[a, e], send.at[i, j], recv.at[i, j], dev)
            cp.start()
            pending.append(cp)
    for i in range(m):
        for j in range(1, experts):
            src = lax.rem(e + experts - j, experts)
            here = outs[i].at[a, src]
            remote(here, here, send.at[i, j], recv.at[i, j], across).wait_recv()
            cp = remote(here, here, xsend.at[i, j], xrecv.at[i, j], across)
            cp.start()
            pending.append(cp)
    for i in range(m):
        for j in range(experts):
            src = lax.rem(e + experts - j, experts)
            there = outs[i].at[1 - a, src]
            remote(there, there, xsend.at[i, j], xrecv.at[i, j], across).wait_recv()
    for cp in pending:
        cp.wait_send()
    for cp in locals_:
        cp.wait()


def dispatch(arrays, dp, experts, cid):
    m = len(arrays)
    shape = (dp,) + arrays[0].shape
    return pl.pallas_call(
        functools.partial(dispatch_kernel, dp, experts),
        out_shape=[jax.ShapeDtypeStruct(shape, x.dtype) for x in arrays],
        in_specs=[ANY] * m,
        out_specs=[ANY] * m,
        scratch_shapes=[pltpu.SemaphoreType.DMA((m, experts)) for _ in range(4)] + [pltpu.SemaphoreType.DMA((m,))],
        compiler_params=pltpu.CompilerParams(collective_id=cid, has_side_effects=True),
        name="dispatch_rows",
    )(*arrays)


def return_kernel(dp, experts, *refs):
    m = (len(refs) - 7) // 2
    ins, outs = refs[:m], refs[m : 2 * m]
    mine, theirs, send, recv, xsend, xrecv, load = refs[2 * m :]
    a = lax.axis_index("dp")
    e = lax.axis_index("expert")
    across = (1 - a, e)
    others = [(a, lax.rem(e + j, experts)) for j in range(1, experts)]
    pending = []
    loads = []
    for i in range(m):
        for j in range(experts):
            dst = lax.rem(e + j, experts)
            cp = pltpu.make_async_copy(ins[i].at[a, dst], mine.at[i, j], load.at[i, j])
            cp.start()
            loads.append(cp)
    greet(others + [across])
    order = list(range(1, experts)) + [0]
    for i in range(m):
        for j in order:
            dst = lax.rem(e + j, experts)
            cp = remote(ins[i].at[1 - a, dst], theirs.at[i, j], xsend.at[i, j], xrecv.at[i, j], across)
            cp.start()
            pending.append(cp)
    for i in range(m):
        for j in order:
            loads[i * experts + j].wait()
            remote(theirs.at[i, j], theirs.at[i, j], xsend.at[i, j], xrecv.at[i, j], across).wait_recv()
            mine[i, j] = (mine[i, j].astype(jnp.float32) + theirs[i, j].astype(jnp.float32)).astype(mine.dtype)
            if j == 0:
                last = pltpu.make_async_copy(mine.at[i, j], outs[i].at[e], load.at[i, j])
                last.start()
                loads[i * experts + j] = last
            else:
                cp = remote(mine.at[i, j], outs[i].at[e], send.at[i, j], recv.at[i, j], others[j - 1])
                cp.start()
                pending.append(cp)
    for i in range(m):
        for j in range(1, experts):
            src = lax.rem(e + experts - j, experts)
            remote(outs[i].at[src], outs[i].at[src], send.at[i, j], recv.at[i, j], across).wait_recv()
        loads[i * experts].wait()
    for cp in pending:
        cp.wait_send()


def give_back(arrays, dp, experts, cid):
    m = len(arrays)
    shape = arrays[0].shape[1:]
    return pl.pallas_call(
        functools.partial(return_kernel, dp, experts),
        out_shape=[jax.ShapeDtypeStruct(shape, x.dtype) for x in arrays],
        in_specs=[ANY] * m,
        out_specs=[ANY] * m,
        scratch_shapes=[pltpu.VMEM((m,) + shape, arrays[0].dtype)] * 2
        + [pltpu.SemaphoreType.DMA((m, experts)) for _ in range(5)],
        compiler_params=pltpu.CompilerParams(collective_id=cid, has_side_effects=True, vmem_limit_bytes=32 * 1024 * 1024),
        name="return_rows",
    )(*arrays)


def reduce_kernel(dp, experts, grad_ref, part_ref, out_ref, total_ref, own, rc, r3, r2, rz, fin, row, tiles,
                  load, csend, crecv, send, recv, fsend, frecv, nsend, nrecv):
    p = Place(dp, experts)
    zs = p.zs
    c = p.core
    n = 4 * zs
    world = dp * experts
    half = own.shape[2]
    deep = own.shape[1] // 2
    partner = (p.a, p.e + 1 - 2 * c)
    second = p.device(c, 0, 1, 0)
    third = p.device(c, 0, 0, 1)
    me = p.flat((p.a, p.e))
    everyone = []
    for j in range(1, world):
        other = lax.rem(me + j, world)
        everyone.append((lax.div(other, experts), lax.rem(other, experts)))
    mycols = pl.ds(pl.multiple_of(c * half, 128), half)
    hiscols = pl.ds(pl.multiple_of((1 - c) * half, 128), half)
    order = list(range(2 * zs, n)) + list(range(zs, 2 * zs)) + list(range(1, zs)) + [0]
    loads = {}
    for k in order:
        loads[k] = pltpu.make_async_copy(grad_ref.at[p.chip(c, *split_index(k, zs)), :, mycols], own.at[k], load.at[k])
        loads[k].start()
    greet(everyone)
    pending = []

    def push(src, dst, ss, rs, dev):
        cp = remote(src, dst, ss, rs, dev)
        cp.start()
        pending.append(cp)

    for k in order:
        push(grad_ref.at[p.chip(1 - c, *split_index(k, zs)), :, hiscols], rc.at[k], csend.at[k], crecv.at[k], partner)

    def got(ref, sem):
        remote(ref, ref, sem, sem, partner).wait_recv()

    for k in order:
        loads[k].wait()
        got(rc.at[k], crecv.at[k])
        total = own[k].astype(jnp.float32) + rc[k].astype(jnp.float32)
        if k < 2 * zs:
            got(r3.at[k], recv.at[2 * zs + k])
            total = total + r3[k].astype(jnp.float32)
        if k < zs:
            got(r2.at[k], recv.at[zs + k])
            total = total + r2[k].astype(jnp.float32)
        if k >= 1:
            own[k] = total.astype(own.dtype)
        if k >= 2 * zs:
            push(own.at[k], r3.at[k - 2 * zs], send.at[k], recv.at[k], third)
        elif k >= zs:
            push(own.at[k], r2.at[k - zs], send.at[k], recv.at[k], second)
        elif k >= 1:
            push(own.at[k], rz.at[k - 1], send.at[k], recv.at[k], p.device(c, k, 0, 0))
        else:
            for j in range(1, zs):
                got(rz.at[j - 1], recv.at[j])
                total = total + rz[j - 1].astype(jnp.float32)
            fin[...] = total
    his = pl.ds(pl.multiple_of((1 - c) * deep, 8), deep)
    mine = pl.ds(pl.multiple_of(c * deep, 8), deep)
    push(fin.at[his], row, fsend, frecv, partner)
    square = part_ref[...]
    for i in range(2 * deep // 8):
        for j in range(half // 128):
            v = fin[pl.ds(8 * i, 8), pl.ds(128 * j, 128)]
            square = square + v * v
    tiles[me] = square
    for j in range(1, world):
        push(tiles.at[me], tiles.at[me], nsend.at[j], nrecv.at[j], everyone[j - 1])
    out_ref[:, mycols] = fin[mine, :]
    got(row, frecv)
    out_ref[:, hiscols] = row[...]
    for j in range(1, world):
        src = lax.rem(me + world - j, world)
        got(tiles.at[src], nrecv.at[j])
    total = tiles[0]
    for j in range(1, world):
        total = total + tiles[j]
    total_ref[...] = total
    for cp in pending:
        cp.wait_send()


def reduce_blocks(grads, part, dp, experts, cid):
    n = dp * experts
    chips, rows, cols = grads.shape
    half = cols // 2
    bf = jnp.bfloat16
    return pl.pallas_call(
        functools.partial(reduce_kernel, dp, experts),
        out_shape=[jax.ShapeDtypeStruct((rows // 2, cols), jnp.float32), jax.ShapeDtypeStruct((8, 128), jnp.float32)],
        in_specs=[ANY, VMEM],
        out_specs=[VMEM, VMEM],
        scratch_shapes=[
            pltpu.VMEM((chips, rows, half), bf),
            pltpu.VMEM((chips, rows, half), bf),
            pltpu.VMEM((chips // 2, rows, half), bf),
            pltpu.VMEM((chips // 4, rows, half), bf),
            pltpu.VMEM((chips // 4 - 1, rows, half), bf),
            pltpu.VMEM((rows, half), jnp.float32),
            pltpu.VMEM((rows // 2, half), jnp.float32),
            pltpu.VMEM((n, 8, 128), jnp.float32),
            pltpu.SemaphoreType.DMA((chips,)),
            pltpu.SemaphoreType.DMA((chips,)),
            pltpu.SemaphoreType.DMA((chips,)),
            pltpu.SemaphoreType.DMA((chips,)),
            pltpu.SemaphoreType.DMA((chips,)),
            pltpu.SemaphoreType.DMA,
            pltpu.SemaphoreType.DMA,
            pltpu.SemaphoreType.DMA((n,)),
            pltpu.SemaphoreType.DMA((n,)),
        ],
        compiler_params=pltpu.CompilerParams(collective_id=cid, has_side_effects=True, vmem_limit_bytes=32 * 1024 * 1024),
        name="reduce_dense",
    )(grads, part)


def fits(dp, experts):
    return dp == 2 and experts == 16


def slot_rows(capacity):
    return -(-capacity // 8) * 8


def fast_shards(
    dp,
    experts,
    tokens,
    cotangent,
    expert_choice,
    priority,
    projection,
    projection_first,
    projection_second,
    output_weight,
    output_first,
    output_second,
    router_weight,
    router_first,
    router_second,
    vectors,
    vectors_first,
    vectors_second,
    expert_inner,
    inner_first,
    inner_second,
    hidden_bias,
    hidden_first,
    hidden_second,
    expert_outer,
    outer_first,
    outer_second,
    return_bias,
    return_first,
    return_second,
):
    model_width = tokens.shape[2]
    patches = tokens.shape[1]
    capacity = max(2, patches // experts)
    stride = slot_rows(capacity)
    slot_count = experts * stride
    score_scale = HEAD_DIM ** (-0.5)
    low = jnp.bfloat16
    my_dp = lax.axis_index("dp")
    shard_rows = projection.shape[0]
    wide = 3 * model_width
    used = wide + model_width + experts + vectors.shape[0]
    packed = jnp.concatenate(
        [projection, output_weight, router_weight, vectors.T, jnp.zeros((shard_rows, -used % 128), jnp.float32)], axis=1
    ).astype(low)
    gathered = gather_blocks(packed, dp, experts, 1).reshape(model_width, packed.shape[1])
    whole_projection = gathered[:, :wide]
    whole_output = gathered[:, wide : wide + model_width]
    whole_router = gathered[:, wide + model_width : wide + model_width + experts]
    vector_rows = gathered[:, wide + model_width + experts : used].T.astype(jnp.float32)
    inner_low = expert_inner[0].astype(low)
    hidden_low = hidden_bias[0].astype(low)
    outer_low = expert_outer[0].astype(low)
    return_low = return_bias[0].astype(low)
    image_rows = tokens[0].astype(jnp.float32)
    normed_one, norm_back_one = jax.vjp(layer_norm, image_rows, vector_rows[0], vector_rows[1])
    normed_low = normed_one.astype(low)
    projected = mixed_dot(normed_low, whole_projection)
    queries = (projected[:, :model_width] + vector_rows[2]).astype(low).reshape(patches, HEADS, HEAD_DIM)
    key_rows = projected[:, model_width : 2 * model_width].astype(low).reshape(patches, HEADS, HEAD_DIM)
    value_rows = (projected[:, 2 * model_width :] + vector_rows[3]).astype(low).reshape(patches, HEADS, HEAD_DIM)
    scores = jnp.einsum("qhd,khd->hqk", queries, key_rows, preferred_element_type=jnp.float32) * score_scale
    score_top = jnp.max(scores, axis=-1, keepdims=True)
    raised = jnp.exp(scores - score_top)
    totals = jnp.sum(raised, axis=-1, keepdims=True)
    attention = raised / totals
    log_total = score_top + jnp.log(totals)
    context = (
        jnp.einsum("hqk,khd->qhd", attention.astype(low), value_rows, preferred_element_type=jnp.float32)
        .reshape(patches, model_width)
        .astype(low)
    )
    middle = image_rows + (mixed_dot(context, whole_output) + vector_rows[4])
    normed_two, norm_back_two = jax.vjp(layer_norm, middle, vector_rows[5], vector_rows[6])
    second_low = normed_two.astype(low)
    logits = mixed_dot(second_low, whole_router)
    chosen = expert_choice[0]

    def gate_choice(values):
        return select_gates(values, chosen, experts)

    gate_values, gate_back = jax.vjp(gate_choice, logits)
    packed_slot, kept_mask = assign_slots(chosen, priority[0], experts, capacity)
    flat_slot = packed_slot + chosen * (stride - capacity)
    matches = slot_matches(flat_slot, kept_mask, slot_count)
    slot_table = jnp.any(matches, axis=2).astype(low)
    dispatched = mixed_dot(slot_table, second_low).astype(low).reshape(experts, stride, model_width)
    upstream = cotangent[0].astype(jnp.float32)
    weighted = jnp.where(kept_mask, gate_values, 0.0)
    slot_gate = jnp.sum(jnp.where(matches, weighted[None, :, :], 0.0), axis=(1, 2))
    slot_grad = (mixed_dot(slot_table, cotangent[0]) * slot_gate[:, None]).astype(low)
    arrived, sent_grad = dispatch([dispatched, slot_grad.reshape(experts, stride, model_width)], dp, experts, 2)
    arrived = arrived.reshape(dp * slot_count, model_width)
    sent_grad = sent_grad.reshape(dp * slot_count, model_width)
    pre_act = mixed_dot(arrived, inner_low) + hidden_low.astype(jnp.float32)
    activated, gelu_back = jax.vjp(smooth_gate, pre_act)
    active_low = activated.astype(low)
    part = model_width // dp
    own_columns = jnp.arange(model_width) // part == my_dp
    return_wide = jnp.where(own_columns, jnp.tile(return_low.astype(jnp.float32), dp), 0.0)
    expert_part = (mixed_dot(active_low, outer_low) + return_wide).astype(low)
    active_grad = columns_product(sent_grad, outer_low)
    (pre_grad,) = gelu_back(active_grad)
    pre_low = pre_grad.astype(low)
    row_part = columns_product(pre_low, inner_low).astype(low)
    outer_grad = rows_product(active_low, sent_grad)[None]
    inner_grad = rows_product(arrived, pre_low)[None]
    hidden_grad = jnp.sum(pre_low, axis=0, dtype=jnp.float32)[None]
    return_sums = jnp.sum(sent_grad, axis=0, dtype=jnp.float32)
    return_grad = lax.dynamic_slice_in_dim(return_sums, my_dp * part, part)[None]
    back = (dp, experts, stride, model_width)
    returned, back_rows = give_back([expert_part.reshape(back), row_part.reshape(back)], dp, experts, 3)
    returned = returned.reshape(slot_count, model_width)
    back_rows = back_rows.reshape(slot_count, model_width)
    picked = returned[flat_slot].astype(jnp.float32)
    final = middle + jnp.sum(weighted[:, :, None] * picked, axis=1)
    block_output = final.astype(low)[None]
    gate_grad = jnp.where(kept_mask, jnp.sum(upstream[:, None, :] * picked, axis=2), 0.0)
    (logit_grad,) = gate_back(gate_grad)
    logit_low = logit_grad.astype(low)
    router_grad = rows_product(second_low, logit_low)
    second_grad = rows_product(slot_table, back_rows) + columns_product(logit_low, whole_router)
    middle_part, gain_two_grad, bias_two_grad = norm_back_two(second_grad)
    middle_grad = upstream + middle_part
    branch_low = middle_grad.astype(low)
    output_grad = rows_product(context, branch_low)
    out_bias_grad = jnp.sum(branch_low, axis=0, dtype=jnp.float32)
    context_grad = columns_product(branch_low, whole_output).astype(low).reshape(patches, HEADS, HEAD_DIM)
    scores = jnp.einsum("qhd,khd->hqk", queries, key_rows, preferred_element_type=jnp.float32) * score_scale
    attention = jnp.exp(scores - log_total)
    attention_grad = jnp.einsum("qhd,khd->hqk", context_grad, value_rows, preferred_element_type=jnp.float32)
    value_grad = jnp.einsum(
        "hqk,qhd->khd", attention.astype(low), context_grad, preferred_element_type=jnp.float32
    ).astype(low)
    centered = jnp.sum(attention * attention_grad, axis=-1, keepdims=True)
    score_grad = (attention * (attention_grad - centered)).astype(low)
    query_grad = (
        (jnp.einsum("hqk,khd->qhd", score_grad, key_rows, preferred_element_type=jnp.float32) * score_scale)
        .astype(low)
        .reshape(patches, model_width)
    )
    key_grad = (
        (jnp.einsum("hqk,qhd->khd", score_grad, queries, preferred_element_type=jnp.float32) * score_scale)
        .astype(low)
        .reshape(patches, model_width)
    )
    value_flat = value_grad.reshape(patches, model_width)
    joined_grad = jnp.concatenate([query_grad, key_grad, value_flat], axis=1)
    projection_grad = rows_product(normed_low, joined_grad)
    normed_grad = columns_product(joined_grad, whole_projection)
    input_part, gain_one_grad, bias_one_grad = norm_back_one(normed_grad)
    input_grad = (middle_grad + input_part)[None]
    vector_grad = jnp.stack(
        [
            gain_one_grad,
            bias_one_grad,
            jnp.sum(query_grad, axis=0, dtype=jnp.float32),
            jnp.sum(value_flat, axis=0, dtype=jnp.float32),
            out_bias_grad,
            gain_two_grad,
            bias_two_grad,
        ]
    )
    expert_grads = (inner_grad, hidden_grad, outer_grad, return_grad)
    expert_square = jnp.sum(inner_grad * inner_grad)
    for gradient in expert_grads[1:]:
        expert_square = expert_square + jnp.sum(gradient * gradient)
    chips = dp * experts // 2
    local_grads = jnp.concatenate(
        [
            projection_grad.astype(low),
            output_grad.astype(low),
            router_grad.astype(low),
            vector_grad.T.astype(low),
            jnp.zeros((model_width, -used % 256), low),
        ],
        axis=1,
    ).reshape(chips, 2 * shard_rows, -1)
    square_tile = jnp.where(jnp.arange(1024).reshape(8, 128) == 0, expert_square, 0.0)
    dense, squares = reduce_blocks(local_grads, square_tile, dp, experts, 4)
    grad_norm = jnp.sqrt(jnp.sum(squares))
    clip_factor = THRESHOLD / jnp.maximum(grad_norm, THRESHOLD)
    projection_new = adam_update(
        projection, projection_first, projection_second, dense[:, :wide], clip_factor, RATE_PROJECTION, DECAY
    )
    output_new = adam_update(
        output_weight,
        output_first,
        output_second,
        dense[:, wide : wide + model_width],
        clip_factor,
        RATE_OUTPUT,
        DECAY,
    )
    router_new = adam_update(
        router_weight,
        router_first,
        router_second,
        dense[:, wide + model_width : wide + model_width + experts],
        clip_factor,
        RATE_ROUTER,
        DECAY,
    )
    vectors_new = adam_update(
        vectors,
        vectors_first,
        vectors_second,
        dense[:, wide + model_width + experts : used].T,
        clip_factor,
        RATE_VECTORS,
        0.0,
    )
    inner_new = adam_update(expert_inner, inner_first, inner_second, inner_grad, clip_factor, RATE_INNER, DECAY)
    hidden_new = adam_update(hidden_bias, hidden_first, hidden_second, hidden_grad, clip_factor, RATE_HIDDEN, 0.0)
    outer_new = adam_update(expert_outer, outer_first, outer_second, outer_grad, clip_factor, RATE_OUTER, DECAY)
    return_new = adam_update(return_bias, return_first, return_second, return_grad, clip_factor, RATE_RETURN, 0.0)
    return (
        block_output,
        input_grad,
        grad_norm,
        *projection_new,
        *output_new,
        *router_new,
        *vectors_new,
        *inner_new,
        *hidden_new,
        *outer_new,
        *return_new,
    )


def solution(mesh):
    dp, experts = mesh.shape["dp"], mesh.shape["expert"]
    body = functools.partial(fast_shards, dp, experts) if fits(dp, experts) else shards
    return jax.shard_map(
        body,
        mesh=mesh,
        in_specs=(
            P(("dp", "expert"), None, None),
            P(("dp", "expert"), None, None),
            P(("dp", "expert"), None, None),
            P(("dp", "expert"), None),
            P(("dp", "expert"), None),
            P(("dp", "expert"), None),
            P(("dp", "expert"), None),
            P(("dp", "expert"), None),
            P(("dp", "expert"), None),
            P(("dp", "expert"), None),
            P(("dp", "expert"), None),
            P(("dp", "expert"), None),
            P(("dp", "expert"), None),
            P(None, ("dp", "expert")),
            P(None, ("dp", "expert")),
            P(None, ("dp", "expert")),
            P("expert", None, "dp"),
            P("expert", None, "dp"),
            P("expert", None, "dp"),
            P("expert", "dp"),
            P("expert", "dp"),
            P("expert", "dp"),
            P("expert", "dp", None),
            P("expert", "dp", None),
            P("expert", "dp", None),
            P("expert", "dp"),
            P("expert", "dp"),
            P("expert", "dp"),
        ),
        out_specs=(
            P(("dp", "expert"), None, None),
            P(("dp", "expert"), None, None),
            P(),
            P(("dp", "expert"), None),
            P(("dp", "expert"), None),
            P(("dp", "expert"), None),
            P(("dp", "expert"), None),
            P(("dp", "expert"), None),
            P(("dp", "expert"), None),
            P(("dp", "expert"), None),
            P(("dp", "expert"), None),
            P(("dp", "expert"), None),
            P(None, ("dp", "expert")),
            P(None, ("dp", "expert")),
            P(None, ("dp", "expert")),
            P("expert", None, "dp"),
            P("expert", None, "dp"),
            P("expert", None, "dp"),
            P("expert", "dp"),
            P("expert", "dp"),
            P("expert", "dp"),
            P("expert", "dp", None),
            P("expert", "dp", None),
            P("expert", "dp", None),
            P("expert", "dp"),
            P("expert", "dp"),
            P("expert", "dp"),
        ),
        check_vma=False,
    )
```

```python
import functools

import jax
import jax.numpy as jnp
from jax import lax
from jax.experimental import pallas as pl
from jax.experimental.pallas import tpu as pltpu
from jax.sharding import PartitionSpec as P

HEADS = 12
HEAD_DIM = 64
STEP = 10


NORM_EPS = 1e-06
ADAM_EPS = 1e-08
BETA_ONE = 0.9
BETA_TWO = 0.999
DECAY = 0.1
THRESHOLD = 1.0
RATE_PROJECTION = 0.1
RATE_OUTPUT = 1.0
RATE_ROUTER = 0.05
RATE_VECTORS = 0.5
RATE_INNER = 0.1
RATE_HIDDEN = 0.25
RATE_OUTER = 1.5
RATE_RETURN = 2.0


def layer_norm(values, norm_gain, norm_bias):
    center = values - jnp.mean(values, axis=-1, keepdims=True)
    spread = jnp.mean(center * center, axis=-1, keepdims=True)
    return center * lax.rsqrt(spread + NORM_EPS) * norm_gain + norm_bias


def smooth_gate(values):
    return jax.nn.gelu(values, approximate=True)


def mixed_dot(left, right):
    return jnp.dot(left, right, preferred_element_type=jnp.float32)


def rows_product(left, right):
    return lax.dot_general(
        left, right, (((0,), (0,)), ((), ())), preferred_element_type=jnp.float32
    )


def columns_product(left, right):
    return lax.dot_general(
        left, right, (((1,), (1,)), ((), ())), preferred_element_type=jnp.float32
    )


def assign_slots(chosen, claim_order, expert_count, capacity):
    patches = chosen.shape[0]
    top_count = chosen.shape[1]
    claim_rank = (
        jnp.arange(top_count, dtype=jnp.int32)[None, :] * patches + claim_order[:, None]
    ).T.reshape(-1)
    flat_choice = chosen.T.reshape(-1)
    onehot = (flat_choice[:, None] == jnp.arange(expert_count, dtype=jnp.int32)[None, :]).astype(
        jnp.float32
    )
    earlier = (claim_rank[None, :] < claim_rank[:, None]).astype(jnp.float32)
    counts = jnp.dot(
        earlier, onehot, precision=lax.Precision.HIGHEST, preferred_element_type=jnp.float32
    )
    position = jnp.sum(counts * onehot, axis=1).astype(jnp.int32).reshape(top_count, patches).T
    kept_mask = position < capacity
    flat_slot = chosen * capacity + jnp.minimum(position, capacity - 1)
    return (flat_slot, kept_mask)


def slot_matches(flat_slot, kept_mask, slot_count):
    slot_ids = jnp.arange(slot_count, dtype=jnp.int32)
    return (flat_slot[None, :, :] == slot_ids[:, None, None]) & kept_mask[None, :, :]


def select_gates(logits, chosen, expert_count):
    router_probs = jax.nn.softmax(logits, axis=-1)
    onehot = chosen[:, :, None] == jnp.arange(expert_count, dtype=jnp.int32)[None, None, :]
    return jnp.sum(jnp.where(onehot, router_probs[:, None, :], 0.0), axis=2)


def adam_update(weight, first_state, second, gradient, clip_factor, step_rate, decay_rate):
    scaled = gradient * clip_factor
    first_new = BETA_ONE * first_state + (1.0 - BETA_ONE) * scaled
    second_new = BETA_TWO * second + (1.0 - BETA_TWO) * scaled * scaled
    first_hat = first_new / (1.0 - BETA_ONE**STEP)
    second_hat = second_new / (1.0 - BETA_TWO**STEP)
    weight_new = weight - step_rate * (
        first_hat / (jnp.sqrt(second_hat) + ADAM_EPS) + decay_rate * weight
    )
    return (weight_new, first_new, second_new)


def shards(
    tokens,
    cotangent,
    expert_choice,
    priority,
    projection,
    projection_first,
    projection_second,
    output_weight,
    output_first,
    output_second,
    router_weight,
    router_first,
    router_second,
    vectors,
    vectors_first,
    vectors_second,
    expert_inner,
    inner_first,
    inner_second,
    hidden_bias,
    hidden_first,
    hidden_second,
    expert_outer,
    outer_first,
    outer_second,
    return_bias,
    return_first,
    return_second,
):
    model_width = tokens.shape[2]
    patches = tokens.shape[1]
    experts = lax.axis_size("expert")
    capacity = max(2, patches // experts)
    slot_count = experts * capacity
    score_scale = HEAD_DIM ** (-0.5)
    dense_shards = (
        projection.astype(jnp.bfloat16),
        output_weight.astype(jnp.bfloat16),
        router_weight.astype(jnp.bfloat16),
        vectors.astype(jnp.bfloat16),
    )
    partial_shards = (
        lax.all_gather(dense_shards[0], "expert", axis=0, tiled=True),
        lax.all_gather(dense_shards[1], "expert", axis=0, tiled=True),
        lax.all_gather(dense_shards[2], "expert", axis=0, tiled=True),
        lax.all_gather(dense_shards[3], "expert", axis=1, tiled=True),
    )
    whole_projection, whole_output, whole_router, whole_vectors = (
        lax.all_gather(partial_shards[0], "dp", axis=0, tiled=True),
        lax.all_gather(partial_shards[1], "dp", axis=0, tiled=True),
        lax.all_gather(partial_shards[2], "dp", axis=0, tiled=True),
        lax.all_gather(partial_shards[3], "dp", axis=1, tiled=True),
    )
    inner_low = expert_inner.astype(jnp.bfloat16)
    hidden_low = hidden_bias.astype(jnp.bfloat16)
    outer_low = expert_outer.astype(jnp.bfloat16)
    return_low = return_bias.astype(jnp.bfloat16)
    inner_all, hidden_all, outer_all, return_all = (
        lax.all_gather(inner_low, "dp", axis=2, tiled=True),
        lax.all_gather(hidden_low, "dp", axis=1, tiled=True),
        lax.all_gather(outer_low, "dp", axis=1, tiled=True),
        lax.all_gather(return_low, "dp", axis=1, tiled=True),
    )
    vector_rows = whole_vectors.astype(jnp.float32)
    image_rows = tokens[0].astype(jnp.float32)
    normed_one, norm_back_one = jax.vjp(layer_norm, image_rows, vector_rows[0], vector_rows[1])
    normed_low = normed_one.astype(jnp.bfloat16)
    projected = mixed_dot(normed_low, whole_projection)
    queries = (
        (projected[:, :model_width] + vector_rows[2])
        .astype(jnp.bfloat16)
        .reshape(patches, HEADS, HEAD_DIM)
    )
    key_rows = (
        projected[:, model_width : 2 * model_width]
        .astype(jnp.bfloat16)
        .reshape(patches, HEADS, HEAD_DIM)
    )
    value_rows = (
        (projected[:, 2 * model_width :] + vector_rows[3])
        .astype(jnp.bfloat16)
        .reshape(patches, HEADS, HEAD_DIM)
    )
    scores = (
        jnp.einsum("qhd,khd->hqk", queries, key_rows, preferred_element_type=jnp.float32)
        * score_scale
    )
    score_top = jnp.max(scores, axis=-1, keepdims=True)
    raised = jnp.exp(scores - score_top)
    totals = jnp.sum(raised, axis=-1, keepdims=True)
    attention = raised / totals
    log_total = score_top + jnp.log(totals)
    context = (
        jnp.einsum(
            "hqk,khd->qhd",
            attention.astype(jnp.bfloat16),
            value_rows,
            preferred_element_type=jnp.float32,
        )
        .reshape(patches, model_width)
        .astype(jnp.bfloat16)
    )
    middle = image_rows + (mixed_dot(context, whole_output) + vector_rows[4])
    normed_two, norm_back_two = jax.vjp(layer_norm, middle, vector_rows[5], vector_rows[6])
    second_low = normed_two.astype(jnp.bfloat16)
    logits = mixed_dot(second_low, whole_router)
    chosen = expert_choice[0]

    def gate_choice(values):
        return select_gates(values, chosen, experts)

    gate_values, gate_back = jax.vjp(gate_choice, logits)
    flat_slot, kept_mask = assign_slots(chosen, priority[0], experts, capacity)
    matches = slot_matches(flat_slot, kept_mask, slot_count)
    slot_table = jnp.any(matches, axis=2).astype(jnp.bfloat16)
    dispatched = (
        mixed_dot(slot_table, second_low)
        .astype(jnp.bfloat16)
        .reshape(experts, capacity, model_width)
    )
    arrived = lax.all_to_all(dispatched, "expert", split_axis=0, concat_axis=0, tiled=True).reshape(
        slot_count, model_width
    )
    pre_act = mixed_dot(arrived, inner_all[0]) + hidden_all[0].astype(jnp.float32)
    activated, gelu_back = jax.vjp(smooth_gate, pre_act)
    active_low = activated.astype(jnp.bfloat16)
    expert_out = (mixed_dot(active_low, outer_all[0]) + return_all[0].astype(jnp.float32)).astype(
        jnp.bfloat16
    )
    returned = lax.all_to_all(
        expert_out.reshape(experts, capacity, model_width),
        "expert",
        split_axis=0,
        concat_axis=0,
        tiled=True,
    ).reshape(slot_count, model_width)
    picked = returned[flat_slot].astype(jnp.float32)
    weighted = jnp.where(kept_mask, gate_values, 0.0)
    final = middle + jnp.sum(weighted[:, :, None] * picked, axis=1)
    block_output = final.astype(jnp.bfloat16)[None]
    upstream = cotangent[0].astype(jnp.float32)
    gate_grad = jnp.where(kept_mask, jnp.sum(upstream[:, None, :] * picked, axis=2), 0.0)
    slot_gate = jnp.sum(jnp.where(matches, weighted[None, :, :], 0.0), axis=(1, 2))
    slot_grad = (mixed_dot(slot_table, cotangent[0]) * slot_gate[:, None]).astype(jnp.bfloat16)
    sent_grad = lax.all_to_all(
        slot_grad.reshape(experts, capacity, model_width),
        "expert",
        split_axis=0,
        concat_axis=0,
        tiled=True,
    ).reshape(slot_count, model_width)
    outer_grad = rows_product(active_low, sent_grad)
    return_grad = jnp.sum(sent_grad, axis=0, dtype=jnp.float32)
    active_grad = columns_product(sent_grad, outer_all[0])
    (pre_grad,) = gelu_back(active_grad)
    pre_low = pre_grad.astype(jnp.bfloat16)
    inner_grad = rows_product(arrived, pre_low)
    hidden_grad = jnp.sum(pre_low, axis=0, dtype=jnp.float32)
    row_grad = columns_product(pre_low, inner_all[0]).astype(jnp.bfloat16)
    expert_grads = (
        lax.psum_scatter(
            inner_grad[None].astype(jnp.bfloat16), "dp", scatter_dimension=2, tiled=True
        ).astype(jnp.float32),
        lax.psum_scatter(
            hidden_grad[None].astype(jnp.bfloat16), "dp", scatter_dimension=1, tiled=True
        ).astype(jnp.float32),
        lax.psum_scatter(
            outer_grad[None].astype(jnp.bfloat16), "dp", scatter_dimension=1, tiled=True
        ).astype(jnp.float32),
        lax.psum_scatter(
            return_grad[None].astype(jnp.bfloat16), "dp", scatter_dimension=1, tiled=True
        ).astype(jnp.float32),
    )
    back_rows = lax.all_to_all(
        row_grad.reshape(experts, capacity, model_width),
        "expert",
        split_axis=0,
        concat_axis=0,
        tiled=True,
    ).reshape(slot_count, model_width)
    (logit_grad,) = gate_back(gate_grad)
    logit_low = logit_grad.astype(jnp.bfloat16)
    router_grad = rows_product(second_low, logit_low)
    second_grad = rows_product(slot_table, back_rows) + columns_product(logit_low, whole_router)
    middle_part, gain_two_grad, bias_two_grad = norm_back_two(second_grad)
    middle_grad = upstream + middle_part
    branch_low = middle_grad.astype(jnp.bfloat16)
    output_grad = rows_product(context, branch_low)
    out_bias_grad = jnp.sum(branch_low, axis=0, dtype=jnp.float32)
    context_grad = (
        columns_product(branch_low, whole_output)
        .astype(jnp.bfloat16)
        .reshape(patches, HEADS, HEAD_DIM)
    )
    scores = (
        jnp.einsum("qhd,khd->hqk", queries, key_rows, preferred_element_type=jnp.float32)
        * score_scale
    )
    attention = jnp.exp(scores - log_total)
    attention_grad = jnp.einsum(
        "qhd,khd->hqk", context_grad, value_rows, preferred_element_type=jnp.float32
    )
    value_grad = jnp.einsum(
        "hqk,qhd->khd",
        attention.astype(jnp.bfloat16),
        context_grad,
        preferred_element_type=jnp.float32,
    ).astype(jnp.bfloat16)
    centered = jnp.sum(attention * attention_grad, axis=-1, keepdims=True)
    score_grad = (attention * (attention_grad - centered)).astype(jnp.bfloat16)
    query_grad = (
        (
            jnp.einsum("hqk,khd->qhd", score_grad, key_rows, preferred_element_type=jnp.float32)
            * score_scale
        )
        .astype(jnp.bfloat16)
        .reshape(patches, model_width)
    )
    key_grad = (
        (
            jnp.einsum("hqk,qhd->khd", score_grad, queries, preferred_element_type=jnp.float32)
            * score_scale
        )
        .astype(jnp.bfloat16)
        .reshape(patches, model_width)
    )
    value_flat = value_grad.reshape(patches, model_width)
    joined_grad = jnp.concatenate([query_grad, key_grad, value_flat], axis=1)
    projection_grad = rows_product(normed_low, joined_grad)
    normed_grad = columns_product(joined_grad, whole_projection)
    input_part, gain_one_grad, bias_one_grad = norm_back_one(normed_grad)
    input_grad = (middle_grad + input_part)[None]
    vector_grad = jnp.stack(
        [
            gain_one_grad,
            bias_one_grad,
            jnp.sum(query_grad, axis=0, dtype=jnp.float32),
            jnp.sum(value_flat, axis=0, dtype=jnp.float32),
            out_bias_grad,
            gain_two_grad,
            bias_two_grad,
        ]
    )
    local_grads = (projection_grad, output_grad, router_grad, vector_grad)
    partial_grads = (
        lax.psum_scatter(
            local_grads[0].astype(jnp.bfloat16), "dp", scatter_dimension=0, tiled=True
        ).astype(jnp.float32),
        lax.psum_scatter(
            local_grads[1].astype(jnp.bfloat16), "dp", scatter_dimension=0, tiled=True
        ).astype(jnp.float32),
        lax.psum_scatter(
            local_grads[2].astype(jnp.bfloat16), "dp", scatter_dimension=0, tiled=True
        ).astype(jnp.float32),
        lax.psum_scatter(
            local_grads[3].astype(jnp.bfloat16), "dp", scatter_dimension=1, tiled=True
        ).astype(jnp.float32),
    )
    dense_grads = (
        lax.psum_scatter(
            partial_grads[0].astype(jnp.bfloat16), "expert", scatter_dimension=0, tiled=True
        ).astype(jnp.float32),
        lax.psum_scatter(
            partial_grads[1].astype(jnp.bfloat16), "expert", scatter_dimension=0, tiled=True
        ).astype(jnp.float32),
        lax.psum_scatter(
            partial_grads[2].astype(jnp.bfloat16), "expert", scatter_dimension=0, tiled=True
        ).astype(jnp.float32),
        lax.psum_scatter(
            partial_grads[3].astype(jnp.bfloat16), "expert", scatter_dimension=1, tiled=True
        ).astype(jnp.float32),
    )
    all_grads = tuple(dense_grads) + tuple(expert_grads)
    local_square = jnp.sum(all_grads[0] * all_grads[0])
    for gradient in all_grads[1:]:
        local_square = local_square + jnp.sum(gradient * gradient)
    square_total = lax.psum(local_square, ("dp", "expert"))
    grad_norm = jnp.sqrt(square_total)
    clip_factor = THRESHOLD / jnp.maximum(grad_norm, THRESHOLD)
    projection_next, projection_moment, projection_square = adam_update(
        projection,
        projection_first,
        projection_second,
        all_grads[0],
        clip_factor,
        RATE_PROJECTION,
        DECAY,
    )
    output_next, output_moment, output_square = adam_update(
        output_weight, output_first, output_second, all_grads[1], clip_factor, RATE_OUTPUT, DECAY
    )
    router_next, router_moment, router_square = adam_update(
        router_weight, router_first, router_second, all_grads[2], clip_factor, RATE_ROUTER, DECAY
    )
    vectors_next, vectors_moment, vectors_square = adam_update(
        vectors, vectors_first, vectors_second, all_grads[3], clip_factor, RATE_VECTORS, 0.0
    )
    inner_next, inner_moment, inner_square = adam_update(
        expert_inner, inner_first, inner_second, all_grads[4], clip_factor, RATE_INNER, DECAY
    )
    hidden_next, hidden_moment, hidden_square = adam_update(
        hidden_bias, hidden_first, hidden_second, all_grads[5], clip_factor, RATE_HIDDEN, 0.0
    )
    outer_next, outer_moment, outer_square = adam_update(
        expert_outer, outer_first, outer_second, all_grads[6], clip_factor, RATE_OUTER, DECAY
    )
    return_next, return_moment, return_square = adam_update(
        return_bias, return_first, return_second, all_grads[7], clip_factor, RATE_RETURN, 0.0
    )
    return (
        block_output,
        input_grad,
        grad_norm,
        projection_next,
        projection_moment,
        projection_square,
        output_next,
        output_moment,
        output_square,
        router_next,
        router_moment,
        router_square,
        vectors_next,
        vectors_moment,
        vectors_square,
        inner_next,
        inner_moment,
        inner_square,
        hidden_next,
        hidden_moment,
        hidden_square,
        outer_next,
        outer_moment,
        outer_square,
        return_next,
        return_moment,
        return_square,
    )


MESH = pl.DeviceIdType.MESH
ANY = pl.BlockSpec(memory_space=pl.ANY)
VMEM = pl.BlockSpec(memory_space=pltpu.VMEM)


class Place:
    def __init__(self, dp, experts):
        self.dp, self.experts = dp, experts
        self.ys = 2
        self.zs = experts // 4
        self.a = lax.axis_index("dp")
        self.e = lax.axis_index("expert")
        self.core = lax.rem(self.e, 2)
        self.y = lax.rem(lax.div(self.e, 2), self.ys)
        self.z = lax.div(self.e, 2 * self.ys)

    def chip_of(self, core, dz, s2, s3):
        zz = lax.rem(self.z + dz, self.zs)
        if s2 == s3:
            fa = fy = s2
        elif s2:
            fa, fy = core, 1 - core
        else:
            fa, fy = 1 - core, core
        aa = lax.rem(self.a + fa, 2)
        yy = lax.rem(self.y + fy, 2)
        return aa, zz, yy

    def device(self, core, dz, s2, s3, own_core=None):
        aa, zz, yy = self.chip_of(core, dz, s2, s3)
        c = core if own_core is None else own_core
        return (aa, (zz * self.ys + yy) * 2 + c)

    def flat(self, dev):
        return dev[0] * self.experts + dev[1]

    def chip(self, core, dz, s2, s3):
        aa, zz, yy = self.chip_of(core, dz, s2, s3)
        return (aa * self.zs + zz) * self.ys + yy


def remote(src, dst, send, recv, dev):
    return pltpu.make_async_remote_copy(src_ref=src, dst_ref=dst, send_sem=send, recv_sem=recv, device_id=dev, device_id_type=MESH)


def greet(devices):
    barrier = pltpu.get_barrier_semaphore()
    for dev in devices:
        pl.semaphore_signal(barrier, inc=1, device_id=dev, device_id_type=MESH)
    pl.semaphore_wait(barrier, len(devices))


def split_index(k, zs):
    return k % zs, (k // zs) % 2, k // (2 * zs)


def gather_kernel(dp, experts, in_ref, out_ref, send, recv, csend, crecv, own):
    p = Place(dp, experts)
    zs = p.zs
    c = p.core
    n = 4 * zs
    partner = (p.a, p.e + 1 - 2 * c)
    peers = [p.device(c, dz, 0, 0) for dz in range(1, zs)]
    second = p.device(c, 0, 1, 0)
    third = p.device(c, 0, 0, 1)
    me = p.flat((p.a, p.e))
    mine = pltpu.make_async_copy(in_ref, out_ref.at[me], own)
    mine.start()
    greet(peers + [second, third, partner])
    pending = []

    def block(k):
        if k == 0:
            return me, in_ref
        dz, s2, s3 = split_index(k, zs)
        at = p.flat(p.device(c, (zs - dz) % zs, s2, s3))
        return at, out_ref.at[at]

    def push(k, slot, dev):
        at, src = block(k)
        cp = remote(src, out_ref.at[at], send.at[slot], recv.at[slot], dev)
        cp.start()
        pending.append(cp)

    def hand(k):
        at, src = block(k)
        cp = remote(src, out_ref.at[at], csend.at[k], crecv.at[k], partner)
        cp.start()
        pending.append(cp)

    def arrived(k):
        at, _ = block(k)
        remote(in_ref, out_ref.at[at], send.at[k], recv.at[k], partner).wait_recv()

    for dz in range(1, zs):
        push(0, dz, peers[dz - 1])
    push(0, zs, second)
    push(0, 2 * zs, third)
    hand(0)
    for k in range(1, zs):
        arrived(k)
        push(k, zs + k, second)
        push(k, 2 * zs + k, third)
        hand(k)
    for k in range(zs, 2 * zs):
        arrived(k)
        push(k, 2 * zs + k, third)
        hand(k)
    for k in range(2 * zs, 4 * zs):
        arrived(k)
        hand(k)
    for k in range(n):
        dz, s2, s3 = split_index(k, zs)
        at = p.flat(p.device(1 - c, (zs - dz) % zs, s2, s3))
        remote(in_ref, out_ref.at[at], csend.at[k], crecv.at[k], partner).wait_recv()
    for cp in pending:
        cp.wait_send()
    mine.wait()


def gather_blocks(block, dp, experts, cid):
    n = dp * experts
    return pl.pallas_call(
        functools.partial(gather_kernel, dp, experts),
        out_shape=jax.ShapeDtypeStruct((n,) + block.shape, block.dtype),
        in_specs=[ANY],
        out_specs=ANY,
        scratch_shapes=[
            pltpu.SemaphoreType.DMA((n // 2,)),
            pltpu.SemaphoreType.DMA((n // 2,)),
            pltpu.SemaphoreType.DMA((n // 2,)),
            pltpu.SemaphoreType.DMA((n // 2,)),
            pltpu.SemaphoreType.DMA,
        ],
        compiler_params=pltpu.CompilerParams(collective_id=cid, has_side_effects=True),
        name="gather_dense",
    )(block)


def dispatch_kernel(dp, experts, *refs):
    m = (len(refs) - 5) // 2
    ins, outs = refs[:m], refs[m : 2 * m]
    send, recv, xsend, xrecv, own = refs[2 * m :]
    a = lax.axis_index("dp")
    e = lax.axis_index("expert")
    across = (1 - a, e)
    others = [(a, lax.rem(e + j, experts)) for j in range(1, experts)]
    locals_ = []
    for i in range(m):
        cp = pltpu.make_async_copy(ins[i].at[e], outs[i].at[a, e], own.at[i])
        cp.start()
        locals_.append(cp)
    greet(others + [across])
    pending = []
    for i in range(m):
        cp = remote(ins[i].at[e], outs[i].at[a, e], xsend.at[i, 0], xrecv.at[i, 0], across)
        cp.start()
        pending.append(cp)
        for j in range(1, experts):
            dev = others[j - 1]
            cp = remote(ins[i].at[dev[1]], outs[i].at[a, e], send.at[i, j], recv.at[i, j], dev)
            cp.start()
            pending.append(cp)
    for i in range(m):
        for j in range(1, experts):
            src = lax.rem(e + experts - j, experts)
            here = outs[i].at[a, src]
            remote(here, here, send.at[i, j], recv.at[i, j], across).wait_recv()
            cp = remote(here, here, xsend.at[i, j], xrecv.at[i, j], across)
            cp.start()
            pending.append(cp)
    for i in range(m):
        for j in range(experts):
            src = lax.rem(e + experts - j, experts)
            there = outs[i].at[1 - a, src]
            remote(there, there, xsend.at[i, j], xrecv.at[i, j], across).wait_recv()
    for cp in pending:
        cp.wait_send()
    for cp in locals_:
        cp.wait()


def dispatch(arrays, dp, experts, cid):
    m = len(arrays)
    shape = (dp,) + arrays[0].shape
    return pl.pallas_call(
        functools.partial(dispatch_kernel, dp, experts),
        out_shape=[jax.ShapeDtypeStruct(shape, x.dtype) for x in arrays],
        in_specs=[ANY] * m,
        out_specs=[ANY] * m,
        scratch_shapes=[pltpu.SemaphoreType.DMA((m, experts)) for _ in range(4)] + [pltpu.SemaphoreType.DMA((m,))],
        compiler_params=pltpu.CompilerParams(collective_id=cid, has_side_effects=True),
        name="dispatch_rows",
    )(*arrays)


def return_kernel(dp, experts, *refs):
    m = (len(refs) - 7) // 2
    ins, outs = refs[:m], refs[m : 2 * m]
    mine, theirs, send, recv, xsend, xrecv, load = refs[2 * m :]
    a = lax.axis_index("dp")
    e = lax.axis_index("expert")
    across = (1 - a, e)
    others = [(a, lax.rem(e + j, experts)) for j in range(1, experts)]
    pending = []
    loads = []
    for i in range(m):
        for j in range(experts):
            dst = lax.rem(e + j, experts)
            cp = pltpu.make_async_copy(ins[i].at[a, dst], mine.at[i, j], load.at[i, j])
            cp.start()
            loads.append(cp)
    greet(others + [across])
    order = list(range(1, experts)) + [0]
    for i in range(m):
        for j in order:
            dst = lax.rem(e + j, experts)
            cp = remote(ins[i].at[1 - a, dst], theirs.at[i, j], xsend.at[i, j], xrecv.at[i, j], across)
            cp.start()
            pending.append(cp)
    for i in range(m):
        for j in order:
            loads[i * experts + j].wait()
            remote(theirs.at[i, j], theirs.at[i, j], xsend.at[i, j], xrecv.at[i, j], across).wait_recv()
            mine[i, j] = (mine[i, j].astype(jnp.float32) + theirs[i, j].astype(jnp.float32)).astype(mine.dtype)
            if j == 0:
                last = pltpu.make_async_copy(mine.at[i, j], outs[i].at[e], load.at[i, j])
                last.start()
                loads[i * experts + j] = last
            else:
                cp = remote(mine.at[i, j], outs[i].at[e], send.at[i, j], recv.at[i, j], others[j - 1])
                cp.start()
                pending.append(cp)
    for i in range(m):
        for j in range(1, experts):
            src = lax.rem(e + experts - j, experts)
            remote(outs[i].at[src], outs[i].at[src], send.at[i, j], recv.at[i, j], across).wait_recv()
        loads[i * experts].wait()
    for cp in pending:
        cp.wait_send()


def give_back(arrays, dp, experts, cid):
    m = len(arrays)
    shape = arrays[0].shape[1:]
    return pl.pallas_call(
        functools.partial(return_kernel, dp, experts),
        out_shape=[jax.ShapeDtypeStruct(shape, x.dtype) for x in arrays],
        in_specs=[ANY] * m,
        out_specs=[ANY] * m,
        scratch_shapes=[pltpu.VMEM((m,) + shape, arrays[0].dtype)] * 2
        + [pltpu.SemaphoreType.DMA((m, experts)) for _ in range(5)],
        compiler_params=pltpu.CompilerParams(collective_id=cid, has_side_effects=True, vmem_limit_bytes=32 * 1024 * 1024),
        name="return_rows",
    )(*arrays)


def reduce_kernel(dp, experts, grad_ref, part_ref, out_ref, total_ref, own, rc, r3, r2, rz, fin, row, tiles,
                  load, csend, crecv, send, recv, fsend, frecv, nsend, nrecv):
    p = Place(dp, experts)
    zs = p.zs
    c = p.core
    n = 4 * zs
    world = dp * experts
    half = own.shape[2]
    deep = own.shape[1] // 2
    partner = (p.a, p.e + 1 - 2 * c)
    second = p.device(c, 0, 1, 0)
    third = p.device(c, 0, 0, 1)
    me = p.flat((p.a, p.e))
    everyone = []
    for j in range(1, world):
        other = lax.rem(me + j, world)
        everyone.append((lax.div(other, experts), lax.rem(other, experts)))
    mycols = pl.ds(pl.multiple_of(c * half, 128), half)
    hiscols = pl.ds(pl.multiple_of((1 - c) * half, 128), half)
    order = list(range(2 * zs, n)) + list(range(zs, 2 * zs)) + list(range(1, zs)) + [0]
    loads = {}
    for k in order:
        loads[k] = pltpu.make_async_copy(grad_ref.at[p.chip(c, *split_index(k, zs)), :, mycols], own.at[k], load.at[k])
        loads[k].start()
    greet(everyone)
    pending = []

    def push(src, dst, ss, rs, dev):
        cp = remote(src, dst, ss, rs, dev)
        cp.start()
        pending.append(cp)

    for k in order:
        push(grad_ref.at[p.chip(1 - c, *split_index(k, zs)), :, hiscols], rc.at[k], csend.at[k], crecv.at[k], partner)

    def got(ref, sem):
        remote(ref, ref, sem, sem, partner).wait_recv()

    for k in order:
        loads[k].wait()
        got(rc.at[k], crecv.at[k])
        total = own[k].astype(jnp.float32) + rc[k].astype(jnp.float32)
        if k < 2 * zs:
            got(r3.at[k], recv.at[2 * zs + k])
            total = total + r3[k].astype(jnp.float32)
        if k < zs:
            got(r2.at[k], recv.at[zs + k])
            total = total + r2[k].astype(jnp.float32)
        if k >= 1:
            own[k] = total.astype(own.dtype)
        if k >= 2 * zs:
            push(own.at[k], r3.at[k - 2 * zs], send.at[k], recv.at[k], third)
        elif k >= zs:
            push(own.at[k], r2.at[k - zs], send.at[k], recv.at[k], second)
        elif k >= 1:
            push(own.at[k], rz.at[k - 1], send.at[k], recv.at[k], p.device(c, k, 0, 0))
        else:
            for j in range(1, zs):
                got(rz.at[j - 1], recv.at[j])
                total = total + rz[j - 1].astype(jnp.float32)
            fin[...] = total
    his = pl.ds(pl.multiple_of((1 - c) * deep, 8), deep)
    mine = pl.ds(pl.multiple_of(c * deep, 8), deep)
    push(fin.at[his], row, fsend, frecv, partner)
    square = part_ref[...]
    for i in range(2 * deep // 8):
        for j in range(half // 128):
            v = fin[pl.ds(8 * i, 8), pl.ds(128 * j, 128)]
            square = square + v * v
    tiles[me] = square
    for j in range(1, world):
        push(tiles.at[me], tiles.at[me], nsend.at[j], nrecv.at[j], everyone[j - 1])
    out_ref[:, mycols] = fin[mine, :]
    got(row, frecv)
    out_ref[:, hiscols] = row[...]
    for j in range(1, world):
        src = lax.rem(me + world - j, world)
        got(tiles.at[src], nrecv.at[j])
    total = tiles[0]
    for j in range(1, world):
        total = total + tiles[j]
    total_ref[...] = total
    for cp in pending:
        cp.wait_send()


def reduce_blocks(grads, part, dp, experts, cid):
    n = dp * experts
    chips, rows, cols = grads.shape
    half = cols // 2
    bf = jnp.bfloat16
    return pl.pallas_call(
        functools.partial(reduce_kernel, dp, experts),
        out_shape=[jax.ShapeDtypeStruct((rows // 2, cols), jnp.float32), jax.ShapeDtypeStruct((8, 128), jnp.float32)],
        in_specs=[ANY, VMEM],
        out_specs=[VMEM, VMEM],
        scratch_shapes=[
            pltpu.VMEM((chips, rows, half), bf),
            pltpu.VMEM((chips, rows, half), bf),
            pltpu.VMEM((chips // 2, rows, half), bf),
            pltpu.VMEM((chips // 4, rows, half), bf),
            pltpu.VMEM((chips // 4 - 1, rows, half), bf),
            pltpu.VMEM((rows, half), jnp.float32),
            pltpu.VMEM((rows // 2, half), jnp.float32),
            pltpu.VMEM((n, 8, 128), jnp.float32),
            pltpu.SemaphoreType.DMA((chips,)),
            pltpu.SemaphoreType.DMA((chips,)),
            pltpu.SemaphoreType.DMA((chips,)),
            pltpu.SemaphoreType.DMA((chips,)),
            pltpu.SemaphoreType.DMA((chips,)),
            pltpu.SemaphoreType.DMA,
            pltpu.SemaphoreType.DMA,
            pltpu.SemaphoreType.DMA((n,)),
            pltpu.SemaphoreType.DMA((n,)),
        ],
        compiler_params=pltpu.CompilerParams(collective_id=cid, has_side_effects=True, vmem_limit_bytes=32 * 1024 * 1024),
        name="reduce_dense",
    )(grads, part)


LANES = 128


def nn(left, right):
    return lax.dot_general(left, right, (((1,), (0,)), ((), ())), preferred_element_type=jnp.float32)


def nt(left, right):
    return lax.dot_general(left, right, (((1,), (1,)), ((), ())), preferred_element_type=jnp.float32)


def lane_ids(rows, start=0):
    return lax.broadcasted_iota(jnp.int32, (rows, LANES), 1) + start


def row_parts(count, size):
    return [pl.ds(i * size, size) for i in range(count // size)]


def norm_parts(values):
    center = values - jnp.mean(values, axis=-1, keepdims=True)
    inverse = lax.rsqrt(jnp.mean(center * center, axis=-1, keepdims=True) + NORM_EPS)
    return center * inverse, inverse


def vector_table(weights, width):
    return jnp.transpose(weights[:, 4 * width :].astype(jnp.float32))


def forward_kernel(
    experts,
    capacity,
    chunk,
    tok_ref,
    cot_ref,
    choice_ref,
    rank_col,
    rank_row,
    weights_any,
    rows_ref,
    dy_ref,
    qkv_ref,
    ctx_ref,
    mid_ref,
    second_ref,
    stat_ref,
    aux_ref,
    probs_ref,
    weights,
    vec,
    normed,
    load,
):
    low = jnp.bfloat16
    patches, width = tok_ref.shape
    fetch = pltpu.make_async_copy(weights_any, weights, load)
    fetch.start()
    lanes = lane_ids(patches)
    first, other = choice_ref[:, 0:1], choice_ref[:, 1:2]
    is_first, is_other = lanes == first, lanes == other
    before = (rank_row[...] < rank_col[...]).astype(jnp.float32).astype(low)
    hot = (is_first | (lanes == other + experts)).astype(jnp.float32)
    counts = nn(before, hot.astype(low))
    totals = jnp.sum(hot, axis=0, keepdims=True)
    place_first = jnp.sum(jnp.where(is_first, counts, 0.0), axis=1, keepdims=True)
    place_other = jnp.sum(
        jnp.where(lanes == other + experts, counts, 0.0) + jnp.where(is_other, totals, 0.0), axis=1, keepdims=True
    )
    fetch.wait()
    vec[...] = vector_table(weights, width)

    def row(i):
        return vec[experts + i : experts + i + 1, :]

    for part in row_parts(patches, chunk):
        unit, _ = norm_parts(tok_ref[part, :].astype(jnp.float32))
        normed[part, :] = (unit * row(0) + row(1)).astype(low)
    third = 256
    for base, bias in ((0, 2), (width, None), (2 * width, 3)):
        for j in range(width // third):
            columns = pl.ds(base + j * third, third)
            product = nn(normed[...], weights[:, columns])
            if bias is not None:
                product = product + vec[experts + bias : experts + bias + 1, pl.ds(j * third, third)]
            qkv_ref[:, columns] = product.astype(low)
    stat_ref[...] = jnp.zeros_like(stat_ref)

    @pl.loop(0, width // LANES)
    def _(pair):
        at = pl.multiple_of(pair * LANES, LANES)
        keys = qkv_ref[:, pl.ds(pl.multiple_of(width + at, LANES), LANES)]
        values = qkv_ref[:, pl.ds(pl.multiple_of(2 * width + at, LANES), LANES)]
        key_lanes = lane_ids(patches)
        values_two = [
            jnp.where(key_lanes < HEAD_DIM, values, (key_lanes == HEAD_DIM).astype(jnp.float32).astype(low)),
            jnp.where(key_lanes >= HEAD_DIM, values, (key_lanes == 0).astype(jnp.float32).astype(low)),
        ]
        for part in row_parts(patches, chunk):
            own = lane_ids(chunk)
            queries = qkv_ref[part, pl.ds(at, LANES)] * jnp.asarray(HEAD_DIM**-0.5, low)
            outs = []
            stat = stat_ref[part, :]
            for head in range(2):
                mine = (own < HEAD_DIM) if head == 0 else (own >= HEAD_DIM)
                scores = nt(jnp.where(mine, queries, jnp.zeros_like(queries)), keys)
                top = jnp.max(scores, axis=1, keepdims=True)
                raised = jnp.exp(scores - top)
                mixed = nn(raised.astype(low), values_two[head])
                spare = HEAD_DIM if head == 0 else 0
                total = mixed[:, spare : spare + 1]
                outs.append(mixed / total)
                stat = jnp.where(own == 2 * pair + head, top + jnp.log(total), stat)
            stat_ref[part, :] = stat
            ctx_ref[part, pl.ds(at, LANES)] = jnp.where(own < HEAD_DIM, outs[0], outs[1]).astype(low)

    for j in range(width // third):
        columns = pl.ds(j * third, third)
        product = nn(ctx_ref[...], weights[:, pl.ds(3 * width + j * third, third)])
        mid_ref[:, columns] = tok_ref[:, columns].astype(jnp.float32) + (
            product + vec[experts + 4 : experts + 5, columns]
        )
    for part in row_parts(patches, chunk):
        unit, _ = norm_parts(mid_ref[part, :])
        second_ref[part, :] = (unit * row(5) + row(6)).astype(low)
    logits = jnp.where(lanes < experts, nn(second_ref[...], weights[:, 4 * width :]), -1e30)
    raised = jnp.exp(logits - jnp.max(logits, axis=1, keepdims=True))
    probs = raised / jnp.sum(raised, axis=1, keepdims=True)
    probs_ref[...] = probs

    def slot_of(place, expert):
        place = place.astype(jnp.int32)
        kept = place < capacity
        slot = (place // 8) * LANES + expert * 8 + place % 8
        tail = kept & (place >= capacity - 4)
        return kept, jnp.where(kept, slot, -1), jnp.where(tail, slot + 4, -1)

    aux = jnp.zeros((patches, LANES), jnp.float32)
    for j, (place, expert, hit) in enumerate(((place_first, first, is_first), (place_other, other, is_other))):
        kept, slot, twin = slot_of(place, expert)
        gate = jnp.where(kept, jnp.sum(jnp.where(hit, probs, 0.0), axis=1, keepdims=True), 0.0)
        for lane, column in ((j, slot.astype(jnp.float32)), (2 + j, twin.astype(jnp.float32)), (4 + j, gate)):
            aux = jnp.where(lanes == lane, column, aux)
    aux_ref[...] = aux
    turned = jnp.transpose(aux)
    slots = [turned[i : i + 1, :] for i in range(4)]
    gates = [turned[4 + i : 5 + i, :] for i in range(2)]
    full = capacity // 8
    for i in range(full + 1):
        ids = (lax.broadcasted_iota(jnp.int32, (LANES, patches), 0) + i * LANES).astype(jnp.float32)
        hits = [ids == slots[0], ids == slots[1]]
        if i == full:
            hits = [hits[0] | (ids == slots[2]), hits[1] | (ids == slots[3])]
        table = (hits[0] | hits[1]).astype(jnp.float32).astype(low)
        gate = jnp.sum(
            jnp.where(hits[0], gates[0], 0.0) + jnp.where(hits[1], gates[1], 0.0), axis=1, keepdims=True
        )
        sent = nn(table, second_ref[...])
        back = nn(table, cot_ref[...]) * gate
        columns = pl.ds(i * width, width)
        if i == full:
            columns = pl.ds(i * width, width // 2)
            left = lax.broadcasted_iota(jnp.int32, (LANES, width // 2), 0) % 8 < 4
            sent = jnp.where(left, sent[:, : width // 2], sent[:, width // 2 :])
            back = jnp.where(left, back[:, : width // 2], back[:, width // 2 :])
        rows_ref[:, columns] = sent.astype(low)
        dy_ref[:, columns] = back.astype(low)


def forward(tokens, cotangent, choice, priority, weights, experts, capacity, chunk=192):
    patches, width = tokens.shape
    low, full = jnp.bfloat16, jnp.float32
    packed = (8 * experts, capacity * width // 8)
    shapes = [
        (packed, low),
        (packed, low),
        ((patches, 3 * width), low),
        ((patches, width), low),
        ((patches, width), full),
        ((patches, width), low),
        ((patches, LANES), full),
        ((patches, LANES), full),
        ((patches, LANES), full),
    ]
    return pl.pallas_call(
        functools.partial(forward_kernel, experts, capacity, chunk),
        out_shape=[jax.ShapeDtypeStruct(*s) for s in shapes],
        in_specs=[VMEM] * 5 + [ANY],
        out_specs=[VMEM] * 9,
        scratch_shapes=[
            pltpu.VMEM(weights.shape, low),
            pltpu.VMEM((LANES, width), full),
            pltpu.VMEM((patches, width), low),
            pltpu.SemaphoreType.DMA,
        ],
        compiler_params=pltpu.CompilerParams(vmem_limit_bytes=56 * 1024 * 1024),
        cost_estimate=pl.CostEstimate(flops=6 * 10**9, bytes_accessed=20 * 10**6, transcendentals=4 * 10**6),
        name="attend_forward",
    )(tokens, cotangent, choice, priority.reshape(patches, 1), priority.reshape(1, patches), weights)


def gelu_both(z):
    root = 0.7978845608028654
    square = z * z
    slope = jnp.tanh(root * z * (1.0 + 0.044715 * square))
    half = 0.5 * (1.0 + slope)
    act = z * half
    grad = half + 0.5 * z * (1.0 - slope * slope) * (root * (1.0 + 3 * 0.044715 * square))
    return act, grad


def tail_picks(count, right):
    rows = lax.broadcasted_iota(jnp.int32, (count // 2, count), 0)
    ids = lax.broadcasted_iota(jnp.int32, (count // 2, count), 1)
    hit = ids == (rows // 4) * 8 + rows % 4 + (4 if right else 0)
    return hit.astype(jnp.float32).astype(jnp.bfloat16)


def expert_kernel(
    dp,
    rows_in,
    dy_in,
    inner_ref,
    hidden_ref,
    outer_ref,
    return_ref,
    y_ref,
    drows_ref,
    dinner_ref,
    dhidden_ref,
    douter_ref,
    dreturn_ref,
    square_ref,
    rows,
    turned,
    dy,
    y_sum,
    drows_sum,
    square,
):
    low = jnp.bfloat16
    step, steps = pl.program_id(0), pl.num_programs(0)
    count, width = rows_in.shape[0], inner_ref.shape[1]
    full = rows_in.shape[1] // width
    half = width // 2
    part = return_ref.shape[1]

    @pl.when(step == 0)
    def _():
        for source, place in ((rows_in, rows), (dy_in, dy)):
            for i in range(full):
                place[pl.ds(i * count, count), :] = source[:, pl.ds(i * width, width)]
            tail = source[:, pl.ds(full * width, half)]
            for right in range(2):
                place[pl.ds(full * count, count // 2), pl.ds(right * half, half)] = nn(
                    tail_picks(count, right), tail
                ).astype(low)
        turned[...] = jnp.transpose(rows[...])
        y_sum[...] = jnp.zeros_like(y_sum)
        drows_sum[...] = jnp.zeros_like(drows_sum)
        own = lax.axis_index("dp")
        total = jnp.zeros((1, width), jnp.float32)
        for i in range(rows.shape[0] // LANES):
            total = total + jnp.sum(dy[pl.ds(i * LANES, LANES), :].astype(jnp.float32), axis=0, keepdims=True)
        picked = total[:, :part]
        for i in range(1, dp):
            picked = jnp.where(own == i, total[:, i * part : (i + 1) * part], picked)
        dreturn_ref[...] = picked
        square[...] = jnp.zeros_like(square)
        flat = picked * picked
        for i in range(part // LANES):
            square[0:1, :] = square[0:1, :] + flat[:, i * LANES : (i + 1) * LANES]

    inner = inner_ref[0].astype(low)
    outer = outer_ref[0].astype(low)
    z = nn(rows[...], inner) + hidden_ref[...].astype(low).astype(jnp.float32)
    act, grad = gelu_both(z)
    act = act.astype(low)
    dz = (nt(dy[...], outer) * grad).astype(low)
    y_sum[...] += nn(act, outer)
    drows_sum[...] += nt(dz, inner)
    douter = nn(jnp.transpose(act), dy[...])
    dinner = nn(turned[...], dz)
    dhidden = jnp.sum(dz.astype(jnp.float32), axis=0, keepdims=True)
    douter_ref[0] = douter.astype(douter_ref.dtype)
    dinner_ref[0] = dinner.astype(dinner_ref.dtype)
    dhidden_ref[...] = dhidden
    outer_square, inner_square, hidden_square = douter * douter, dinner * dinner, dhidden * dhidden
    parts = jnp.zeros((8, LANES), jnp.float32)
    folded = jnp.sum(outer_square.reshape(-1, 8, width), axis=0)
    for i in range(width // LANES):
        parts = parts + folded[:, i * LANES : (i + 1) * LANES]
    chunk = dz.shape[1]
    folded = jnp.sum(inner_square.reshape(-1, 8, chunk), axis=0)
    for i in range(chunk // LANES):
        parts = parts + folded[:, i * LANES : (i + 1) * LANES]
        square[0:1, :] = square[0:1, :] + hidden_square[:, i * LANES : (i + 1) * LANES]
    square[...] += parts

    @pl.when(step == steps - 1)
    def _():
        square_ref[...] = square[...]
        own = lax.axis_index("dp")
        bias = return_ref[...].astype(low).astype(jnp.float32)
        for i in range(dp):
            columns = pl.ds(i * part, part)
            y_sum[:, columns] = y_sum[:, columns] + jnp.where(own == i, bias, 0.0)
        for total, place in ((y_sum, y_ref), (drows_sum, drows_ref)):
            for i in range(full):
                place[:, pl.ds(i * width, width)] = total[pl.ds(i * count, count), :].astype(low)
            tail = total[pl.ds(full * count, count // 2), :].astype(low)
            spread = None
            for right in range(2):
                piece = lax.dot_general(
                    tail_picks(count, right),
                    tail[:, right * half : (right + 1) * half],
                    (((0,), (0,)), ((), ())),
                    preferred_element_type=jnp.float32,
                )
                spread = piece if spread is None else spread + piece
            place[:, pl.ds(full * width, half)] = spread.astype(low)


def expert_pass(rows, dy, inner, hidden, outer, back, dp, chunk=256):
    count, packed = rows.shape
    width, units = inner.shape[1:]
    total = count * packed // width
    low, full = jnp.bfloat16, jnp.float32
    whole = lambda shape: pl.BlockSpec(shape, lambda i: (0,) * len(shape))
    return pl.pallas_call(
        functools.partial(expert_kernel, dp),
        grid=(units // chunk,),
        out_shape=[
            jax.ShapeDtypeStruct((count, packed), low),
            jax.ShapeDtypeStruct((count, packed), low),
            jax.ShapeDtypeStruct(inner.shape, low),
            jax.ShapeDtypeStruct(hidden.shape, full),
            jax.ShapeDtypeStruct(outer.shape, low),
            jax.ShapeDtypeStruct(back.shape, full),
            jax.ShapeDtypeStruct((8, LANES), full),
        ],
        in_specs=[
            whole((count, packed)),
            whole((count, packed)),
            pl.BlockSpec((1, width, chunk), lambda i: (0, 0, i)),
            pl.BlockSpec((1, chunk), lambda i: (0, i)),
            pl.BlockSpec((1, chunk, width), lambda i: (0, i, 0)),
            whole(back.shape),
        ],
        out_specs=[
            whole((count, packed)),
            whole((count, packed)),
            pl.BlockSpec((1, width, chunk), lambda i: (0, 0, i)),
            pl.BlockSpec((1, chunk), lambda i: (0, i)),
            pl.BlockSpec((1, chunk, width), lambda i: (0, i, 0)),
            whole(back.shape),
            whole((8, LANES)),
        ],
        scratch_shapes=[
            pltpu.VMEM((total, width), low),
            pltpu.VMEM((width, total), low),
            pltpu.VMEM((total, width), low),
            pltpu.VMEM((total, width), full),
            pltpu.VMEM((total, width), full),
            pltpu.VMEM((8, LANES), full),
        ],
        compiler_params=pltpu.CompilerParams(
            vmem_limit_bytes=56 * 1024 * 1024, dimension_semantics=("arbitrary",)
        ),
        cost_estimate=pl.CostEstimate(flops=17 * 10**9, bytes_accessed=25 * 10**6, transcendentals=2 * 10**6),
        name="expert_pass",
    )(rows, dy, inner, hidden, outer, back)


def backward_kernel(
    experts,
    capacity,
    chunk,
    tok_ref,
    cot_ref,
    choice_ref,
    ret_ref,
    back_ref,
    aux_ref,
    probs_ref,
    mid_ref,
    second_ref,
    ctx_ref,
    stat_ref,
    qkv_ref,
    weights_any,
    out_ref,
    input_ref,
    grad_ref,
    weights,
    vec,
    stacked,
    normed,
    branch,
    dctx,
    joined,
    turned_query,
    dmid,
    work,
    sums,
    load,
):
    low = jnp.bfloat16
    patches, width = tok_ref.shape
    fetch = pltpu.make_async_copy(weights_any, weights, load)
    fetch.start()
    full = capacity // 8
    half = width // 2
    lanes = lane_ids(patches)
    aux = aux_ref[...]
    slots = [aux[:, i : i + 1] for i in range(4)]
    gates = [aux[:, 4 + i : 5 + i] for i in range(2)]
    ids = lax.broadcasted_iota(jnp.int32, (patches, full * LANES), 1).astype(jnp.float32)
    tail_ids = lane_ids(patches, full * LANES).astype(jnp.float32)
    hits = [ids == slots[0], ids == slots[1]]
    lefts = [tail_ids == slots[0], tail_ids == slots[1]]
    rights = [tail_ids == slots[2], tail_ids == slots[3]]

    def mix(marks):
        return (jnp.where(marks[0], gates[0], 0.0) + jnp.where(marks[1], gates[1], 0.0)).astype(low)

    def pick(marks):
        return (marks[0] | marks[1]).astype(jnp.float32).astype(low)

    for i in range(full):
        stacked[pl.ds(i * LANES, LANES), :] = ret_ref[:, pl.ds(i * width, width)]
    tail = ret_ref[:, pl.ds(full * width, half)]
    left_mix, right_mix = nn(mix(lefts), tail), nn(mix(rights), tail)
    final = nn(mix(hits), stacked[...])
    out_ref[:, :half] = (mid_ref[:, :half] + (final[:, :half] + left_mix)).astype(low)
    out_ref[:, half:] = (mid_ref[:, half:] + (final[:, half:] + right_mix)).astype(low)
    along = nt(cot_ref[...], stacked[...])
    along_left, along_right = nt(cot_ref[:, :half], tail), nt(cot_ref[:, half:], tail)
    dprobs = jnp.zeros((patches, LANES), jnp.float32)
    for j in range(2):
        dgate = jnp.sum(jnp.where(hits[j], along, 0.0), axis=1, keepdims=True) + jnp.sum(
            jnp.where(lefts[j], along_left, 0.0) + jnp.where(rights[j], along_right, 0.0), axis=1, keepdims=True
        )
        dprobs = dprobs + jnp.where(lanes == choice_ref[:, j : j + 1], dgate, 0.0)
    probs = probs_ref[...]
    dlogits = (probs * (dprobs - jnp.sum(probs * dprobs, axis=1, keepdims=True))).astype(low)
    for i in range(full):
        stacked[pl.ds(i * LANES, LANES), :] = back_ref[:, pl.ds(i * width, width)]
    tail = back_ref[:, pl.ds(full * width, half)]
    fetch.wait()
    vec[...] = vector_table(weights, width)

    def row(i):
        return vec[experts + i : experts + i + 1, :]

    routed = weights[:, 4 * width :]
    work[...] = nn(pick(hits), stacked[...]) + nt(dlogits, routed)
    work[:, :half] = work[:, :half] + nn(pick(lefts), tail)
    work[:, half:] = work[:, half:] + nn(pick(rights), tail)
    sums[...] = jnp.zeros_like(sums)

    def column_sum(slot, values):
        sums[pl.ds(8 * slot, 8), :] = sums[pl.ds(8 * slot, 8), :] + jnp.sum(
            values.reshape(-1, 8, values.shape[-1]), axis=0
        )

    def norm_back(grad, unit, inverse, gain):
        weighted = grad * gain
        return inverse * (
            weighted
            - jnp.mean(weighted, axis=-1, keepdims=True)
            - unit * jnp.mean(weighted * unit, axis=-1, keepdims=True)
        )

    for part in row_parts(patches, chunk):
        unit, inverse = norm_parts(mid_ref[part, :])
        grad = work[part, :]
        column_sum(5, grad * unit)
        column_sum(6, grad)
        total = cot_ref[part, :].astype(jnp.float32) + norm_back(grad, unit, inverse, row(5))
        dmid[part, :] = total
        rounded = total.astype(low)
        branch[part, :] = rounded
        column_sum(4, rounded.astype(jnp.float32))
    third = 256
    for j in range(width // third):
        rows = pl.ds(j * third, third)
        dctx[:, rows] = nt(branch[...], weights[rows, pl.ds(3 * width, width)]).astype(low)
    second_turned = jnp.transpose(second_ref[...])
    router_grad = nn(second_turned, dlogits)
    ctx_turned = jnp.transpose(ctx_ref[...])
    for j in range(width // third):
        columns = pl.ds(j * third, third)
        grad_ref[:, pl.ds(3 * width + j * third, third)] = nn(ctx_turned, branch[:, columns]).astype(low)
    heads = (
        lax.broadcasted_iota(jnp.int32, (16, width), 1) // HEAD_DIM == lax.broadcasted_iota(jnp.int32, (16, width), 0)
    ).astype(jnp.float32).astype(low)
    product = dctx[...].astype(jnp.float32) * ctx_ref[...].astype(jnp.float32)
    upper = product.astype(low)
    center = nt(heads, upper) + nt(heads, (product - upper.astype(jnp.float32)).astype(low))
    logs = jnp.transpose(stat_ref[...])
    sums_rows = jnp.concatenate([logs[:16], center], axis=0)
    vec_rows = work
    vec_rows[0:32, :patches] = sums_rows

    @pl.loop(0, width // LANES)
    def _(pair):
        at = pl.multiple_of(pair * LANES, LANES)
        key_at = pl.ds(pl.multiple_of(width + at, LANES), LANES)
        value_at = pl.ds(pl.multiple_of(2 * width + at, LANES), LANES)
        scale = jnp.asarray(HEAD_DIM**-0.5, low)
        queries = qkv_ref[:, pl.ds(at, LANES)] * scale
        given = dctx[:, pl.ds(at, LANES)]
        own = lane_ids(patches)
        zero = jnp.zeros_like(queries)
        marks = [own < HEAD_DIM, own >= HEAD_DIM]
        head_queries = [jnp.where(m, queries, zero) for m in marks]
        head_given = [jnp.where(m, given, zero) for m in marks]
        turned_keys = jnp.transpose(qkv_ref[:, key_at] * scale)
        query_parts = [None, None]
        for part in row_parts(patches, chunk):
            keys = qkv_ref[part, key_at]
            values = qkv_ref[part, value_at]
            value_out, key_out = [], []
            for head in range(2):
                log_row = work[pl.ds(2 * pair + head, 1), :patches]
                center_row = work[pl.ds(16 + 2 * pair + head, 1), :patches]
                prob = jnp.exp(nt(keys, head_queries[head]) - log_row)
                value_out.append(nn(prob.astype(low), given))
                dscore = (prob * (nt(values, head_given[head]) - center_row)).astype(low)
                key_out.append(nn(dscore, queries))
                piece = nn(turned_keys[HEAD_DIM * head : HEAD_DIM * (head + 1), part.start : part.start + part.size], dscore)
                query_parts[head] = piece if query_parts[head] is None else query_parts[head] + piece
            side = lane_ids(chunk) < HEAD_DIM
            joined[part, key_at] = jnp.where(side, key_out[0], key_out[1]).astype(low)
            joined[part, value_at] = jnp.where(side, value_out[0], value_out[1]).astype(low)
        turned_query[...] = jnp.concatenate(query_parts, axis=0)
        joined[:, pl.ds(at, LANES)] = jnp.transpose(turned_query[...]).astype(low)

    for part in row_parts(patches, chunk):
        unit, _ = norm_parts(tok_ref[part, :].astype(jnp.float32))
        normed[part, :] = (unit * row(0) + row(1)).astype(low)
        column_sum(2, joined[part, :width].astype(jnp.float32))
        column_sum(3, joined[part, 2 * width :].astype(jnp.float32))
    normed_turned = jnp.transpose(normed[...])
    for j in range(3 * width // third):
        columns = pl.ds(j * third, third)
        grad_ref[:, columns] = nn(normed_turned, joined[:, columns]).astype(low)
    for j in range(width // third):
        rows = pl.ds(j * third, third)
        work[:, rows] = nt(joined[...], weights[rows, : 3 * width])
    for part in row_parts(patches, chunk):
        unit, inverse = norm_parts(tok_ref[part, :].astype(jnp.float32))
        grad = work[part, :]
        column_sum(0, grad * unit)
        column_sum(1, grad)
        input_ref[part, :] = dmid[part, :] + norm_back(grad, unit, inverse, row(0))
    vec[...] = jnp.zeros_like(vec)
    for i in range(7):
        vec[experts + i : experts + i + 1, :] = jnp.sum(sums[pl.ds(8 * i, 8), :], axis=0, keepdims=True)
    last = router_grad + jnp.transpose(vec[...])
    grad_ref[:, pl.ds(4 * width, LANES)] = last.astype(low)
    rest = grad_ref.shape[1] - 4 * width - LANES
    grad_ref[:, pl.ds(4 * width + LANES, rest)] = jnp.zeros((width, rest), low)


def backward(
    tokens, cotangent, choice, ret, back, aux, probs, mid, second, ctx, stat, qkv, weights, experts, capacity, chunk=192
):
    patches, width = tokens.shape
    low, full = jnp.bfloat16, jnp.float32
    columns = -(-weights.shape[1] // 256) * 256
    return pl.pallas_call(
        functools.partial(backward_kernel, experts, capacity, chunk),
        out_shape=[
            jax.ShapeDtypeStruct((patches, width), low),
            jax.ShapeDtypeStruct((patches, width), full),
            jax.ShapeDtypeStruct((width, columns), low),
        ],
        in_specs=[VMEM] * 12 + [ANY],
        out_specs=[VMEM] * 3,
        scratch_shapes=[
            pltpu.VMEM(weights.shape, low),
            pltpu.VMEM((LANES, width), full),
            pltpu.VMEM((capacity // 8 * LANES, width), low),
            pltpu.VMEM((patches, width), low),
            pltpu.VMEM((patches, width), low),
            pltpu.VMEM((patches, width), low),
            pltpu.VMEM((patches, 3 * width), low),
            pltpu.VMEM((LANES, patches), full),
            pltpu.VMEM((patches, width), full),
            pltpu.VMEM((patches, width), full),
            pltpu.VMEM((56, width), full),
            pltpu.SemaphoreType.DMA,
        ],
        compiler_params=pltpu.CompilerParams(vmem_limit_bytes=60 * 1024 * 1024),
        cost_estimate=pl.CostEstimate(flops=15 * 10**9, bytes_accessed=30 * 10**6, transcendentals=4 * 10**6),
        name="attend_backward",
    )(tokens, cotangent, choice, ret, back, aux, probs, mid, second, ctx, stat, qkv, weights)


def fits(dp, experts):
    return dp == 2 and experts == 16


def fast_shards(
    dp,
    experts,
    tokens,
    cotangent,
    expert_choice,
    priority,
    projection,
    projection_first,
    projection_second,
    output_weight,
    output_first,
    output_second,
    router_weight,
    router_first,
    router_second,
    vectors,
    vectors_first,
    vectors_second,
    expert_inner,
    inner_first,
    inner_second,
    hidden_bias,
    hidden_first,
    hidden_second,
    expert_outer,
    outer_first,
    outer_second,
    return_bias,
    return_first,
    return_second,
):
    model_width = tokens.shape[2]
    patches = tokens.shape[1]
    capacity = max(2, patches // experts)
    low = jnp.bfloat16
    shard_rows = projection.shape[0]
    wide = 3 * model_width
    used = wide + model_width + experts + vectors.shape[0]
    packed = jnp.concatenate(
        [projection, output_weight, router_weight, vectors.T, jnp.zeros((shard_rows, -used % 128), jnp.float32)], axis=1
    ).astype(low)
    weights = gather_blocks(packed, dp, experts, 1).reshape(model_width, packed.shape[1])
    rows, dy, qkv, ctx, mid, second, stat, aux, probs = forward(
        tokens[0], cotangent[0], expert_choice[0], priority[0], weights, experts, capacity
    )
    blocks = (experts, 8, rows.shape[1])
    arrived, given = dispatch([rows.reshape(blocks), dy.reshape(blocks)], dp, experts, 2)
    both = (dp * experts * 8, rows.shape[1])
    y_part, row_part, inner_grad, hidden_grad, outer_grad, return_grad, expert_square = expert_pass(
        arrived.reshape(both), given.reshape(both), expert_inner, hidden_bias, expert_outer, return_bias, dp
    )
    returned, back_rows = give_back(
        [y_part.reshape((dp,) + blocks), row_part.reshape((dp,) + blocks)], dp, experts, 3
    )
    block_output, input_grad, local_grads = backward(
        tokens[0],
        cotangent[0],
        expert_choice[0],
        returned.reshape(rows.shape),
        back_rows.reshape(rows.shape),
        aux,
        probs,
        mid,
        second,
        ctx,
        stat,
        qkv,
        weights,
        experts,
        capacity,
    )
    block_output, input_grad = block_output[None], input_grad[None]
    chips = dp * experts // 2
    dense, squares = reduce_blocks(
        local_grads.reshape(chips, 2 * shard_rows, -1), expert_square, dp, experts, 4
    )
    inner_grad, outer_grad = inner_grad.astype(jnp.float32), outer_grad.astype(jnp.float32)
    grad_norm = jnp.sqrt(jnp.sum(squares))
    clip_factor = THRESHOLD / jnp.maximum(grad_norm, THRESHOLD)
    projection_new = adam_update(
        projection, projection_first, projection_second, dense[:, :wide], clip_factor, RATE_PROJECTION, DECAY
    )
    output_new = adam_update(
        output_weight,
        output_first,
        output_second,
        dense[:, wide : wide + model_width],
        clip_factor,
        RATE_OUTPUT,
        DECAY,
    )
    router_new = adam_update(
        router_weight,
        router_first,
        router_second,
        dense[:, wide + model_width : wide + model_width + experts],
        clip_factor,
        RATE_ROUTER,
        DECAY,
    )
    vectors_new = adam_update(
        vectors,
        vectors_first,
        vectors_second,
        dense[:, wide + model_width + experts : used].T,
        clip_factor,
        RATE_VECTORS,
        0.0,
    )
    inner_new = adam_update(expert_inner, inner_first, inner_second, inner_grad, clip_factor, RATE_INNER, DECAY)
    hidden_new = adam_update(hidden_bias, hidden_first, hidden_second, hidden_grad, clip_factor, RATE_HIDDEN, 0.0)
    outer_new = adam_update(expert_outer, outer_first, outer_second, outer_grad, clip_factor, RATE_OUTER, DECAY)
    return_new = adam_update(return_bias, return_first, return_second, return_grad, clip_factor, RATE_RETURN, 0.0)
    return (
        block_output,
        input_grad,
        grad_norm,
        *projection_new,
        *output_new,
        *router_new,
        *vectors_new,
        *inner_new,
        *hidden_new,
        *outer_new,
        *return_new,
    )


def solution(mesh):
    dp, experts = mesh.shape["dp"], mesh.shape["expert"]
    body = functools.partial(fast_shards, dp, experts) if fits(dp, experts) else shards
    return jax.shard_map(
        body,
        mesh=mesh,
        in_specs=(
            P(("dp", "expert"), None, None),
            P(("dp", "expert"), None, None),
            P(("dp", "expert"), None, None),
            P(("dp", "expert"), None),
            P(("dp", "expert"), None),
            P(("dp", "expert"), None),
            P(("dp", "expert"), None),
            P(("dp", "expert"), None),
            P(("dp", "expert"), None),
            P(("dp", "expert"), None),
            P(("dp", "expert"), None),
            P(("dp", "expert"), None),
            P(("dp", "expert"), None),
            P(None, ("dp", "expert")),
            P(None, ("dp", "expert")),
            P(None, ("dp", "expert")),
            P("expert", None, "dp"),
            P("expert", None, "dp"),
            P("expert", None, "dp"),
            P("expert", "dp"),
            P("expert", "dp"),
            P("expert", "dp"),
            P("expert", "dp", None),
            P("expert", "dp", None),
            P("expert", "dp", None),
            P("expert", "dp"),
            P("expert", "dp"),
            P("expert", "dp"),
        ),
        out_specs=(
            P(("dp", "expert"), None, None),
            P(("dp", "expert"), None, None),
            P(),
            P(("dp", "expert"), None),
            P(("dp", "expert"), None),
            P(("dp", "expert"), None),
            P(("dp", "expert"), None),
            P(("dp", "expert"), None),
            P(("dp", "expert"), None),
            P(("dp", "expert"), None),
            P(("dp", "expert"), None),
            P(("dp", "expert"), None),
            P(None, ("dp", "expert")),
            P(None, ("dp", "expert")),
            P(None, ("dp", "expert")),
            P("expert", None, "dp"),
            P("expert", None, "dp"),
            P("expert", None, "dp"),
            P("expert", "dp"),
            P("expert", "dp"),
            P("expert", "dp"),
            P("expert", "dp", None),
            P("expert", "dp", None),
            P("expert", "dp", None),
            P("expert", "dp"),
            P("expert", "dp"),
            P("expert", "dp"),
        ),
        check_vma=False,
    )
```

```python
import functools

import jax
import jax.numpy as jnp
from jax import lax
from jax.experimental import pallas as pl
from jax.experimental.pallas import tpu as pltpu
from jax.sharding import PartitionSpec as P

HEADS = 12
HEAD_DIM = 64
STEP = 10


NORM_EPS = 1e-06
ADAM_EPS = 1e-08
BETA_ONE = 0.9
BETA_TWO = 0.999
DECAY = 0.1
THRESHOLD = 1.0
RATE_PROJECTION = 0.1
RATE_OUTPUT = 1.0
RATE_ROUTER = 0.05
RATE_VECTORS = 0.5
RATE_INNER = 0.1
RATE_HIDDEN = 0.25
RATE_OUTER = 1.5
RATE_RETURN = 2.0


def layer_norm(values, norm_gain, norm_bias):
    center = values - jnp.mean(values, axis=-1, keepdims=True)
    spread = jnp.mean(center * center, axis=-1, keepdims=True)
    return center * lax.rsqrt(spread + NORM_EPS) * norm_gain + norm_bias


def smooth_gate(values):
    return jax.nn.gelu(values, approximate=True)


def mixed_dot(left, right):
    return jnp.dot(left, right, preferred_element_type=jnp.float32)


def rows_product(left, right):
    return lax.dot_general(
        left, right, (((0,), (0,)), ((), ())), preferred_element_type=jnp.float32
    )


def columns_product(left, right):
    return lax.dot_general(
        left, right, (((1,), (1,)), ((), ())), preferred_element_type=jnp.float32
    )


def assign_slots(chosen, claim_order, expert_count, capacity):
    patches = chosen.shape[0]
    top_count = chosen.shape[1]
    claim_rank = (
        jnp.arange(top_count, dtype=jnp.int32)[None, :] * patches + claim_order[:, None]
    ).T.reshape(-1)
    flat_choice = chosen.T.reshape(-1)
    onehot = (flat_choice[:, None] == jnp.arange(expert_count, dtype=jnp.int32)[None, :]).astype(
        jnp.float32
    )
    earlier = (claim_rank[None, :] < claim_rank[:, None]).astype(jnp.float32)
    counts = jnp.dot(
        earlier, onehot, precision=lax.Precision.HIGHEST, preferred_element_type=jnp.float32
    )
    position = jnp.sum(counts * onehot, axis=1).astype(jnp.int32).reshape(top_count, patches).T
    kept_mask = position < capacity
    flat_slot = chosen * capacity + jnp.minimum(position, capacity - 1)
    return (flat_slot, kept_mask)


def slot_matches(flat_slot, kept_mask, slot_count):
    slot_ids = jnp.arange(slot_count, dtype=jnp.int32)
    return (flat_slot[None, :, :] == slot_ids[:, None, None]) & kept_mask[None, :, :]


def select_gates(logits, chosen, expert_count):
    router_probs = jax.nn.softmax(logits, axis=-1)
    onehot = chosen[:, :, None] == jnp.arange(expert_count, dtype=jnp.int32)[None, None, :]
    return jnp.sum(jnp.where(onehot, router_probs[:, None, :], 0.0), axis=2)


def adam_update(weight, first_state, second, gradient, clip_factor, step_rate, decay_rate):
    scaled = gradient * clip_factor
    first_new = BETA_ONE * first_state + (1.0 - BETA_ONE) * scaled
    second_new = BETA_TWO * second + (1.0 - BETA_TWO) * scaled * scaled
    first_hat = first_new / (1.0 - BETA_ONE**STEP)
    second_hat = second_new / (1.0 - BETA_TWO**STEP)
    weight_new = weight - step_rate * (
        first_hat / (jnp.sqrt(second_hat) + ADAM_EPS) + decay_rate * weight
    )
    return (weight_new, first_new, second_new)


def shards(
    tokens,
    cotangent,
    expert_choice,
    priority,
    projection,
    projection_first,
    projection_second,
    output_weight,
    output_first,
    output_second,
    router_weight,
    router_first,
    router_second,
    vectors,
    vectors_first,
    vectors_second,
    expert_inner,
    inner_first,
    inner_second,
    hidden_bias,
    hidden_first,
    hidden_second,
    expert_outer,
    outer_first,
    outer_second,
    return_bias,
    return_first,
    return_second,
):
    model_width = tokens.shape[2]
    patches = tokens.shape[1]
    experts = lax.axis_size("expert")
    capacity = max(2, patches // experts)
    slot_count = experts * capacity
    score_scale = HEAD_DIM ** (-0.5)
    dense_shards = (
        projection.astype(jnp.bfloat16),
        output_weight.astype(jnp.bfloat16),
        router_weight.astype(jnp.bfloat16),
        vectors.astype(jnp.bfloat16),
    )
    partial_shards = (
        lax.all_gather(dense_shards[0], "expert", axis=0, tiled=True),
        lax.all_gather(dense_shards[1], "expert", axis=0, tiled=True),
        lax.all_gather(dense_shards[2], "expert", axis=0, tiled=True),
        lax.all_gather(dense_shards[3], "expert", axis=1, tiled=True),
    )
    whole_projection, whole_output, whole_router, whole_vectors = (
        lax.all_gather(partial_shards[0], "dp", axis=0, tiled=True),
        lax.all_gather(partial_shards[1], "dp", axis=0, tiled=True),
        lax.all_gather(partial_shards[2], "dp", axis=0, tiled=True),
        lax.all_gather(partial_shards[3], "dp", axis=1, tiled=True),
    )
    inner_low = expert_inner.astype(jnp.bfloat16)
    hidden_low = hidden_bias.astype(jnp.bfloat16)
    outer_low = expert_outer.astype(jnp.bfloat16)
    return_low = return_bias.astype(jnp.bfloat16)
    inner_all, hidden_all, outer_all, return_all = (
        lax.all_gather(inner_low, "dp", axis=2, tiled=True),
        lax.all_gather(hidden_low, "dp", axis=1, tiled=True),
        lax.all_gather(outer_low, "dp", axis=1, tiled=True),
        lax.all_gather(return_low, "dp", axis=1, tiled=True),
    )
    vector_rows = whole_vectors.astype(jnp.float32)
    image_rows = tokens[0].astype(jnp.float32)
    normed_one, norm_back_one = jax.vjp(layer_norm, image_rows, vector_rows[0], vector_rows[1])
    normed_low = normed_one.astype(jnp.bfloat16)
    projected = mixed_dot(normed_low, whole_projection)
    queries = (
        (projected[:, :model_width] + vector_rows[2])
        .astype(jnp.bfloat16)
        .reshape(patches, HEADS, HEAD_DIM)
    )
    key_rows = (
        projected[:, model_width : 2 * model_width]
        .astype(jnp.bfloat16)
        .reshape(patches, HEADS, HEAD_DIM)
    )
    value_rows = (
        (projected[:, 2 * model_width :] + vector_rows[3])
        .astype(jnp.bfloat16)
        .reshape(patches, HEADS, HEAD_DIM)
    )
    scores = (
        jnp.einsum("qhd,khd->hqk", queries, key_rows, preferred_element_type=jnp.float32)
        * score_scale
    )
    score_top = jnp.max(scores, axis=-1, keepdims=True)
    raised = jnp.exp(scores - score_top)
    totals = jnp.sum(raised, axis=-1, keepdims=True)
    attention = raised / totals
    log_total = score_top + jnp.log(totals)
    context = (
        jnp.einsum(
            "hqk,khd->qhd",
            attention.astype(jnp.bfloat16),
            value_rows,
            preferred_element_type=jnp.float32,
        )
        .reshape(patches, model_width)
        .astype(jnp.bfloat16)
    )
    middle = image_rows + (mixed_dot(context, whole_output) + vector_rows[4])
    normed_two, norm_back_two = jax.vjp(layer_norm, middle, vector_rows[5], vector_rows[6])
    second_low = normed_two.astype(jnp.bfloat16)
    logits = mixed_dot(second_low, whole_router)
    chosen = expert_choice[0]

    def gate_choice(values):
        return select_gates(values, chosen, experts)

    gate_values, gate_back = jax.vjp(gate_choice, logits)
    flat_slot, kept_mask = assign_slots(chosen, priority[0], experts, capacity)
    matches = slot_matches(flat_slot, kept_mask, slot_count)
    slot_table = jnp.any(matches, axis=2).astype(jnp.bfloat16)
    dispatched = (
        mixed_dot(slot_table, second_low)
        .astype(jnp.bfloat16)
        .reshape(experts, capacity, model_width)
    )
    arrived = lax.all_to_all(dispatched, "expert", split_axis=0, concat_axis=0, tiled=True).reshape(
        slot_count, model_width
    )
    pre_act = mixed_dot(arrived, inner_all[0]) + hidden_all[0].astype(jnp.float32)
    activated, gelu_back = jax.vjp(smooth_gate, pre_act)
    active_low = activated.astype(jnp.bfloat16)
    expert_out = (mixed_dot(active_low, outer_all[0]) + return_all[0].astype(jnp.float32)).astype(
        jnp.bfloat16
    )
    returned = lax.all_to_all(
        expert_out.reshape(experts, capacity, model_width),
        "expert",
        split_axis=0,
        concat_axis=0,
        tiled=True,
    ).reshape(slot_count, model_width)
    picked = returned[flat_slot].astype(jnp.float32)
    weighted = jnp.where(kept_mask, gate_values, 0.0)
    final = middle + jnp.sum(weighted[:, :, None] * picked, axis=1)
    block_output = final.astype(jnp.bfloat16)[None]
    upstream = cotangent[0].astype(jnp.float32)
    gate_grad = jnp.where(kept_mask, jnp.sum(upstream[:, None, :] * picked, axis=2), 0.0)
    slot_gate = jnp.sum(jnp.where(matches, weighted[None, :, :], 0.0), axis=(1, 2))
    slot_grad = (mixed_dot(slot_table, cotangent[0]) * slot_gate[:, None]).astype(jnp.bfloat16)
    sent_grad = lax.all_to_all(
        slot_grad.reshape(experts, capacity, model_width),
        "expert",
        split_axis=0,
        concat_axis=0,
        tiled=True,
    ).reshape(slot_count, model_width)
    outer_grad = rows_product(active_low, sent_grad)
    return_grad = jnp.sum(sent_grad, axis=0, dtype=jnp.float32)
    active_grad = columns_product(sent_grad, outer_all[0])
    (pre_grad,) = gelu_back(active_grad)
    pre_low = pre_grad.astype(jnp.bfloat16)
    inner_grad = rows_product(arrived, pre_low)
    hidden_grad = jnp.sum(pre_low, axis=0, dtype=jnp.float32)
    row_grad = columns_product(pre_low, inner_all[0]).astype(jnp.bfloat16)
    expert_grads = (
        lax.psum_scatter(
            inner_grad[None].astype(jnp.bfloat16), "dp", scatter_dimension=2, tiled=True
        ).astype(jnp.float32),
        lax.psum_scatter(
            hidden_grad[None].astype(jnp.bfloat16), "dp", scatter_dimension=1, tiled=True
        ).astype(jnp.float32),
        lax.psum_scatter(
            outer_grad[None].astype(jnp.bfloat16), "dp", scatter_dimension=1, tiled=True
        ).astype(jnp.float32),
        lax.psum_scatter(
            return_grad[None].astype(jnp.bfloat16), "dp", scatter_dimension=1, tiled=True
        ).astype(jnp.float32),
    )
    back_rows = lax.all_to_all(
        row_grad.reshape(experts, capacity, model_width),
        "expert",
        split_axis=0,
        concat_axis=0,
        tiled=True,
    ).reshape(slot_count, model_width)
    (logit_grad,) = gate_back(gate_grad)
    logit_low = logit_grad.astype(jnp.bfloat16)
    router_grad = rows_product(second_low, logit_low)
    second_grad = rows_product(slot_table, back_rows) + columns_product(logit_low, whole_router)
    middle_part, gain_two_grad, bias_two_grad = norm_back_two(second_grad)
    middle_grad = upstream + middle_part
    branch_low = middle_grad.astype(jnp.bfloat16)
    output_grad = rows_product(context, branch_low)
    out_bias_grad = jnp.sum(branch_low, axis=0, dtype=jnp.float32)
    context_grad = (
        columns_product(branch_low, whole_output)
        .astype(jnp.bfloat16)
        .reshape(patches, HEADS, HEAD_DIM)
    )
    scores = (
        jnp.einsum("qhd,khd->hqk", queries, key_rows, preferred_element_type=jnp.float32)
        * score_scale
    )
    attention = jnp.exp(scores - log_total)
    attention_grad = jnp.einsum(
        "qhd,khd->hqk", context_grad, value_rows, preferred_element_type=jnp.float32
    )
    value_grad = jnp.einsum(
        "hqk,qhd->khd",
        attention.astype(jnp.bfloat16),
        context_grad,
        preferred_element_type=jnp.float32,
    ).astype(jnp.bfloat16)
    centered = jnp.sum(attention * attention_grad, axis=-1, keepdims=True)
    score_grad = (attention * (attention_grad - centered)).astype(jnp.bfloat16)
    query_grad = (
        (
            jnp.einsum("hqk,khd->qhd", score_grad, key_rows, preferred_element_type=jnp.float32)
            * score_scale
        )
        .astype(jnp.bfloat16)
        .reshape(patches, model_width)
    )
    key_grad = (
        (
            jnp.einsum("hqk,qhd->khd", score_grad, queries, preferred_element_type=jnp.float32)
            * score_scale
        )
        .astype(jnp.bfloat16)
        .reshape(patches, model_width)
    )
    value_flat = value_grad.reshape(patches, model_width)
    joined_grad = jnp.concatenate([query_grad, key_grad, value_flat], axis=1)
    projection_grad = rows_product(normed_low, joined_grad)
    normed_grad = columns_product(joined_grad, whole_projection)
    input_part, gain_one_grad, bias_one_grad = norm_back_one(normed_grad)
    input_grad = (middle_grad + input_part)[None]
    vector_grad = jnp.stack(
        [
            gain_one_grad,
            bias_one_grad,
            jnp.sum(query_grad, axis=0, dtype=jnp.float32),
            jnp.sum(value_flat, axis=0, dtype=jnp.float32),
            out_bias_grad,
            gain_two_grad,
            bias_two_grad,
        ]
    )
    local_grads = (projection_grad, output_grad, router_grad, vector_grad)
    partial_grads = (
        lax.psum_scatter(
            local_grads[0].astype(jnp.bfloat16), "dp", scatter_dimension=0, tiled=True
        ).astype(jnp.float32),
        lax.psum_scatter(
            local_grads[1].astype(jnp.bfloat16), "dp", scatter_dimension=0, tiled=True
        ).astype(jnp.float32),
        lax.psum_scatter(
            local_grads[2].astype(jnp.bfloat16), "dp", scatter_dimension=0, tiled=True
        ).astype(jnp.float32),
        lax.psum_scatter(
            local_grads[3].astype(jnp.bfloat16), "dp", scatter_dimension=1, tiled=True
        ).astype(jnp.float32),
    )
    dense_grads = (
        lax.psum_scatter(
            partial_grads[0].astype(jnp.bfloat16), "expert", scatter_dimension=0, tiled=True
        ).astype(jnp.float32),
        lax.psum_scatter(
            partial_grads[1].astype(jnp.bfloat16), "expert", scatter_dimension=0, tiled=True
        ).astype(jnp.float32),
        lax.psum_scatter(
            partial_grads[2].astype(jnp.bfloat16), "expert", scatter_dimension=0, tiled=True
        ).astype(jnp.float32),
        lax.psum_scatter(
            partial_grads[3].astype(jnp.bfloat16), "expert", scatter_dimension=1, tiled=True
        ).astype(jnp.float32),
    )
    all_grads = tuple(dense_grads) + tuple(expert_grads)
    local_square = jnp.sum(all_grads[0] * all_grads[0])
    for gradient in all_grads[1:]:
        local_square = local_square + jnp.sum(gradient * gradient)
    square_total = lax.psum(local_square, ("dp", "expert"))
    grad_norm = jnp.sqrt(square_total)
    clip_factor = THRESHOLD / jnp.maximum(grad_norm, THRESHOLD)
    projection_next, projection_moment, projection_square = adam_update(
        projection,
        projection_first,
        projection_second,
        all_grads[0],
        clip_factor,
        RATE_PROJECTION,
        DECAY,
    )
    output_next, output_moment, output_square = adam_update(
        output_weight, output_first, output_second, all_grads[1], clip_factor, RATE_OUTPUT, DECAY
    )
    router_next, router_moment, router_square = adam_update(
        router_weight, router_first, router_second, all_grads[2], clip_factor, RATE_ROUTER, DECAY
    )
    vectors_next, vectors_moment, vectors_square = adam_update(
        vectors, vectors_first, vectors_second, all_grads[3], clip_factor, RATE_VECTORS, 0.0
    )
    inner_next, inner_moment, inner_square = adam_update(
        expert_inner, inner_first, inner_second, all_grads[4], clip_factor, RATE_INNER, DECAY
    )
    hidden_next, hidden_moment, hidden_square = adam_update(
        hidden_bias, hidden_first, hidden_second, all_grads[5], clip_factor, RATE_HIDDEN, 0.0
    )
    outer_next, outer_moment, outer_square = adam_update(
        expert_outer, outer_first, outer_second, all_grads[6], clip_factor, RATE_OUTER, DECAY
    )
    return_next, return_moment, return_square = adam_update(
        return_bias, return_first, return_second, all_grads[7], clip_factor, RATE_RETURN, 0.0
    )
    return (
        block_output,
        input_grad,
        grad_norm,
        projection_next,
        projection_moment,
        projection_square,
        output_next,
        output_moment,
        output_square,
        router_next,
        router_moment,
        router_square,
        vectors_next,
        vectors_moment,
        vectors_square,
        inner_next,
        inner_moment,
        inner_square,
        hidden_next,
        hidden_moment,
        hidden_square,
        outer_next,
        outer_moment,
        outer_square,
        return_next,
        return_moment,
        return_square,
    )


MESH = pl.DeviceIdType.MESH
ANY = pl.BlockSpec(memory_space=pl.ANY)
VMEM = pl.BlockSpec(memory_space=pltpu.VMEM)


class Place:
    def __init__(self, dp, experts):
        self.dp, self.experts = dp, experts
        self.ys = 2
        self.zs = experts // 4
        self.a = lax.axis_index("dp")
        self.e = lax.axis_index("expert")
        self.core = lax.rem(self.e, 2)
        self.y = lax.rem(lax.div(self.e, 2), self.ys)
        self.z = lax.div(self.e, 2 * self.ys)

    def chip_of(self, core, dz, s2, s3):
        zz = lax.rem(self.z + dz, self.zs)
        if s2 == s3:
            fa = fy = s2
        elif s2:
            fa, fy = core, 1 - core
        else:
            fa, fy = 1 - core, core
        aa = lax.rem(self.a + fa, 2)
        yy = lax.rem(self.y + fy, 2)
        return aa, zz, yy

    def device(self, core, dz, s2, s3, own_core=None):
        aa, zz, yy = self.chip_of(core, dz, s2, s3)
        c = core if own_core is None else own_core
        return (aa, (zz * self.ys + yy) * 2 + c)

    def flat(self, dev):
        return dev[0] * self.experts + dev[1]

    def chip(self, core, dz, s2, s3):
        aa, zz, yy = self.chip_of(core, dz, s2, s3)
        return (aa * self.zs + zz) * self.ys + yy


def remote(src, dst, send, recv, dev):
    return pltpu.make_async_remote_copy(src_ref=src, dst_ref=dst, send_sem=send, recv_sem=recv, device_id=dev, device_id_type=MESH)


def greet(devices):
    barrier = pltpu.get_barrier_semaphore()
    for dev in devices:
        pl.semaphore_signal(barrier, inc=1, device_id=dev, device_id_type=MESH)
    pl.semaphore_wait(barrier, len(devices))


def split_index(k, zs):
    return k % zs, (k // zs) % 2, k // (2 * zs)


def gather_kernel(dp, experts, in_ref, out_ref, send, recv, csend, crecv, own):
    p = Place(dp, experts)
    zs = p.zs
    c = p.core
    n = 4 * zs
    partner = (p.a, p.e + 1 - 2 * c)
    peers = [p.device(c, dz, 0, 0) for dz in range(1, zs)]
    second = p.device(c, 0, 1, 0)
    third = p.device(c, 0, 0, 1)
    me = p.flat((p.a, p.e))
    mine = pltpu.make_async_copy(in_ref, out_ref.at[me], own)
    mine.start()
    greet(peers + [second, third, partner])
    pending = []

    def block(k):
        if k == 0:
            return me, in_ref
        dz, s2, s3 = split_index(k, zs)
        at = p.flat(p.device(c, (zs - dz) % zs, s2, s3))
        return at, out_ref.at[at]

    def push(k, slot, dev):
        at, src = block(k)
        cp = remote(src, out_ref.at[at], send.at[slot], recv.at[slot], dev)
        cp.start()
        pending.append(cp)

    def hand(k):
        at, src = block(k)
        cp = remote(src, out_ref.at[at], csend.at[k], crecv.at[k], partner)
        cp.start()
        pending.append(cp)

    def arrived(k):
        at, _ = block(k)
        remote(in_ref, out_ref.at[at], send.at[k], recv.at[k], partner).wait_recv()

    for dz in range(1, zs):
        push(0, dz, peers[dz - 1])
    push(0, zs, second)
    push(0, 2 * zs, third)
    hand(0)
    for k in range(1, zs):
        arrived(k)
        push(k, zs + k, second)
        push(k, 2 * zs + k, third)
        hand(k)
    for k in range(zs, 2 * zs):
        arrived(k)
        push(k, 2 * zs + k, third)
        hand(k)
    for k in range(2 * zs, 4 * zs):
        arrived(k)
        hand(k)
    for k in range(n):
        dz, s2, s3 = split_index(k, zs)
        at = p.flat(p.device(1 - c, (zs - dz) % zs, s2, s3))
        remote(in_ref, out_ref.at[at], csend.at[k], crecv.at[k], partner).wait_recv()
    for cp in pending:
        cp.wait_send()
    mine.wait()


def gather_blocks(block, dp, experts, cid):
    n = dp * experts
    return pl.pallas_call(
        functools.partial(gather_kernel, dp, experts),
        out_shape=jax.ShapeDtypeStruct((n,) + block.shape, block.dtype),
        in_specs=[ANY],
        out_specs=ANY,
        scratch_shapes=[
            pltpu.SemaphoreType.DMA((n // 2,)),
            pltpu.SemaphoreType.DMA((n // 2,)),
            pltpu.SemaphoreType.DMA((n // 2,)),
            pltpu.SemaphoreType.DMA((n // 2,)),
            pltpu.SemaphoreType.DMA,
        ],
        compiler_params=pltpu.CompilerParams(collective_id=cid, has_side_effects=True),
        name="gather_dense",
    )(block)


def reduce_kernel(dp, experts, grad_ref, part_ref, out_ref, total_ref, own, rc, r3, r2, rz, fin, row, tiles,
                  load, csend, crecv, send, recv, fsend, frecv, nsend, nrecv):
    p = Place(dp, experts)
    zs = p.zs
    c = p.core
    n = 4 * zs
    world = dp * experts
    half = own.shape[2]
    deep = own.shape[1] // 2
    partner = (p.a, p.e + 1 - 2 * c)
    second = p.device(c, 0, 1, 0)
    third = p.device(c, 0, 0, 1)
    me = p.flat((p.a, p.e))
    everyone = []
    for j in range(1, world):
        other = lax.rem(me + j, world)
        everyone.append((lax.div(other, experts), lax.rem(other, experts)))
    mycols = pl.ds(pl.multiple_of(c * half, 128), half)
    hiscols = pl.ds(pl.multiple_of((1 - c) * half, 128), half)
    order = list(range(2 * zs, n)) + list(range(zs, 2 * zs)) + list(range(1, zs)) + [0]
    loads = {}
    for k in order:
        loads[k] = pltpu.make_async_copy(grad_ref.at[p.chip(c, *split_index(k, zs)), :, mycols], own.at[k], load.at[k])
        loads[k].start()
    greet(everyone)
    pending = []

    def push(src, dst, ss, rs, dev):
        cp = remote(src, dst, ss, rs, dev)
        cp.start()
        pending.append(cp)

    for k in order:
        push(grad_ref.at[p.chip(1 - c, *split_index(k, zs)), :, hiscols], rc.at[k], csend.at[k], crecv.at[k], partner)

    def got(ref, sem):
        remote(ref, ref, sem, sem, partner).wait_recv()

    for k in order:
        loads[k].wait()
        got(rc.at[k], crecv.at[k])
        total = own[k].astype(jnp.float32) + rc[k].astype(jnp.float32)
        if k < 2 * zs:
            got(r3.at[k], recv.at[2 * zs + k])
            total = total + r3[k].astype(jnp.float32)
        if k < zs:
            got(r2.at[k], recv.at[zs + k])
            total = total + r2[k].astype(jnp.float32)
        if k >= 1:
            own[k] = total.astype(own.dtype)
        if k >= 2 * zs:
            push(own.at[k], r3.at[k - 2 * zs], send.at[k], recv.at[k], third)
        elif k >= zs:
            push(own.at[k], r2.at[k - zs], send.at[k], recv.at[k], second)
        elif k >= 1:
            push(own.at[k], rz.at[k - 1], send.at[k], recv.at[k], p.device(c, k, 0, 0))
        else:
            for j in range(1, zs):
                got(rz.at[j - 1], recv.at[j])
                total = total + rz[j - 1].astype(jnp.float32)
            fin[...] = total
    his = pl.ds(pl.multiple_of((1 - c) * deep, 8), deep)
    mine = pl.ds(pl.multiple_of(c * deep, 8), deep)
    push(fin.at[his], row, fsend, frecv, partner)
    square = part_ref[...]
    for i in range(2 * deep // 8):
        for j in range(half // 128):
            v = fin[pl.ds(8 * i, 8), pl.ds(128 * j, 128)]
            square = square + v * v
    tiles[me] = square
    for j in range(1, world):
        push(tiles.at[me], tiles.at[me], nsend.at[j], nrecv.at[j], everyone[j - 1])
    out_ref[:, mycols] = fin[mine, :]
    got(row, frecv)
    out_ref[:, hiscols] = row[...]
    for j in range(1, world):
        src = lax.rem(me + world - j, world)
        got(tiles.at[src], nrecv.at[j])
    total = tiles[0]
    for j in range(1, world):
        total = total + tiles[j]
    total_ref[...] = total
    for cp in pending:
        cp.wait_send()


def reduce_blocks(grads, part, dp, experts, cid):
    n = dp * experts
    chips, rows, cols = grads.shape
    half = cols // 2
    bf = jnp.bfloat16
    return pl.pallas_call(
        functools.partial(reduce_kernel, dp, experts),
        out_shape=[jax.ShapeDtypeStruct((rows // 2, cols), jnp.float32), jax.ShapeDtypeStruct((8, 128), jnp.float32)],
        in_specs=[ANY, VMEM],
        out_specs=[VMEM, VMEM],
        scratch_shapes=[
            pltpu.VMEM((chips, rows, half), bf),
            pltpu.VMEM((chips, rows, half), bf),
            pltpu.VMEM((chips // 2, rows, half), bf),
            pltpu.VMEM((chips // 4, rows, half), bf),
            pltpu.VMEM((chips // 4 - 1, rows, half), bf),
            pltpu.VMEM((rows, half), jnp.float32),
            pltpu.VMEM((rows // 2, half), jnp.float32),
            pltpu.VMEM((n, 8, 128), jnp.float32),
            pltpu.SemaphoreType.DMA((chips,)),
            pltpu.SemaphoreType.DMA((chips,)),
            pltpu.SemaphoreType.DMA((chips,)),
            pltpu.SemaphoreType.DMA((chips,)),
            pltpu.SemaphoreType.DMA((chips,)),
            pltpu.SemaphoreType.DMA,
            pltpu.SemaphoreType.DMA,
            pltpu.SemaphoreType.DMA((n,)),
            pltpu.SemaphoreType.DMA((n,)),
        ],
        compiler_params=pltpu.CompilerParams(collective_id=cid, has_side_effects=True, vmem_limit_bytes=32 * 1024 * 1024),
        name="reduce_dense",
    )(grads, part)


LANES = 128


def nn(left, right):
    return lax.dot_general(left, right, (((1,), (0,)), ((), ())), preferred_element_type=jnp.float32)


def nt(left, right):
    return lax.dot_general(left, right, (((1,), (1,)), ((), ())), preferred_element_type=jnp.float32)


def lane_ids(rows, start=0):
    return lax.broadcasted_iota(jnp.int32, (rows, LANES), 1) + start


def row_parts(count, size):
    return [pl.ds(i * size, size) for i in range(count // size)]


def norm_parts(values):
    center = values - jnp.mean(values, axis=-1, keepdims=True)
    inverse = lax.rsqrt(jnp.mean(center * center, axis=-1, keepdims=True) + NORM_EPS)
    return center * inverse, inverse


def vector_table(weights, width):
    return jnp.transpose(weights[:, 4 * width :].astype(jnp.float32))


def forward_kernel(
    experts,
    capacity,
    chunk,
    tok_ref,
    cot_ref,
    choice_ref,
    rank_col,
    rank_row,
    weights_any,
    rows_ref,
    dy_ref,
    qkv_ref,
    ctx_ref,
    mid_ref,
    second_ref,
    stat_ref,
    aux_ref,
    probs_ref,
    weights,
    vec,
    normed,
    load,
):
    low = jnp.bfloat16
    patches, width = tok_ref.shape
    fetch = pltpu.make_async_copy(weights_any, weights, load)
    fetch.start()
    lanes = lane_ids(patches)
    first, other = choice_ref[:, 0:1], choice_ref[:, 1:2]
    is_first, is_other = lanes == first, lanes == other
    before = (rank_row[...] < rank_col[...]).astype(jnp.float32).astype(low)
    hot = (is_first | (lanes == other + experts)).astype(jnp.float32)
    counts = nn(before, hot.astype(low))
    totals = jnp.sum(hot, axis=0, keepdims=True)
    place_first = jnp.sum(jnp.where(is_first, counts, 0.0), axis=1, keepdims=True)
    place_other = jnp.sum(
        jnp.where(lanes == other + experts, counts, 0.0) + jnp.where(is_other, totals, 0.0), axis=1, keepdims=True
    )
    fetch.wait()
    vec[...] = vector_table(weights, width)

    def row(i):
        return vec[experts + i : experts + i + 1, :]

    for part in row_parts(patches, chunk):
        unit, _ = norm_parts(tok_ref[part, :].astype(jnp.float32))
        normed[part, :] = (unit * row(0) + row(1)).astype(low)
    third = 256
    for base, bias in ((0, 2), (width, None), (2 * width, 3)):
        for j in range(width // third):
            columns = pl.ds(base + j * third, third)
            product = nn(normed[...], weights[:, columns])
            if bias is not None:
                product = product + vec[experts + bias : experts + bias + 1, pl.ds(j * third, third)]
            qkv_ref[:, columns] = product.astype(low)
    stat_ref[...] = jnp.zeros_like(stat_ref)

    @pl.loop(0, width // LANES)
    def _(pair):
        at = pl.multiple_of(pair * LANES, LANES)
        keys = qkv_ref[:, pl.ds(pl.multiple_of(width + at, LANES), LANES)]
        values = qkv_ref[:, pl.ds(pl.multiple_of(2 * width + at, LANES), LANES)]
        key_lanes = lane_ids(patches)
        values_two = [
            jnp.where(key_lanes < HEAD_DIM, values, (key_lanes == HEAD_DIM).astype(jnp.float32).astype(low)),
            jnp.where(key_lanes >= HEAD_DIM, values, (key_lanes == 0).astype(jnp.float32).astype(low)),
        ]
        for part in row_parts(patches, chunk):
            own = lane_ids(chunk)
            queries = qkv_ref[part, pl.ds(at, LANES)] * jnp.asarray(HEAD_DIM**-0.5, low)
            outs = []
            stat = stat_ref[part, :]
            for head in range(2):
                mine = (own < HEAD_DIM) if head == 0 else (own >= HEAD_DIM)
                scores = nt(jnp.where(mine, queries, jnp.zeros_like(queries)), keys)
                top = jnp.max(scores, axis=1, keepdims=True)
                raised = jnp.exp(scores - top)
                mixed = nn(raised.astype(low), values_two[head])
                spare = HEAD_DIM if head == 0 else 0
                total = mixed[:, spare : spare + 1]
                outs.append(mixed / total)
                stat = jnp.where(own == 2 * pair + head, top + jnp.log(total), stat)
            stat_ref[part, :] = stat
            ctx_ref[part, pl.ds(at, LANES)] = jnp.where(own < HEAD_DIM, outs[0], outs[1]).astype(low)

    for j in range(width // third):
        columns = pl.ds(j * third, third)
        product = nn(ctx_ref[...], weights[:, pl.ds(3 * width + j * third, third)])
        mid_ref[:, columns] = tok_ref[:, columns].astype(jnp.float32) + (
            product + vec[experts + 4 : experts + 5, columns]
        )
    for part in row_parts(patches, chunk):
        unit, _ = norm_parts(mid_ref[part, :])
        second_ref[part, :] = (unit * row(5) + row(6)).astype(low)
    logits = jnp.where(lanes < experts, nn(second_ref[...], weights[:, 4 * width :]), -1e30)
    raised = jnp.exp(logits - jnp.max(logits, axis=1, keepdims=True))
    probs = raised / jnp.sum(raised, axis=1, keepdims=True)
    probs_ref[...] = probs

    def slot_of(place, expert):
        place = place.astype(jnp.int32)
        kept = place < capacity
        slot = (place // 8) * LANES + expert * 8 + place % 8
        tail = kept & (place >= capacity - 4)
        return kept, jnp.where(kept, slot, -1), jnp.where(tail, slot + 4, -1)

    aux = jnp.zeros((patches, LANES), jnp.float32)
    for j, (place, expert, hit) in enumerate(((place_first, first, is_first), (place_other, other, is_other))):
        kept, slot, twin = slot_of(place, expert)
        gate = jnp.where(kept, jnp.sum(jnp.where(hit, probs, 0.0), axis=1, keepdims=True), 0.0)
        for lane, column in ((j, slot.astype(jnp.float32)), (2 + j, twin.astype(jnp.float32)), (4 + j, gate)):
            aux = jnp.where(lanes == lane, column, aux)
    aux_ref[...] = aux
    turned = jnp.transpose(aux)
    slots = [turned[i : i + 1, :] for i in range(4)]
    gates = [turned[4 + i : 5 + i, :] for i in range(2)]
    full = capacity // 8
    for i in range(full + 1):
        ids = (lax.broadcasted_iota(jnp.int32, (LANES, patches), 0) + i * LANES).astype(jnp.float32)
        hits = [ids == slots[0], ids == slots[1]]
        if i == full:
            hits = [hits[0] | (ids == slots[2]), hits[1] | (ids == slots[3])]
        table = (hits[0] | hits[1]).astype(jnp.float32).astype(low)
        gate = jnp.sum(
            jnp.where(hits[0], gates[0], 0.0) + jnp.where(hits[1], gates[1], 0.0), axis=1, keepdims=True
        )
        sent = nn(table, second_ref[...])
        back = nn(table, cot_ref[...]) * gate
        columns = pl.ds(i * width, width)
        if i == full:
            columns = pl.ds(i * width, width // 2)
            left = lax.broadcasted_iota(jnp.int32, (LANES, width // 2), 0) % 8 < 4
            sent = jnp.where(left, sent[:, : width // 2], sent[:, width // 2 :])
            back = jnp.where(left, back[:, : width // 2], back[:, width // 2 :])
        rows_ref[:, columns] = sent.astype(low)
        dy_ref[:, columns] = back.astype(low)


def forward(tokens, cotangent, choice, priority, weights, experts, capacity, chunk=192):
    patches, width = tokens.shape
    low, full = jnp.bfloat16, jnp.float32
    packed = (8 * experts, capacity * width // 8)
    shapes = [
        (packed, low),
        (packed, low),
        ((patches, 3 * width), low),
        ((patches, width), low),
        ((patches, width), full),
        ((patches, width), low),
        ((patches, LANES), full),
        ((patches, LANES), full),
        ((patches, LANES), full),
    ]
    return pl.pallas_call(
        functools.partial(forward_kernel, experts, capacity, chunk),
        out_shape=[jax.ShapeDtypeStruct(*s) for s in shapes],
        in_specs=[VMEM] * 5 + [ANY],
        out_specs=[VMEM] * 9,
        scratch_shapes=[
            pltpu.VMEM(weights.shape, low),
            pltpu.VMEM((LANES, width), full),
            pltpu.VMEM((patches, width), low),
            pltpu.SemaphoreType.DMA,
        ],
        compiler_params=pltpu.CompilerParams(vmem_limit_bytes=56 * 1024 * 1024),
        cost_estimate=pl.CostEstimate(flops=6 * 10**9, bytes_accessed=20 * 10**6, transcendentals=4 * 10**6),
        name="attend_forward",
    )(tokens, cotangent, choice, priority.reshape(patches, 1), priority.reshape(1, patches), weights)


def gelu_both(z):
    root = 0.7978845608028654
    square = z * z
    slope = jnp.tanh(root * z * (1.0 + 0.044715 * square))
    half = 0.5 * (1.0 + slope)
    act = z * half
    grad = half + 0.5 * z * (1.0 - slope * slope) * (root * (1.0 + 3 * 0.044715 * square))
    return act, grad


def tail_picks(count, right):
    rows = lax.broadcasted_iota(jnp.int32, (count // 2, count), 0)
    ids = lax.broadcasted_iota(jnp.int32, (count // 2, count), 1)
    hit = ids == (rows // 4) * 8 + rows % 4 + (4 if right else 0)
    return hit.astype(jnp.float32).astype(jnp.bfloat16)


def backward_kernel(
    experts,
    capacity,
    chunk,
    tok_ref,
    cot_ref,
    choice_ref,
    ret_ref,
    back_ref,
    aux_ref,
    probs_ref,
    mid_ref,
    second_ref,
    ctx_ref,
    stat_ref,
    qkv_ref,
    weights_any,
    out_ref,
    input_ref,
    grad_ref,
    weights,
    vec,
    stacked,
    normed,
    branch,
    dctx,
    joined,
    turned_query,
    dmid,
    work,
    sums,
    load,
):
    low = jnp.bfloat16
    patches, width = tok_ref.shape
    fetch = pltpu.make_async_copy(weights_any, weights, load)
    fetch.start()
    full = capacity // 8
    half = width // 2
    lanes = lane_ids(patches)
    aux = aux_ref[...]
    slots = [aux[:, i : i + 1] for i in range(4)]
    gates = [aux[:, 4 + i : 5 + i] for i in range(2)]
    ids = lax.broadcasted_iota(jnp.int32, (patches, full * LANES), 1).astype(jnp.float32)
    tail_ids = lane_ids(patches, full * LANES).astype(jnp.float32)
    hits = [ids == slots[0], ids == slots[1]]
    lefts = [tail_ids == slots[0], tail_ids == slots[1]]
    rights = [tail_ids == slots[2], tail_ids == slots[3]]

    def mix(marks):
        return (jnp.where(marks[0], gates[0], 0.0) + jnp.where(marks[1], gates[1], 0.0)).astype(low)

    def pick(marks):
        return (marks[0] | marks[1]).astype(jnp.float32).astype(low)

    for i in range(full):
        stacked[pl.ds(i * LANES, LANES), :] = ret_ref[:, pl.ds(i * width, width)]
    tail = ret_ref[:, pl.ds(full * width, half)]
    left_mix, right_mix = nn(mix(lefts), tail), nn(mix(rights), tail)
    final = nn(mix(hits), stacked[...])
    out_ref[:, :half] = (mid_ref[:, :half] + (final[:, :half] + left_mix)).astype(low)
    out_ref[:, half:] = (mid_ref[:, half:] + (final[:, half:] + right_mix)).astype(low)
    along = nt(cot_ref[...], stacked[...])
    along_left, along_right = nt(cot_ref[:, :half], tail), nt(cot_ref[:, half:], tail)
    dprobs = jnp.zeros((patches, LANES), jnp.float32)
    for j in range(2):
        dgate = jnp.sum(jnp.where(hits[j], along, 0.0), axis=1, keepdims=True) + jnp.sum(
            jnp.where(lefts[j], along_left, 0.0) + jnp.where(rights[j], along_right, 0.0), axis=1, keepdims=True
        )
        dprobs = dprobs + jnp.where(lanes == choice_ref[:, j : j + 1], dgate, 0.0)
    probs = probs_ref[...]
    dlogits = (probs * (dprobs - jnp.sum(probs * dprobs, axis=1, keepdims=True))).astype(low)
    for i in range(full):
        stacked[pl.ds(i * LANES, LANES), :] = back_ref[:, pl.ds(i * width, width)]
    tail = back_ref[:, pl.ds(full * width, half)]
    fetch.wait()
    vec[...] = vector_table(weights, width)

    def row(i):
        return vec[experts + i : experts + i + 1, :]

    routed = weights[:, 4 * width :]
    work[...] = nn(pick(hits), stacked[...]) + nt(dlogits, routed)
    work[:, :half] = work[:, :half] + nn(pick(lefts), tail)
    work[:, half:] = work[:, half:] + nn(pick(rights), tail)
    sums[...] = jnp.zeros_like(sums)

    def column_sum(slot, values):
        sums[pl.ds(8 * slot, 8), :] = sums[pl.ds(8 * slot, 8), :] + jnp.sum(
            values.reshape(-1, 8, values.shape[-1]), axis=0
        )

    def norm_back(grad, unit, inverse, gain):
        weighted = grad * gain
        return inverse * (
            weighted
            - jnp.mean(weighted, axis=-1, keepdims=True)
            - unit * jnp.mean(weighted * unit, axis=-1, keepdims=True)
        )

    for part in row_parts(patches, chunk):
        unit, inverse = norm_parts(mid_ref[part, :])
        grad = work[part, :]
        column_sum(5, grad * unit)
        column_sum(6, grad)
        total = cot_ref[part, :].astype(jnp.float32) + norm_back(grad, unit, inverse, row(5))
        dmid[part, :] = total
        rounded = total.astype(low)
        branch[part, :] = rounded
        column_sum(4, rounded.astype(jnp.float32))
    third = 256
    for j in range(width // third):
        rows = pl.ds(j * third, third)
        dctx[:, rows] = nt(branch[...], weights[rows, pl.ds(3 * width, width)]).astype(low)
    second_turned = jnp.transpose(second_ref[...])
    router_grad = nn(second_turned, dlogits)
    ctx_turned = jnp.transpose(ctx_ref[...])
    for j in range(width // third):
        columns = pl.ds(j * third, third)
        grad_ref[:, pl.ds(3 * width + j * third, third)] = nn(ctx_turned, branch[:, columns]).astype(low)
    heads = (
        lax.broadcasted_iota(jnp.int32, (16, width), 1) // HEAD_DIM == lax.broadcasted_iota(jnp.int32, (16, width), 0)
    ).astype(jnp.float32).astype(low)
    product = dctx[...].astype(jnp.float32) * ctx_ref[...].astype(jnp.float32)
    upper = product.astype(low)
    center = nt(heads, upper) + nt(heads, (product - upper.astype(jnp.float32)).astype(low))
    logs = jnp.transpose(stat_ref[...])
    sums_rows = jnp.concatenate([logs[:16], center], axis=0)
    vec_rows = work
    vec_rows[0:32, :patches] = sums_rows

    @pl.loop(0, width // LANES)
    def _(pair):
        at = pl.multiple_of(pair * LANES, LANES)
        key_at = pl.ds(pl.multiple_of(width + at, LANES), LANES)
        value_at = pl.ds(pl.multiple_of(2 * width + at, LANES), LANES)
        scale = jnp.asarray(HEAD_DIM**-0.5, low)
        queries = qkv_ref[:, pl.ds(at, LANES)] * scale
        given = dctx[:, pl.ds(at, LANES)]
        own = lane_ids(patches)
        zero = jnp.zeros_like(queries)
        marks = [own < HEAD_DIM, own >= HEAD_DIM]
        head_queries = [jnp.where(m, queries, zero) for m in marks]
        head_given = [jnp.where(m, given, zero) for m in marks]
        turned_keys = jnp.transpose(qkv_ref[:, key_at] * scale)
        query_parts = [None, None]
        for part in row_parts(patches, chunk):
            keys = qkv_ref[part, key_at]
            values = qkv_ref[part, value_at]
            value_out, key_out = [], []
            for head in range(2):
                log_row = work[pl.ds(2 * pair + head, 1), :patches]
                center_row = work[pl.ds(16 + 2 * pair + head, 1), :patches]
                prob = jnp.exp(nt(keys, head_queries[head]) - log_row)
                value_out.append(nn(prob.astype(low), given))
                dscore = (prob * (nt(values, head_given[head]) - center_row)).astype(low)
                key_out.append(nn(dscore, queries))
                piece = nn(turned_keys[HEAD_DIM * head : HEAD_DIM * (head + 1), part.start : part.start + part.size], dscore)
                query_parts[head] = piece if query_parts[head] is None else query_parts[head] + piece
            side = lane_ids(chunk) < HEAD_DIM
            joined[part, key_at] = jnp.where(side, key_out[0], key_out[1]).astype(low)
            joined[part, value_at] = jnp.where(side, value_out[0], value_out[1]).astype(low)
        turned_query[...] = jnp.concatenate(query_parts, axis=0)
        joined[:, pl.ds(at, LANES)] = jnp.transpose(turned_query[...]).astype(low)

    for part in row_parts(patches, chunk):
        unit, _ = norm_parts(tok_ref[part, :].astype(jnp.float32))
        normed[part, :] = (unit * row(0) + row(1)).astype(low)
        column_sum(2, joined[part, :width].astype(jnp.float32))
        column_sum(3, joined[part, 2 * width :].astype(jnp.float32))
    normed_turned = jnp.transpose(normed[...])
    for j in range(3 * width // third):
        columns = pl.ds(j * third, third)
        grad_ref[:, columns] = nn(normed_turned, joined[:, columns]).astype(low)
    for j in range(width // third):
        rows = pl.ds(j * third, third)
        work[:, rows] = nt(joined[...], weights[rows, : 3 * width])
    for part in row_parts(patches, chunk):
        unit, inverse = norm_parts(tok_ref[part, :].astype(jnp.float32))
        grad = work[part, :]
        column_sum(0, grad * unit)
        column_sum(1, grad)
        input_ref[part, :] = dmid[part, :] + norm_back(grad, unit, inverse, row(0))
    vec[...] = jnp.zeros_like(vec)
    for i in range(7):
        vec[experts + i : experts + i + 1, :] = jnp.sum(sums[pl.ds(8 * i, 8), :], axis=0, keepdims=True)
    last = router_grad + jnp.transpose(vec[...])
    grad_ref[:, pl.ds(4 * width, LANES)] = last.astype(low)
    rest = grad_ref.shape[1] - 4 * width - LANES
    grad_ref[:, pl.ds(4 * width + LANES, rest)] = jnp.zeros((width, rest), low)


def backward(
    tokens, cotangent, choice, ret, back, aux, probs, mid, second, ctx, stat, qkv, weights, experts, capacity, chunk=192
):
    patches, width = tokens.shape
    low, full = jnp.bfloat16, jnp.float32
    columns = -(-weights.shape[1] // 256) * 256
    return pl.pallas_call(
        functools.partial(backward_kernel, experts, capacity, chunk),
        out_shape=[
            jax.ShapeDtypeStruct((patches, width), low),
            jax.ShapeDtypeStruct((patches, width), full),
            jax.ShapeDtypeStruct((width, columns), low),
        ],
        in_specs=[VMEM] * 12 + [ANY],
        out_specs=[VMEM] * 3,
        scratch_shapes=[
            pltpu.VMEM(weights.shape, low),
            pltpu.VMEM((LANES, width), full),
            pltpu.VMEM((capacity // 8 * LANES, width), low),
            pltpu.VMEM((patches, width), low),
            pltpu.VMEM((patches, width), low),
            pltpu.VMEM((patches, width), low),
            pltpu.VMEM((patches, 3 * width), low),
            pltpu.VMEM((LANES, patches), full),
            pltpu.VMEM((patches, width), full),
            pltpu.VMEM((patches, width), full),
            pltpu.VMEM((56, width), full),
            pltpu.SemaphoreType.DMA,
        ],
        compiler_params=pltpu.CompilerParams(vmem_limit_bytes=60 * 1024 * 1024),
        cost_estimate=pl.CostEstimate(flops=15 * 10**9, bytes_accessed=30 * 10**6, transcendentals=4 * 10**6),
        name="attend_backward",
    )(tokens, cotangent, choice, ret, back, aux, probs, mid, second, ctx, stat, qkv, weights)


def moe_kernel(
    dp,
    experts,
    chunk,
    rows_any,
    dy_any,
    inner_any,
    hidden_ref,
    outer_any,
    return_ref,
    y_any,
    drows_any,
    dinner_any,
    dhidden_ref,
    douter_any,
    dreturn_ref,
    square_ref,
    rows_all,
    dy_all,
    y_pack,
    drows_pack,
    y_theirs,
    drows_theirs,
    rows,
    turned,
    dy,
    inner,
    outer,
    act,
    grad,
    dz,
    acc,
    inner_stage,
    outer_stage,
    dinner_stage,
    douter_stage,
    square,
    own_sem,
    in_send,
    in_recv,
    over_send,
    over_recv,
    part_send,
    part_recv,
    out_send,
    out_recv,
    stage_sem,
    store_sem,
):
    low, full32 = jnp.bfloat16, jnp.float32
    width = rows.shape[1]
    count = dp * experts * 8
    half = width // 2
    full = rows_all.shape[3] // width
    steps = inner.shape[1] // chunk
    each = -(-(experts - 1) // (steps - 1))
    a = lax.axis_index("dp")
    e = lax.axis_index("expert")
    across = (1 - a, e)
    ins, alls = (rows_any, dy_any), (rows_all, dy_all)
    packs, theirs, outs = (y_pack, drows_pack), (y_theirs, drows_theirs), (y_any, drows_any)

    def to(j):
        return lax.rem(e + j, experts)

    def source(j):
        return lax.rem(e + experts - j, experts)

    def stage(k, slot):
        columns = pl.ds(pl.multiple_of(k * chunk, chunk), chunk)
        return (
            pltpu.make_async_copy(inner_any.at[0, :, columns], inner_stage.at[slot], stage_sem.at[0, slot]),
            pltpu.make_async_copy(outer_any.at[0, columns, :], outer_stage.at[slot], stage_sem.at[1, slot]),
        )

    def own_block(i):
        return pltpu.make_async_copy(ins[i].at[e], alls[i].at[a, e], own_sem.at[i])

    for slot in range(2):
        for copy in stage(slot, slot):
            copy.start()
    for i in range(2):
        own_block(i).start()
    greet([(a, to(j)) for j in range(1, experts)] + [across])

    def first_send(i, j):
        return remote(ins[i].at[to(j)], alls[i].at[a, e], in_send.at[i, j], in_recv.at[i, j], (a, to(j)))

    def forward_own(i):
        return remote(ins[i].at[e], alls[i].at[a, e], over_send.at[i, 0], over_recv.at[i, 0], across)

    def pass_on(i, j):
        block = alls[i].at[a, source(j)]
        return remote(block, block, over_send.at[i, j], over_recv.at[i, j], across)

    def received(i, j):
        block = alls[i].at[a, source(j)]
        return remote(block, block, in_send.at[i, j], in_recv.at[i, j], across)

    def from_across(i, j):
        block = alls[i].at[1 - a, source(j)]
        return remote(block, block, over_send.at[i, j], over_recv.at[i, j], across)

    def part_copy(i, j):
        return remote(
            packs[i].at[1 - a, to(j)], theirs[i].at[j], part_send.at[i, j], part_recv.at[i, j], across
        )

    def result_copy(i, j):
        return remote(packs[i].at[a, to(j)], outs[i].at[e], out_send.at[i, j], out_recv.at[i, j], (a, to(j)))

    for i in range(2):
        forward_own(i).start()

        @pl.loop(1, experts)
        def _(j):
            first_send(i, j).start()

    def take_in(i, k):
        @pl.when(k < steps - 1)
        def _():
            @pl.loop(0, each)
            def _(d):
                j = 1 + k * each + d

                @pl.when(j < experts)
                def _():
                    received(i, j).wait_recv()
                    pass_on(i, j).start()

    def hand_out(i, k):
        @pl.when(k < steps - 1)
        def _():
            @pl.loop(0, each)
            def _(d):
                j = 1 + k * each + d

                @pl.when(j < experts)
                def _():
                    part_copy(i, j).wait_recv()
                    at = to(j)
                    packs[i][a, at] = (packs[i][a, at].astype(full32) + theirs[i][j].astype(full32)).astype(low)
                    result_copy(i, j).start()

    @pl.loop(0, steps)
    def _(k):
        slot = lax.rem(k, 2)
        columns = pl.ds(pl.multiple_of(k * chunk, chunk), chunk)
        for copy in stage(k, slot):
            copy.wait()
        inner[:, columns] = inner_stage[slot].astype(low)
        outer[columns, :] = outer_stage[slot].astype(low)

        @pl.when(k + 2 < steps)
        def _():
            for copy in stage(k + 2, slot):
                copy.start()

        take_in(0, k)

    def unpack(i, place):
        own_block(i).wait()

        @pl.loop(0, experts)
        def _(j):
            from_across(i, j).wait_recv()

        group = 8
        for plane in range(dp):
            for s in range(0, experts, group):
                base = (plane * experts + s) * 8
                for b in range(full):
                    piece = alls[i][plane, s : s + group, :, b * width : (b + 1) * width].astype(full32)
                    place[pl.ds(b * count + base, 8 * group), :] = piece.reshape(8 * group, width).astype(low)
        tails = [
            alls[i][plane, :, :, full * width :].astype(full32).reshape(experts * 8, half) for plane in range(dp)
        ]
        tail = jnp.concatenate(tails, axis=0).astype(low)
        for right in range(2):
            place[pl.ds(full * count, count // 2), pl.ds(right * half, half)] = nn(
                tail_picks(count, right), tail
            ).astype(low)

    def pack(i):
        group = 8
        for plane in range(dp):
            for s in range(0, experts, group):
                base = (plane * experts + s) * 8
                for b in range(full):
                    piece = acc[pl.ds(b * count + base, 8 * group), :].reshape(group, 8, width)
                    packs[i][plane, s : s + group, :, b * width : (b + 1) * width] = piece.astype(low)
        tail = acc[pl.ds(full * count, count // 2), :].astype(low)
        spread = None
        for right in range(2):
            piece = lax.dot_general(
                tail_picks(count, right),
                tail[:, right * half : (right + 1) * half],
                (((0,), (0,)), ((), ())),
                preferred_element_type=full32,
            )
            spread = piece if spread is None else spread + piece
        for plane in range(dp):
            piece = spread[plane * experts * 8 : (plane + 1) * experts * 8].reshape(experts, 8, half)
            packs[i][plane, :, :, full * width :] = piece.astype(low)

        @pl.loop(0, experts)
        def _(d):
            part_copy(i, lax.rem(d + 1, experts)).start()

    unpack(0, rows)
    turned[...] = jnp.transpose(rows[...])
    acc[...] = jnp.zeros_like(acc)

    @pl.loop(0, steps)
    def _(k):
        columns = pl.ds(pl.multiple_of(k * chunk, chunk), chunk)
        z = nn(rows[...], inner[:, columns]) + hidden_ref[:, columns].astype(low).astype(full32)
        value, slope = gelu_both(z)
        act[:, columns] = value.astype(low)
        grad[:, columns] = slope
        acc[...] += nn(act[:, columns], outer[columns, :])
        take_in(1, k)

    part = return_ref.shape[1]
    bias = return_ref[...].astype(low).astype(full32)
    for i in range(dp):
        columns = pl.ds(i * part, part)
        acc[:, columns] = acc[:, columns] + jnp.where(a == i, bias, 0.0)
    pack(0)
    unpack(1, dy)
    total = jnp.zeros((1, width), full32)
    for i in range(rows.shape[0] // LANES):
        total = total + jnp.sum(dy[pl.ds(i * LANES, LANES), :].astype(full32), axis=0, keepdims=True)
    picked = total[:, :part]
    for i in range(1, dp):
        picked = jnp.where(a == i, total[:, i * part : (i + 1) * part], picked)
    dreturn_ref[...] = picked
    square[...] = jnp.zeros_like(square)
    flat = picked * picked
    for i in range(part // LANES):
        square[0:1, :] = square[0:1, :] + flat[:, i * LANES : (i + 1) * LANES]
    acc[...] = jnp.zeros_like(acc)

    @pl.loop(0, steps)
    def _(k):
        columns = pl.ds(pl.multiple_of(k * chunk, chunk), chunk)
        dz[:, columns] = (nt(dy[...], outer[columns, :]) * grad[:, columns]).astype(low)
        acc[...] += nt(dz[:, columns], inner[:, columns])
        hand_out(0, k)

    pack(1)

    def finish(i):
        part_copy(i, 0).wait_recv()
        packs[i][a, e] = (packs[i][a, e].astype(full32) + theirs[i][0].astype(full32)).astype(low)
        pltpu.make_async_copy(packs[i].at[a, e], outs[i].at[e], own_sem.at[i]).start()

    def store(k, slot):
        columns = pl.ds(pl.multiple_of(k * chunk, chunk), chunk)
        return (
            pltpu.make_async_copy(dinner_stage.at[slot], dinner_any.at[0, :, columns], store_sem.at[0, slot]),
            pltpu.make_async_copy(douter_stage.at[slot], douter_any.at[0, columns, :], store_sem.at[1, slot]),
        )

    finish(0)

    @pl.loop(0, steps)
    def _(k):
        slot = lax.rem(k, 2)
        columns = pl.ds(pl.multiple_of(k * chunk, chunk), chunk)
        douter = nn(jnp.transpose(act[:, columns]), dy[...])
        dinner = nn(turned[...], dz[:, columns])
        dhidden = jnp.sum(dz[:, columns].astype(full32), axis=0, keepdims=True)

        @pl.when(k >= 2)
        def _():
            for copy in store(k - 2, slot):
                copy.wait()

        douter_stage[slot] = douter.astype(low)
        dinner_stage[slot] = dinner.astype(low)
        for copy in store(k, slot):
            copy.start()
        dhidden_ref[:, columns] = dhidden
        parts = jnp.zeros((8, LANES), full32)
        folded = jnp.sum((douter * douter).reshape(-1, 8, width), axis=0)
        for i in range(width // LANES):
            parts = parts + folded[:, i * LANES : (i + 1) * LANES]
        folded = jnp.sum((dinner * dinner).reshape(-1, 8, chunk), axis=0)
        hidden_square = dhidden * dhidden
        for i in range(chunk // LANES):
            parts = parts + folded[:, i * LANES : (i + 1) * LANES]
            square[0:1, :] = square[0:1, :] + hidden_square[:, i * LANES : (i + 1) * LANES]
        square[...] += parts
        hand_out(1, k)

    finish(1)
    square_ref[...] = square[...]
    for k in range(steps - 2, steps):
        for copy in store(k, k % 2):
            copy.wait()
    for i in range(2):

        @pl.loop(1, experts)
        def _(j):
            block = outs[i].at[source(j)]
            remote(block, block, out_send.at[i, j], out_recv.at[i, j], across).wait_recv()

    for i in range(2):
        pltpu.make_async_copy(packs[i].at[a, e], outs[i].at[e], own_sem.at[i]).wait()
        forward_own(i).wait_send()
        part_copy(i, 0).wait_send()

        @pl.loop(1, experts)
        def _(j):
            first_send(i, j).wait_send()
            pass_on(i, j).wait_send()
            part_copy(i, j).wait_send()
            result_copy(i, j).wait_send()


def mixture(rows, dy, inner, hidden, outer, back, dp, cid, chunk=256):
    experts, _, packed = rows.shape
    width, units = inner.shape[1:]
    count = dp * experts * 8
    total = count * packed // width
    low, full = jnp.bfloat16, jnp.float32
    both = (dp, experts, 8, packed)
    sems = [pltpu.SemaphoreType.DMA((2, experts)) for _ in range(8)]
    return pl.pallas_call(
        functools.partial(moe_kernel, dp, experts, chunk),
        out_shape=[
            jax.ShapeDtypeStruct(rows.shape, low),
            jax.ShapeDtypeStruct(rows.shape, low),
            jax.ShapeDtypeStruct(inner.shape, low),
            jax.ShapeDtypeStruct(hidden.shape, full),
            jax.ShapeDtypeStruct(outer.shape, low),
            jax.ShapeDtypeStruct(back.shape, full),
            jax.ShapeDtypeStruct((8, LANES), full),
        ],
        in_specs=[ANY, ANY, ANY, VMEM, ANY, VMEM],
        out_specs=[ANY, ANY, ANY, VMEM, ANY, VMEM, VMEM],
        scratch_shapes=[
            pltpu.VMEM(both, low),
            pltpu.VMEM(both, low),
            pltpu.VMEM(both, low),
            pltpu.VMEM(both, low),
            pltpu.VMEM(both[1:], low),
            pltpu.VMEM(both[1:], low),
            pltpu.VMEM((total, width), low),
            pltpu.VMEM((width, total), low),
            pltpu.VMEM((total, width), low),
            pltpu.VMEM((width, units), low),
            pltpu.VMEM((units, width), low),
            pltpu.VMEM((total, units), low),
            pltpu.VMEM((total, units), full),
            pltpu.VMEM((total, units), low),
            pltpu.VMEM((total, width), full),
            pltpu.VMEM((2, width, chunk), full),
            pltpu.VMEM((2, chunk, width), full),
            pltpu.VMEM((2, width, chunk), low),
            pltpu.VMEM((2, chunk, width), low),
            pltpu.VMEM((8, LANES), full),
            pltpu.SemaphoreType.DMA((2,)),
            *sems,
            pltpu.SemaphoreType.DMA((2, 2)),
            pltpu.SemaphoreType.DMA((2, 2)),
        ],
        compiler_params=pltpu.CompilerParams(
            collective_id=cid, has_side_effects=True, vmem_limit_bytes=60 * 1024 * 1024
        ),
        cost_estimate=pl.CostEstimate(flops=17 * 10**9, bytes_accessed=25 * 10**6, transcendentals=2 * 10**6),
        name="mixture",
    )(rows, dy, inner, hidden, outer, back)


def adam_kernel(rates, decays, big, norm_ref, *refs):
    count = len(rates)
    ins, outs = refs[: 4 * count], refs[4 * count :]
    total = jnp.sum(jnp.sum(norm_ref[...], axis=0, keepdims=True), axis=1, keepdims=True)
    clip = THRESHOLD / jnp.maximum(jnp.sqrt(total), THRESHOLD)

    def update(i):
        weight, first, second, grad = ins[4 * i : 4 * i + 4]
        new = adam_update(
            weight[...],
            first[...],
            second[...],
            grad[...].astype(jnp.float32),
            clip,
            rates[i],
            decays[i],
        )
        for place, value in zip(outs[3 * i : 3 * i + 3], new):
            place[...] = value

    for i in range(big):
        update(i)

    @pl.when(pl.program_id(0) == 0)
    def _():
        for i in range(big, count):
            update(i)


def adam_all(squares, large, small, steps=8):
    groups = list(large) + list(small)
    specs, shapes, operands = [], [], []
    in_specs = [pl.BlockSpec(squares.shape, lambda i: (0, 0))]
    for g, group in enumerate(groups):
        shape = group[0].shape
        if g < len(large):
            spec = pl.BlockSpec((shape[0] // steps, shape[1]), lambda i: (i, 0))
        else:
            spec = pl.BlockSpec(shape, lambda i: (0, 0))
        in_specs += [spec] * 4
        specs += [spec] * 3
        shapes += [jax.ShapeDtypeStruct(shape, jnp.float32)] * 3
        operands += list(group[:4])
    rates, decays = [g[4] for g in groups], [g[5] for g in groups]
    out = pl.pallas_call(
        functools.partial(adam_kernel, rates, decays, len(large)),
        grid=(steps,),
        out_shape=shapes,
        in_specs=in_specs,
        out_specs=specs,
        compiler_params=pltpu.CompilerParams(
            vmem_limit_bytes=48 * 1024 * 1024, dimension_semantics=("arbitrary",)
        ),
        cost_estimate=pl.CostEstimate(flops=5 * 10**7, bytes_accessed=62 * 10**6, transcendentals=10**7),
        name="adam_all",
    )(squares, *operands)
    return [tuple(out[3 * i : 3 * i + 3]) for i in range(len(groups))]


def fits(dp, experts):
    return dp == 2 and experts == 16


def fast_shards(
    dp,
    experts,
    tokens,
    cotangent,
    expert_choice,
    priority,
    projection,
    projection_first,
    projection_second,
    output_weight,
    output_first,
    output_second,
    router_weight,
    router_first,
    router_second,
    vectors,
    vectors_first,
    vectors_second,
    expert_inner,
    inner_first,
    inner_second,
    hidden_bias,
    hidden_first,
    hidden_second,
    expert_outer,
    outer_first,
    outer_second,
    return_bias,
    return_first,
    return_second,
):
    model_width = tokens.shape[2]
    patches = tokens.shape[1]
    capacity = max(2, patches // experts)
    low = jnp.bfloat16
    shard_rows = projection.shape[0]
    wide = 3 * model_width
    used = wide + model_width + experts + vectors.shape[0]
    packed = jnp.concatenate(
        [projection, output_weight, router_weight, vectors.T, jnp.zeros((shard_rows, -used % 128), jnp.float32)], axis=1
    ).astype(low)
    weights = gather_blocks(packed, dp, experts, 1).reshape(model_width, packed.shape[1])
    rows, dy, qkv, ctx, mid, second, stat, aux, probs = forward(
        tokens[0], cotangent[0], expert_choice[0], priority[0], weights, experts, capacity
    )
    blocks = (experts, 8, rows.shape[1])
    returned, back_rows, inner_grad, hidden_grad, outer_grad, return_grad, expert_square = mixture(
        rows.reshape(blocks),
        dy.reshape(blocks),
        expert_inner,
        hidden_bias,
        expert_outer,
        return_bias,
        dp,
        2,
    )
    block_output, input_grad, local_grads = backward(
        tokens[0],
        cotangent[0],
        expert_choice[0],
        returned.reshape(rows.shape),
        back_rows.reshape(rows.shape),
        aux,
        probs,
        mid,
        second,
        ctx,
        stat,
        qkv,
        weights,
        experts,
        capacity,
    )
    chips = dp * experts // 2
    dense, squares = reduce_blocks(
        local_grads.reshape(chips, 2 * shard_rows, -1), expert_square, dp, experts, 4
    )
    cut = wide + model_width
    inner_new, outer_new, projection_new, output_new, router_new, vectors_new, hidden_new, return_new = adam_all(
        squares,
        [
            (expert_inner[0], inner_first[0], inner_second[0], inner_grad[0], RATE_INNER, DECAY),
            (expert_outer[0], outer_first[0], outer_second[0], outer_grad[0], RATE_OUTER, DECAY),
        ],
        [
            (projection, projection_first, projection_second, dense[:, :wide], RATE_PROJECTION, DECAY),
            (output_weight, output_first, output_second, dense[:, wide:cut], RATE_OUTPUT, DECAY),
            (router_weight, router_first, router_second, dense[:, cut : cut + experts], RATE_ROUTER, DECAY),
            (vectors, vectors_first, vectors_second, dense[:, cut + experts : used].T, RATE_VECTORS, 0.0),
            (hidden_bias, hidden_first, hidden_second, hidden_grad, RATE_HIDDEN, 0.0),
            (return_bias, return_first, return_second, return_grad, RATE_RETURN, 0.0),
        ],
    )
    return (
        block_output[None],
        input_grad[None],
        jnp.sqrt(jnp.sum(squares)),
        *projection_new,
        *output_new,
        *router_new,
        *vectors_new,
        *(v[None] for v in inner_new),
        *hidden_new,
        *(v[None] for v in outer_new),
        *return_new,
    )


def solution(mesh):
    dp, experts = mesh.shape["dp"], mesh.shape["expert"]
    body = functools.partial(fast_shards, dp, experts) if fits(dp, experts) else shards
    return jax.shard_map(
        body,
        mesh=mesh,
        in_specs=(
            P(("dp", "expert"), None, None),
            P(("dp", "expert"), None, None),
            P(("dp", "expert"), None, None),
            P(("dp", "expert"), None),
            P(("dp", "expert"), None),
            P(("dp", "expert"), None),
            P(("dp", "expert"), None),
            P(("dp", "expert"), None),
            P(("dp", "expert"), None),
            P(("dp", "expert"), None),
            P(("dp", "expert"), None),
            P(("dp", "expert"), None),
            P(("dp", "expert"), None),
            P(None, ("dp", "expert")),
            P(None, ("dp", "expert")),
            P(None, ("dp", "expert")),
            P("expert", None, "dp"),
            P("expert", None, "dp"),
            P("expert", None, "dp"),
            P("expert", "dp"),
            P("expert", "dp"),
            P("expert", "dp"),
            P("expert", "dp", None),
            P("expert", "dp", None),
            P("expert", "dp", None),
            P("expert", "dp"),
            P("expert", "dp"),
            P("expert", "dp"),
        ),
        out_specs=(
            P(("dp", "expert"), None, None),
            P(("dp", "expert"), None, None),
            P(),
            P(("dp", "expert"), None),
            P(("dp", "expert"), None),
            P(("dp", "expert"), None),
            P(("dp", "expert"), None),
            P(("dp", "expert"), None),
            P(("dp", "expert"), None),
            P(("dp", "expert"), None),
            P(("dp", "expert"), None),
            P(("dp", "expert"), None),
            P(None, ("dp", "expert")),
            P(None, ("dp", "expert")),
            P(None, ("dp", "expert")),
            P("expert", None, "dp"),
            P("expert", None, "dp"),
            P("expert", None, "dp"),
            P("expert", "dp"),
            P("expert", "dp"),
            P("expert", "dp"),
            P("expert", "dp", None),
            P("expert", "dp", None),
            P("expert", "dp", None),
            P("expert", "dp"),
            P("expert", "dp"),
            P("expert", "dp"),
        ),
        check_vma=False,
    )
```

```python
import functools

import jax
import jax.numpy as jnp
from jax import lax
from jax.experimental import pallas as pl
from jax.experimental.pallas import tpu as pltpu
from jax.sharding import PartitionSpec as P

HEADS = 12
HEAD_DIM = 64
STEP = 10


NORM_EPS = 1e-06
ADAM_EPS = 1e-08
BETA_ONE = 0.9
BETA_TWO = 0.999
DECAY = 0.1
THRESHOLD = 1.0
RATE_PROJECTION = 0.1
RATE_OUTPUT = 1.0
RATE_ROUTER = 0.05
RATE_VECTORS = 0.5
RATE_INNER = 0.1
RATE_HIDDEN = 0.25
RATE_OUTER = 1.5
RATE_RETURN = 2.0


def layer_norm(values, norm_gain, norm_bias):
    center = values - jnp.mean(values, axis=-1, keepdims=True)
    spread = jnp.mean(center * center, axis=-1, keepdims=True)
    return center * lax.rsqrt(spread + NORM_EPS) * norm_gain + norm_bias


def smooth_gate(values):
    return jax.nn.gelu(values, approximate=True)


def mixed_dot(left, right):
    return jnp.dot(left, right, preferred_element_type=jnp.float32)


def rows_product(left, right):
    return lax.dot_general(
        left, right, (((0,), (0,)), ((), ())), preferred_element_type=jnp.float32
    )


def columns_product(left, right):
    return lax.dot_general(
        left, right, (((1,), (1,)), ((), ())), preferred_element_type=jnp.float32
    )


def assign_slots(chosen, claim_order, expert_count, capacity):
    patches = chosen.shape[0]
    top_count = chosen.shape[1]
    claim_rank = (
        jnp.arange(top_count, dtype=jnp.int32)[None, :] * patches + claim_order[:, None]
    ).T.reshape(-1)
    flat_choice = chosen.T.reshape(-1)
    onehot = (flat_choice[:, None] == jnp.arange(expert_count, dtype=jnp.int32)[None, :]).astype(
        jnp.float32
    )
    earlier = (claim_rank[None, :] < claim_rank[:, None]).astype(jnp.float32)
    counts = jnp.dot(
        earlier, onehot, precision=lax.Precision.HIGHEST, preferred_element_type=jnp.float32
    )
    position = jnp.sum(counts * onehot, axis=1).astype(jnp.int32).reshape(top_count, patches).T
    kept_mask = position < capacity
    flat_slot = chosen * capacity + jnp.minimum(position, capacity - 1)
    return (flat_slot, kept_mask)


def slot_matches(flat_slot, kept_mask, slot_count):
    slot_ids = jnp.arange(slot_count, dtype=jnp.int32)
    return (flat_slot[None, :, :] == slot_ids[:, None, None]) & kept_mask[None, :, :]


def select_gates(logits, chosen, expert_count):
    router_probs = jax.nn.softmax(logits, axis=-1)
    onehot = chosen[:, :, None] == jnp.arange(expert_count, dtype=jnp.int32)[None, None, :]
    return jnp.sum(jnp.where(onehot, router_probs[:, None, :], 0.0), axis=2)


def adam_update(weight, first_state, second, gradient, clip_factor, step_rate, decay_rate):
    scaled = gradient * clip_factor
    first_new = BETA_ONE * first_state + (1.0 - BETA_ONE) * scaled
    second_new = BETA_TWO * second + (1.0 - BETA_TWO) * scaled * scaled
    first_hat = first_new / (1.0 - BETA_ONE**STEP)
    second_hat = second_new / (1.0 - BETA_TWO**STEP)
    weight_new = weight - step_rate * (
        first_hat / (jnp.sqrt(second_hat) + ADAM_EPS) + decay_rate * weight
    )
    return (weight_new, first_new, second_new)


def shards(
    tokens,
    cotangent,
    expert_choice,
    priority,
    projection,
    projection_first,
    projection_second,
    output_weight,
    output_first,
    output_second,
    router_weight,
    router_first,
    router_second,
    vectors,
    vectors_first,
    vectors_second,
    expert_inner,
    inner_first,
    inner_second,
    hidden_bias,
    hidden_first,
    hidden_second,
    expert_outer,
    outer_first,
    outer_second,
    return_bias,
    return_first,
    return_second,
):
    model_width = tokens.shape[2]
    patches = tokens.shape[1]
    experts = lax.axis_size("expert")
    capacity = max(2, patches // experts)
    slot_count = experts * capacity
    score_scale = HEAD_DIM ** (-0.5)
    dense_shards = (
        projection.astype(jnp.bfloat16),
        output_weight.astype(jnp.bfloat16),
        router_weight.astype(jnp.bfloat16),
        vectors.astype(jnp.bfloat16),
    )
    partial_shards = (
        lax.all_gather(dense_shards[0], "expert", axis=0, tiled=True),
        lax.all_gather(dense_shards[1], "expert", axis=0, tiled=True),
        lax.all_gather(dense_shards[2], "expert", axis=0, tiled=True),
        lax.all_gather(dense_shards[3], "expert", axis=1, tiled=True),
    )
    whole_projection, whole_output, whole_router, whole_vectors = (
        lax.all_gather(partial_shards[0], "dp", axis=0, tiled=True),
        lax.all_gather(partial_shards[1], "dp", axis=0, tiled=True),
        lax.all_gather(partial_shards[2], "dp", axis=0, tiled=True),
        lax.all_gather(partial_shards[3], "dp", axis=1, tiled=True),
    )
    inner_low = expert_inner.astype(jnp.bfloat16)
    hidden_low = hidden_bias.astype(jnp.bfloat16)
    outer_low = expert_outer.astype(jnp.bfloat16)
    return_low = return_bias.astype(jnp.bfloat16)
    inner_all, hidden_all, outer_all, return_all = (
        lax.all_gather(inner_low, "dp", axis=2, tiled=True),
        lax.all_gather(hidden_low, "dp", axis=1, tiled=True),
        lax.all_gather(outer_low, "dp", axis=1, tiled=True),
        lax.all_gather(return_low, "dp", axis=1, tiled=True),
    )
    vector_rows = whole_vectors.astype(jnp.float32)
    image_rows = tokens[0].astype(jnp.float32)
    normed_one, norm_back_one = jax.vjp(layer_norm, image_rows, vector_rows[0], vector_rows[1])
    normed_low = normed_one.astype(jnp.bfloat16)
    projected = mixed_dot(normed_low, whole_projection)
    queries = (
        (projected[:, :model_width] + vector_rows[2])
        .astype(jnp.bfloat16)
        .reshape(patches, HEADS, HEAD_DIM)
    )
    key_rows = (
        projected[:, model_width : 2 * model_width]
        .astype(jnp.bfloat16)
        .reshape(patches, HEADS, HEAD_DIM)
    )
    value_rows = (
        (projected[:, 2 * model_width :] + vector_rows[3])
        .astype(jnp.bfloat16)
        .reshape(patches, HEADS, HEAD_DIM)
    )
    scores = (
        jnp.einsum("qhd,khd->hqk", queries, key_rows, preferred_element_type=jnp.float32)
        * score_scale
    )
    score_top = jnp.max(scores, axis=-1, keepdims=True)
    raised = jnp.exp(scores - score_top)
    totals = jnp.sum(raised, axis=-1, keepdims=True)
    attention = raised / totals
    log_total = score_top + jnp.log(totals)
    context = (
        jnp.einsum(
            "hqk,khd->qhd",
            attention.astype(jnp.bfloat16),
            value_rows,
            preferred_element_type=jnp.float32,
        )
        .reshape(patches, model_width)
        .astype(jnp.bfloat16)
    )
    middle = image_rows + (mixed_dot(context, whole_output) + vector_rows[4])
    normed_two, norm_back_two = jax.vjp(layer_norm, middle, vector_rows[5], vector_rows[6])
    second_low = normed_two.astype(jnp.bfloat16)
    logits = mixed_dot(second_low, whole_router)
    chosen = expert_choice[0]

    def gate_choice(values):
        return select_gates(values, chosen, experts)

    gate_values, gate_back = jax.vjp(gate_choice, logits)
    flat_slot, kept_mask = assign_slots(chosen, priority[0], experts, capacity)
    matches = slot_matches(flat_slot, kept_mask, slot_count)
    slot_table = jnp.any(matches, axis=2).astype(jnp.bfloat16)
    dispatched = (
        mixed_dot(slot_table, second_low)
        .astype(jnp.bfloat16)
        .reshape(experts, capacity, model_width)
    )
    arrived = lax.all_to_all(dispatched, "expert", split_axis=0, concat_axis=0, tiled=True).reshape(
        slot_count, model_width
    )
    pre_act = mixed_dot(arrived, inner_all[0]) + hidden_all[0].astype(jnp.float32)
    activated, gelu_back = jax.vjp(smooth_gate, pre_act)
    active_low = activated.astype(jnp.bfloat16)
    expert_out = (mixed_dot(active_low, outer_all[0]) + return_all[0].astype(jnp.float32)).astype(
        jnp.bfloat16
    )
    returned = lax.all_to_all(
        expert_out.reshape(experts, capacity, model_width),
        "expert",
        split_axis=0,
        concat_axis=0,
        tiled=True,
    ).reshape(slot_count, model_width)
    picked = returned[flat_slot].astype(jnp.float32)
    weighted = jnp.where(kept_mask, gate_values, 0.0)
    final = middle + jnp.sum(weighted[:, :, None] * picked, axis=1)
    block_output = final.astype(jnp.bfloat16)[None]
    upstream = cotangent[0].astype(jnp.float32)
    gate_grad = jnp.where(kept_mask, jnp.sum(upstream[:, None, :] * picked, axis=2), 0.0)
    slot_gate = jnp.sum(jnp.where(matches, weighted[None, :, :], 0.0), axis=(1, 2))
    slot_grad = (mixed_dot(slot_table, cotangent[0]) * slot_gate[:, None]).astype(jnp.bfloat16)
    sent_grad = lax.all_to_all(
        slot_grad.reshape(experts, capacity, model_width),
        "expert",
        split_axis=0,
        concat_axis=0,
        tiled=True,
    ).reshape(slot_count, model_width)
    outer_grad = rows_product(active_low, sent_grad)
    return_grad = jnp.sum(sent_grad, axis=0, dtype=jnp.float32)
    active_grad = columns_product(sent_grad, outer_all[0])
    (pre_grad,) = gelu_back(active_grad)
    pre_low = pre_grad.astype(jnp.bfloat16)
    inner_grad = rows_product(arrived, pre_low)
    hidden_grad = jnp.sum(pre_low, axis=0, dtype=jnp.float32)
    row_grad = columns_product(pre_low, inner_all[0]).astype(jnp.bfloat16)
    expert_grads = (
        lax.psum_scatter(
            inner_grad[None].astype(jnp.bfloat16), "dp", scatter_dimension=2, tiled=True
        ).astype(jnp.float32),
        lax.psum_scatter(
            hidden_grad[None].astype(jnp.bfloat16), "dp", scatter_dimension=1, tiled=True
        ).astype(jnp.float32),
        lax.psum_scatter(
            outer_grad[None].astype(jnp.bfloat16), "dp", scatter_dimension=1, tiled=True
        ).astype(jnp.float32),
        lax.psum_scatter(
            return_grad[None].astype(jnp.bfloat16), "dp", scatter_dimension=1, tiled=True
        ).astype(jnp.float32),
    )
    back_rows = lax.all_to_all(
        row_grad.reshape(experts, capacity, model_width),
        "expert",
        split_axis=0,
        concat_axis=0,
        tiled=True,
    ).reshape(slot_count, model_width)
    (logit_grad,) = gate_back(gate_grad)
    logit_low = logit_grad.astype(jnp.bfloat16)
    router_grad = rows_product(second_low, logit_low)
    second_grad = rows_product(slot_table, back_rows) + columns_product(logit_low, whole_router)
    middle_part, gain_two_grad, bias_two_grad = norm_back_two(second_grad)
    middle_grad = upstream + middle_part
    branch_low = middle_grad.astype(jnp.bfloat16)
    output_grad = rows_product(context, branch_low)
    out_bias_grad = jnp.sum(branch_low, axis=0, dtype=jnp.float32)
    context_grad = (
        columns_product(branch_low, whole_output)
        .astype(jnp.bfloat16)
        .reshape(patches, HEADS, HEAD_DIM)
    )
    scores = (
        jnp.einsum("qhd,khd->hqk", queries, key_rows, preferred_element_type=jnp.float32)
        * score_scale
    )
    attention = jnp.exp(scores - log_total)
    attention_grad = jnp.einsum(
        "qhd,khd->hqk", context_grad, value_rows, preferred_element_type=jnp.float32
    )
    value_grad = jnp.einsum(
        "hqk,qhd->khd",
        attention.astype(jnp.bfloat16),
        context_grad,
        preferred_element_type=jnp.float32,
    ).astype(jnp.bfloat16)
    centered = jnp.sum(attention * attention_grad, axis=-1, keepdims=True)
    score_grad = (attention * (attention_grad - centered)).astype(jnp.bfloat16)
    query_grad = (
        (
            jnp.einsum("hqk,khd->qhd", score_grad, key_rows, preferred_element_type=jnp.float32)
            * score_scale
        )
        .astype(jnp.bfloat16)
        .reshape(patches, model_width)
    )
    key_grad = (
        (
            jnp.einsum("hqk,qhd->khd", score_grad, queries, preferred_element_type=jnp.float32)
            * score_scale
        )
        .astype(jnp.bfloat16)
        .reshape(patches, model_width)
    )
    value_flat = value_grad.reshape(patches, model_width)
    joined_grad = jnp.concatenate([query_grad, key_grad, value_flat], axis=1)
    projection_grad = rows_product(normed_low, joined_grad)
    normed_grad = columns_product(joined_grad, whole_projection)
    input_part, gain_one_grad, bias_one_grad = norm_back_one(normed_grad)
    input_grad = (middle_grad + input_part)[None]
    vector_grad = jnp.stack(
        [
            gain_one_grad,
            bias_one_grad,
            jnp.sum(query_grad, axis=0, dtype=jnp.float32),
            jnp.sum(value_flat, axis=0, dtype=jnp.float32),
            out_bias_grad,
            gain_two_grad,
            bias_two_grad,
        ]
    )
    local_grads = (projection_grad, output_grad, router_grad, vector_grad)
    partial_grads = (
        lax.psum_scatter(
            local_grads[0].astype(jnp.bfloat16), "dp", scatter_dimension=0, tiled=True
        ).astype(jnp.float32),
        lax.psum_scatter(
            local_grads[1].astype(jnp.bfloat16), "dp", scatter_dimension=0, tiled=True
        ).astype(jnp.float32),
        lax.psum_scatter(
            local_grads[2].astype(jnp.bfloat16), "dp", scatter_dimension=0, tiled=True
        ).astype(jnp.float32),
        lax.psum_scatter(
            local_grads[3].astype(jnp.bfloat16), "dp", scatter_dimension=1, tiled=True
        ).astype(jnp.float32),
    )
    dense_grads = (
        lax.psum_scatter(
            partial_grads[0].astype(jnp.bfloat16), "expert", scatter_dimension=0, tiled=True
        ).astype(jnp.float32),
        lax.psum_scatter(
            partial_grads[1].astype(jnp.bfloat16), "expert", scatter_dimension=0, tiled=True
        ).astype(jnp.float32),
        lax.psum_scatter(
            partial_grads[2].astype(jnp.bfloat16), "expert", scatter_dimension=0, tiled=True
        ).astype(jnp.float32),
        lax.psum_scatter(
            partial_grads[3].astype(jnp.bfloat16), "expert", scatter_dimension=1, tiled=True
        ).astype(jnp.float32),
    )
    all_grads = tuple(dense_grads) + tuple(expert_grads)
    local_square = jnp.sum(all_grads[0] * all_grads[0])
    for gradient in all_grads[1:]:
        local_square = local_square + jnp.sum(gradient * gradient)
    square_total = lax.psum(local_square, ("dp", "expert"))
    grad_norm = jnp.sqrt(square_total)
    clip_factor = THRESHOLD / jnp.maximum(grad_norm, THRESHOLD)
    projection_next, projection_moment, projection_square = adam_update(
        projection,
        projection_first,
        projection_second,
        all_grads[0],
        clip_factor,
        RATE_PROJECTION,
        DECAY,
    )
    output_next, output_moment, output_square = adam_update(
        output_weight, output_first, output_second, all_grads[1], clip_factor, RATE_OUTPUT, DECAY
    )
    router_next, router_moment, router_square = adam_update(
        router_weight, router_first, router_second, all_grads[2], clip_factor, RATE_ROUTER, DECAY
    )
    vectors_next, vectors_moment, vectors_square = adam_update(
        vectors, vectors_first, vectors_second, all_grads[3], clip_factor, RATE_VECTORS, 0.0
    )
    inner_next, inner_moment, inner_square = adam_update(
        expert_inner, inner_first, inner_second, all_grads[4], clip_factor, RATE_INNER, DECAY
    )
    hidden_next, hidden_moment, hidden_square = adam_update(
        hidden_bias, hidden_first, hidden_second, all_grads[5], clip_factor, RATE_HIDDEN, 0.0
    )
    outer_next, outer_moment, outer_square = adam_update(
        expert_outer, outer_first, outer_second, all_grads[6], clip_factor, RATE_OUTER, DECAY
    )
    return_next, return_moment, return_square = adam_update(
        return_bias, return_first, return_second, all_grads[7], clip_factor, RATE_RETURN, 0.0
    )
    return (
        block_output,
        input_grad,
        grad_norm,
        projection_next,
        projection_moment,
        projection_square,
        output_next,
        output_moment,
        output_square,
        router_next,
        router_moment,
        router_square,
        vectors_next,
        vectors_moment,
        vectors_square,
        inner_next,
        inner_moment,
        inner_square,
        hidden_next,
        hidden_moment,
        hidden_square,
        outer_next,
        outer_moment,
        outer_square,
        return_next,
        return_moment,
        return_square,
    )


MESH = pl.DeviceIdType.MESH
ANY = pl.BlockSpec(memory_space=pl.ANY)
VMEM = pl.BlockSpec(memory_space=pltpu.VMEM)


class Place:
    def __init__(self, dp, experts):
        self.dp, self.experts = dp, experts
        self.ys = 2
        self.zs = experts // 4
        self.a = lax.axis_index("dp")
        self.e = lax.axis_index("expert")
        self.core = lax.rem(self.e, 2)
        self.y = lax.rem(lax.div(self.e, 2), self.ys)
        self.z = lax.div(self.e, 2 * self.ys)

    def chip_of(self, core, dz, s2, s3):
        zz = lax.rem(self.z + dz, self.zs)
        if s2 == s3:
            fa = fy = s2
        elif s2:
            fa, fy = core, 1 - core
        else:
            fa, fy = 1 - core, core
        aa = lax.rem(self.a + fa, 2)
        yy = lax.rem(self.y + fy, 2)
        return aa, zz, yy

    def device(self, core, dz, s2, s3, own_core=None):
        aa, zz, yy = self.chip_of(core, dz, s2, s3)
        c = core if own_core is None else own_core
        return (aa, (zz * self.ys + yy) * 2 + c)

    def flat(self, dev):
        return dev[0] * self.experts + dev[1]

    def chip(self, core, dz, s2, s3):
        aa, zz, yy = self.chip_of(core, dz, s2, s3)
        return (aa * self.zs + zz) * self.ys + yy


def remote(src, dst, send, recv, dev):
    return pltpu.make_async_remote_copy(src_ref=src, dst_ref=dst, send_sem=send, recv_sem=recv, device_id=dev, device_id_type=MESH)


def greet(devices):
    barrier = pltpu.get_barrier_semaphore()
    for dev in devices:
        pl.semaphore_signal(barrier, inc=1, device_id=dev, device_id_type=MESH)
    pl.semaphore_wait(barrier, len(devices))


def split_index(k, zs):
    return k % zs, (k // zs) % 2, k // (2 * zs)


def gather_kernel(dp, experts, in_ref, out_ref, send, recv, csend, crecv, own):
    p = Place(dp, experts)
    zs = p.zs
    c = p.core
    n = 4 * zs
    partner = (p.a, p.e + 1 - 2 * c)
    peers = [p.device(c, dz, 0, 0) for dz in range(1, zs)]
    second = p.device(c, 0, 1, 0)
    third = p.device(c, 0, 0, 1)
    me = p.flat((p.a, p.e))
    mine = pltpu.make_async_copy(in_ref, out_ref.at[me], own)
    mine.start()
    greet(peers + [second, third, partner])
    pending = []

    def block(k):
        if k == 0:
            return me, in_ref
        dz, s2, s3 = split_index(k, zs)
        at = p.flat(p.device(c, (zs - dz) % zs, s2, s3))
        return at, out_ref.at[at]

    def push(k, slot, dev):
        at, src = block(k)
        cp = remote(src, out_ref.at[at], send.at[slot], recv.at[slot], dev)
        cp.start()
        pending.append(cp)

    def hand(k):
        at, src = block(k)
        cp = remote(src, out_ref.at[at], csend.at[k], crecv.at[k], partner)
        cp.start()
        pending.append(cp)

    def arrived(k):
        at, _ = block(k)
        remote(in_ref, out_ref.at[at], send.at[k], recv.at[k], partner).wait_recv()

    for dz in range(1, zs):
        push(0, dz, peers[dz - 1])
    push(0, zs, second)
    push(0, 2 * zs, third)
    hand(0)
    for k in range(1, zs):
        arrived(k)
        push(k, zs + k, second)
        push(k, 2 * zs + k, third)
        hand(k)
    for k in range(zs, 2 * zs):
        arrived(k)
        push(k, 2 * zs + k, third)
        hand(k)
    for k in range(2 * zs, 4 * zs):
        arrived(k)
        hand(k)
    for k in range(n):
        dz, s2, s3 = split_index(k, zs)
        at = p.flat(p.device(1 - c, (zs - dz) % zs, s2, s3))
        remote(in_ref, out_ref.at[at], csend.at[k], crecv.at[k], partner).wait_recv()
    for cp in pending:
        cp.wait_send()
    mine.wait()


def gather_blocks(block, dp, experts, cid):
    n = dp * experts
    return pl.pallas_call(
        functools.partial(gather_kernel, dp, experts),
        out_shape=jax.ShapeDtypeStruct((n,) + block.shape, block.dtype),
        in_specs=[ANY],
        out_specs=ANY,
        scratch_shapes=[
            pltpu.SemaphoreType.DMA((n // 2,)),
            pltpu.SemaphoreType.DMA((n // 2,)),
            pltpu.SemaphoreType.DMA((n // 2,)),
            pltpu.SemaphoreType.DMA((n // 2,)),
            pltpu.SemaphoreType.DMA,
        ],
        compiler_params=pltpu.CompilerParams(collective_id=cid, has_side_effects=True),
        name="gather_dense",
    )(block)


LANES = 128


def nn(left, right):
    return lax.dot_general(left, right, (((1,), (0,)), ((), ())), preferred_element_type=jnp.float32)


def nt(left, right):
    return lax.dot_general(left, right, (((1,), (1,)), ((), ())), preferred_element_type=jnp.float32)


def lane_ids(rows, start=0):
    return lax.broadcasted_iota(jnp.int32, (rows, LANES), 1) + start


def row_parts(count, size):
    return [pl.ds(i * size, size) for i in range(count // size)]


def norm_parts(values):
    center = values - jnp.mean(values, axis=-1, keepdims=True)
    inverse = lax.rsqrt(jnp.mean(center * center, axis=-1, keepdims=True) + NORM_EPS)
    return center * inverse, inverse


def vector_table(weights, width):
    return jnp.transpose(weights[:, 4 * width :].astype(jnp.float32))


def forward_kernel(
    experts,
    capacity,
    chunk,
    tok_ref,
    cot_ref,
    choice_ref,
    rank_col,
    rank_row,
    weights_any,
    rows_ref,
    dy_ref,
    qkv_ref,
    ctx_ref,
    mid_ref,
    second_ref,
    stat_ref,
    aux_ref,
    probs_ref,
    weights,
    vec,
    normed,
    load,
):
    low = jnp.bfloat16
    patches, width = tok_ref.shape
    fetch = pltpu.make_async_copy(weights_any, weights, load)
    fetch.start()
    lanes = lane_ids(patches)
    first, other = choice_ref[:, 0:1], choice_ref[:, 1:2]
    is_first, is_other = lanes == first, lanes == other
    before = (rank_row[...] < rank_col[...]).astype(jnp.float32).astype(low)
    hot = (is_first | (lanes == other + experts)).astype(jnp.float32)
    counts = nn(before, hot.astype(low))
    totals = jnp.sum(hot, axis=0, keepdims=True)
    place_first = jnp.sum(jnp.where(is_first, counts, 0.0), axis=1, keepdims=True)
    place_other = jnp.sum(
        jnp.where(lanes == other + experts, counts, 0.0) + jnp.where(is_other, totals, 0.0), axis=1, keepdims=True
    )
    fetch.wait()
    vec[...] = vector_table(weights, width)

    def row(i):
        return vec[experts + i : experts + i + 1, :]

    for part in row_parts(patches, chunk):
        unit, _ = norm_parts(tok_ref[part, :].astype(jnp.float32))
        normed[part, :] = (unit * row(0) + row(1)).astype(low)
    third = 256
    stat_ref[...] = jnp.zeros_like(stat_ref)

    @pl.loop(0, width // LANES)
    def _(pair):
        at = pl.multiple_of(pair * LANES, LANES)
        trio = pl.multiple_of(3 * at, LANES)
        product = nn(normed[...], weights[:, pl.ds(trio, 3 * LANES)])
        query_bias = vec[experts + 2 : experts + 3, pl.ds(at, LANES)]
        value_bias = vec[experts + 3 : experts + 4, pl.ds(at, LANES)]
        qkv_ref[:, pl.ds(trio, LANES)] = (product[:, :LANES] + query_bias).astype(low)
        keys = product[:, LANES : 2 * LANES].astype(low)
        values = (product[:, 2 * LANES :] + value_bias).astype(low)
        qkv_ref[:, pl.ds(pl.multiple_of(trio + LANES, LANES), LANES)] = keys
        qkv_ref[:, pl.ds(pl.multiple_of(trio + 2 * LANES, LANES), LANES)] = values
        key_lanes = lane_ids(patches)
        values_two = [
            jnp.where(key_lanes < HEAD_DIM, values, (key_lanes == HEAD_DIM).astype(jnp.float32).astype(low)),
            jnp.where(key_lanes >= HEAD_DIM, values, (key_lanes == 0).astype(jnp.float32).astype(low)),
        ]
        for part in row_parts(patches, chunk):
            own = lane_ids(chunk)
            queries = qkv_ref[part, pl.ds(trio, LANES)] * jnp.asarray(HEAD_DIM**-0.5, low)
            outs = []
            stat = stat_ref[part, :]
            for head in range(2):
                mine = (own < HEAD_DIM) if head == 0 else (own >= HEAD_DIM)
                scores = nt(jnp.where(mine, queries, jnp.zeros_like(queries)), keys)
                top = jnp.max(scores, axis=1, keepdims=True)
                raised = jnp.exp(scores - top)
                mixed = nn(raised.astype(low), values_two[head])
                spare = HEAD_DIM if head == 0 else 0
                total = mixed[:, spare : spare + 1]
                outs.append(mixed / total)
                stat = jnp.where(own == 2 * pair + head, top + jnp.log(total), stat)
            stat_ref[part, :] = stat
            ctx_ref[part, pl.ds(at, LANES)] = jnp.where(own < HEAD_DIM, outs[0], outs[1]).astype(low)

    for j in range(width // third):
        columns = pl.ds(j * third, third)
        product = nn(ctx_ref[...], weights[:, pl.ds(3 * width + j * third, third)])
        mid_ref[:, columns] = tok_ref[:, columns].astype(jnp.float32) + (
            product + vec[experts + 4 : experts + 5, columns]
        )
    for part in row_parts(patches, chunk):
        unit, _ = norm_parts(mid_ref[part, :])
        second_ref[part, :] = (unit * row(5) + row(6)).astype(low)
    logits = jnp.where(lanes < experts, nn(second_ref[...], weights[:, 4 * width :]), -1e30)
    raised = jnp.exp(logits - jnp.max(logits, axis=1, keepdims=True))
    probs = raised / jnp.sum(raised, axis=1, keepdims=True)
    probs_ref[...] = probs

    def slot_of(place, expert):
        place = place.astype(jnp.int32)
        kept = place < capacity
        slot = (place // 8) * LANES + expert * 8 + place % 8
        tail = kept & (place >= capacity - 4)
        return kept, jnp.where(kept, slot, -1), jnp.where(tail, slot + 4, -1)

    aux = jnp.zeros((patches, LANES), jnp.float32)
    for j, (place, expert, hit) in enumerate(((place_first, first, is_first), (place_other, other, is_other))):
        kept, slot, twin = slot_of(place, expert)
        gate = jnp.where(kept, jnp.sum(jnp.where(hit, probs, 0.0), axis=1, keepdims=True), 0.0)
        for lane, column in ((j, slot.astype(jnp.float32)), (2 + j, twin.astype(jnp.float32)), (4 + j, gate)):
            aux = jnp.where(lanes == lane, column, aux)
    aux_ref[...] = aux
    turned = jnp.transpose(aux)
    slots = [turned[i : i + 1, :] for i in range(4)]
    gates = [turned[4 + i : 5 + i, :] for i in range(2)]
    full = capacity // 8
    for i in range(full + 1):
        ids = (lax.broadcasted_iota(jnp.int32, (LANES, patches), 0) + i * LANES).astype(jnp.float32)
        hits = [ids == slots[0], ids == slots[1]]
        if i == full:
            hits = [hits[0] | (ids == slots[2]), hits[1] | (ids == slots[3])]
        table = (hits[0] | hits[1]).astype(jnp.float32).astype(low)
        gate = jnp.sum(
            jnp.where(hits[0], gates[0], 0.0) + jnp.where(hits[1], gates[1], 0.0), axis=1, keepdims=True
        )
        sent = nn(table, second_ref[...])
        back = nn(table, cot_ref[...]) * gate
        columns = pl.ds(i * width, width)
        if i == full:
            columns = pl.ds(i * width, width // 2)
            left = lax.broadcasted_iota(jnp.int32, (LANES, width // 2), 0) % 8 < 4
            sent = jnp.where(left, sent[:, : width // 2], sent[:, width // 2 :])
            back = jnp.where(left, back[:, : width // 2], back[:, width // 2 :])
        rows_ref[:, columns] = sent.astype(low)
        dy_ref[:, columns] = back.astype(low)


def forward(tokens, cotangent, choice, priority, weights, experts, capacity, chunk=192):
    patches, width = tokens.shape
    low, full = jnp.bfloat16, jnp.float32
    packed = (8 * experts, capacity * width // 8)
    shapes = [
        (packed, low),
        (packed, low),
        ((patches, 3 * width), low),
        ((patches, width), low),
        ((patches, width), full),
        ((patches, width), low),
        ((patches, LANES), full),
        ((patches, LANES), full),
        ((patches, LANES), full),
    ]
    return pl.pallas_call(
        functools.partial(forward_kernel, experts, capacity, chunk),
        out_shape=[jax.ShapeDtypeStruct(*s) for s in shapes],
        in_specs=[VMEM] * 5 + [ANY],
        out_specs=[VMEM] * 9,
        scratch_shapes=[
            pltpu.VMEM(weights.shape, low),
            pltpu.VMEM((LANES, width), full),
            pltpu.VMEM((patches, width), low),
            pltpu.SemaphoreType.DMA,
        ],
        compiler_params=pltpu.CompilerParams(vmem_limit_bytes=56 * 1024 * 1024),
        cost_estimate=pl.CostEstimate(flops=6 * 10**9, bytes_accessed=20 * 10**6, transcendentals=4 * 10**6),
        name="attend_forward",
    )(tokens, cotangent, choice, priority.reshape(patches, 1), priority.reshape(1, patches), weights)


def gelu_both(z):
    root = 0.7978845608028654
    square = z * z
    slope = jnp.tanh(root * z * (1.0 + 0.044715 * square))
    half = 0.5 * (1.0 + slope)
    act = z * half
    grad = half + 0.5 * z * (1.0 - slope * slope) * (root * (1.0 + 3 * 0.044715 * square))
    return act, grad


def tail_picks(count, right):
    rows = lax.broadcasted_iota(jnp.int32, (count // 2, count), 0)
    ids = lax.broadcasted_iota(jnp.int32, (count // 2, count), 1)
    hit = ids == (rows // 4) * 8 + rows % 4 + (4 if right else 0)
    return hit.astype(jnp.float32).astype(jnp.bfloat16)


class Stages:
    def __init__(self, place, refs):
        (self.grads, self.other, self.give3, self.take3, self.give2, self.take2, self.givez, self.takez, self.total) = refs[:9]
        (self.cs, self.cr, self.s3, self.r3, self.s2, self.r2, self.sz, self.rz) = refs[9:]
        self.p, self.zs, self.core = place, place.zs, place.core
        self.partner = (place.a, place.e + 1 - 2 * place.core)

    def to_partner(self, c):
        return remote(
            self.grads.at[c, 1 - self.core], self.other.at[c], self.cs.at[c], self.cr.at[c], self.partner
        )

    def to_third(self, c):
        return remote(
            self.give3.at[c], self.take3.at[c], self.s3.at[c], self.r3.at[c], self.p.device(self.core, 0, 0, 1)
        )

    def to_second(self, c):
        return remote(
            self.give2.at[c], self.take2.at[c], self.s2.at[c], self.r2.at[c], self.p.device(self.core, 0, 1, 0)
        )

    def along(self, c, dz):
        return remote(
            self.givez.at[c, dz - 1],
            self.takez.at[c, dz - 1],
            self.sz.at[c, dz],
            self.rz.at[c, dz],
            self.p.device(self.core, dz, 0, 0),
        )

    def sum_of(self, c, k, *more):
        at = self.p.chip(self.core, *split_index(k, self.zs))
        total = self.grads[c, self.core, at].astype(jnp.float32) + self.other[c, at].astype(jnp.float32)
        for ref in more:
            total = total + ref[c, k].astype(jnp.float32)
        return total

    def step0(self, c):
        self.to_partner(c).start()

    def step1(self, c):
        self.to_partner(c).wait_recv()
        zs = self.zs
        for k in range(2 * zs, 4 * zs):
            self.give3[c, k - 2 * zs] = self.sum_of(c, k).astype(self.give3.dtype)
        self.to_third(c).start()

    def step2(self, c):
        self.to_third(c).wait_recv()
        zs = self.zs
        for k in range(zs, 2 * zs):
            self.give2[c, k - zs] = self.sum_of(c, k, self.take3).astype(self.give2.dtype)
        self.to_second(c).start()

    def step3(self, c):
        self.to_second(c).wait_recv()
        for dz in range(1, self.zs):
            self.givez[c, dz - 1] = self.sum_of(c, dz, self.take3, self.take2).astype(self.givez.dtype)
            self.along(c, dz).start()

    def step4(self, c):
        total = self.sum_of(c, 0, self.take3, self.take2)
        for dz in range(1, self.zs):
            self.along(c, dz).wait_recv()
            total = total + self.takez[c, dz - 1].astype(jnp.float32)
        self.total[c] = total

    def finish(self, count):
        for c in range(count):
            self.to_partner(c).wait_send()
            self.to_third(c).wait_send()
            self.to_second(c).wait_send()
            for dz in range(1, self.zs):
                self.along(c, dz).wait_send()


def stage_scratch(chunks, chips, rows, columns):
    low = jnp.bfloat16
    zs = chips // 4
    shapes = [
        (chunks, 2, chips, rows, columns),
        (chunks, chips, rows, columns),
        (chunks, 2 * zs, rows, columns),
        (chunks, 2 * zs, rows, columns),
        (chunks, zs, rows, columns),
        (chunks, zs, rows, columns),
        (chunks, zs - 1, rows, columns),
        (chunks, zs - 1, rows, columns),
    ]
    sems = [pltpu.SemaphoreType.DMA((chunks,)) for _ in range(6)]
    sems += [pltpu.SemaphoreType.DMA((chunks, zs)) for _ in range(2)]
    return [pltpu.VMEM(s, low) for s in shapes] + [pltpu.VMEM((chunks, rows, columns), jnp.float32)] + sems


STAGE_REFS = 17


def backward_kernel(
    dp,
    experts,
    capacity,
    chunk,
    tok_ref,
    cot_ref,
    choice_ref,
    ret_ref,
    aux_ref,
    probs_ref,
    mid_ref,
    part_ref,
    back_any,
    second_any,
    ctx_any,
    stat_any,
    qkv_any,
    weights_any,
    out_ref,
    input_ref,
    dense_ref,
    total_ref,
    back_ref,
    second_ref,
    ctx_ref,
    stat_ref,
    qkv_ref,
    weights,
    vec,
    stacked,
    normed_turned,
    branch,
    dctx,
    joined,
    turned_query,
    dmid,
    work,
    sums,
    load,
    row,
    row_tail,
    tiles,
    row_send,
    row_recv,
    tile_send,
    tile_recv,
    *stage_refs,
):
    low, full32 = jnp.bfloat16, jnp.float32
    patches, width = tok_ref.shape
    trio_width = 3 * LANES
    p = Place(dp, experts)
    world = dp * experts
    me = p.flat((p.a, p.e))
    main, last = Stages(p, stage_refs[:STAGE_REFS]), Stages(p, stage_refs[STAGE_REFS:])
    chips, shard2 = main.grads.shape[2:4]
    pieces = [
        (back_any, back_ref),
        (weights_any, weights),
        (ctx_any, ctx_ref),
        (second_any, second_ref),
        (stat_any, stat_ref),
        (qkv_any, qkv_ref),
    ]
    fetch = [pltpu.make_async_copy(s, d, load.at[i]) for i, (s, d) in enumerate(pieces)]
    for copy in fetch:
        copy.start()
    barrier = pltpu.get_barrier_semaphore()

    def other_device(j):
        at = lax.rem(me + j, world)
        return lax.div(at, experts), lax.rem(at, experts)

    @pl.loop(1, world)
    def _(j):
        pl.semaphore_signal(barrier, inc=1, device_id=other_device(j), device_id_type=MESH)

    full = capacity // 8
    half = width // 2
    lanes = lane_ids(patches)
    aux = aux_ref[...]
    slots = [aux[:, i : i + 1] for i in range(4)]
    gates = [aux[:, 4 + i : 5 + i] for i in range(2)]
    ids = lax.broadcasted_iota(jnp.int32, (patches, full * LANES), 1).astype(full32)
    tail_ids = lane_ids(patches, full * LANES).astype(full32)
    hits = [ids == slots[0], ids == slots[1]]
    lefts = [tail_ids == slots[0], tail_ids == slots[1]]
    rights = [tail_ids == slots[2], tail_ids == slots[3]]

    def mix(marks):
        return (jnp.where(marks[0], gates[0], 0.0) + jnp.where(marks[1], gates[1], 0.0)).astype(low)

    def pick(marks):
        return (marks[0] | marks[1]).astype(full32).astype(low)

    for i in range(full):
        stacked[pl.ds(i * LANES, LANES), :] = ret_ref[:, pl.ds(i * width, width)]
    tail = ret_ref[:, pl.ds(full * width, half)]
    left_mix, right_mix = nn(mix(lefts), tail), nn(mix(rights), tail)
    final = nn(mix(hits), stacked[...])
    out_ref[:, :half] = (mid_ref[:, :half] + (final[:, :half] + left_mix)).astype(low)
    out_ref[:, half:] = (mid_ref[:, half:] + (final[:, half:] + right_mix)).astype(low)
    along = nt(cot_ref[...], stacked[...])
    along_left, along_right = nt(cot_ref[:, :half], tail), nt(cot_ref[:, half:], tail)
    dprobs = jnp.zeros((patches, LANES), full32)
    for j in range(2):
        dgate = jnp.sum(jnp.where(hits[j], along, 0.0), axis=1, keepdims=True) + jnp.sum(
            jnp.where(lefts[j], along_left, 0.0) + jnp.where(rights[j], along_right, 0.0), axis=1, keepdims=True
        )
        dprobs = dprobs + jnp.where(lanes == choice_ref[:, j : j + 1], dgate, 0.0)
    probs = probs_ref[...]
    dlogits = (probs * (dprobs - jnp.sum(probs * dprobs, axis=1, keepdims=True))).astype(low)
    fetch[0].wait()
    for i in range(full):
        stacked[pl.ds(i * LANES, LANES), :] = back_ref[:, pl.ds(i * width, width)]
    tail = back_ref[:, pl.ds(full * width, half)]
    fetch[1].wait()
    vec[...] = vector_table(weights, width)

    def vector(i):
        return vec[experts + i : experts + i + 1, :]

    routed = weights[:, 4 * width :]
    work[...] = nn(pick(hits), stacked[...]) + nt(dlogits, routed)
    work[:, :half] = work[:, :half] + nn(pick(lefts), tail)
    work[:, half:] = work[:, half:] + nn(pick(rights), tail)
    sums[...] = jnp.zeros_like(sums)

    def column_sum(slot, values):
        sums[pl.ds(8 * slot, 8), :] = sums[pl.ds(8 * slot, 8), :] + jnp.sum(
            values.reshape(-1, 8, values.shape[-1]), axis=0
        )

    def norm_back(grad, unit, inverse, gain):
        weighted = grad * gain
        return inverse * (
            weighted
            - jnp.mean(weighted, axis=-1, keepdims=True)
            - unit * jnp.mean(weighted * unit, axis=-1, keepdims=True)
        )

    for part in row_parts(patches, chunk):
        unit, inverse = norm_parts(mid_ref[part, :])
        grad = work[part, :]
        column_sum(5, grad * unit)
        column_sum(6, grad)
        total = cot_ref[part, :].astype(full32) + norm_back(grad, unit, inverse, vector(5))
        dmid[part, :] = total
        rounded = total.astype(low)
        branch[part, :] = rounded
        column_sum(4, rounded.astype(full32))
    fetch[2].wait()
    ctx_turned = jnp.transpose(ctx_ref[...])
    for core in range(2):
        columns = pl.ds(core * half, half)
        product = nn(ctx_turned, branch[:, columns])
        main.grads[0, core] = product.reshape(chips, shard2, half).astype(low)
    pl.semaphore_wait(barrier, world - 1)
    main.step0(0)
    third = 256
    for j in range(width // third):
        rows = pl.ds(j * third, third)
        dctx[:, rows] = nt(branch[...], weights[rows, pl.ds(3 * width, width)]).astype(low)
    fetch[3].wait()
    router_rows = nn(jnp.transpose(dlogits.astype(full32)).astype(low), second_ref[...])
    for part in row_parts(patches, chunk):
        unit, _ = norm_parts(tok_ref[part, :].astype(full32))
        second_ref[part, :] = (unit * vector(0) + vector(1)).astype(low)
    normed_turned[...] = jnp.transpose(second_ref[...])
    heads = (
        lax.broadcasted_iota(jnp.int32, (16, width), 1) // HEAD_DIM == lax.broadcasted_iota(jnp.int32, (16, width), 0)
    ).astype(full32).astype(low)
    product = dctx[...].astype(full32) * ctx_ref[...].astype(full32)
    upper = product.astype(low)
    center = nt(heads, upper) + nt(heads, (product - upper.astype(full32)).astype(low))
    fetch[4].wait()
    logs = jnp.transpose(stat_ref[...])
    work[0:32, :patches] = jnp.concatenate([logs[:16], center], axis=0)
    fetch[5].wait()

    def attend(pair, c, core):
        at = pl.multiple_of(pair * LANES, LANES)
        trio = pl.multiple_of(pair * trio_width, LANES)
        key_at = pl.ds(pl.multiple_of(trio + LANES, LANES), LANES)
        value_at = pl.ds(pl.multiple_of(trio + 2 * LANES, LANES), LANES)
        scale = jnp.asarray(HEAD_DIM**-0.5, low)
        queries = qkv_ref[:, pl.ds(trio, LANES)] * scale
        given = dctx[:, pl.ds(at, LANES)]
        own = lane_ids(patches)
        zero = jnp.zeros_like(queries)
        marks = [own < HEAD_DIM, own >= HEAD_DIM]
        head_queries = [jnp.where(m, queries, zero) for m in marks]
        head_given = [jnp.where(m, given, zero) for m in marks]
        turned_keys = jnp.transpose(qkv_ref[:, key_at] * scale)
        query_parts = [None, None]
        for part in row_parts(patches, chunk):
            keys = qkv_ref[part, key_at]
            values = qkv_ref[part, value_at]
            value_out, key_out = [], []
            for head in range(2):
                log_row = work[pl.ds(2 * pair + head, 1), :patches]
                center_row = work[pl.ds(16 + 2 * pair + head, 1), :patches]
                prob = jnp.exp(nt(keys, head_queries[head]) - log_row)
                value_out.append(nn(prob.astype(low), given))
                dscore = (prob * (nt(values, head_given[head]) - center_row)).astype(low)
                key_out.append(nn(dscore, queries))
                head_keys = turned_keys[HEAD_DIM * head : HEAD_DIM * (head + 1), part.start : part.start + part.size]
                piece = nn(head_keys, dscore)
                query_parts[head] = piece if query_parts[head] is None else query_parts[head] + piece
            side = lane_ids(chunk) < HEAD_DIM
            joined[part, key_at] = jnp.where(side, key_out[0], key_out[1]).astype(low)
            joined[part, value_at] = jnp.where(side, value_out[0], value_out[1]).astype(low)
        turned_query[...] = jnp.concatenate(query_parts, axis=0)
        joined[:, pl.ds(trio, LANES)] = jnp.transpose(turned_query[...]).astype(low)
        product = nn(normed_turned[...], joined[:, pl.ds(trio, trio_width)])
        main.grads[c, core] = product.reshape(chips, shard2, trio_width).astype(low)

    pair_chunks = width // LANES // 2

    for i in range(pair_chunks):
        attend(2 * i, i + 1, 0)
        main.step1(i)
        if i >= 1:
            main.step3(i - 1)
        attend(2 * i + 1, i + 1, 1)
        main.step0(i + 1)
        main.step2(i)
        if i >= 1:
            main.step4(i - 1)

    end = pair_chunks
    ones = jnp.ones((8, patches), low)
    for j in range(width // LANES):
        column_parts = nn(ones, joined[:, pl.ds(j * trio_width, trio_width)])
        sums[16:17, pl.ds(j * LANES, LANES)] = column_parts[0:1, :LANES]
        sums[24:25, pl.ds(j * LANES, LANES)] = column_parts[0:1, 2 * LANES :]
    for j in range(width // third):
        rows = pl.ds(j * third, third)
        work[:, rows] = nt(joined[...], weights[rows, : 3 * width])
        if j == 0:
            main.step1(end)
            main.step3(end - 1)
    main.step2(end)
    main.step4(end - 1)
    parts = row_parts(patches, chunk)
    for part in parts:
        unit, inverse = norm_parts(tok_ref[part, :].astype(full32))
        grad = work[part, :]
        column_sum(0, grad * unit)
        column_sum(1, grad)
        input_ref[part, :] = dmid[part, :] + norm_back(grad, unit, inverse, vector(0))
    vec[...] = router_rows
    for i in range(7):
        vec[experts + i : experts + i + 1, :] = jnp.sum(sums[pl.ds(8 * i, 8), :], axis=0, keepdims=True)
    last.grads[0, 0] = jnp.transpose(vec[...]).reshape(chips, shard2, LANES).astype(low)
    last.grads[0, 1] = jnp.zeros((chips, shard2, LANES), low)
    last.step0(0)
    main.step3(end)
    last.step1(0)
    last.step2(0)
    main.step4(end)
    last.step3(0)
    last.step4(0)
    deep = shard2 // 2
    his = pl.ds(pl.multiple_of((1 - p.core) * deep, 8), deep)
    mine = pl.ds(pl.multiple_of(p.core * deep, 8), deep)
    rows_copy = [
        remote(main.total.at[:, his], row, row_send.at[0], row_recv.at[0], main.partner),
        remote(last.total.at[:, his], row_tail, row_send.at[1], row_recv.at[1], main.partner),
    ]
    for copy in rows_copy:
        copy.start()
    square = part_ref[...]
    for stage, count in ((main, end + 1), (last, 1)):
        for c in range(count):
            values = stage.total[c]
            folded = jnp.sum((values * values).reshape(-1, 8, values.shape[1]), axis=0)
            for j in range(values.shape[1] // LANES):
                square = square + folded[:, j * LANES : (j + 1) * LANES]
    tiles[me] = square

    def tile_copy(j):
        return remote(tiles.at[me], tiles.at[me], tile_send.at[j], tile_recv.at[j], other_device(j))

    @pl.loop(1, world)
    def _(j):
        tile_copy(j).start()

    def put(core, values, tail_values):
        for c in range(end + 1):
            dense_ref[:, pl.ds(pl.multiple_of(c * width + core * half, LANES), half)] = values(c)
        dense_ref[:, pl.ds(pl.multiple_of(4 * width + core * LANES, LANES), LANES)] = tail_values

    put(p.core, lambda c: main.total[c, mine, :], last.total[0, mine, :])
    for copy in rows_copy:
        copy.wait_recv()
    put(1 - p.core, lambda c: row[c], row_tail[0])

    @pl.loop(1, world)
    def _(j):
        block = tiles.at[lax.rem(me + world - j, world)]
        remote(block, block, tile_send.at[j], tile_recv.at[j], main.partner).wait_recv()

    total = tiles[0]
    for j in range(1, world):
        total = total + tiles[j]
    total_ref[...] = total
    main.finish(end + 1)
    last.finish(1)
    for copy in rows_copy:
        copy.wait_send()

    @pl.loop(1, world)
    def _(j):
        tile_copy(j).wait_send()


def backward(
    tokens,
    cotangent,
    choice,
    ret,
    back,
    aux,
    probs,
    mid,
    second,
    ctx,
    stat,
    qkv,
    weights,
    part,
    dp,
    experts,
    capacity,
    cid,
    chunk=192,
):
    patches, width = tokens.shape
    low, full = jnp.bfloat16, jnp.float32
    world = dp * experts
    chips, rows = world // 2, 2 * width // world
    chunks = width // LANES // 2 + 1
    columns = 4 * width + 2 * LANES
    return pl.pallas_call(
        functools.partial(backward_kernel, dp, experts, capacity, chunk),
        out_shape=[
            jax.ShapeDtypeStruct((patches, width), low),
            jax.ShapeDtypeStruct((patches, width), full),
            jax.ShapeDtypeStruct((rows // 2, columns), full),
            jax.ShapeDtypeStruct((8, LANES), full),
        ],
        in_specs=[VMEM] * 8 + [ANY] * 6,
        out_specs=[VMEM] * 4,
        scratch_shapes=[
            pltpu.VMEM(back.shape, low),
            pltpu.VMEM((patches, width), low),
            pltpu.VMEM((patches, width), low),
            pltpu.VMEM(stat.shape, full),
            pltpu.VMEM(qkv.shape, low),
            pltpu.VMEM(weights.shape, low),
            pltpu.VMEM((LANES, width), full),
            pltpu.VMEM((capacity // 8 * LANES, width), low),
            pltpu.VMEM((width, patches), low),
            pltpu.VMEM((patches, width), low),
            pltpu.VMEM((patches, width), low),
            pltpu.VMEM((patches, 3 * width), low),
            pltpu.VMEM((LANES, patches), full),
            pltpu.VMEM((patches, width), full),
            pltpu.VMEM((patches, width), full),
            pltpu.VMEM((56, width), full),
            pltpu.SemaphoreType.DMA((6,)),
            pltpu.VMEM((chunks, rows // 2, width // 2), full),
            pltpu.VMEM((1, rows // 2, LANES), full),
            pltpu.VMEM((world, 8, LANES), full),
            pltpu.SemaphoreType.DMA((2,)),
            pltpu.SemaphoreType.DMA((2,)),
            pltpu.SemaphoreType.DMA((world,)),
            pltpu.SemaphoreType.DMA((world,)),
            *stage_scratch(chunks, chips, rows, width // 2),
            *stage_scratch(1, chips, rows, LANES),
        ],
        compiler_params=pltpu.CompilerParams(
            collective_id=cid, has_side_effects=True, vmem_limit_bytes=60 * 1024 * 1024
        ),
        cost_estimate=pl.CostEstimate(flops=15 * 10**9, bytes_accessed=30 * 10**6, transcendentals=4 * 10**6),
        name="attend_backward",
    )(tokens, cotangent, choice, ret, aux, probs, mid, part, back, second, ctx, stat, qkv, weights)


def moe_kernel(
    dp,
    experts,
    chunk,
    rows_any,
    dy_any,
    inner_any,
    hidden_ref,
    outer_any,
    return_ref,
    y_any,
    drows_any,
    dinner_any,
    dhidden_ref,
    douter_any,
    dreturn_ref,
    square_ref,
    rows_all,
    dy_all,
    y_pack,
    drows_pack,
    y_theirs,
    drows_theirs,
    rows,
    turned,
    dy,
    inner,
    outer,
    act,
    grad,
    dz,
    acc,
    inner_stage,
    outer_stage,
    dinner_stage,
    douter_stage,
    square,
    own_sem,
    in_send,
    in_recv,
    over_send,
    over_recv,
    part_send,
    part_recv,
    out_send,
    out_recv,
    stage_sem,
    store_sem,
):
    low, full32 = jnp.bfloat16, jnp.float32
    width = rows.shape[1]
    count = dp * experts * 8
    half = width // 2
    full = rows_all.shape[3] // width
    steps = inner.shape[1] // chunk
    each = -(-(experts - 1) // (steps - 1))
    a = lax.axis_index("dp")
    e = lax.axis_index("expert")
    across = (1 - a, e)
    ins, alls = (rows_any, dy_any), (rows_all, dy_all)
    packs, theirs, outs = (y_pack, drows_pack), (y_theirs, drows_theirs), (y_any, drows_any)

    def to(j):
        return lax.rem(e + j, experts)

    def source(j):
        return lax.rem(e + experts - j, experts)

    def stage(k, slot):
        columns = pl.ds(pl.multiple_of(k * chunk, chunk), chunk)
        return (
            pltpu.make_async_copy(inner_any.at[0, :, columns], inner_stage.at[slot], stage_sem.at[0, slot]),
            pltpu.make_async_copy(outer_any.at[0, columns, :], outer_stage.at[slot], stage_sem.at[1, slot]),
        )

    def own_block(i):
        return pltpu.make_async_copy(ins[i].at[e], alls[i].at[a, e], own_sem.at[i])

    for slot in range(2):
        for copy in stage(slot, slot):
            copy.start()
    for i in range(2):
        own_block(i).start()
    greet([(a, to(j)) for j in range(1, experts)] + [across])

    def first_send(i, j):
        return remote(ins[i].at[to(j)], alls[i].at[a, e], in_send.at[i, j], in_recv.at[i, j], (a, to(j)))

    def forward_own(i):
        return remote(ins[i].at[e], alls[i].at[a, e], over_send.at[i, 0], over_recv.at[i, 0], across)

    def pass_on(i, j):
        block = alls[i].at[a, source(j)]
        return remote(block, block, over_send.at[i, j], over_recv.at[i, j], across)

    def received(i, j):
        block = alls[i].at[a, source(j)]
        return remote(block, block, in_send.at[i, j], in_recv.at[i, j], across)

    def from_across(i, j):
        block = alls[i].at[1 - a, source(j)]
        return remote(block, block, over_send.at[i, j], over_recv.at[i, j], across)

    def part_copy(i, j):
        return remote(
            packs[i].at[1 - a, to(j)], theirs[i].at[j], part_send.at[i, j], part_recv.at[i, j], across
        )

    def result_copy(i, j):
        return remote(packs[i].at[a, to(j)], outs[i].at[e], out_send.at[i, j], out_recv.at[i, j], (a, to(j)))

    for i in range(2):
        forward_own(i).start()

        @pl.loop(1, experts)
        def _(j):
            first_send(i, j).start()

    def take_in(i, k):
        @pl.when(k < steps - 1)
        def _():
            @pl.loop(0, each)
            def _(d):
                j = 1 + k * each + d

                @pl.when(j < experts)
                def _():
                    received(i, j).wait_recv()
                    pass_on(i, j).start()

    def hand_out(i, k):
        @pl.when(k < steps - 1)
        def _():
            @pl.loop(0, each)
            def _(d):
                j = 1 + k * each + d

                @pl.when(j < experts)
                def _():
                    part_copy(i, j).wait_recv()
                    at = to(j)
                    packs[i][a, at] = (packs[i][a, at].astype(full32) + theirs[i][j].astype(full32)).astype(low)
                    result_copy(i, j).start()

    @pl.loop(0, steps)
    def _(k):
        slot = lax.rem(k, 2)
        columns = pl.ds(pl.multiple_of(k * chunk, chunk), chunk)
        for copy in stage(k, slot):
            copy.wait()
        inner[:, columns] = inner_stage[slot].astype(low)
        outer[columns, :] = outer_stage[slot].astype(low)

        @pl.when(k + 2 < steps)
        def _():
            for copy in stage(k + 2, slot):
                copy.start()

        take_in(0, k)

    def unpack(i, place):
        own_block(i).wait()

        @pl.loop(0, experts)
        def _(j):
            from_across(i, j).wait_recv()

        group = 8
        for plane in range(dp):
            for s in range(0, experts, group):
                base = (plane * experts + s) * 8
                for b in range(full):
                    piece = alls[i][plane, s : s + group, :, b * width : (b + 1) * width].astype(full32)
                    place[pl.ds(b * count + base, 8 * group), :] = piece.reshape(8 * group, width).astype(low)
        tails = [
            alls[i][plane, :, :, full * width :].astype(full32).reshape(experts * 8, half) for plane in range(dp)
        ]
        tail = jnp.concatenate(tails, axis=0).astype(low)
        for right in range(2):
            place[pl.ds(full * count, count // 2), pl.ds(right * half, half)] = nn(
                tail_picks(count, right), tail
            ).astype(low)

    def pack(i):
        group = 8
        for plane in range(dp):
            for s in range(0, experts, group):
                base = (plane * experts + s) * 8
                for b in range(full):
                    piece = acc[pl.ds(b * count + base, 8 * group), :].reshape(group, 8, width)
                    packs[i][plane, s : s + group, :, b * width : (b + 1) * width] = piece.astype(low)
        tail = acc[pl.ds(full * count, count // 2), :].astype(low)
        spread = None
        for right in range(2):
            piece = lax.dot_general(
                tail_picks(count, right),
                tail[:, right * half : (right + 1) * half],
                (((0,), (0,)), ((), ())),
                preferred_element_type=full32,
            )
            spread = piece if spread is None else spread + piece
        for plane in range(dp):
            piece = spread[plane * experts * 8 : (plane + 1) * experts * 8].reshape(experts, 8, half)
            packs[i][plane, :, :, full * width :] = piece.astype(low)

        @pl.loop(0, experts)
        def _(d):
            part_copy(i, lax.rem(d + 1, experts)).start()

    unpack(0, rows)
    turned[...] = jnp.transpose(rows[...])
    acc[...] = jnp.zeros_like(acc)

    @pl.loop(0, steps)
    def _(k):
        columns = pl.ds(pl.multiple_of(k * chunk, chunk), chunk)
        z = nn(rows[...], inner[:, columns]) + hidden_ref[:, columns].astype(low).astype(full32)
        value, slope = gelu_both(z)
        act[:, columns] = value.astype(low)
        grad[:, columns] = slope
        acc[...] += nn(act[:, columns], outer[columns, :])
        take_in(1, k)

    part = return_ref.shape[1]
    bias = return_ref[...].astype(low).astype(full32)
    for i in range(dp):
        columns = pl.ds(i * part, part)
        acc[:, columns] = acc[:, columns] + jnp.where(a == i, bias, 0.0)
    pack(0)
    unpack(1, dy)
    total = jnp.zeros((1, width), full32)
    for i in range(rows.shape[0] // LANES):
        total = total + jnp.sum(dy[pl.ds(i * LANES, LANES), :].astype(full32), axis=0, keepdims=True)
    picked = total[:, :part]
    for i in range(1, dp):
        picked = jnp.where(a == i, total[:, i * part : (i + 1) * part], picked)
    dreturn_ref[...] = picked
    square[...] = jnp.zeros_like(square)
    flat = picked * picked
    for i in range(part // LANES):
        square[0:1, :] = square[0:1, :] + flat[:, i * LANES : (i + 1) * LANES]
    acc[...] = jnp.zeros_like(acc)

    @pl.loop(0, steps)
    def _(k):
        columns = pl.ds(pl.multiple_of(k * chunk, chunk), chunk)
        dz[:, columns] = (nt(dy[...], outer[columns, :]) * grad[:, columns]).astype(low)
        acc[...] += nt(dz[:, columns], inner[:, columns])
        hand_out(0, k)

    pack(1)

    def finish(i):
        part_copy(i, 0).wait_recv()
        packs[i][a, e] = (packs[i][a, e].astype(full32) + theirs[i][0].astype(full32)).astype(low)
        pltpu.make_async_copy(packs[i].at[a, e], outs[i].at[e], own_sem.at[i]).start()

    def store(k, slot):
        columns = pl.ds(pl.multiple_of(k * chunk, chunk), chunk)
        return (
            pltpu.make_async_copy(dinner_stage.at[slot], dinner_any.at[0, :, columns], store_sem.at[0, slot]),
            pltpu.make_async_copy(douter_stage.at[slot], douter_any.at[0, columns, :], store_sem.at[1, slot]),
        )

    finish(0)

    @pl.loop(0, steps)
    def _(k):
        slot = lax.rem(k, 2)
        columns = pl.ds(pl.multiple_of(k * chunk, chunk), chunk)
        douter = nn(jnp.transpose(act[:, columns]), dy[...])
        dinner = nn(turned[...], dz[:, columns])
        dhidden = jnp.sum(dz[:, columns].astype(full32), axis=0, keepdims=True)

        @pl.when(k >= 2)
        def _():
            for copy in store(k - 2, slot):
                copy.wait()

        douter_stage[slot] = douter.astype(low)
        dinner_stage[slot] = dinner.astype(low)
        for copy in store(k, slot):
            copy.start()
        dhidden_ref[:, columns] = dhidden
        parts = jnp.zeros((8, LANES), full32)
        folded = jnp.sum((douter * douter).reshape(-1, 8, width), axis=0)
        for i in range(width // LANES):
            parts = parts + folded[:, i * LANES : (i + 1) * LANES]
        folded = jnp.sum((dinner * dinner).reshape(-1, 8, chunk), axis=0)
        hidden_square = dhidden * dhidden
        for i in range(chunk // LANES):
            parts = parts + folded[:, i * LANES : (i + 1) * LANES]
            square[0:1, :] = square[0:1, :] + hidden_square[:, i * LANES : (i + 1) * LANES]
        square[...] += parts
        hand_out(1, k)

    finish(1)
    square_ref[...] = square[...]
    for k in range(steps - 2, steps):
        for copy in store(k, k % 2):
            copy.wait()
    for i in range(2):

        @pl.loop(1, experts)
        def _(j):
            block = outs[i].at[source(j)]
            remote(block, block, out_send.at[i, j], out_recv.at[i, j], across).wait_recv()

    for i in range(2):
        pltpu.make_async_copy(packs[i].at[a, e], outs[i].at[e], own_sem.at[i]).wait()
        forward_own(i).wait_send()
        part_copy(i, 0).wait_send()

        @pl.loop(1, experts)
        def _(j):
            first_send(i, j).wait_send()
            pass_on(i, j).wait_send()
            part_copy(i, j).wait_send()
            result_copy(i, j).wait_send()


def mixture(rows, dy, inner, hidden, outer, back, dp, cid, chunk=256):
    experts, _, packed = rows.shape
    width, units = inner.shape[1:]
    count = dp * experts * 8
    total = count * packed // width
    low, full = jnp.bfloat16, jnp.float32
    both = (dp, experts, 8, packed)
    sems = [pltpu.SemaphoreType.DMA((2, experts)) for _ in range(8)]
    return pl.pallas_call(
        functools.partial(moe_kernel, dp, experts, chunk),
        out_shape=[
            jax.ShapeDtypeStruct(rows.shape, low),
            jax.ShapeDtypeStruct(rows.shape, low),
            jax.ShapeDtypeStruct(inner.shape, low),
            jax.ShapeDtypeStruct(hidden.shape, full),
            jax.ShapeDtypeStruct(outer.shape, low),
            jax.ShapeDtypeStruct(back.shape, full),
            jax.ShapeDtypeStruct((8, LANES), full),
        ],
        in_specs=[ANY, ANY, ANY, VMEM, ANY, VMEM],
        out_specs=[ANY, ANY, ANY, VMEM, ANY, VMEM, VMEM],
        scratch_shapes=[
            pltpu.VMEM(both, low),
            pltpu.VMEM(both, low),
            pltpu.VMEM(both, low),
            pltpu.VMEM(both, low),
            pltpu.VMEM(both[1:], low),
            pltpu.VMEM(both[1:], low),
            pltpu.VMEM((total, width), low),
            pltpu.VMEM((width, total), low),
            pltpu.VMEM((total, width), low),
            pltpu.VMEM((width, units), low),
            pltpu.VMEM((units, width), low),
            pltpu.VMEM((total, units), low),
            pltpu.VMEM((total, units), full),
            pltpu.VMEM((total, units), low),
            pltpu.VMEM((total, width), full),
            pltpu.VMEM((2, width, chunk), full),
            pltpu.VMEM((2, chunk, width), full),
            pltpu.VMEM((2, width, chunk), low),
            pltpu.VMEM((2, chunk, width), low),
            pltpu.VMEM((8, LANES), full),
            pltpu.SemaphoreType.DMA((2,)),
            *sems,
            pltpu.SemaphoreType.DMA((2, 2)),
            pltpu.SemaphoreType.DMA((2, 2)),
        ],
        compiler_params=pltpu.CompilerParams(
            collective_id=cid, has_side_effects=True, vmem_limit_bytes=60 * 1024 * 1024
        ),
        cost_estimate=pl.CostEstimate(flops=17 * 10**9, bytes_accessed=25 * 10**6, transcendentals=2 * 10**6),
        name="mixture",
    )(rows, dy, inner, hidden, outer, back)


def adam_values(weight, first, second, gradient, clip, rate, decay):
    scaled = gradient * clip
    first_new = BETA_ONE * first + (1.0 - BETA_ONE) * scaled
    second_new = BETA_TWO * second + (1.0 - BETA_TWO) * scaled * scaled
    first_hat = first_new * (1.0 / (1.0 - BETA_ONE**STEP))
    second_hat = second_new * (1.0 / (1.0 - BETA_TWO**STEP))
    weight_new = weight - rate * (first_hat / (jnp.sqrt(second_hat) + ADAM_EPS) + decay * weight)
    return weight_new, first_new, second_new


def adam_kernel(experts, norm_ref, dense_ref, *refs):
    ins, outs = refs[:28], refs[28:]
    total = jnp.sum(jnp.sum(norm_ref[...], axis=0, keepdims=True), axis=1, keepdims=True)
    norm = jnp.sqrt(total)
    clip = THRESHOLD / jnp.maximum(norm, THRESHOLD)

    def update(i, grad, rate, decay, columns=slice(None)):
        weight, first, second = (ref[:, columns] for ref in ins[3 * i : 3 * i + 3])
        new = adam_values(weight, first, second, grad, clip, rate, decay)
        for place, value in zip(outs[3 * i : 3 * i + 3], new):
            place[:, columns] = value

    inner_grad, outer_grad, hidden_grad, return_grad = ins[24:28]
    update(0, inner_grad[...].astype(jnp.float32), RATE_INNER, DECAY)
    update(1, outer_grad[...].astype(jnp.float32), RATE_OUTER, DECAY)

    @pl.when(pl.program_id(0) == 0)
    def _():
        outs[24][...] = norm
        width = ins[9].shape[1]
        trio = 3 * LANES
        for pair in range(width // LANES):
            for kind in range(3):
                update(
                    2,
                    dense_ref[:, width + pair * trio + kind * LANES : width + pair * trio + (kind + 1) * LANES],
                    RATE_PROJECTION,
                    DECAY,
                    slice(kind * width + pair * LANES, kind * width + (pair + 1) * LANES),
                )
        update(3, dense_ref[:, :width], RATE_OUTPUT, DECAY)
        turned = jnp.transpose(dense_ref[:, 4 * width : 4 * width + LANES])
        update(4, turned[:experts], RATE_ROUTER, DECAY)
        update(5, turned[experts : experts + 7], RATE_VECTORS, 0.0)
        update(6, hidden_grad[...], RATE_HIDDEN, 0.0)
        update(7, return_grad[...], RATE_RETURN, 0.0)


def adam_all(experts, squares, dense, states, grads, steps=8):
    operands, in_specs, out_specs, shapes = [squares, dense], [], [], []

    def spec_of(array, blocks):
        shape = array.shape
        if blocks:
            return pl.BlockSpec((shape[0] // steps, shape[1]), lambda i: (i, 0))
        return pl.BlockSpec(shape, lambda i: (0, 0))

    in_specs += [spec_of(squares, False), spec_of(dense, False)]
    for g, group in enumerate(states):
        spec = spec_of(group[0], g < 2)
        in_specs += [spec] * 3
        out_specs += [spec] * 3
        shapes += [jax.ShapeDtypeStruct(group[0].shape, jnp.float32)] * 3
        operands += list(group)
    for g, grad in enumerate(grads):
        in_specs.append(spec_of(grad, g < 2))
        operands.append(grad)
    out = pl.pallas_call(
        functools.partial(adam_kernel, experts),
        grid=(steps,),
        out_shape=shapes + [jax.ShapeDtypeStruct((1, 1), jnp.float32)],
        in_specs=in_specs,
        out_specs=out_specs + [pl.BlockSpec((1, 1), lambda i: (0, 0))],
        compiler_params=pltpu.CompilerParams(
            vmem_limit_bytes=60 * 1024 * 1024, dimension_semantics=("arbitrary",)
        ),
        cost_estimate=pl.CostEstimate(flops=5 * 10**7, bytes_accessed=62 * 10**6, transcendentals=10**7),
        name="adam_all",
    )(*operands)
    return [tuple(out[3 * i : 3 * i + 3]) for i in range(len(states))], out[-1].reshape(())


def fits(dp, experts):
    return dp == 2 and experts == 16


def fast_shards(
    dp,
    experts,
    tokens,
    cotangent,
    expert_choice,
    priority,
    projection,
    projection_first,
    projection_second,
    output_weight,
    output_first,
    output_second,
    router_weight,
    router_first,
    router_second,
    vectors,
    vectors_first,
    vectors_second,
    expert_inner,
    inner_first,
    inner_second,
    hidden_bias,
    hidden_first,
    hidden_second,
    expert_outer,
    outer_first,
    outer_second,
    return_bias,
    return_first,
    return_second,
):
    model_width = tokens.shape[2]
    patches = tokens.shape[1]
    capacity = max(2, patches // experts)
    low = jnp.bfloat16
    shard_rows = projection.shape[0]
    used = 4 * model_width + experts + vectors.shape[0]
    by_pair = projection.reshape(shard_rows, 3, -1, LANES).transpose(0, 2, 1, 3).reshape(projection.shape)
    packed = jnp.concatenate(
        [by_pair, output_weight, router_weight, vectors.T, jnp.zeros((shard_rows, -used % 128), jnp.float32)], axis=1
    ).astype(low)
    weights = gather_blocks(packed, dp, experts, 1).reshape(model_width, packed.shape[1])
    rows, dy, qkv, ctx, mid, second, stat, aux, probs = forward(
        tokens[0], cotangent[0], expert_choice[0], priority[0], weights, experts, capacity
    )
    blocks = (experts, 8, rows.shape[1])
    returned, back_rows, inner_grad, hidden_grad, outer_grad, return_grad, expert_square = mixture(
        rows.reshape(blocks),
        dy.reshape(blocks),
        expert_inner,
        hidden_bias,
        expert_outer,
        return_bias,
        dp,
        2,
    )
    block_output, input_grad, dense, squares = backward(
        tokens[0],
        cotangent[0],
        expert_choice[0],
        returned.reshape(rows.shape),
        back_rows.reshape(rows.shape),
        aux,
        probs,
        mid,
        second,
        ctx,
        stat,
        qkv,
        weights,
        expert_square,
        dp,
        experts,
        capacity,
        4,
    )
    states, grad_norm = adam_all(
        experts,
        squares,
        dense,
        [
            (expert_inner[0], inner_first[0], inner_second[0]),
            (expert_outer[0], outer_first[0], outer_second[0]),
            (projection, projection_first, projection_second),
            (output_weight, output_first, output_second),
            (router_weight.T, router_first.T, router_second.T),
            (vectors, vectors_first, vectors_second),
            (hidden_bias, hidden_first, hidden_second),
            (return_bias, return_first, return_second),
        ],
        [inner_grad[0], outer_grad[0], hidden_grad, return_grad],
    )
    inner_new, outer_new, projection_new, output_new, router_new, vectors_new, hidden_new, return_new = states
    return (
        block_output[None],
        input_grad[None],
        grad_norm,
        *projection_new,
        *output_new,
        *(v.T for v in router_new),
        *vectors_new,
        *(v[None] for v in inner_new),
        *hidden_new,
        *(v[None] for v in outer_new),
        *return_new,
    )


def solution(mesh):
    dp, experts = mesh.shape["dp"], mesh.shape["expert"]
    body = functools.partial(fast_shards, dp, experts) if fits(dp, experts) else shards
    return jax.shard_map(
        body,
        mesh=mesh,
        in_specs=(
            P(("dp", "expert"), None, None),
            P(("dp", "expert"), None, None),
            P(("dp", "expert"), None, None),
            P(("dp", "expert"), None),
            P(("dp", "expert"), None),
            P(("dp", "expert"), None),
            P(("dp", "expert"), None),
            P(("dp", "expert"), None),
            P(("dp", "expert"), None),
            P(("dp", "expert"), None),
            P(("dp", "expert"), None),
            P(("dp", "expert"), None),
            P(("dp", "expert"), None),
            P(None, ("dp", "expert")),
            P(None, ("dp", "expert")),
            P(None, ("dp", "expert")),
            P("expert", None, "dp"),
            P("expert", None, "dp"),
            P("expert", None, "dp"),
            P("expert", "dp"),
            P("expert", "dp"),
            P("expert", "dp"),
            P("expert", "dp", None),
            P("expert", "dp", None),
            P("expert", "dp", None),
            P("expert", "dp"),
            P("expert", "dp"),
            P("expert", "dp"),
        ),
        out_specs=(
            P(("dp", "expert"), None, None),
            P(("dp", "expert"), None, None),
            P(),
            P(("dp", "expert"), None),
            P(("dp", "expert"), None),
            P(("dp", "expert"), None),
            P(("dp", "expert"), None),
            P(("dp", "expert"), None),
            P(("dp", "expert"), None),
            P(("dp", "expert"), None),
            P(("dp", "expert"), None),
            P(("dp", "expert"), None),
            P(None, ("dp", "expert")),
            P(None, ("dp", "expert")),
            P(None, ("dp", "expert")),
            P("expert", None, "dp"),
            P("expert", None, "dp"),
            P("expert", None, "dp"),
            P("expert", "dp"),
            P("expert", "dp"),
            P("expert", "dp"),
            P("expert", "dp", None),
            P("expert", "dp", None),
            P("expert", "dp", None),
            P("expert", "dp"),
            P("expert", "dp"),
            P("expert", "dp"),
        ),
        check_vma=False,
    )
```

```python
import functools

import jax
import jax.numpy as jnp
from jax import lax
from jax.experimental import pallas as pl
from jax.experimental.pallas import tpu as pltpu
from jax.sharding import PartitionSpec as P

HEADS = 12
HEAD_DIM = 64
STEP = 10


NORM_EPS = 1e-06
ADAM_EPS = 1e-08
BETA_ONE = 0.9
BETA_TWO = 0.999
DECAY = 0.1
THRESHOLD = 1.0
RATE_PROJECTION = 0.1
RATE_OUTPUT = 1.0
RATE_ROUTER = 0.05
RATE_VECTORS = 0.5
RATE_INNER = 0.1
RATE_HIDDEN = 0.25
RATE_OUTER = 1.5
RATE_RETURN = 2.0


def layer_norm(values, norm_gain, norm_bias):
    center = values - jnp.mean(values, axis=-1, keepdims=True)
    spread = jnp.mean(center * center, axis=-1, keepdims=True)
    return center * lax.rsqrt(spread + NORM_EPS) * norm_gain + norm_bias


def smooth_gate(values):
    return jax.nn.gelu(values, approximate=True)


def mixed_dot(left, right):
    return jnp.dot(left, right, preferred_element_type=jnp.float32)


def rows_product(left, right):
    return lax.dot_general(
        left, right, (((0,), (0,)), ((), ())), preferred_element_type=jnp.float32
    )


def columns_product(left, right):
    return lax.dot_general(
        left, right, (((1,), (1,)), ((), ())), preferred_element_type=jnp.float32
    )


def assign_slots(chosen, claim_order, expert_count, capacity):
    patches = chosen.shape[0]
    top_count = chosen.shape[1]
    claim_rank = (
        jnp.arange(top_count, dtype=jnp.int32)[None, :] * patches + claim_order[:, None]
    ).T.reshape(-1)
    flat_choice = chosen.T.reshape(-1)
    onehot = (flat_choice[:, None] == jnp.arange(expert_count, dtype=jnp.int32)[None, :]).astype(
        jnp.float32
    )
    earlier = (claim_rank[None, :] < claim_rank[:, None]).astype(jnp.float32)
    counts = jnp.dot(
        earlier, onehot, precision=lax.Precision.HIGHEST, preferred_element_type=jnp.float32
    )
    position = jnp.sum(counts * onehot, axis=1).astype(jnp.int32).reshape(top_count, patches).T
    kept_mask = position < capacity
    flat_slot = chosen * capacity + jnp.minimum(position, capacity - 1)
    return (flat_slot, kept_mask)


def slot_matches(flat_slot, kept_mask, slot_count):
    slot_ids = jnp.arange(slot_count, dtype=jnp.int32)
    return (flat_slot[None, :, :] == slot_ids[:, None, None]) & kept_mask[None, :, :]


def select_gates(logits, chosen, expert_count):
    router_probs = jax.nn.softmax(logits, axis=-1)
    onehot = chosen[:, :, None] == jnp.arange(expert_count, dtype=jnp.int32)[None, None, :]
    return jnp.sum(jnp.where(onehot, router_probs[:, None, :], 0.0), axis=2)


def adam_update(weight, first_state, second, gradient, clip_factor, step_rate, decay_rate):
    scaled = gradient * clip_factor
    first_new = BETA_ONE * first_state + (1.0 - BETA_ONE) * scaled
    second_new = BETA_TWO * second + (1.0 - BETA_TWO) * scaled * scaled
    first_hat = first_new / (1.0 - BETA_ONE**STEP)
    second_hat = second_new / (1.0 - BETA_TWO**STEP)
    weight_new = weight - step_rate * (
        first_hat / (jnp.sqrt(second_hat) + ADAM_EPS) + decay_rate * weight
    )
    return (weight_new, first_new, second_new)


def shards(
    tokens,
    cotangent,
    expert_choice,
    priority,
    projection,
    projection_first,
    projection_second,
    output_weight,
    output_first,
    output_second,
    router_weight,
    router_first,
    router_second,
    vectors,
    vectors_first,
    vectors_second,
    expert_inner,
    inner_first,
    inner_second,
    hidden_bias,
    hidden_first,
    hidden_second,
    expert_outer,
    outer_first,
    outer_second,
    return_bias,
    return_first,
    return_second,
):
    model_width = tokens.shape[2]
    patches = tokens.shape[1]
    experts = lax.axis_size("expert")
    capacity = max(2, patches // experts)
    slot_count = experts * capacity
    score_scale = HEAD_DIM ** (-0.5)
    dense_shards = (
        projection.astype(jnp.bfloat16),
        output_weight.astype(jnp.bfloat16),
        router_weight.astype(jnp.bfloat16),
        vectors.astype(jnp.bfloat16),
    )
    partial_shards = (
        lax.all_gather(dense_shards[0], "expert", axis=0, tiled=True),
        lax.all_gather(dense_shards[1], "expert", axis=0, tiled=True),
        lax.all_gather(dense_shards[2], "expert", axis=0, tiled=True),
        lax.all_gather(dense_shards[3], "expert", axis=1, tiled=True),
    )
    whole_projection, whole_output, whole_router, whole_vectors = (
        lax.all_gather(partial_shards[0], "dp", axis=0, tiled=True),
        lax.all_gather(partial_shards[1], "dp", axis=0, tiled=True),
        lax.all_gather(partial_shards[2], "dp", axis=0, tiled=True),
        lax.all_gather(partial_shards[3], "dp", axis=1, tiled=True),
    )
    inner_low = expert_inner.astype(jnp.bfloat16)
    hidden_low = hidden_bias.astype(jnp.bfloat16)
    outer_low = expert_outer.astype(jnp.bfloat16)
    return_low = return_bias.astype(jnp.bfloat16)
    inner_all, hidden_all, outer_all, return_all = (
        lax.all_gather(inner_low, "dp", axis=2, tiled=True),
        lax.all_gather(hidden_low, "dp", axis=1, tiled=True),
        lax.all_gather(outer_low, "dp", axis=1, tiled=True),
        lax.all_gather(return_low, "dp", axis=1, tiled=True),
    )
    vector_rows = whole_vectors.astype(jnp.float32)
    image_rows = tokens[0].astype(jnp.float32)
    normed_one, norm_back_one = jax.vjp(layer_norm, image_rows, vector_rows[0], vector_rows[1])
    normed_low = normed_one.astype(jnp.bfloat16)
    projected = mixed_dot(normed_low, whole_projection)
    queries = (
        (projected[:, :model_width] + vector_rows[2])
        .astype(jnp.bfloat16)
        .reshape(patches, HEADS, HEAD_DIM)
    )
    key_rows = (
        projected[:, model_width : 2 * model_width]
        .astype(jnp.bfloat16)
        .reshape(patches, HEADS, HEAD_DIM)
    )
    value_rows = (
        (projected[:, 2 * model_width :] + vector_rows[3])
        .astype(jnp.bfloat16)
        .reshape(patches, HEADS, HEAD_DIM)
    )
    scores = (
        jnp.einsum("qhd,khd->hqk", queries, key_rows, preferred_element_type=jnp.float32)
        * score_scale
    )
    score_top = jnp.max(scores, axis=-1, keepdims=True)
    raised = jnp.exp(scores - score_top)
    totals = jnp.sum(raised, axis=-1, keepdims=True)
    attention = raised / totals
    log_total = score_top + jnp.log(totals)
    context = (
        jnp.einsum(
            "hqk,khd->qhd",
            attention.astype(jnp.bfloat16),
            value_rows,
            preferred_element_type=jnp.float32,
        )
        .reshape(patches, model_width)
        .astype(jnp.bfloat16)
    )
    middle = image_rows + (mixed_dot(context, whole_output) + vector_rows[4])
    normed_two, norm_back_two = jax.vjp(layer_norm, middle, vector_rows[5], vector_rows[6])
    second_low = normed_two.astype(jnp.bfloat16)
    logits = mixed_dot(second_low, whole_router)
    chosen = expert_choice[0]

    def gate_choice(values):
        return select_gates(values, chosen, experts)

    gate_values, gate_back = jax.vjp(gate_choice, logits)
    flat_slot, kept_mask = assign_slots(chosen, priority[0], experts, capacity)
    matches = slot_matches(flat_slot, kept_mask, slot_count)
    slot_table = jnp.any(matches, axis=2).astype(jnp.bfloat16)
    dispatched = (
        mixed_dot(slot_table, second_low)
        .astype(jnp.bfloat16)
        .reshape(experts, capacity, model_width)
    )
    arrived = lax.all_to_all(dispatched, "expert", split_axis=0, concat_axis=0, tiled=True).reshape(
        slot_count, model_width
    )
    pre_act = mixed_dot(arrived, inner_all[0]) + hidden_all[0].astype(jnp.float32)
    activated, gelu_back = jax.vjp(smooth_gate, pre_act)
    active_low = activated.astype(jnp.bfloat16)
    expert_out = (mixed_dot(active_low, outer_all[0]) + return_all[0].astype(jnp.float32)).astype(
        jnp.bfloat16
    )
    returned = lax.all_to_all(
        expert_out.reshape(experts, capacity, model_width),
        "expert",
        split_axis=0,
        concat_axis=0,
        tiled=True,
    ).reshape(slot_count, model_width)
    picked = returned[flat_slot].astype(jnp.float32)
    weighted = jnp.where(kept_mask, gate_values, 0.0)
    final = middle + jnp.sum(weighted[:, :, None] * picked, axis=1)
    block_output = final.astype(jnp.bfloat16)[None]
    upstream = cotangent[0].astype(jnp.float32)
    gate_grad = jnp.where(kept_mask, jnp.sum(upstream[:, None, :] * picked, axis=2), 0.0)
    slot_gate = jnp.sum(jnp.where(matches, weighted[None, :, :], 0.0), axis=(1, 2))
    slot_grad = (mixed_dot(slot_table, cotangent[0]) * slot_gate[:, None]).astype(jnp.bfloat16)
    sent_grad = lax.all_to_all(
        slot_grad.reshape(experts, capacity, model_width),
        "expert",
        split_axis=0,
        concat_axis=0,
        tiled=True,
    ).reshape(slot_count, model_width)
    outer_grad = rows_product(active_low, sent_grad)
    return_grad = jnp.sum(sent_grad, axis=0, dtype=jnp.float32)
    active_grad = columns_product(sent_grad, outer_all[0])
    (pre_grad,) = gelu_back(active_grad)
    pre_low = pre_grad.astype(jnp.bfloat16)
    inner_grad = rows_product(arrived, pre_low)
    hidden_grad = jnp.sum(pre_low, axis=0, dtype=jnp.float32)
    row_grad = columns_product(pre_low, inner_all[0]).astype(jnp.bfloat16)
    expert_grads = (
        lax.psum_scatter(
            inner_grad[None].astype(jnp.bfloat16), "dp", scatter_dimension=2, tiled=True
        ).astype(jnp.float32),
        lax.psum_scatter(
            hidden_grad[None].astype(jnp.bfloat16), "dp", scatter_dimension=1, tiled=True
        ).astype(jnp.float32),
        lax.psum_scatter(
            outer_grad[None].astype(jnp.bfloat16), "dp", scatter_dimension=1, tiled=True
        ).astype(jnp.float32),
        lax.psum_scatter(
            return_grad[None].astype(jnp.bfloat16), "dp", scatter_dimension=1, tiled=True
        ).astype(jnp.float32),
    )
    back_rows = lax.all_to_all(
        row_grad.reshape(experts, capacity, model_width),
        "expert",
        split_axis=0,
        concat_axis=0,
        tiled=True,
    ).reshape(slot_count, model_width)
    (logit_grad,) = gate_back(gate_grad)
    logit_low = logit_grad.astype(jnp.bfloat16)
    router_grad = rows_product(second_low, logit_low)
    second_grad = rows_product(slot_table, back_rows) + columns_product(logit_low, whole_router)
    middle_part, gain_two_grad, bias_two_grad = norm_back_two(second_grad)
    middle_grad = upstream + middle_part
    branch_low = middle_grad.astype(jnp.bfloat16)
    output_grad = rows_product(context, branch_low)
    out_bias_grad = jnp.sum(branch_low, axis=0, dtype=jnp.float32)
    context_grad = (
        columns_product(branch_low, whole_output)
        .astype(jnp.bfloat16)
        .reshape(patches, HEADS, HEAD_DIM)
    )
    scores = (
        jnp.einsum("qhd,khd->hqk", queries, key_rows, preferred_element_type=jnp.float32)
        * score_scale
    )
    attention = jnp.exp(scores - log_total)
    attention_grad = jnp.einsum(
        "qhd,khd->hqk", context_grad, value_rows, preferred_element_type=jnp.float32
    )
    value_grad = jnp.einsum(
        "hqk,qhd->khd",
        attention.astype(jnp.bfloat16),
        context_grad,
        preferred_element_type=jnp.float32,
    ).astype(jnp.bfloat16)
    centered = jnp.sum(attention * attention_grad, axis=-1, keepdims=True)
    score_grad = (attention * (attention_grad - centered)).astype(jnp.bfloat16)
    query_grad = (
        (
            jnp.einsum("hqk,khd->qhd", score_grad, key_rows, preferred_element_type=jnp.float32)
            * score_scale
        )
        .astype(jnp.bfloat16)
        .reshape(patches, model_width)
    )
    key_grad = (
        (
            jnp.einsum("hqk,qhd->khd", score_grad, queries, preferred_element_type=jnp.float32)
            * score_scale
        )
        .astype(jnp.bfloat16)
        .reshape(patches, model_width)
    )
    value_flat = value_grad.reshape(patches, model_width)
    joined_grad = jnp.concatenate([query_grad, key_grad, value_flat], axis=1)
    projection_grad = rows_product(normed_low, joined_grad)
    normed_grad = columns_product(joined_grad, whole_projection)
    input_part, gain_one_grad, bias_one_grad = norm_back_one(normed_grad)
    input_grad = (middle_grad + input_part)[None]
    vector_grad = jnp.stack(
        [
            gain_one_grad,
            bias_one_grad,
            jnp.sum(query_grad, axis=0, dtype=jnp.float32),
            jnp.sum(value_flat, axis=0, dtype=jnp.float32),
            out_bias_grad,
            gain_two_grad,
            bias_two_grad,
        ]
    )
    local_grads = (projection_grad, output_grad, router_grad, vector_grad)
    partial_grads = (
        lax.psum_scatter(
            local_grads[0].astype(jnp.bfloat16), "dp", scatter_dimension=0, tiled=True
        ).astype(jnp.float32),
        lax.psum_scatter(
            local_grads[1].astype(jnp.bfloat16), "dp", scatter_dimension=0, tiled=True
        ).astype(jnp.float32),
        lax.psum_scatter(
            local_grads[2].astype(jnp.bfloat16), "dp", scatter_dimension=0, tiled=True
        ).astype(jnp.float32),
        lax.psum_scatter(
            local_grads[3].astype(jnp.bfloat16), "dp", scatter_dimension=1, tiled=True
        ).astype(jnp.float32),
    )
    dense_grads = (
        lax.psum_scatter(
            partial_grads[0].astype(jnp.bfloat16), "expert", scatter_dimension=0, tiled=True
        ).astype(jnp.float32),
        lax.psum_scatter(
            partial_grads[1].astype(jnp.bfloat16), "expert", scatter_dimension=0, tiled=True
        ).astype(jnp.float32),
        lax.psum_scatter(
            partial_grads[2].astype(jnp.bfloat16), "expert", scatter_dimension=0, tiled=True
        ).astype(jnp.float32),
        lax.psum_scatter(
            partial_grads[3].astype(jnp.bfloat16), "expert", scatter_dimension=1, tiled=True
        ).astype(jnp.float32),
    )
    all_grads = tuple(dense_grads) + tuple(expert_grads)
    local_square = jnp.sum(all_grads[0] * all_grads[0])
    for gradient in all_grads[1:]:
        local_square = local_square + jnp.sum(gradient * gradient)
    square_total = lax.psum(local_square, ("dp", "expert"))
    grad_norm = jnp.sqrt(square_total)
    clip_factor = THRESHOLD / jnp.maximum(grad_norm, THRESHOLD)
    projection_next, projection_moment, projection_square = adam_update(
        projection,
        projection_first,
        projection_second,
        all_grads[0],
        clip_factor,
        RATE_PROJECTION,
        DECAY,
    )
    output_next, output_moment, output_square = adam_update(
        output_weight, output_first, output_second, all_grads[1], clip_factor, RATE_OUTPUT, DECAY
    )
    router_next, router_moment, router_square = adam_update(
        router_weight, router_first, router_second, all_grads[2], clip_factor, RATE_ROUTER, DECAY
    )
    vectors_next, vectors_moment, vectors_square = adam_update(
        vectors, vectors_first, vectors_second, all_grads[3], clip_factor, RATE_VECTORS, 0.0
    )
    inner_next, inner_moment, inner_square = adam_update(
        expert_inner, inner_first, inner_second, all_grads[4], clip_factor, RATE_INNER, DECAY
    )
    hidden_next, hidden_moment, hidden_square = adam_update(
        hidden_bias, hidden_first, hidden_second, all_grads[5], clip_factor, RATE_HIDDEN, 0.0
    )
    outer_next, outer_moment, outer_square = adam_update(
        expert_outer, outer_first, outer_second, all_grads[6], clip_factor, RATE_OUTER, DECAY
    )
    return_next, return_moment, return_square = adam_update(
        return_bias, return_first, return_second, all_grads[7], clip_factor, RATE_RETURN, 0.0
    )
    return (
        block_output,
        input_grad,
        grad_norm,
        projection_next,
        projection_moment,
        projection_square,
        output_next,
        output_moment,
        output_square,
        router_next,
        router_moment,
        router_square,
        vectors_next,
        vectors_moment,
        vectors_square,
        inner_next,
        inner_moment,
        inner_square,
        hidden_next,
        hidden_moment,
        hidden_square,
        outer_next,
        outer_moment,
        outer_square,
        return_next,
        return_moment,
        return_square,
    )


MESH = pl.DeviceIdType.MESH
ANY = pl.BlockSpec(memory_space=pl.ANY)
VMEM = pl.BlockSpec(memory_space=pltpu.VMEM)


class Place:
    def __init__(self, dp, experts):
        self.dp, self.experts = dp, experts
        self.ys = 2
        self.zs = experts // 4
        self.a = lax.axis_index("dp")
        self.e = lax.axis_index("expert")
        self.core = lax.rem(self.e, 2)
        self.y = lax.rem(lax.div(self.e, 2), self.ys)
        self.z = lax.div(self.e, 2 * self.ys)

    def chip_of(self, core, dz, s2, s3):
        zz = lax.rem(self.z + dz, self.zs)
        if s2 == s3:
            fa = fy = s2
        elif s2:
            fa, fy = core, 1 - core
        else:
            fa, fy = 1 - core, core
        aa = lax.rem(self.a + fa, 2)
        yy = lax.rem(self.y + fy, 2)
        return aa, zz, yy

    def device(self, core, dz, s2, s3, own_core=None):
        aa, zz, yy = self.chip_of(core, dz, s2, s3)
        c = core if own_core is None else own_core
        return (aa, (zz * self.ys + yy) * 2 + c)

    def flat(self, dev):
        return dev[0] * self.experts + dev[1]

    def chip(self, core, dz, s2, s3):
        aa, zz, yy = self.chip_of(core, dz, s2, s3)
        return (aa * self.zs + zz) * self.ys + yy


def remote(src, dst, send, recv, dev):
    return pltpu.make_async_remote_copy(src_ref=src, dst_ref=dst, send_sem=send, recv_sem=recv, device_id=dev, device_id_type=MESH)


def greet(devices):
    barrier = pltpu.get_barrier_semaphore()
    for dev in devices:
        pl.semaphore_signal(barrier, inc=1, device_id=dev, device_id_type=MESH)
    pl.semaphore_wait(barrier, len(devices))


def split_index(k, zs):
    return k % zs, (k // zs) % 2, k // (2 * zs)


LANES = 128


def nn(left, right):
    return lax.dot_general(left, right, (((1,), (0,)), ((), ())), preferred_element_type=jnp.float32)


def nt(left, right):
    return lax.dot_general(left, right, (((1,), (1,)), ((), ())), preferred_element_type=jnp.float32)


def lane_ids(rows, start=0):
    return lax.broadcasted_iota(jnp.int32, (rows, LANES), 1) + start


def row_parts(count, size):
    return [pl.ds(i * size, size) for i in range(count // size)]


def norm_parts(values):
    center = values - jnp.mean(values, axis=-1, keepdims=True)
    inverse = lax.rsqrt(jnp.mean(center * center, axis=-1, keepdims=True) + NORM_EPS)
    return center * inverse, inverse


def vector_table(weights, width):
    return jnp.transpose(weights[:, 4 * width :].astype(jnp.float32))


def forward_kernel(
    dp,
    experts,
    capacity,
    chunk,
    tok_ref,
    cot_ref,
    choice_ref,
    rank_col,
    rank_row,
    projection_ref,
    output_ref,
    router_ref,
    vectors_ref,
    rows_ref,
    dy_ref,
    qkv_ref,
    ctx_ref,
    mid_ref,
    second_ref,
    stat_ref,
    aux_ref,
    probs_ref,
    weights_any,
    weights,
    vec,
    normed,
    mine,
    theirs,
    land_first,
    land,
    pre_send,
    pre_recv,
    line_send,
    line_recv,
    second_send,
    second_recv,
    third_send,
    third_recv,
    core_send,
    core_recv,
    store,
):
    low, full32 = jnp.bfloat16, jnp.float32
    patches, width = tok_ref.shape
    half = width // 2
    trio_width = 3 * LANES
    p = Place(dp, experts)
    c, zs = p.core, p.zs
    deep = projection_ref.shape[0]
    partner = (p.a, p.e + 1 - 2 * c)
    second, third = p.device(c, 0, 1, 0), p.device(c, 0, 0, 1)
    peers = [p.device(c, dz, 0, 0) for dz in range(1, zs)]
    narrow = jnp.concatenate(
        [router_ref[...], vectors_ref[...], jnp.zeros((LANES - experts - vectors_ref.shape[0], deep), full32)], axis=0
    )
    for h in range(2):
        mine[h, :, :LANES] = jnp.transpose(narrow) if h == 0 else jnp.zeros((deep, LANES), full32)
        for i in range(width // LANES // 2):
            for kind in range(3):
                at = kind * width + (2 * i + h) * LANES
                mine[h, :, LANES + i * trio_width + kind * LANES : LANES + i * trio_width + (kind + 1) * LANES] = (
                    projection_ref[:, at : at + LANES]
                )
        mine[h, :, LANES + 3 * half :] = output_ref[:, h * half : (h + 1) * half]
    greet(peers + [second, third, partner])
    before_all = remote(mine.at[1 - c], theirs, pre_send, pre_recv, partner)
    before_all.start()
    lanes = lane_ids(patches)
    first, other = choice_ref[:, 0:1], choice_ref[:, 1:2]
    is_first, is_other = lanes == first, lanes == other
    chunks = width // LANES // 2 + 1
    lands = [land_first] + [land.at[i] for i in range(chunks - 1)]
    my_line = p.a * p.ys + p.y
    second_line = jnp.where(c == 0, p.a * p.ys + 1 - p.y, (1 - p.a) * p.ys + p.y)
    third_lines = [
        jnp.where(c == 0, (1 - p.a) * p.ys + p.y, p.a * p.ys + 1 - p.y),
        (1 - p.a) * p.ys + 1 - p.y,
    ]

    def line_copy(i, dz):
        block = lands[i].at[c, my_line, p.z]
        return remote(block, block, line_send.at[i, dz], line_recv.at[i, dz], peers[dz - 1])

    def second_copy(i):
        block = lands[i].at[c, my_line]
        return remote(block, block, second_send.at[i], second_recv.at[i], second)

    def third_copy(i, which):
        block = lands[i].at[c, my_line if which == 0 else second_line]
        return remote(block, block, third_send.at[i, which], third_recv.at[i, which], third)

    def core_copy(i, which):
        block = lands[i].at[c, (my_line, second_line, *third_lines)[which]]
        return remote(block, block, core_send.at[i, which], core_recv.at[i, which], partner)

    def step0(i):
        for dz in range(1, zs):
            line_copy(i, dz).start()

    def step1(i):
        for dz in range(1, zs):
            block = lands[i].at[c, my_line, lax.rem(p.z + zs - dz, zs)]
            remote(block, block, line_send.at[i, dz], line_recv.at[i, dz], partner).wait_recv()
        third_copy(i, 0).start()
        second_copy(i).start()
        core_copy(i, 0).start()

    def step2(i):
        second_copy(i).wait_recv()
        third_copy(i, 1).start()
        core_copy(i, 1).start()

    def step3(i):
        for which in range(2):
            third_copy(i, which).wait_recv()
            core_copy(i, 2 + which).start()

    def unpack(i):
        for which in range(4):
            core_copy(i, which).wait_recv()
        for line in range(2 * p.ys):
            for z in range(zs):
                at = (line // p.ys * zs + z) * p.ys + line % p.ys
                rows = pl.ds(2 * deep * at, 2 * deep)
                for h in range(2):
                    if i == 0:
                        weights[rows, h * trio_width : (h + 1) * trio_width] = land_first[h, line, z, :, LANES:]
                    else:
                        columns = pl.ds((2 * i + h) * half, half)
                        weights[rows, columns] = land[i - 1, h, line, z]
                if i == 0:
                    weights[rows, 4 * width :] = land_first[0, line, z, :, :LANES]

    before_all.wait_recv()
    own, their = mine[c], theirs[...]
    top, bottom = jnp.where(c == 0, own, their), jnp.where(c == 0, their, own)
    block = jnp.concatenate([top, bottom], axis=0).astype(low)
    land_first[c, my_line, p.z] = block[:, : LANES + half]
    for i in range(1, chunks):
        land[i - 1, c, my_line, p.z] = block[:, LANES + i * half : LANES + (i + 1) * half]
    for i in range(chunks):
        step0(i)
    earlier = (rank_row[...] < rank_col[...]).astype(full32).astype(low)
    hot = (is_first | (lanes == other + experts)).astype(full32)
    counts = nn(earlier, hot.astype(low))
    totals = jnp.sum(hot, axis=0, keepdims=True)
    place_first = jnp.sum(jnp.where(is_first, counts, 0.0), axis=1, keepdims=True)
    place_other = jnp.sum(
        jnp.where(lanes == other + experts, counts, 0.0) + jnp.where(is_other, totals, 0.0), axis=1, keepdims=True
    )
    aux_ref[...] = jnp.where(lanes == 0, place_first, jnp.where(lanes == 1, place_other, 0.0))

    def row(i):
        return vec[experts + i : experts + i + 1, :]

    def attend(pair):
        at = pair * LANES
        trio = pair * trio_width
        product = nn(normed[...], weights[:, trio : trio + trio_width])
        queries_all = (product[:, :LANES] + vec[experts + 2 : experts + 3, at : at + LANES]).astype(low)
        keys = product[:, LANES : 2 * LANES].astype(low)
        values = (product[:, 2 * LANES :] + vec[experts + 3 : experts + 4, at : at + LANES]).astype(low)
        qkv_ref[:, trio : trio + LANES] = queries_all
        qkv_ref[:, trio + LANES : trio + 2 * LANES] = keys
        qkv_ref[:, trio + 2 * LANES : trio + 3 * LANES] = values
        key_lanes = lane_ids(patches)
        values_two = [
            jnp.where(key_lanes < HEAD_DIM, values, (key_lanes == HEAD_DIM).astype(full32).astype(low)),
            jnp.where(key_lanes >= HEAD_DIM, values, (key_lanes == 0).astype(full32).astype(low)),
        ]
        for part in row_parts(patches, chunk):
            own_lanes = lane_ids(chunk)
            queries = qkv_ref[part, trio : trio + LANES] * jnp.asarray(HEAD_DIM**-0.5, low)
            outs = []
            stat = stat_ref[part, :]
            for head in range(2):
                side = (own_lanes < HEAD_DIM) if head == 0 else (own_lanes >= HEAD_DIM)
                scores = nt(jnp.where(side, queries, jnp.zeros_like(queries)), keys)
                peak = jnp.max(scores, axis=1, keepdims=True)
                raised = jnp.exp(scores - peak)
                mixed = nn(raised.astype(low), values_two[head])
                spare = HEAD_DIM if head == 0 else 0
                total = mixed[:, spare : spare + 1]
                outs.append(mixed / total)
                stat = jnp.where(own_lanes == 2 * pair + head, peak + jnp.log(total), stat)
            stat_ref[part, :] = stat
            ctx_ref[part, at : at + LANES] = jnp.where(own_lanes < HEAD_DIM, outs[0], outs[1]).astype(low)

    stat_ref[...] = jnp.zeros_like(stat_ref)
    step1(0)
    step1(1)
    step2(0)
    step1(2)
    step2(1)
    step3(0)
    step1(3)
    unpack(0)
    vec[...] = vector_table(weights, width)
    for part in row_parts(patches, chunk):
        unit, _ = norm_parts(tok_ref[part, :].astype(full32))
        normed[part, :] = (unit * row(0) + row(1)).astype(low)
    step2(2)
    step3(1)
    attend(0)
    step2(3)
    attend(1)
    step3(2)
    unpack(1)
    attend(2)
    step3(3)
    attend(3)
    unpack(2)
    attend(4)
    attend(5)
    unpack(3)
    keep = pltpu.make_async_copy(weights, weights_any, store)
    keep.start()
    third_columns = 256
    for j in range(width // third_columns):
        columns = pl.ds(j * third_columns, third_columns)
        product = nn(ctx_ref[...], weights[:, pl.ds(3 * width + j * third_columns, third_columns)])
        mid_ref[:, columns] = tok_ref[:, columns].astype(full32) + (product + vec[experts + 4 : experts + 5, columns])
    for part in row_parts(patches, chunk):
        unit, _ = norm_parts(mid_ref[part, :])
        second_ref[part, :] = (unit * row(5) + row(6)).astype(low)
    logits = jnp.where(lanes < experts, nn(second_ref[...], weights[:, 4 * width :]), -1e30)
    raised = jnp.exp(logits - jnp.max(logits, axis=1, keepdims=True))
    probs = raised / jnp.sum(raised, axis=1, keepdims=True)
    probs_ref[...] = probs
    place_first, place_other = aux_ref[:, 0:1], aux_ref[:, 1:2]

    def slot_of(place, expert):
        place = place.astype(jnp.int32)
        kept = place < capacity
        slot = (place // 8) * LANES + expert * 8 + place % 8
        tail = kept & (place >= capacity - 4)
        return kept, jnp.where(kept, slot, -1), jnp.where(tail, slot + 4, -1)

    aux = jnp.zeros((patches, LANES), jnp.float32)
    for j, (place, expert, hit) in enumerate(((place_first, first, is_first), (place_other, other, is_other))):
        kept, slot, twin = slot_of(place, expert)
        gate = jnp.where(kept, jnp.sum(jnp.where(hit, probs, 0.0), axis=1, keepdims=True), 0.0)
        for lane, column in ((j, slot.astype(jnp.float32)), (2 + j, twin.astype(jnp.float32)), (4 + j, gate)):
            aux = jnp.where(lanes == lane, column, aux)
    aux_ref[...] = aux
    turned = jnp.transpose(aux)
    slots = [turned[i : i + 1, :] for i in range(4)]
    gates = [turned[4 + i : 5 + i, :] for i in range(2)]
    full = capacity // 8
    for i in range(full + 1):
        ids = (lax.broadcasted_iota(jnp.int32, (LANES, patches), 0) + i * LANES).astype(jnp.float32)
        hits = [ids == slots[0], ids == slots[1]]
        if i == full:
            hits = [hits[0] | (ids == slots[2]), hits[1] | (ids == slots[3])]
        table = (hits[0] | hits[1]).astype(jnp.float32).astype(low)
        gate = jnp.sum(
            jnp.where(hits[0], gates[0], 0.0) + jnp.where(hits[1], gates[1], 0.0), axis=1, keepdims=True
        )
        sent = nn(table, second_ref[...])
        back = nn(table, cot_ref[...]) * gate
        columns = pl.ds(i * width, width)
        if i == full:
            columns = pl.ds(i * width, width // 2)
            left = lax.broadcasted_iota(jnp.int32, (LANES, width // 2), 0) % 8 < 4
            sent = jnp.where(left, sent[:, : width // 2], sent[:, width // 2 :])
            back = jnp.where(left, back[:, : width // 2], back[:, width // 2 :])
        rows_ref[:, columns] = sent.astype(low)
        dy_ref[:, columns] = back.astype(low)
    keep.wait()
    before_all.wait_send()
    for i in range(chunks):
        for dz in range(1, zs):
            line_copy(i, dz).wait_send()
        second_copy(i).wait_send()
        for which in range(2):
            third_copy(i, which).wait_send()
        for which in range(4):
            core_copy(i, which).wait_send()


def forward(
    tokens,
    cotangent,
    choice,
    priority,
    projection,
    output_weight,
    router_weight,
    vectors,
    dp,
    experts,
    capacity,
    cid,
    chunk=576,
):
    patches, width = tokens.shape
    low, full = jnp.bfloat16, jnp.float32
    packed = (8 * experts, capacity * width // 8)
    shapes = [
        (packed, low),
        (packed, low),
        ((patches, 3 * width), low),
        ((patches, width), low),
        ((patches, width), full),
        ((patches, width), low),
        ((patches, LANES), full),
        ((patches, LANES), full),
        ((patches, LANES), full),
        ((width, 4 * width + LANES), low),
    ]
    deep, half = projection.shape[0], width // 2
    chunks = width // LANES // 2 + 1
    zs = experts // 4
    lines = dp * experts // 2 // zs
    dma = pltpu.SemaphoreType.DMA
    return pl.pallas_call(
        functools.partial(forward_kernel, dp, experts, capacity, chunk),
        out_shape=[jax.ShapeDtypeStruct(*s) for s in shapes],
        in_specs=[VMEM] * 9,
        out_specs=[VMEM] * 9 + [ANY],
        scratch_shapes=[
            pltpu.VMEM(shapes[-1][0], low),
            pltpu.VMEM((LANES, width), full),
            pltpu.VMEM((patches, width), low),
            pltpu.VMEM((2, deep, LANES + 4 * half), full),
            pltpu.VMEM((deep, LANES + 4 * half), full),
            pltpu.VMEM((2, lines, zs, 2 * deep, LANES + half), low),
            pltpu.VMEM((chunks - 1, 2, lines, zs, 2 * deep, half), low),
            dma,
            dma,
            dma((chunks, zs)),
            dma((chunks, zs)),
            dma((chunks,)),
            dma((chunks,)),
            dma((chunks, 2)),
            dma((chunks, 2)),
            dma((chunks, 4)),
            dma((chunks, 4)),
            dma,
        ],
        compiler_params=pltpu.CompilerParams(
            collective_id=cid, has_side_effects=True, vmem_limit_bytes=60 * 1024 * 1024
        ),
        cost_estimate=pl.CostEstimate(flops=6 * 10**9, bytes_accessed=20 * 10**6, transcendentals=4 * 10**6),
        name="attend_forward",
    )(
        tokens,
        cotangent,
        choice,
        priority.reshape(patches, 1),
        priority.reshape(1, patches),
        projection,
        output_weight,
        router_weight.T,
        vectors,
    )


def gelu_both(z):
    root = 0.7978845608028654
    square = z * z
    slope = jnp.tanh(root * z * (1.0 + 0.044715 * square))
    half = 0.5 * (1.0 + slope)
    act = z * half
    grad = half + 0.5 * z * (1.0 - slope * slope) * (root * (1.0 + 3 * 0.044715 * square))
    return act, grad


def tail_picks(count, right):
    rows = lax.broadcasted_iota(jnp.int32, (count // 2, count), 0)
    ids = lax.broadcasted_iota(jnp.int32, (count // 2, count), 1)
    hit = ids == (rows // 4) * 8 + rows % 4 + (4 if right else 0)
    return hit.astype(jnp.float32).astype(jnp.bfloat16)


class Stages:
    def __init__(self, place, refs):
        (self.grads, self.other, self.give3, self.take3, self.give2, self.take2, self.givez, self.takez, self.total) = refs[:9]
        (self.cs, self.cr, self.s3, self.r3, self.s2, self.r2, self.sz, self.rz) = refs[9:]
        self.p, self.zs, self.core = place, place.zs, place.core
        self.partner = (place.a, place.e + 1 - 2 * place.core)

    def to_partner(self, c):
        return remote(
            self.grads.at[c, 1 - self.core], self.other.at[c], self.cs.at[c], self.cr.at[c], self.partner
        )

    def to_third(self, c):
        return remote(
            self.give3.at[c], self.take3.at[c], self.s3.at[c], self.r3.at[c], self.p.device(self.core, 0, 0, 1)
        )

    def to_second(self, c):
        return remote(
            self.give2.at[c], self.take2.at[c], self.s2.at[c], self.r2.at[c], self.p.device(self.core, 0, 1, 0)
        )

    def along(self, c, dz):
        return remote(
            self.givez.at[c, dz - 1],
            self.takez.at[c, dz - 1],
            self.sz.at[c, dz],
            self.rz.at[c, dz],
            self.p.device(self.core, dz, 0, 0),
        )

    def sum_of(self, c, k, *more):
        at = self.p.chip(self.core, *split_index(k, self.zs))
        total = self.grads[c, self.core, at].astype(jnp.float32) + self.other[c, at].astype(jnp.float32)
        for ref in more:
            total = total + ref[c, k].astype(jnp.float32)
        return total

    def step0(self, c):
        self.to_partner(c).start()

    def step1(self, c):
        self.to_partner(c).wait_recv()
        zs = self.zs
        for k in range(2 * zs, 4 * zs):
            self.give3[c, k - 2 * zs] = self.sum_of(c, k).astype(self.give3.dtype)
        self.to_third(c).start()

    def step2(self, c):
        self.to_third(c).wait_recv()
        zs = self.zs
        for k in range(zs, 2 * zs):
            self.give2[c, k - zs] = self.sum_of(c, k, self.take3).astype(self.give2.dtype)
        self.to_second(c).start()

    def step3(self, c):
        self.to_second(c).wait_recv()
        for dz in range(1, self.zs):
            self.givez[c, dz - 1] = self.sum_of(c, dz, self.take3, self.take2).astype(self.givez.dtype)
            self.along(c, dz).start()

    def step4(self, c):
        total = self.sum_of(c, 0, self.take3, self.take2)
        for dz in range(1, self.zs):
            self.along(c, dz).wait_recv()
            total = total + self.takez[c, dz - 1].astype(jnp.float32)
        self.total[c] = total

    def finish(self, count):
        for c in range(count):
            self.to_partner(c).wait_send()
            self.to_third(c).wait_send()
            self.to_second(c).wait_send()
            for dz in range(1, self.zs):
                self.along(c, dz).wait_send()


def stage_scratch(chunks, chips, rows, columns):
    low = jnp.bfloat16
    zs = chips // 4
    shapes = [
        (chunks, 2, chips, rows, columns),
        (chunks, chips, rows, columns),
        (chunks, 2 * zs, rows, columns),
        (chunks, 2 * zs, rows, columns),
        (chunks, zs, rows, columns),
        (chunks, zs, rows, columns),
        (chunks, zs - 1, rows, columns),
        (chunks, zs - 1, rows, columns),
    ]
    sems = [pltpu.SemaphoreType.DMA((chunks,)) for _ in range(6)]
    sems += [pltpu.SemaphoreType.DMA((chunks, zs)) for _ in range(2)]
    return [pltpu.VMEM(s, low) for s in shapes] + [pltpu.VMEM((chunks, rows, columns), jnp.float32)] + sems


STAGE_REFS = 17


def backward_kernel(
    dp,
    experts,
    capacity,
    chunk,
    tok_ref,
    cot_ref,
    choice_ref,
    ret_ref,
    aux_ref,
    probs_ref,
    mid_ref,
    part_ref,
    back_any,
    second_any,
    ctx_any,
    stat_any,
    qkv_any,
    weights_any,
    out_ref,
    input_ref,
    dense_ref,
    total_ref,
    back_ref,
    second_ref,
    ctx_ref,
    stat_ref,
    qkv_ref,
    weights,
    vec,
    stacked,
    normed_turned,
    branch,
    dctx,
    joined,
    turned_query,
    dmid,
    work,
    sums,
    load,
    row,
    row_tail,
    tiles,
    row_send,
    row_recv,
    tile_send,
    tile_recv,
    *stage_refs,
):
    low, full32 = jnp.bfloat16, jnp.float32
    patches, width = tok_ref.shape
    trio_width = 3 * LANES
    p = Place(dp, experts)
    world = dp * experts
    me = p.flat((p.a, p.e))
    main, last = Stages(p, stage_refs[:STAGE_REFS]), Stages(p, stage_refs[STAGE_REFS:])
    chips, shard2 = main.grads.shape[2:4]
    pieces = [
        (back_any, back_ref),
        (weights_any, weights),
        (ctx_any, ctx_ref),
        (second_any, second_ref),
        (stat_any, stat_ref),
        (qkv_any, qkv_ref),
    ]
    fetch = [pltpu.make_async_copy(s, d, load.at[i]) for i, (s, d) in enumerate(pieces)]
    for copy in fetch:
        copy.start()
    barrier = pltpu.get_barrier_semaphore()

    def other_device(j):
        at = lax.rem(me + j, world)
        return lax.div(at, experts), lax.rem(at, experts)

    @pl.loop(1, world)
    def _(j):
        pl.semaphore_signal(barrier, inc=1, device_id=other_device(j), device_id_type=MESH)

    full = capacity // 8
    half = width // 2
    lanes = lane_ids(patches)
    aux = aux_ref[...]
    slots = [aux[:, i : i + 1] for i in range(4)]
    gates = [aux[:, 4 + i : 5 + i] for i in range(2)]
    ids = lax.broadcasted_iota(jnp.int32, (patches, full * LANES), 1).astype(full32)
    tail_ids = lane_ids(patches, full * LANES).astype(full32)
    hits = [ids == slots[0], ids == slots[1]]
    lefts = [tail_ids == slots[0], tail_ids == slots[1]]
    rights = [tail_ids == slots[2], tail_ids == slots[3]]

    def mix(marks):
        return (jnp.where(marks[0], gates[0], 0.0) + jnp.where(marks[1], gates[1], 0.0)).astype(low)

    def pick(marks):
        return (marks[0] | marks[1]).astype(full32).astype(low)

    for i in range(full):
        stacked[pl.ds(i * LANES, LANES), :] = ret_ref[:, pl.ds(i * width, width)]
    tail = ret_ref[:, pl.ds(full * width, half)]
    left_mix, right_mix = nn(mix(lefts), tail), nn(mix(rights), tail)
    final = nn(mix(hits), stacked[...])
    out_ref[:, :half] = (mid_ref[:, :half] + (final[:, :half] + left_mix)).astype(low)
    out_ref[:, half:] = (mid_ref[:, half:] + (final[:, half:] + right_mix)).astype(low)
    along = nt(cot_ref[...], stacked[...])
    along_left, along_right = nt(cot_ref[:, :half], tail), nt(cot_ref[:, half:], tail)
    dprobs = jnp.zeros((patches, LANES), full32)
    for j in range(2):
        dgate = jnp.sum(jnp.where(hits[j], along, 0.0), axis=1, keepdims=True) + jnp.sum(
            jnp.where(lefts[j], along_left, 0.0) + jnp.where(rights[j], along_right, 0.0), axis=1, keepdims=True
        )
        dprobs = dprobs + jnp.where(lanes == choice_ref[:, j : j + 1], dgate, 0.0)
    probs = probs_ref[...]
    dlogits = (probs * (dprobs - jnp.sum(probs * dprobs, axis=1, keepdims=True))).astype(low)
    fetch[0].wait()
    for i in range(full):
        stacked[pl.ds(i * LANES, LANES), :] = back_ref[:, pl.ds(i * width, width)]
    tail = back_ref[:, pl.ds(full * width, half)]
    fetch[1].wait()
    vec[...] = vector_table(weights, width)

    def vector(i):
        return vec[experts + i : experts + i + 1, :]

    routed = weights[:, 4 * width :]
    work[...] = nn(pick(hits), stacked[...]) + nt(dlogits, routed)
    work[:, :half] = work[:, :half] + nn(pick(lefts), tail)
    work[:, half:] = work[:, half:] + nn(pick(rights), tail)
    sums[...] = jnp.zeros_like(sums)

    def column_sum(slot, values):
        sums[pl.ds(8 * slot, 8), :] = sums[pl.ds(8 * slot, 8), :] + jnp.sum(
            values.reshape(-1, 8, values.shape[-1]), axis=0
        )

    def norm_back(grad, unit, inverse, gain):
        weighted = grad * gain
        return inverse * (
            weighted
            - jnp.mean(weighted, axis=-1, keepdims=True)
            - unit * jnp.mean(weighted * unit, axis=-1, keepdims=True)
        )

    for part in row_parts(patches, chunk):
        unit, inverse = norm_parts(mid_ref[part, :])
        grad = work[part, :]
        column_sum(5, grad * unit)
        column_sum(6, grad)
        total = cot_ref[part, :].astype(full32) + norm_back(grad, unit, inverse, vector(5))
        dmid[part, :] = total
        rounded = total.astype(low)
        branch[part, :] = rounded
        column_sum(4, rounded.astype(full32))
    fetch[2].wait()
    ctx_turned = jnp.transpose(ctx_ref[...])
    for core in range(2):
        columns = pl.ds(core * half, half)
        product = nn(ctx_turned, branch[:, columns])
        main.grads[0, core] = product.reshape(chips, shard2, half).astype(low)
    pl.semaphore_wait(barrier, world - 1)
    main.step0(0)
    third = 256
    for j in range(width // third):
        rows = pl.ds(j * third, third)
        dctx[:, rows] = nt(branch[...], weights[rows, pl.ds(3 * width, width)]).astype(low)
    fetch[3].wait()
    router_rows = nn(jnp.transpose(dlogits.astype(full32)).astype(low), second_ref[...])
    for part in row_parts(patches, chunk):
        unit, _ = norm_parts(tok_ref[part, :].astype(full32))
        second_ref[part, :] = (unit * vector(0) + vector(1)).astype(low)
    normed_turned[...] = jnp.transpose(second_ref[...])
    heads = (
        lax.broadcasted_iota(jnp.int32, (16, width), 1) // HEAD_DIM == lax.broadcasted_iota(jnp.int32, (16, width), 0)
    ).astype(full32).astype(low)
    product = dctx[...].astype(full32) * ctx_ref[...].astype(full32)
    upper = product.astype(low)
    center = nt(heads, upper) + nt(heads, (product - upper.astype(full32)).astype(low))
    fetch[4].wait()
    logs = jnp.transpose(stat_ref[...])
    work[0:32, :patches] = jnp.concatenate([logs[:16], center], axis=0)
    fetch[5].wait()

    def attend(pair, c, core):
        at = pl.multiple_of(pair * LANES, LANES)
        trio = pl.multiple_of(pair * trio_width, LANES)
        key_at = pl.ds(pl.multiple_of(trio + LANES, LANES), LANES)
        value_at = pl.ds(pl.multiple_of(trio + 2 * LANES, LANES), LANES)
        scale = jnp.asarray(HEAD_DIM**-0.5, low)
        queries = qkv_ref[:, pl.ds(trio, LANES)] * scale
        given = dctx[:, pl.ds(at, LANES)]
        own = lane_ids(patches)
        zero = jnp.zeros_like(queries)
        marks = [own < HEAD_DIM, own >= HEAD_DIM]
        head_queries = [jnp.where(m, queries, zero) for m in marks]
        head_given = [jnp.where(m, given, zero) for m in marks]
        turned_keys = jnp.transpose(qkv_ref[:, key_at] * scale)
        query_parts = [None, None]
        for part in row_parts(patches, chunk):
            keys = qkv_ref[part, key_at]
            values = qkv_ref[part, value_at]
            value_out, key_out = [], []
            for head in range(2):
                log_row = work[pl.ds(2 * pair + head, 1), :patches]
                center_row = work[pl.ds(16 + 2 * pair + head, 1), :patches]
                prob = jnp.exp(nt(keys, head_queries[head]) - log_row)
                value_out.append(nn(prob.astype(low), given))
                dscore = (prob * (nt(values, head_given[head]) - center_row)).astype(low)
                key_out.append(nn(dscore, queries))
                head_keys = turned_keys[HEAD_DIM * head : HEAD_DIM * (head + 1), part.start : part.start + part.size]
                piece = nn(head_keys, dscore)
                query_parts[head] = piece if query_parts[head] is None else query_parts[head] + piece
            side = lane_ids(chunk) < HEAD_DIM
            joined[part, key_at] = jnp.where(side, key_out[0], key_out[1]).astype(low)
            joined[part, value_at] = jnp.where(side, value_out[0], value_out[1]).astype(low)
        turned_query[...] = jnp.concatenate(query_parts, axis=0)
        joined[:, pl.ds(trio, LANES)] = jnp.transpose(turned_query[...]).astype(low)
        product = nn(normed_turned[...], joined[:, pl.ds(trio, trio_width)])
        main.grads[c, core] = product.reshape(chips, shard2, trio_width).astype(low)

    pair_chunks = width // LANES // 2

    for i in range(pair_chunks):
        attend(2 * i, i + 1, 0)
        main.step1(i)
        if i >= 1:
            main.step3(i - 1)
        attend(2 * i + 1, i + 1, 1)
        main.step0(i + 1)
        main.step2(i)
        if i >= 1:
            main.step4(i - 1)

    end = pair_chunks
    ones = jnp.ones((8, patches), low)
    for j in range(width // LANES):
        column_parts = nn(ones, joined[:, pl.ds(j * trio_width, trio_width)])
        sums[16:17, pl.ds(j * LANES, LANES)] = column_parts[0:1, :LANES]
        sums[24:25, pl.ds(j * LANES, LANES)] = column_parts[0:1, 2 * LANES :]
    for j in range(width // third):
        rows = pl.ds(j * third, third)
        work[:, rows] = nt(joined[...], weights[rows, : 3 * width])
        if j == 0:
            main.step1(end)
            main.step3(end - 1)
    main.step2(end)
    main.step4(end - 1)
    parts = row_parts(patches, chunk)
    for part in parts:
        unit, inverse = norm_parts(tok_ref[part, :].astype(full32))
        grad = work[part, :]
        column_sum(0, grad * unit)
        column_sum(1, grad)
        input_ref[part, :] = dmid[part, :] + norm_back(grad, unit, inverse, vector(0))
    vec[...] = router_rows
    for i in range(7):
        vec[experts + i : experts + i + 1, :] = jnp.sum(sums[pl.ds(8 * i, 8), :], axis=0, keepdims=True)
    last.grads[0, 0] = jnp.transpose(vec[...]).reshape(chips, shard2, LANES).astype(low)
    last.grads[0, 1] = jnp.zeros((chips, shard2, LANES), low)
    last.step0(0)
    main.step3(end)
    last.step1(0)
    last.step2(0)
    main.step4(end)
    last.step3(0)
    last.step4(0)
    deep = shard2 // 2
    his = pl.ds(pl.multiple_of((1 - p.core) * deep, 8), deep)
    mine = pl.ds(pl.multiple_of(p.core * deep, 8), deep)
    rows_copy = [
        remote(main.total.at[:, his], row, row_send.at[0], row_recv.at[0], main.partner),
        remote(last.total.at[:, his], row_tail, row_send.at[1], row_recv.at[1], main.partner),
    ]
    for copy in rows_copy:
        copy.start()
    square = part_ref[...]
    for stage, count in ((main, end + 1), (last, 1)):
        for c in range(count):
            values = stage.total[c]
            folded = jnp.sum((values * values).reshape(-1, 8, values.shape[1]), axis=0)
            for j in range(values.shape[1] // LANES):
                square = square + folded[:, j * LANES : (j + 1) * LANES]
    tiles[me] = square

    def tile_copy(j):
        return remote(tiles.at[me], tiles.at[me], tile_send.at[j], tile_recv.at[j], other_device(j))

    @pl.loop(1, world)
    def _(j):
        tile_copy(j).start()

    def put(core, values, tail_values):
        for c in range(end + 1):
            dense_ref[:, pl.ds(pl.multiple_of(c * width + core * half, LANES), half)] = values(c)
        dense_ref[:, pl.ds(pl.multiple_of(4 * width + core * LANES, LANES), LANES)] = tail_values

    put(p.core, lambda c: main.total[c, mine, :], last.total[0, mine, :])
    for copy in rows_copy:
        copy.wait_recv()
    put(1 - p.core, lambda c: row[c], row_tail[0])

    @pl.loop(1, world)
    def _(j):
        block = tiles.at[lax.rem(me + world - j, world)]
        remote(block, block, tile_send.at[j], tile_recv.at[j], main.partner).wait_recv()

    total = tiles[0]
    for j in range(1, world):
        total = total + tiles[j]
    total_ref[...] = total
    main.finish(end + 1)
    last.finish(1)
    for copy in rows_copy:
        copy.wait_send()

    @pl.loop(1, world)
    def _(j):
        tile_copy(j).wait_send()


def backward(
    tokens,
    cotangent,
    choice,
    ret,
    back,
    aux,
    probs,
    mid,
    second,
    ctx,
    stat,
    qkv,
    weights,
    part,
    dp,
    experts,
    capacity,
    cid,
    chunk=576,
):
    patches, width = tokens.shape
    low, full = jnp.bfloat16, jnp.float32
    world = dp * experts
    chips, rows = world // 2, 2 * width // world
    chunks = width // LANES // 2 + 1
    columns = 4 * width + 2 * LANES
    return pl.pallas_call(
        functools.partial(backward_kernel, dp, experts, capacity, chunk),
        out_shape=[
            jax.ShapeDtypeStruct((patches, width), low),
            jax.ShapeDtypeStruct((patches, width), full),
            jax.ShapeDtypeStruct((rows // 2, columns), full),
            jax.ShapeDtypeStruct((8, LANES), full),
        ],
        in_specs=[VMEM] * 8 + [ANY] * 6,
        out_specs=[VMEM] * 4,
        scratch_shapes=[
            pltpu.VMEM(back.shape, low),
            pltpu.VMEM((patches, width), low),
            pltpu.VMEM((patches, width), low),
            pltpu.VMEM(stat.shape, full),
            pltpu.VMEM(qkv.shape, low),
            pltpu.VMEM(weights.shape, low),
            pltpu.VMEM((LANES, width), full),
            pltpu.VMEM((capacity // 8 * LANES, width), low),
            pltpu.VMEM((width, patches), low),
            pltpu.VMEM((patches, width), low),
            pltpu.VMEM((patches, width), low),
            pltpu.VMEM((patches, 3 * width), low),
            pltpu.VMEM((LANES, patches), full),
            pltpu.VMEM((patches, width), full),
            pltpu.VMEM((patches, width), full),
            pltpu.VMEM((56, width), full),
            pltpu.SemaphoreType.DMA((6,)),
            pltpu.VMEM((chunks, rows // 2, width // 2), full),
            pltpu.VMEM((1, rows // 2, LANES), full),
            pltpu.VMEM((world, 8, LANES), full),
            pltpu.SemaphoreType.DMA((2,)),
            pltpu.SemaphoreType.DMA((2,)),
            pltpu.SemaphoreType.DMA((world,)),
            pltpu.SemaphoreType.DMA((world,)),
            *stage_scratch(chunks, chips, rows, width // 2),
            *stage_scratch(1, chips, rows, LANES),
        ],
        compiler_params=pltpu.CompilerParams(
            collective_id=cid, has_side_effects=True, vmem_limit_bytes=60 * 1024 * 1024
        ),
        cost_estimate=pl.CostEstimate(flops=15 * 10**9, bytes_accessed=30 * 10**6, transcendentals=4 * 10**6),
        name="attend_backward",
    )(tokens, cotangent, choice, ret, aux, probs, mid, part, back, second, ctx, stat, qkv, weights)


def moe_kernel(
    dp,
    experts,
    chunk,
    rows_any,
    dy_any,
    inner_any,
    hidden_ref,
    outer_any,
    return_ref,
    y_any,
    drows_any,
    dinner_any,
    dhidden_ref,
    douter_any,
    dreturn_ref,
    square_ref,
    rows_all,
    dy_all,
    y_pack,
    drows_pack,
    y_theirs,
    drows_theirs,
    rows,
    turned,
    dy,
    inner,
    outer,
    act,
    grad,
    dz,
    acc,
    inner_stage,
    outer_stage,
    dinner_stage,
    douter_stage,
    square,
    own_sem,
    in_send,
    in_recv,
    over_send,
    over_recv,
    part_send,
    part_recv,
    out_send,
    out_recv,
    stage_sem,
    store_sem,
):
    low, full32 = jnp.bfloat16, jnp.float32
    width = rows.shape[1]
    count = dp * experts * 8
    half = width // 2
    full = rows_all.shape[3] // width
    steps = inner.shape[1] // chunk
    each = -(-(experts - 1) // (steps - 1))
    a = lax.axis_index("dp")
    e = lax.axis_index("expert")
    across = (1 - a, e)
    ins, alls = (rows_any, dy_any), (rows_all, dy_all)
    packs, theirs, outs = (y_pack, drows_pack), (y_theirs, drows_theirs), (y_any, drows_any)

    def to(j):
        return lax.rem(e + j, experts)

    def source(j):
        return lax.rem(e + experts - j, experts)

    def stage(k, slot):
        columns = pl.ds(pl.multiple_of(k * chunk, chunk), chunk)
        return (
            pltpu.make_async_copy(inner_any.at[0, :, columns], inner_stage.at[slot], stage_sem.at[0, slot]),
            pltpu.make_async_copy(outer_any.at[0, columns, :], outer_stage.at[slot], stage_sem.at[1, slot]),
        )

    def own_block(i):
        return pltpu.make_async_copy(ins[i].at[e], alls[i].at[a, e], own_sem.at[i])

    for slot in range(2):
        for copy in stage(slot, slot):
            copy.start()
    for i in range(2):
        own_block(i).start()
    greet([(a, to(j)) for j in range(1, experts)] + [across])

    def first_send(i, j):
        return remote(ins[i].at[to(j)], alls[i].at[a, e], in_send.at[i, j], in_recv.at[i, j], (a, to(j)))

    def forward_own(i):
        return remote(ins[i].at[e], alls[i].at[a, e], over_send.at[i, 0], over_recv.at[i, 0], across)

    def pass_on(i, j):
        block = alls[i].at[a, source(j)]
        return remote(block, block, over_send.at[i, j], over_recv.at[i, j], across)

    def received(i, j):
        block = alls[i].at[a, source(j)]
        return remote(block, block, in_send.at[i, j], in_recv.at[i, j], across)

    def from_across(i, j):
        block = alls[i].at[1 - a, source(j)]
        return remote(block, block, over_send.at[i, j], over_recv.at[i, j], across)

    def part_copy(i, j):
        return remote(
            packs[i].at[1 - a, to(j)], theirs[i].at[j], part_send.at[i, j], part_recv.at[i, j], across
        )

    def result_copy(i, j):
        return remote(packs[i].at[a, to(j)], outs[i].at[e], out_send.at[i, j], out_recv.at[i, j], (a, to(j)))

    for i in range(2):
        forward_own(i).start()

        @pl.loop(1, experts)
        def _(j):
            first_send(i, j).start()

    def take_in(i, k):
        @pl.when(k < steps - 1)
        def _():
            @pl.loop(0, each)
            def _(d):
                j = 1 + k * each + d

                @pl.when(j < experts)
                def _():
                    received(i, j).wait_recv()
                    pass_on(i, j).start()

    def hand_out(i, k):
        @pl.when(k < steps - 1)
        def _():
            @pl.loop(0, each)
            def _(d):
                j = 1 + k * each + d

                @pl.when(j < experts)
                def _():
                    part_copy(i, j).wait_recv()
                    at = to(j)
                    packs[i][a, at] = (packs[i][a, at].astype(full32) + theirs[i][j].astype(full32)).astype(low)
                    result_copy(i, j).start()

    @pl.loop(0, steps)
    def _(k):
        slot = lax.rem(k, 2)
        columns = pl.ds(pl.multiple_of(k * chunk, chunk), chunk)
        for copy in stage(k, slot):
            copy.wait()
        inner[:, columns] = inner_stage[slot].astype(low)
        outer[columns, :] = outer_stage[slot].astype(low)

        @pl.when(k + 2 < steps)
        def _():
            for copy in stage(k + 2, slot):
                copy.start()

        take_in(0, k)

    def unpack(i, place):
        own_block(i).wait()

        @pl.loop(0, experts)
        def _(j):
            from_across(i, j).wait_recv()

        group = 8
        for plane in range(dp):
            for s in range(0, experts, group):
                base = (plane * experts + s) * 8
                for b in range(full):
                    piece = alls[i][plane, s : s + group, :, b * width : (b + 1) * width].astype(full32)
                    place[pl.ds(b * count + base, 8 * group), :] = piece.reshape(8 * group, width).astype(low)
        tails = [
            alls[i][plane, :, :, full * width :].astype(full32).reshape(experts * 8, half) for plane in range(dp)
        ]
        tail = jnp.concatenate(tails, axis=0).astype(low)
        for right in range(2):
            place[pl.ds(full * count, count // 2), pl.ds(right * half, half)] = nn(
                tail_picks(count, right), tail
            ).astype(low)

    def pack(i):
        group = 8
        for plane in range(dp):
            for s in range(0, experts, group):
                base = (plane * experts + s) * 8
                for b in range(full):
                    piece = acc[pl.ds(b * count + base, 8 * group), :].reshape(group, 8, width)
                    packs[i][plane, s : s + group, :, b * width : (b + 1) * width] = piece.astype(low)
        tail = acc[pl.ds(full * count, count // 2), :].astype(low)
        spread = None
        for right in range(2):
            piece = lax.dot_general(
                tail_picks(count, right),
                tail[:, right * half : (right + 1) * half],
                (((0,), (0,)), ((), ())),
                preferred_element_type=full32,
            )
            spread = piece if spread is None else spread + piece
        for plane in range(dp):
            piece = spread[plane * experts * 8 : (plane + 1) * experts * 8].reshape(experts, 8, half)
            packs[i][plane, :, :, full * width :] = piece.astype(low)

        @pl.loop(0, experts)
        def _(d):
            part_copy(i, lax.rem(d + 1, experts)).start()

    unpack(0, rows)
    turned[...] = jnp.transpose(rows[...])
    acc[...] = jnp.zeros_like(acc)

    @pl.loop(0, steps)
    def _(k):
        columns = pl.ds(pl.multiple_of(k * chunk, chunk), chunk)
        z = nn(rows[...], inner[:, columns]) + hidden_ref[:, columns].astype(low).astype(full32)
        value, slope = gelu_both(z)
        act[:, columns] = value.astype(low)
        grad[:, columns] = slope
        acc[...] += nn(act[:, columns], outer[columns, :])
        take_in(1, k)

    part = return_ref.shape[1]
    bias = return_ref[...].astype(low).astype(full32)
    for i in range(dp):
        columns = pl.ds(i * part, part)
        acc[:, columns] = acc[:, columns] + jnp.where(a == i, bias, 0.0)
    pack(0)
    unpack(1, dy)
    total = jnp.zeros((1, width), full32)
    for i in range(rows.shape[0] // LANES):
        total = total + jnp.sum(dy[pl.ds(i * LANES, LANES), :].astype(full32), axis=0, keepdims=True)
    picked = total[:, :part]
    for i in range(1, dp):
        picked = jnp.where(a == i, total[:, i * part : (i + 1) * part], picked)
    dreturn_ref[...] = picked
    square[...] = jnp.zeros_like(square)
    flat = picked * picked
    for i in range(part // LANES):
        square[0:1, :] = square[0:1, :] + flat[:, i * LANES : (i + 1) * LANES]
    acc[...] = jnp.zeros_like(acc)

    @pl.loop(0, steps)
    def _(k):
        columns = pl.ds(pl.multiple_of(k * chunk, chunk), chunk)
        dz[:, columns] = (nt(dy[...], outer[columns, :]) * grad[:, columns]).astype(low)
        acc[...] += nt(dz[:, columns], inner[:, columns])
        hand_out(0, k)

    pack(1)

    def finish(i):
        part_copy(i, 0).wait_recv()
        packs[i][a, e] = (packs[i][a, e].astype(full32) + theirs[i][0].astype(full32)).astype(low)
        pltpu.make_async_copy(packs[i].at[a, e], outs[i].at[e], own_sem.at[i]).start()

    def store(k, slot):
        columns = pl.ds(pl.multiple_of(k * chunk, chunk), chunk)
        return (
            pltpu.make_async_copy(dinner_stage.at[slot], dinner_any.at[0, :, columns], store_sem.at[0, slot]),
            pltpu.make_async_copy(douter_stage.at[slot], douter_any.at[0, columns, :], store_sem.at[1, slot]),
        )

    finish(0)

    @pl.loop(0, steps)
    def _(k):
        slot = lax.rem(k, 2)
        columns = pl.ds(pl.multiple_of(k * chunk, chunk), chunk)
        douter = nn(jnp.transpose(act[:, columns]), dy[...])
        dinner = nn(turned[...], dz[:, columns])
        dhidden = jnp.sum(dz[:, columns].astype(full32), axis=0, keepdims=True)

        @pl.when(k >= 2)
        def _():
            for copy in store(k - 2, slot):
                copy.wait()

        douter_stage[slot] = douter.astype(low)
        dinner_stage[slot] = dinner.astype(low)
        for copy in store(k, slot):
            copy.start()
        dhidden_ref[:, columns] = dhidden
        parts = jnp.zeros((8, LANES), full32)
        folded = jnp.sum((douter * douter).reshape(-1, 8, width), axis=0)
        for i in range(width // LANES):
            parts = parts + folded[:, i * LANES : (i + 1) * LANES]
        folded = jnp.sum((dinner * dinner).reshape(-1, 8, chunk), axis=0)
        hidden_square = dhidden * dhidden
        for i in range(chunk // LANES):
            parts = parts + folded[:, i * LANES : (i + 1) * LANES]
            square[0:1, :] = square[0:1, :] + hidden_square[:, i * LANES : (i + 1) * LANES]
        square[...] += parts
        hand_out(1, k)

    finish(1)
    square_ref[...] = square[...]
    for k in range(steps - 2, steps):
        for copy in store(k, k % 2):
            copy.wait()
    for i in range(2):

        @pl.loop(1, experts)
        def _(j):
            block = outs[i].at[source(j)]
            remote(block, block, out_send.at[i, j], out_recv.at[i, j], across).wait_recv()

    for i in range(2):
        pltpu.make_async_copy(packs[i].at[a, e], outs[i].at[e], own_sem.at[i]).wait()
        forward_own(i).wait_send()
        part_copy(i, 0).wait_send()

        @pl.loop(1, experts)
        def _(j):
            first_send(i, j).wait_send()
            pass_on(i, j).wait_send()
            part_copy(i, j).wait_send()
            result_copy(i, j).wait_send()


def mixture(rows, dy, inner, hidden, outer, back, dp, cid, chunk=256):
    experts, _, packed = rows.shape
    width, units = inner.shape[1:]
    count = dp * experts * 8
    total = count * packed // width
    low, full = jnp.bfloat16, jnp.float32
    both = (dp, experts, 8, packed)
    sems = [pltpu.SemaphoreType.DMA((2, experts)) for _ in range(8)]
    return pl.pallas_call(
        functools.partial(moe_kernel, dp, experts, chunk),
        out_shape=[
            jax.ShapeDtypeStruct(rows.shape, low),
            jax.ShapeDtypeStruct(rows.shape, low),
            jax.ShapeDtypeStruct(inner.shape, low),
            jax.ShapeDtypeStruct(hidden.shape, full),
            jax.ShapeDtypeStruct(outer.shape, low),
            jax.ShapeDtypeStruct(back.shape, full),
            jax.ShapeDtypeStruct((8, LANES), full),
        ],
        in_specs=[ANY, ANY, ANY, VMEM, ANY, VMEM],
        out_specs=[ANY, ANY, ANY, VMEM, ANY, VMEM, VMEM],
        scratch_shapes=[
            pltpu.VMEM(both, low),
            pltpu.VMEM(both, low),
            pltpu.VMEM(both, low),
            pltpu.VMEM(both, low),
            pltpu.VMEM(both[1:], low),
            pltpu.VMEM(both[1:], low),
            pltpu.VMEM((total, width), low),
            pltpu.VMEM((width, total), low),
            pltpu.VMEM((total, width), low),
            pltpu.VMEM((width, units), low),
            pltpu.VMEM((units, width), low),
            pltpu.VMEM((total, units), low),
            pltpu.VMEM((total, units), full),
            pltpu.VMEM((total, units), low),
            pltpu.VMEM((total, width), full),
            pltpu.VMEM((2, width, chunk), full),
            pltpu.VMEM((2, chunk, width), full),
            pltpu.VMEM((2, width, chunk), low),
            pltpu.VMEM((2, chunk, width), low),
            pltpu.VMEM((8, LANES), full),
            pltpu.SemaphoreType.DMA((2,)),
            *sems,
            pltpu.SemaphoreType.DMA((2, 2)),
            pltpu.SemaphoreType.DMA((2, 2)),
        ],
        compiler_params=pltpu.CompilerParams(
            collective_id=cid, has_side_effects=True, vmem_limit_bytes=60 * 1024 * 1024
        ),
        cost_estimate=pl.CostEstimate(flops=17 * 10**9, bytes_accessed=25 * 10**6, transcendentals=2 * 10**6),
        name="mixture",
    )(rows, dy, inner, hidden, outer, back)


def adam_values(weight, first, second, gradient, clip, rate, decay):
    scaled = gradient * clip
    first_new = BETA_ONE * first + (1.0 - BETA_ONE) * scaled
    second_new = BETA_TWO * second + (1.0 - BETA_TWO) * scaled * scaled
    first_hat = first_new * (1.0 / (1.0 - BETA_ONE**STEP))
    second_hat = second_new * (1.0 / (1.0 - BETA_TWO**STEP))
    weight_new = weight - rate * (first_hat / (jnp.sqrt(second_hat) + ADAM_EPS) + decay * weight)
    return weight_new, first_new, second_new


def adam_kernel(experts, norm_ref, dense_ref, *refs):
    ins, outs = refs[:28], refs[28:]
    total = jnp.sum(jnp.sum(norm_ref[...], axis=0, keepdims=True), axis=1, keepdims=True)
    norm = jnp.sqrt(total)
    clip = THRESHOLD / jnp.maximum(norm, THRESHOLD)

    def update(i, grad, rate, decay, columns=slice(None)):
        weight, first, second = (ref[:, columns] for ref in ins[3 * i : 3 * i + 3])
        new = adam_values(weight, first, second, grad, clip, rate, decay)
        for place, value in zip(outs[3 * i : 3 * i + 3], new):
            place[:, columns] = value

    inner_grad, outer_grad, hidden_grad, return_grad = ins[24:28]
    update(0, inner_grad[...].astype(jnp.float32), RATE_INNER, DECAY)
    update(1, outer_grad[...].astype(jnp.float32), RATE_OUTER, DECAY)

    @pl.when(pl.program_id(0) == 0)
    def _():
        outs[24][...] = norm
        width = ins[9].shape[1]
        trio = 3 * LANES
        for pair in range(width // LANES):
            for kind in range(3):
                update(
                    2,
                    dense_ref[:, width + pair * trio + kind * LANES : width + pair * trio + (kind + 1) * LANES],
                    RATE_PROJECTION,
                    DECAY,
                    slice(kind * width + pair * LANES, kind * width + (pair + 1) * LANES),
                )
        update(3, dense_ref[:, :width], RATE_OUTPUT, DECAY)
        turned = jnp.transpose(dense_ref[:, 4 * width : 4 * width + LANES])
        update(4, turned[:experts], RATE_ROUTER, DECAY)
        update(5, turned[experts : experts + 7], RATE_VECTORS, 0.0)
        update(6, hidden_grad[...], RATE_HIDDEN, 0.0)
        update(7, return_grad[...], RATE_RETURN, 0.0)


def adam_all(experts, squares, dense, states, grads, steps=8):
    operands, in_specs, out_specs, shapes = [squares, dense], [], [], []

    def spec_of(array, blocks):
        shape = array.shape
        if blocks:
            return pl.BlockSpec((shape[0] // steps, shape[1]), lambda i: (i, 0))
        return pl.BlockSpec(shape, lambda i: (0, 0))

    in_specs += [spec_of(squares, False), spec_of(dense, False)]
    for g, group in enumerate(states):
        spec = spec_of(group[0], g < 2)
        in_specs += [spec] * 3
        out_specs += [spec] * 3
        shapes += [jax.ShapeDtypeStruct(group[0].shape, jnp.float32)] * 3
        operands += list(group)
    for g, grad in enumerate(grads):
        in_specs.append(spec_of(grad, g < 2))
        operands.append(grad)
    out = pl.pallas_call(
        functools.partial(adam_kernel, experts),
        grid=(steps,),
        out_shape=shapes + [jax.ShapeDtypeStruct((1, 1), jnp.float32)],
        in_specs=in_specs,
        out_specs=out_specs + [pl.BlockSpec((1, 1), lambda i: (0, 0))],
        compiler_params=pltpu.CompilerParams(
            vmem_limit_bytes=60 * 1024 * 1024, dimension_semantics=("arbitrary",)
        ),
        cost_estimate=pl.CostEstimate(flops=5 * 10**7, bytes_accessed=62 * 10**6, transcendentals=10**7),
        name="adam_all",
    )(*operands)
    return [tuple(out[3 * i : 3 * i + 3]) for i in range(len(states))], out[-1].reshape(())


def fits(dp, experts):
    return dp == 2 and experts == 16


def fast_shards(
    dp,
    experts,
    tokens,
    cotangent,
    expert_choice,
    priority,
    projection,
    projection_first,
    projection_second,
    output_weight,
    output_first,
    output_second,
    router_weight,
    router_first,
    router_second,
    vectors,
    vectors_first,
    vectors_second,
    expert_inner,
    inner_first,
    inner_second,
    hidden_bias,
    hidden_first,
    hidden_second,
    expert_outer,
    outer_first,
    outer_second,
    return_bias,
    return_first,
    return_second,
):
    patches = tokens.shape[1]
    capacity = max(2, patches // experts)
    rows, dy, qkv, ctx, mid, second, stat, aux, probs, weights = forward(
        tokens[0],
        cotangent[0],
        expert_choice[0],
        priority[0],
        projection,
        output_weight,
        router_weight,
        vectors,
        dp,
        experts,
        capacity,
        1,
    )
    blocks = (experts, 8, rows.shape[1])
    returned, back_rows, inner_grad, hidden_grad, outer_grad, return_grad, expert_square = mixture(
        rows.reshape(blocks),
        dy.reshape(blocks),
        expert_inner,
        hidden_bias,
        expert_outer,
        return_bias,
        dp,
        2,
    )
    block_output, input_grad, dense, squares = backward(
        tokens[0],
        cotangent[0],
        expert_choice[0],
        returned.reshape(rows.shape),
        back_rows.reshape(rows.shape),
        aux,
        probs,
        mid,
        second,
        ctx,
        stat,
        qkv,
        weights,
        expert_square,
        dp,
        experts,
        capacity,
        4,
    )
    states, grad_norm = adam_all(
        experts,
        squares,
        dense,
        [
            (expert_inner[0], inner_first[0], inner_second[0]),
            (expert_outer[0], outer_first[0], outer_second[0]),
            (projection, projection_first, projection_second),
            (output_weight, output_first, output_second),
            (router_weight.T, router_first.T, router_second.T),
            (vectors, vectors_first, vectors_second),
            (hidden_bias, hidden_first, hidden_second),
            (return_bias, return_first, return_second),
        ],
        [inner_grad[0], outer_grad[0], hidden_grad, return_grad],
    )
    inner_new, outer_new, projection_new, output_new, router_new, vectors_new, hidden_new, return_new = states
    return (
        block_output[None],
        input_grad[None],
        grad_norm,
        *projection_new,
        *output_new,
        *(v.T for v in router_new),
        *vectors_new,
        *(v[None] for v in inner_new),
        *hidden_new,
        *(v[None] for v in outer_new),
        *return_new,
    )


def solution(mesh):
    dp, experts = mesh.shape["dp"], mesh.shape["expert"]
    body = functools.partial(fast_shards, dp, experts) if fits(dp, experts) else shards
    return jax.shard_map(
        body,
        mesh=mesh,
        in_specs=(
            P(("dp", "expert"), None, None),
            P(("dp", "expert"), None, None),
            P(("dp", "expert"), None, None),
            P(("dp", "expert"), None),
            P(("dp", "expert"), None),
            P(("dp", "expert"), None),
            P(("dp", "expert"), None),
            P(("dp", "expert"), None),
            P(("dp", "expert"), None),
            P(("dp", "expert"), None),
            P(("dp", "expert"), None),
            P(("dp", "expert"), None),
            P(("dp", "expert"), None),
            P(None, ("dp", "expert")),
            P(None, ("dp", "expert")),
            P(None, ("dp", "expert")),
            P("expert", None, "dp"),
            P("expert", None, "dp"),
            P("expert", None, "dp"),
            P("expert", "dp"),
            P("expert", "dp"),
            P("expert", "dp"),
            P("expert", "dp", None),
            P("expert", "dp", None),
            P("expert", "dp", None),
            P("expert", "dp"),
            P("expert", "dp"),
            P("expert", "dp"),
        ),
        out_specs=(
            P(("dp", "expert"), None, None),
            P(("dp", "expert"), None, None),
            P(),
            P(("dp", "expert"), None),
            P(("dp", "expert"), None),
            P(("dp", "expert"), None),
            P(("dp", "expert"), None),
            P(("dp", "expert"), None),
            P(("dp", "expert"), None),
            P(("dp", "expert"), None),
            P(("dp", "expert"), None),
            P(("dp", "expert"), None),
            P(None, ("dp", "expert")),
            P(None, ("dp", "expert")),
            P(None, ("dp", "expert")),
            P("expert", None, "dp"),
            P("expert", None, "dp"),
            P("expert", None, "dp"),
            P("expert", "dp"),
            P("expert", "dp"),
            P("expert", "dp"),
            P("expert", "dp", None),
            P("expert", "dp", None),
            P("expert", "dp", None),
            P("expert", "dp"),
            P("expert", "dp"),
            P("expert", "dp"),
        ),
        check_vma=False,
    )
```

```python
import functools

import jax
import jax.numpy as jnp
from jax import lax
from jax.experimental import pallas as pl
from jax.experimental.pallas import tpu as pltpu
from jax.sharding import PartitionSpec as P

HEADS = 12
HEAD_DIM = 64
STEP = 10


NORM_EPS = 1e-06
ADAM_EPS = 1e-08
BETA_ONE = 0.9
BETA_TWO = 0.999
DECAY = 0.1
THRESHOLD = 1.0
RATE_PROJECTION = 0.1
RATE_OUTPUT = 1.0
RATE_ROUTER = 0.05
RATE_VECTORS = 0.5
RATE_INNER = 0.1
RATE_HIDDEN = 0.25
RATE_OUTER = 1.5
RATE_RETURN = 2.0


def layer_norm(values, norm_gain, norm_bias):
    center = values - jnp.mean(values, axis=-1, keepdims=True)
    spread = jnp.mean(center * center, axis=-1, keepdims=True)
    return center * lax.rsqrt(spread + NORM_EPS) * norm_gain + norm_bias


def smooth_gate(values):
    return jax.nn.gelu(values, approximate=True)


def mixed_dot(left, right):
    return jnp.dot(left, right, preferred_element_type=jnp.float32)


def rows_product(left, right):
    return lax.dot_general(
        left, right, (((0,), (0,)), ((), ())), preferred_element_type=jnp.float32
    )


def columns_product(left, right):
    return lax.dot_general(
        left, right, (((1,), (1,)), ((), ())), preferred_element_type=jnp.float32
    )


def assign_slots(chosen, claim_order, expert_count, capacity):
    patches = chosen.shape[0]
    top_count = chosen.shape[1]
    claim_rank = (
        jnp.arange(top_count, dtype=jnp.int32)[None, :] * patches + claim_order[:, None]
    ).T.reshape(-1)
    flat_choice = chosen.T.reshape(-1)
    onehot = (flat_choice[:, None] == jnp.arange(expert_count, dtype=jnp.int32)[None, :]).astype(
        jnp.float32
    )
    earlier = (claim_rank[None, :] < claim_rank[:, None]).astype(jnp.float32)
    counts = jnp.dot(
        earlier, onehot, precision=lax.Precision.HIGHEST, preferred_element_type=jnp.float32
    )
    position = jnp.sum(counts * onehot, axis=1).astype(jnp.int32).reshape(top_count, patches).T
    kept_mask = position < capacity
    flat_slot = chosen * capacity + jnp.minimum(position, capacity - 1)
    return (flat_slot, kept_mask)


def slot_matches(flat_slot, kept_mask, slot_count):
    slot_ids = jnp.arange(slot_count, dtype=jnp.int32)
    return (flat_slot[None, :, :] == slot_ids[:, None, None]) & kept_mask[None, :, :]


def select_gates(logits, chosen, expert_count):
    router_probs = jax.nn.softmax(logits, axis=-1)
    onehot = chosen[:, :, None] == jnp.arange(expert_count, dtype=jnp.int32)[None, None, :]
    return jnp.sum(jnp.where(onehot, router_probs[:, None, :], 0.0), axis=2)


def adam_update(weight, first_state, second, gradient, clip_factor, step_rate, decay_rate):
    scaled = gradient * clip_factor
    first_new = BETA_ONE * first_state + (1.0 - BETA_ONE) * scaled
    second_new = BETA_TWO * second + (1.0 - BETA_TWO) * scaled * scaled
    first_hat = first_new / (1.0 - BETA_ONE**STEP)
    second_hat = second_new / (1.0 - BETA_TWO**STEP)
    weight_new = weight - step_rate * (
        first_hat / (jnp.sqrt(second_hat) + ADAM_EPS) + decay_rate * weight
    )
    return (weight_new, first_new, second_new)


def shards(
    tokens,
    cotangent,
    expert_choice,
    priority,
    projection,
    projection_first,
    projection_second,
    output_weight,
    output_first,
    output_second,
    router_weight,
    router_first,
    router_second,
    vectors,
    vectors_first,
    vectors_second,
    expert_inner,
    inner_first,
    inner_second,
    hidden_bias,
    hidden_first,
    hidden_second,
    expert_outer,
    outer_first,
    outer_second,
    return_bias,
    return_first,
    return_second,
):
    model_width = tokens.shape[2]
    patches = tokens.shape[1]
    experts = lax.axis_size("expert")
    capacity = max(2, patches // experts)
    slot_count = experts * capacity
    score_scale = HEAD_DIM ** (-0.5)
    dense_shards = (
        projection.astype(jnp.bfloat16),
        output_weight.astype(jnp.bfloat16),
        router_weight.astype(jnp.bfloat16),
        vectors.astype(jnp.bfloat16),
    )
    partial_shards = (
        lax.all_gather(dense_shards[0], "expert", axis=0, tiled=True),
        lax.all_gather(dense_shards[1], "expert", axis=0, tiled=True),
        lax.all_gather(dense_shards[2], "expert", axis=0, tiled=True),
        lax.all_gather(dense_shards[3], "expert", axis=1, tiled=True),
    )
    whole_projection, whole_output, whole_router, whole_vectors = (
        lax.all_gather(partial_shards[0], "dp", axis=0, tiled=True),
        lax.all_gather(partial_shards[1], "dp", axis=0, tiled=True),
        lax.all_gather(partial_shards[2], "dp", axis=0, tiled=True),
        lax.all_gather(partial_shards[3], "dp", axis=1, tiled=True),
    )
    inner_low = expert_inner.astype(jnp.bfloat16)
    hidden_low = hidden_bias.astype(jnp.bfloat16)
    outer_low = expert_outer.astype(jnp.bfloat16)
    return_low = return_bias.astype(jnp.bfloat16)
    inner_all, hidden_all, outer_all, return_all = (
        lax.all_gather(inner_low, "dp", axis=2, tiled=True),
        lax.all_gather(hidden_low, "dp", axis=1, tiled=True),
        lax.all_gather(outer_low, "dp", axis=1, tiled=True),
        lax.all_gather(return_low, "dp", axis=1, tiled=True),
    )
    vector_rows = whole_vectors.astype(jnp.float32)
    image_rows = tokens[0].astype(jnp.float32)
    normed_one, norm_back_one = jax.vjp(layer_norm, image_rows, vector_rows[0], vector_rows[1])
    normed_low = normed_one.astype(jnp.bfloat16)
    projected = mixed_dot(normed_low, whole_projection)
    queries = (
        (projected[:, :model_width] + vector_rows[2])
        .astype(jnp.bfloat16)
        .reshape(patches, HEADS, HEAD_DIM)
    )
    key_rows = (
        projected[:, model_width : 2 * model_width]
        .astype(jnp.bfloat16)
        .reshape(patches, HEADS, HEAD_DIM)
    )
    value_rows = (
        (projected[:, 2 * model_width :] + vector_rows[3])
        .astype(jnp.bfloat16)
        .reshape(patches, HEADS, HEAD_DIM)
    )
    scores = (
        jnp.einsum("qhd,khd->hqk", queries, key_rows, preferred_element_type=jnp.float32)
        * score_scale
    )
    score_top = jnp.max(scores, axis=-1, keepdims=True)
    raised = jnp.exp(scores - score_top)
    totals = jnp.sum(raised, axis=-1, keepdims=True)
    attention = raised / totals
    log_total = score_top + jnp.log(totals)
    context = (
        jnp.einsum(
            "hqk,khd->qhd",
            attention.astype(jnp.bfloat16),
            value_rows,
            preferred_element_type=jnp.float32,
        )
        .reshape(patches, model_width)
        .astype(jnp.bfloat16)
    )
    middle = image_rows + (mixed_dot(context, whole_output) + vector_rows[4])
    normed_two, norm_back_two = jax.vjp(layer_norm, middle, vector_rows[5], vector_rows[6])
    second_low = normed_two.astype(jnp.bfloat16)
    logits = mixed_dot(second_low, whole_router)
    chosen = expert_choice[0]

    def gate_choice(values):
        return select_gates(values, chosen, experts)

    gate_values, gate_back = jax.vjp(gate_choice, logits)
    flat_slot, kept_mask = assign_slots(chosen, priority[0], experts, capacity)
    matches = slot_matches(flat_slot, kept_mask, slot_count)
    slot_table = jnp.any(matches, axis=2).astype(jnp.bfloat16)
    dispatched = (
        mixed_dot(slot_table, second_low)
        .astype(jnp.bfloat16)
        .reshape(experts, capacity, model_width)
    )
    arrived = lax.all_to_all(dispatched, "expert", split_axis=0, concat_axis=0, tiled=True).reshape(
        slot_count, model_width
    )
    pre_act = mixed_dot(arrived, inner_all[0]) + hidden_all[0].astype(jnp.float32)
    activated, gelu_back = jax.vjp(smooth_gate, pre_act)
    active_low = activated.astype(jnp.bfloat16)
    expert_out = (mixed_dot(active_low, outer_all[0]) + return_all[0].astype(jnp.float32)).astype(
        jnp.bfloat16
    )
    returned = lax.all_to_all(
        expert_out.reshape(experts, capacity, model_width),
        "expert",
        split_axis=0,
        concat_axis=0,
        tiled=True,
    ).reshape(slot_count, model_width)
    picked = returned[flat_slot].astype(jnp.float32)
    weighted = jnp.where(kept_mask, gate_values, 0.0)
    final = middle + jnp.sum(weighted[:, :, None] * picked, axis=1)
    block_output = final.astype(jnp.bfloat16)[None]
    upstream = cotangent[0].astype(jnp.float32)
    gate_grad = jnp.where(kept_mask, jnp.sum(upstream[:, None, :] * picked, axis=2), 0.0)
    slot_gate = jnp.sum(jnp.where(matches, weighted[None, :, :], 0.0), axis=(1, 2))
    slot_grad = (mixed_dot(slot_table, cotangent[0]) * slot_gate[:, None]).astype(jnp.bfloat16)
    sent_grad = lax.all_to_all(
        slot_grad.reshape(experts, capacity, model_width),
        "expert",
        split_axis=0,
        concat_axis=0,
        tiled=True,
    ).reshape(slot_count, model_width)
    outer_grad = rows_product(active_low, sent_grad)
    return_grad = jnp.sum(sent_grad, axis=0, dtype=jnp.float32)
    active_grad = columns_product(sent_grad, outer_all[0])
    (pre_grad,) = gelu_back(active_grad)
    pre_low = pre_grad.astype(jnp.bfloat16)
    inner_grad = rows_product(arrived, pre_low)
    hidden_grad = jnp.sum(pre_low, axis=0, dtype=jnp.float32)
    row_grad = columns_product(pre_low, inner_all[0]).astype(jnp.bfloat16)
    expert_grads = (
        lax.psum_scatter(
            inner_grad[None].astype(jnp.bfloat16), "dp", scatter_dimension=2, tiled=True
        ).astype(jnp.float32),
        lax.psum_scatter(
            hidden_grad[None].astype(jnp.bfloat16), "dp", scatter_dimension=1, tiled=True
        ).astype(jnp.float32),
        lax.psum_scatter(
            outer_grad[None].astype(jnp.bfloat16), "dp", scatter_dimension=1, tiled=True
        ).astype(jnp.float32),
        lax.psum_scatter(
            return_grad[None].astype(jnp.bfloat16), "dp", scatter_dimension=1, tiled=True
        ).astype(jnp.float32),
    )
    back_rows = lax.all_to_all(
        row_grad.reshape(experts, capacity, model_width),
        "expert",
        split_axis=0,
        concat_axis=0,
        tiled=True,
    ).reshape(slot_count, model_width)
    (logit_grad,) = gate_back(gate_grad)
    logit_low = logit_grad.astype(jnp.bfloat16)
    router_grad = rows_product(second_low, logit_low)
    second_grad = rows_product(slot_table, back_rows) + columns_product(logit_low, whole_router)
    middle_part, gain_two_grad, bias_two_grad = norm_back_two(second_grad)
    middle_grad = upstream + middle_part
    branch_low = middle_grad.astype(jnp.bfloat16)
    output_grad = rows_product(context, branch_low)
    out_bias_grad = jnp.sum(branch_low, axis=0, dtype=jnp.float32)
    context_grad = (
        columns_product(branch_low, whole_output)
        .astype(jnp.bfloat16)
        .reshape(patches, HEADS, HEAD_DIM)
    )
    scores = (
        jnp.einsum("qhd,khd->hqk", queries, key_rows, preferred_element_type=jnp.float32)
        * score_scale
    )
    attention = jnp.exp(scores - log_total)
    attention_grad = jnp.einsum(
        "qhd,khd->hqk", context_grad, value_rows, preferred_element_type=jnp.float32
    )
    value_grad = jnp.einsum(
        "hqk,qhd->khd",
        attention.astype(jnp.bfloat16),
        context_grad,
        preferred_element_type=jnp.float32,
    ).astype(jnp.bfloat16)
    centered = jnp.sum(attention * attention_grad, axis=-1, keepdims=True)
    score_grad = (attention * (attention_grad - centered)).astype(jnp.bfloat16)
    query_grad = (
        (
            jnp.einsum("hqk,khd->qhd", score_grad, key_rows, preferred_element_type=jnp.float32)
            * score_scale
        )
        .astype(jnp.bfloat16)
        .reshape(patches, model_width)
    )
    key_grad = (
        (
            jnp.einsum("hqk,qhd->khd", score_grad, queries, preferred_element_type=jnp.float32)
            * score_scale
        )
        .astype(jnp.bfloat16)
        .reshape(patches, model_width)
    )
    value_flat = value_grad.reshape(patches, model_width)
    joined_grad = jnp.concatenate([query_grad, key_grad, value_flat], axis=1)
    projection_grad = rows_product(normed_low, joined_grad)
    normed_grad = columns_product(joined_grad, whole_projection)
    input_part, gain_one_grad, bias_one_grad = norm_back_one(normed_grad)
    input_grad = (middle_grad + input_part)[None]
    vector_grad = jnp.stack(
        [
            gain_one_grad,
            bias_one_grad,
            jnp.sum(query_grad, axis=0, dtype=jnp.float32),
            jnp.sum(value_flat, axis=0, dtype=jnp.float32),
            out_bias_grad,
            gain_two_grad,
            bias_two_grad,
        ]
    )
    local_grads = (projection_grad, output_grad, router_grad, vector_grad)
    partial_grads = (
        lax.psum_scatter(
            local_grads[0].astype(jnp.bfloat16), "dp", scatter_dimension=0, tiled=True
        ).astype(jnp.float32),
        lax.psum_scatter(
            local_grads[1].astype(jnp.bfloat16), "dp", scatter_dimension=0, tiled=True
        ).astype(jnp.float32),
        lax.psum_scatter(
            local_grads[2].astype(jnp.bfloat16), "dp", scatter_dimension=0, tiled=True
        ).astype(jnp.float32),
        lax.psum_scatter(
            local_grads[3].astype(jnp.bfloat16), "dp", scatter_dimension=1, tiled=True
        ).astype(jnp.float32),
    )
    dense_grads = (
        lax.psum_scatter(
            partial_grads[0].astype(jnp.bfloat16), "expert", scatter_dimension=0, tiled=True
        ).astype(jnp.float32),
        lax.psum_scatter(
            partial_grads[1].astype(jnp.bfloat16), "expert", scatter_dimension=0, tiled=True
        ).astype(jnp.float32),
        lax.psum_scatter(
            partial_grads[2].astype(jnp.bfloat16), "expert", scatter_dimension=0, tiled=True
        ).astype(jnp.float32),
        lax.psum_scatter(
            partial_grads[3].astype(jnp.bfloat16), "expert", scatter_dimension=1, tiled=True
        ).astype(jnp.float32),
    )
    all_grads = tuple(dense_grads) + tuple(expert_grads)
    local_square = jnp.sum(all_grads[0] * all_grads[0])
    for gradient in all_grads[1:]:
        local_square = local_square + jnp.sum(gradient * gradient)
    square_total = lax.psum(local_square, ("dp", "expert"))
    grad_norm = jnp.sqrt(square_total)
    clip_factor = THRESHOLD / jnp.maximum(grad_norm, THRESHOLD)
    projection_next, projection_moment, projection_square = adam_update(
        projection,
        projection_first,
        projection_second,
        all_grads[0],
        clip_factor,
        RATE_PROJECTION,
        DECAY,
    )
    output_next, output_moment, output_square = adam_update(
        output_weight, output_first, output_second, all_grads[1], clip_factor, RATE_OUTPUT, DECAY
    )
    router_next, router_moment, router_square = adam_update(
        router_weight, router_first, router_second, all_grads[2], clip_factor, RATE_ROUTER, DECAY
    )
    vectors_next, vectors_moment, vectors_square = adam_update(
        vectors, vectors_first, vectors_second, all_grads[3], clip_factor, RATE_VECTORS, 0.0
    )
    inner_next, inner_moment, inner_square = adam_update(
        expert_inner, inner_first, inner_second, all_grads[4], clip_factor, RATE_INNER, DECAY
    )
    hidden_next, hidden_moment, hidden_square = adam_update(
        hidden_bias, hidden_first, hidden_second, all_grads[5], clip_factor, RATE_HIDDEN, 0.0
    )
    outer_next, outer_moment, outer_square = adam_update(
        expert_outer, outer_first, outer_second, all_grads[6], clip_factor, RATE_OUTER, DECAY
    )
    return_next, return_moment, return_square = adam_update(
        return_bias, return_first, return_second, all_grads[7], clip_factor, RATE_RETURN, 0.0
    )
    return (
        block_output,
        input_grad,
        grad_norm,
        projection_next,
        projection_moment,
        projection_square,
        output_next,
        output_moment,
        output_square,
        router_next,
        router_moment,
        router_square,
        vectors_next,
        vectors_moment,
        vectors_square,
        inner_next,
        inner_moment,
        inner_square,
        hidden_next,
        hidden_moment,
        hidden_square,
        outer_next,
        outer_moment,
        outer_square,
        return_next,
        return_moment,
        return_square,
    )


MESH = pl.DeviceIdType.MESH
ANY = pl.BlockSpec(memory_space=pl.ANY)
VMEM = pl.BlockSpec(memory_space=pltpu.VMEM)


class Place:
    def __init__(self, dp, experts):
        self.dp, self.experts = dp, experts
        self.ys = 2
        self.zs = experts // 4
        self.a = lax.axis_index("dp")
        self.e = lax.axis_index("expert")
        self.core = lax.rem(self.e, 2)
        self.y = lax.rem(lax.div(self.e, 2), self.ys)
        self.z = lax.div(self.e, 2 * self.ys)

    def chip_of(self, core, dz, s2, s3):
        zz = lax.rem(self.z + dz, self.zs)
        if s2 == s3:
            fa = fy = s2
        elif s2:
            fa, fy = core, 1 - core
        else:
            fa, fy = 1 - core, core
        aa = lax.rem(self.a + fa, 2)
        yy = lax.rem(self.y + fy, 2)
        return aa, zz, yy

    def device(self, core, dz, s2, s3, own_core=None):
        aa, zz, yy = self.chip_of(core, dz, s2, s3)
        c = core if own_core is None else own_core
        return (aa, (zz * self.ys + yy) * 2 + c)

    def flat(self, dev):
        return dev[0] * self.experts + dev[1]

    def chip(self, core, dz, s2, s3):
        aa, zz, yy = self.chip_of(core, dz, s2, s3)
        return (aa * self.zs + zz) * self.ys + yy


def remote(src, dst, send, recv, dev):
    return pltpu.make_async_remote_copy(src_ref=src, dst_ref=dst, send_sem=send, recv_sem=recv, device_id=dev, device_id_type=MESH)


def greet(devices):
    barrier = pltpu.get_barrier_semaphore()
    for dev in devices:
        pl.semaphore_signal(barrier, inc=1, device_id=dev, device_id_type=MESH)
    pl.semaphore_wait(barrier, len(devices))


def split_index(k, zs):
    return k % zs, (k // zs) % 2, k // (2 * zs)


LANES = 128


def nn(left, right):
    return lax.dot_general(left, right, (((1,), (0,)), ((), ())), preferred_element_type=jnp.float32)


def nt(left, right):
    return lax.dot_general(left, right, (((1,), (1,)), ((), ())), preferred_element_type=jnp.float32)


def lane_ids(rows, start=0):
    return lax.broadcasted_iota(jnp.int32, (rows, LANES), 1) + start


def row_parts(count, size):
    return [pl.ds(i * size, size) for i in range(count // size)]


def norm_parts(values):
    center = values - jnp.mean(values, axis=-1, keepdims=True)
    inverse = lax.rsqrt(jnp.mean(center * center, axis=-1, keepdims=True) + NORM_EPS)
    return center * inverse, inverse


def vector_table(weights, width):
    return jnp.transpose(weights[:, 4 * width :].astype(jnp.float32))


def forward_kernel(
    dp,
    experts,
    capacity,
    chunk,
    tok_ref,
    cot_ref,
    choice_ref,
    rank_row,
    projection_ref,
    output_ref,
    router_ref,
    vectors_ref,
    rows_ref,
    dy_ref,
    aux_ref,
    probs_ref,
    qkv_any,
    ctx_any,
    mid_any,
    second_any,
    stat_any,
    weights_any,
    qkv_ref,
    ctx_ref,
    mid_ref,
    second_ref,
    stat_ref,
    weights,
    vec,
    normed,
    mine,
    theirs,
    land_first,
    land,
    pre_send,
    pre_recv,
    line_send,
    line_recv,
    second_send,
    second_recv,
    third_send,
    third_recv,
    core_send,
    core_recv,
    store,
):
    low, full32 = jnp.bfloat16, jnp.float32
    patches, width = tok_ref.shape
    half = width // 2
    trio_width = 3 * LANES
    p = Place(dp, experts)
    c, zs = p.core, p.zs
    deep = projection_ref.shape[0]
    partner = (p.a, p.e + 1 - 2 * c)
    second, third = p.device(c, 0, 1, 0), p.device(c, 0, 0, 1)
    peers = [p.device(c, dz, 0, 0) for dz in range(1, zs)]
    narrow = jnp.concatenate(
        [router_ref[...], vectors_ref[...], jnp.zeros((LANES - experts - vectors_ref.shape[0], deep), full32)], axis=0
    )
    for h in range(2):
        mine[h, :, :LANES] = jnp.transpose(narrow) if h == 0 else jnp.zeros((deep, LANES), full32)
        for i in range(width // LANES // 2):
            for kind in range(3):
                at = kind * width + (2 * i + h) * LANES
                mine[h, :, LANES + i * trio_width + kind * LANES : LANES + i * trio_width + (kind + 1) * LANES] = (
                    projection_ref[:, at : at + LANES]
                )
        mine[h, :, LANES + 3 * half :] = output_ref[:, h * half : (h + 1) * half]
    greet(peers + [second, third, partner])
    before_all = remote(mine.at[1 - c], theirs, pre_send, pre_recv, partner)
    before_all.start()
    lanes = lane_ids(patches)
    named = jnp.concatenate([choice_ref[...], rank_row[...]], axis=0).astype(full32)
    named = jnp.transpose(jnp.concatenate([named, jnp.zeros((LANES - 3, patches), full32)], axis=0))
    first, other = named[:, 0:1].astype(jnp.int32), named[:, 1:2].astype(jnp.int32)
    is_first, is_other = lanes == first, lanes == other
    chunks = width // LANES // 2 + 1
    lands = [land_first] + [land.at[i] for i in range(chunks - 1)]
    my_line = p.a * p.ys + p.y
    second_line = jnp.where(c == 0, p.a * p.ys + 1 - p.y, (1 - p.a) * p.ys + p.y)
    third_lines = [
        jnp.where(c == 0, (1 - p.a) * p.ys + p.y, p.a * p.ys + 1 - p.y),
        (1 - p.a) * p.ys + 1 - p.y,
    ]

    def line_copy(i, dz):
        block = lands[i].at[c, my_line, p.z]
        return remote(block, block, line_send.at[i, dz], line_recv.at[i, dz], peers[dz - 1])

    def second_copy(i):
        block = lands[i].at[c, my_line]
        return remote(block, block, second_send.at[i], second_recv.at[i], second)

    def third_copy(i, which):
        block = lands[i].at[c, my_line if which == 0 else second_line]
        return remote(block, block, third_send.at[i, which], third_recv.at[i, which], third)

    def core_copy(i, which):
        block = lands[i].at[c, (my_line, second_line, *third_lines)[which]]
        return remote(block, block, core_send.at[i, which], core_recv.at[i, which], partner)

    def step0(i):
        for dz in range(1, zs):
            line_copy(i, dz).start()

    def step1(i):
        for dz in range(1, zs):
            block = lands[i].at[c, my_line, lax.rem(p.z + zs - dz, zs)]
            remote(block, block, line_send.at[i, dz], line_recv.at[i, dz], partner).wait_recv()
        third_copy(i, 0).start()
        second_copy(i).start()
        core_copy(i, 0).start()

    def step2(i):
        second_copy(i).wait_recv()
        third_copy(i, 1).start()
        core_copy(i, 1).start()

    def step3(i):
        for which in range(2):
            third_copy(i, which).wait_recv()
            core_copy(i, 2 + which).start()

    def unpack(i):
        for which in range(4):
            core_copy(i, which).wait_recv()
        for line in range(2 * p.ys):
            for z in range(zs):
                at = (line // p.ys * zs + z) * p.ys + line % p.ys
                rows = pl.ds(2 * deep * at, 2 * deep)
                for h in range(2):
                    if i == 0:
                        weights[rows, h * trio_width : (h + 1) * trio_width] = land_first[h, line, z, :, LANES:]
                    else:
                        columns = pl.ds((2 * i + h) * half, half)
                        weights[rows, columns] = land[i - 1, h, line, z]
                if i == 0:
                    weights[rows, 4 * width :] = land_first[0, line, z, :, :LANES]

    before_all.wait_recv()
    own, their = mine[c], theirs[...]
    top, bottom = jnp.where(c == 0, own, their), jnp.where(c == 0, their, own)
    block = jnp.concatenate([top, bottom], axis=0).astype(low)
    land_first[c, my_line, p.z] = block[:, : LANES + half]
    for i in range(1, chunks):
        land[i - 1, c, my_line, p.z] = block[:, LANES + i * half : LANES + (i + 1) * half]
    for i in range(chunks):
        step0(i)
    earlier = (rank_row[...].astype(full32) < named[:, 2:3]).astype(full32).astype(low)
    hot = (is_first | (lanes == other + experts)).astype(full32)
    counts = nn(earlier, hot.astype(low))
    totals = jnp.sum(hot, axis=0, keepdims=True)
    place_first = jnp.sum(jnp.where(is_first, counts, 0.0), axis=1, keepdims=True)
    place_other = jnp.sum(
        jnp.where(lanes == other + experts, counts, 0.0) + jnp.where(is_other, totals, 0.0), axis=1, keepdims=True
    )
    aux_ref[...] = jnp.where(lanes == 0, place_first, jnp.where(lanes == 1, place_other, 0.0))

    def row(i):
        return vec[experts + i : experts + i + 1, :]

    def attend(pair):
        at = pair * LANES
        trio = pair * trio_width
        product = nn(normed[...], weights[:, trio : trio + trio_width])
        queries_all = (product[:, :LANES] + vec[experts + 2 : experts + 3, at : at + LANES]).astype(low)
        keys = product[:, LANES : 2 * LANES].astype(low)
        values = (product[:, 2 * LANES :] + vec[experts + 3 : experts + 4, at : at + LANES]).astype(low)
        qkv_ref[:, trio : trio + LANES] = queries_all
        qkv_ref[:, trio + LANES : trio + 2 * LANES] = keys
        qkv_ref[:, trio + 2 * LANES : trio + 3 * LANES] = values
        key_lanes = lane_ids(patches)
        values_two = [
            jnp.where(key_lanes < HEAD_DIM, values, (key_lanes == HEAD_DIM).astype(full32).astype(low)),
            jnp.where(key_lanes >= HEAD_DIM, values, (key_lanes == 0).astype(full32).astype(low)),
        ]
        for part in row_parts(patches, chunk):
            own_lanes = lane_ids(chunk)
            queries = qkv_ref[part, trio : trio + LANES] * jnp.asarray(HEAD_DIM**-0.5, low)
            outs = []
            stat = stat_ref[part, :]
            for head in range(2):
                side = (own_lanes < HEAD_DIM) if head == 0 else (own_lanes >= HEAD_DIM)
                scores = nt(jnp.where(side, queries, jnp.zeros_like(queries)), keys)
                peak = jnp.max(scores, axis=1, keepdims=True)
                raised = jnp.exp(scores - peak)
                mixed = nn(raised.astype(low), values_two[head])
                spare = HEAD_DIM if head == 0 else 0
                total = mixed[:, spare : spare + 1]
                outs.append(mixed / total)
                stat = jnp.where(own_lanes == 2 * pair + head, peak + jnp.log(total), stat)
            stat_ref[part, :] = stat
            ctx_ref[part, at : at + LANES] = jnp.where(own_lanes < HEAD_DIM, outs[0], outs[1]).astype(low)

    stat_ref[...] = jnp.zeros_like(stat_ref)
    step1(0)
    step1(1)
    step2(0)
    step1(2)
    step2(1)
    step3(0)
    step1(3)
    unpack(0)
    vec[...] = vector_table(weights, width)
    for part in row_parts(patches, chunk):
        unit, _ = norm_parts(tok_ref[part, :].astype(full32))
        normed[part, :] = (unit * row(0) + row(1)).astype(low)
    step2(2)
    step3(1)
    attend(0)
    step2(3)
    attend(1)
    step3(2)
    unpack(1)
    attend(2)
    step3(3)
    attend(3)
    unpack(2)
    attend(4)
    attend(5)
    unpack(3)
    kept = [(weights, weights_any), (qkv_ref, qkv_any), (ctx_ref, ctx_any), (stat_ref, stat_any)]
    kept += [(mid_ref, mid_any), (second_ref, second_any)]
    keep = [pltpu.make_async_copy(s, d, store.at[i]) for i, (s, d) in enumerate(kept)]
    for copy in keep[:4]:
        copy.start()
    third_columns = 256
    for j in range(width // third_columns):
        columns = pl.ds(j * third_columns, third_columns)
        product = nn(ctx_ref[...], weights[:, pl.ds(3 * width + j * third_columns, third_columns)])
        mid_ref[:, columns] = tok_ref[:, columns].astype(full32) + (product + vec[experts + 4 : experts + 5, columns])
    for part in row_parts(patches, chunk):
        unit, _ = norm_parts(mid_ref[part, :])
        second_ref[part, :] = (unit * row(5) + row(6)).astype(low)
    keep[4].start()
    keep[5].start()
    logits = jnp.where(lanes < experts, nn(second_ref[...], weights[:, 4 * width :]), -1e30)
    raised = jnp.exp(logits - jnp.max(logits, axis=1, keepdims=True))
    probs = raised / jnp.sum(raised, axis=1, keepdims=True)
    probs_ref[...] = probs
    place_first, place_other = aux_ref[:, 0:1], aux_ref[:, 1:2]

    def slot_of(place, expert):
        place = place.astype(jnp.int32)
        kept = place < capacity
        slot = (place // 8) * LANES + expert * 8 + place % 8
        tail = kept & (place >= capacity - 4)
        return kept, jnp.where(kept, slot, -1), jnp.where(tail, slot + 4, -1)

    aux = jnp.zeros((patches, LANES), jnp.float32)
    for j, (place, expert, hit) in enumerate(((place_first, first, is_first), (place_other, other, is_other))):
        kept, slot, twin = slot_of(place, expert)
        gate = jnp.where(kept, jnp.sum(jnp.where(hit, probs, 0.0), axis=1, keepdims=True), 0.0)
        for lane, column in ((j, slot.astype(jnp.float32)), (2 + j, twin.astype(jnp.float32)), (4 + j, gate), (6 + j, expert.astype(jnp.float32))):
            aux = jnp.where(lanes == lane, column, aux)
    aux_ref[...] = aux
    turned = jnp.transpose(aux)
    slots = [turned[i : i + 1, :] for i in range(4)]
    gates = [turned[4 + i : 5 + i, :] for i in range(2)]
    full = capacity // 8
    for i in range(full + 1):
        ids = (lax.broadcasted_iota(jnp.int32, (LANES, patches), 0) + i * LANES).astype(jnp.float32)
        hits = [ids == slots[0], ids == slots[1]]
        if i == full:
            hits = [hits[0] | (ids == slots[2]), hits[1] | (ids == slots[3])]
        table = (hits[0] | hits[1]).astype(jnp.float32).astype(low)
        gate = jnp.sum(
            jnp.where(hits[0], gates[0], 0.0) + jnp.where(hits[1], gates[1], 0.0), axis=1, keepdims=True
        )
        sent = nn(table, second_ref[...])
        back = nn(table, cot_ref[...]) * gate
        columns = pl.ds(i * width, width)
        if i == full:
            columns = pl.ds(i * width, width // 2)
            left = lax.broadcasted_iota(jnp.int32, (LANES, width // 2), 0) % 8 < 4
            sent = jnp.where(left, sent[:, : width // 2], sent[:, width // 2 :])
            back = jnp.where(left, back[:, : width // 2], back[:, width // 2 :])
        rows_ref[:, columns] = sent.astype(low)
        dy_ref[:, columns] = back.astype(low)
    for copy in keep:
        copy.wait()
    before_all.wait_send()
    for i in range(chunks):
        for dz in range(1, zs):
            line_copy(i, dz).wait_send()
        second_copy(i).wait_send()
        for which in range(2):
            third_copy(i, which).wait_send()
        for which in range(4):
            core_copy(i, which).wait_send()


def forward(
    tokens,
    cotangent,
    choice,
    priority,
    projection,
    output_weight,
    router_weight,
    vectors,
    dp,
    experts,
    capacity,
    cid,
    chunk=576,
):
    patches, width = tokens.shape
    low, full = jnp.bfloat16, jnp.float32
    packed = (8 * experts, capacity * width // 8)
    shapes = [
        (packed, low),
        (packed, low),
        ((patches, LANES), full),
        ((patches, LANES), full),
        ((patches, 3 * width), low),
        ((patches, width), low),
        ((patches, width), full),
        ((patches, width), low),
        ((patches, LANES), full),
        ((width, 4 * width + LANES), low),
    ]
    deep, half = projection.shape[0], width // 2
    chunks = width // LANES // 2 + 1
    zs = experts // 4
    lines = dp * experts // 2 // zs
    dma = pltpu.SemaphoreType.DMA
    return pl.pallas_call(
        functools.partial(forward_kernel, dp, experts, capacity, chunk),
        out_shape=[jax.ShapeDtypeStruct(*s) for s in shapes],
        in_specs=[VMEM] * 8,
        out_specs=[VMEM] * 4 + [ANY] * 6,
        scratch_shapes=[
            *(pltpu.VMEM(*shape) for shape in shapes[4:]),
            pltpu.VMEM((LANES, width), full),
            pltpu.VMEM((patches, width), low),
            pltpu.VMEM((2, deep, LANES + 4 * half), full),
            pltpu.VMEM((deep, LANES + 4 * half), full),
            pltpu.VMEM((2, lines, zs, 2 * deep, LANES + half), low),
            pltpu.VMEM((chunks - 1, 2, lines, zs, 2 * deep, half), low),
            dma,
            dma,
            dma((chunks, zs)),
            dma((chunks, zs)),
            dma((chunks,)),
            dma((chunks,)),
            dma((chunks, 2)),
            dma((chunks, 2)),
            dma((chunks, 4)),
            dma((chunks, 4)),
            dma((6,)),
        ],
        compiler_params=pltpu.CompilerParams(
            collective_id=cid, has_side_effects=True, vmem_limit_bytes=60 * 1024 * 1024
        ),
        cost_estimate=pl.CostEstimate(flops=6 * 10**9, bytes_accessed=20 * 10**6, transcendentals=4 * 10**6),
        name="attend_forward",
    )(
        tokens,
        cotangent,
        choice.T,
        priority.reshape(1, patches),
        projection,
        output_weight,
        router_weight.T,
        vectors,
    )


def gelu_both(z):
    root = 0.7978845608028654
    square = z * z
    slope = jnp.tanh(root * z * (1.0 + 0.044715 * square))
    half = 0.5 * (1.0 + slope)
    act = z * half
    grad = half + 0.5 * z * (1.0 - slope * slope) * (root * (1.0 + 3 * 0.044715 * square))
    return act, grad


def tail_picks(count, right):
    rows = lax.broadcasted_iota(jnp.int32, (count // 2, count), 0)
    ids = lax.broadcasted_iota(jnp.int32, (count // 2, count), 1)
    hit = ids == (rows // 4) * 8 + rows % 4 + (4 if right else 0)
    return hit.astype(jnp.float32).astype(jnp.bfloat16)


class Stages:
    def __init__(self, place, refs):
        (self.grads, self.other, self.give3, self.take3, self.give2, self.take2, self.givez, self.takez, self.total) = refs[:9]
        (self.cs, self.cr, self.s3, self.r3, self.s2, self.r2, self.sz, self.rz) = refs[9:]
        self.p, self.zs, self.core = place, place.zs, place.core
        self.partner = (place.a, place.e + 1 - 2 * place.core)

    def to_partner(self, c):
        return remote(
            self.grads.at[c, 1 - self.core], self.other.at[c], self.cs.at[c], self.cr.at[c], self.partner
        )

    def to_third(self, c):
        return remote(
            self.give3.at[c], self.take3.at[c], self.s3.at[c], self.r3.at[c], self.p.device(self.core, 0, 0, 1)
        )

    def to_second(self, c):
        return remote(
            self.give2.at[c], self.take2.at[c], self.s2.at[c], self.r2.at[c], self.p.device(self.core, 0, 1, 0)
        )

    def along(self, c, dz):
        return remote(
            self.givez.at[c, dz - 1],
            self.takez.at[c, dz - 1],
            self.sz.at[c, dz],
            self.rz.at[c, dz],
            self.p.device(self.core, dz, 0, 0),
        )

    def sum_of(self, c, k, *more):
        at = self.p.chip(self.core, *split_index(k, self.zs))
        total = self.grads[c, self.core, at].astype(jnp.float32) + self.other[c, at].astype(jnp.float32)
        for ref in more:
            total = total + ref[c, k].astype(jnp.float32)
        return total

    def step0(self, c):
        self.to_partner(c).start()

    def step1(self, c):
        self.to_partner(c).wait_recv()
        zs = self.zs
        for k in range(2 * zs, 4 * zs):
            self.give3[c, k - 2 * zs] = self.sum_of(c, k).astype(self.give3.dtype)
        self.to_third(c).start()

    def step2(self, c):
        self.to_third(c).wait_recv()
        zs = self.zs
        for k in range(zs, 2 * zs):
            self.give2[c, k - zs] = self.sum_of(c, k, self.take3).astype(self.give2.dtype)
        self.to_second(c).start()

    def step3(self, c):
        self.to_second(c).wait_recv()
        for dz in range(1, self.zs):
            self.givez[c, dz - 1] = self.sum_of(c, dz, self.take3, self.take2).astype(self.givez.dtype)
            self.along(c, dz).start()

    def step4(self, c):
        total = self.sum_of(c, 0, self.take3, self.take2)
        for dz in range(1, self.zs):
            self.along(c, dz).wait_recv()
            total = total + self.takez[c, dz - 1].astype(jnp.float32)
        self.total[c] = total

    def finish(self, count):
        for c in range(count):
            self.to_partner(c).wait_send()
            self.to_third(c).wait_send()
            self.to_second(c).wait_send()
            for dz in range(1, self.zs):
                self.along(c, dz).wait_send()


def stage_scratch(chunks, chips, rows, columns):
    low = jnp.bfloat16
    zs = chips // 4
    shapes = [
        (chunks, 2, chips, rows, columns),
        (chunks, chips, rows, columns),
        (chunks, 2 * zs, rows, columns),
        (chunks, 2 * zs, rows, columns),
        (chunks, zs, rows, columns),
        (chunks, zs, rows, columns),
        (chunks, zs - 1, rows, columns),
        (chunks, zs - 1, rows, columns),
    ]
    sems = [pltpu.SemaphoreType.DMA((chunks,)) for _ in range(6)]
    sems += [pltpu.SemaphoreType.DMA((chunks, zs)) for _ in range(2)]
    return [pltpu.VMEM(s, low) for s in shapes] + [pltpu.VMEM((chunks, rows, columns), jnp.float32)] + sems


STAGE_REFS = 17


def backward_kernel(
    dp,
    experts,
    capacity,
    chunk,
    tok_ref,
    cot_ref,
    ret_ref,
    aux_ref,
    probs_ref,
    mid_ref,
    part_ref,
    back_any,
    second_any,
    ctx_any,
    stat_any,
    qkv_any,
    weights_any,
    out_any,
    input_any,
    dense_ref,
    total_ref,
    out_ref,
    unit_ref,
    inverse_ref,
    logs_ref,
    back_ref,
    second_ref,
    ctx_ref,
    stat_ref,
    qkv_ref,
    weights,
    vec,
    stacked,
    normed_turned,
    branch,
    dctx,
    joined,
    turned_query,
    dmid,
    work,
    sums,
    load,
    row,
    row_fine,
    plane_tiles,
    line_tiles,
    row_send,
    row_recv,
    tile_send,
    tile_recv,
    store,
    *stage_refs,
):
    low, full32 = jnp.bfloat16, jnp.float32
    patches, width = tok_ref.shape
    trio_width = 3 * LANES
    p = Place(dp, experts)
    main, fine = Stages(p, stage_refs[:STAGE_REFS]), Stages(p, stage_refs[STAGE_REFS:])
    coarse, chips, shard2 = main.grads.shape[0], *main.grads.shape[2:4]
    thin = fine.grads.shape[4]
    pieces = [
        (back_any, back_ref),
        (weights_any, weights),
        (ctx_any, ctx_ref),
        (second_any, second_ref),
        (stat_any, stat_ref),
        (qkv_any, qkv_ref),
    ]
    fetch = [pltpu.make_async_copy(s, d, load.at[i]) for i, (s, d) in enumerate(pieces)]
    for copy in fetch:
        copy.start()
    barrier = pltpu.get_barrier_semaphore()

    def flip(value, bit):
        return value + bit - 2 * bit * value

    mates = []
    for f in range(1, 8):
        chip_y = p.z * p.ys + flip(p.y, (f // 2) % 2)
        mates.append((flip(p.a, f // 4), chip_y * 2 + flip(p.core, f % 2)))
    peers = [p.device(p.core, dz, 0, 0) for dz in range(1, p.zs)]
    for device in mates + peers:
        pl.semaphore_signal(barrier, inc=1, device_id=device, device_id_type=MESH)

    full = capacity // 8
    half = width // 2
    lanes = lane_ids(patches)
    aux = aux_ref[...]
    slots = [aux[:, i : i + 1] for i in range(4)]
    gates = [aux[:, 4 + i : 5 + i] for i in range(2)]
    ids = lax.broadcasted_iota(jnp.int32, (patches, full * LANES), 1).astype(full32)
    tail_ids = lane_ids(patches, full * LANES).astype(full32)
    hits = [ids == slots[0], ids == slots[1]]
    lefts = [tail_ids == slots[0], tail_ids == slots[1]]
    rights = [tail_ids == slots[2], tail_ids == slots[3]]

    def mix(marks):
        return (jnp.where(marks[0], gates[0], 0.0) + jnp.where(marks[1], gates[1], 0.0)).astype(low)

    def pick(marks):
        return (marks[0] | marks[1]).astype(full32).astype(low)

    for i in range(full):
        stacked[pl.ds(i * LANES, LANES), :] = ret_ref[:, pl.ds(i * width, width)]
    tail = ret_ref[:, pl.ds(full * width, half)]
    left_mix, right_mix = nn(mix(lefts), tail), nn(mix(rights), tail)
    final = nn(mix(hits), stacked[...])
    out_ref[:, :half] = (mid_ref[:, :half] + (final[:, :half] + left_mix)).astype(low)
    out_ref[:, half:] = (mid_ref[:, half:] + (final[:, half:] + right_mix)).astype(low)
    keep_out = pltpu.make_async_copy(out_ref, out_any, store.at[0])
    keep_out.start()
    along = nt(cot_ref[...], stacked[...])
    along_left, along_right = nt(cot_ref[:, :half], tail), nt(cot_ref[:, half:], tail)
    dprobs = jnp.zeros((patches, LANES), full32)
    for j in range(2):
        dgate = jnp.sum(jnp.where(hits[j], along, 0.0), axis=1, keepdims=True) + jnp.sum(
            jnp.where(lefts[j], along_left, 0.0) + jnp.where(rights[j], along_right, 0.0), axis=1, keepdims=True
        )
        dprobs = dprobs + jnp.where(lanes == aux[:, 6 + j : 7 + j].astype(jnp.int32), dgate, 0.0)
    probs = probs_ref[...]
    dlogits = (probs * (dprobs - jnp.sum(probs * dprobs, axis=1, keepdims=True))).astype(low)
    fetch[0].wait()
    for i in range(full):
        stacked[pl.ds(i * LANES, LANES), :] = back_ref[:, pl.ds(i * width, width)]
    tail = back_ref[:, pl.ds(full * width, half)]
    fetch[1].wait()
    vec[...] = vector_table(weights, width)

    def vector(i):
        return vec[experts + i : experts + i + 1, :]

    routed = weights[:, 4 * width :]
    work[...] = nn(pick(hits), stacked[...]) + nt(dlogits, routed)
    work[:, :half] = work[:, :half] + nn(pick(lefts), tail)
    work[:, half:] = work[:, half:] + nn(pick(rights), tail)
    sums[...] = jnp.zeros_like(sums)

    def column_sum(slot, values):
        sums[pl.ds(8 * slot, 8), :] = sums[pl.ds(8 * slot, 8), :] + jnp.sum(
            values.reshape(-1, 8, values.shape[-1]), axis=0
        )

    def norm_back(grad, unit, inverse, gain):
        weighted = grad * gain
        return inverse * (
            weighted
            - jnp.mean(weighted, axis=-1, keepdims=True)
            - unit * jnp.mean(weighted * unit, axis=-1, keepdims=True)
        )

    for part in row_parts(patches, chunk):
        unit, inverse = norm_parts(mid_ref[part, :])
        grad = work[part, :]
        column_sum(5, grad * unit)
        column_sum(6, grad)
        total = cot_ref[part, :].astype(full32) + norm_back(grad, unit, inverse, vector(5))
        dmid[part, :] = total
        rounded = total.astype(low)
        branch[part, :] = rounded
        column_sum(4, rounded.astype(full32))
    fetch[2].wait()
    ctx_turned = jnp.transpose(ctx_ref[...])
    for core in range(2):
        columns = pl.ds(core * half, half)
        product = nn(ctx_turned, branch[:, columns])
        main.grads[0, core] = product.reshape(chips, shard2, half).astype(low)
    pl.semaphore_wait(barrier, len(mates) + len(peers))
    main.step0(0)
    third = 256
    for j in range(width // third):
        rows = pl.ds(j * third, third)
        dctx[:, rows] = nt(branch[...], weights[rows, pl.ds(3 * width, width)]).astype(low)
    fetch[3].wait()
    router_rows = nn(jnp.transpose(dlogits.astype(full32)).astype(low), second_ref[...])
    for part in row_parts(patches, chunk):
        unit, inverse = norm_parts(tok_ref[part, :].astype(full32))
        second_ref[part, :] = (unit * vector(0) + vector(1)).astype(low)
        unit_ref[part, :] = unit
        inverse_ref[part, :] = jnp.broadcast_to(inverse, (chunk, LANES))
    normed_turned[...] = jnp.transpose(second_ref[...])
    heads = (
        lax.broadcasted_iota(jnp.int32, (16, width), 1) // HEAD_DIM == lax.broadcasted_iota(jnp.int32, (16, width), 0)
    ).astype(full32).astype(low)
    product = dctx[...].astype(full32) * ctx_ref[...].astype(full32)
    upper = product.astype(low)
    center = nt(heads, upper) + nt(heads, (product - upper.astype(full32)).astype(low))
    fetch[4].wait()
    logs = jnp.transpose(stat_ref[...])
    logs_ref[...] = jnp.concatenate([logs[:16], center], axis=0)
    fetch[5].wait()

    ones = jnp.ones((8, patches), low)
    scale = jnp.asarray(HEAD_DIM**-0.5, low)

    def attend(pair):
        at, trio = pair * LANES, pair * trio_width
        key_at, value_at = pl.ds(trio + LANES, LANES), pl.ds(trio + 2 * LANES, LANES)
        queries = qkv_ref[:, pl.ds(trio, LANES)] * scale
        given = dctx[:, pl.ds(at, LANES)]
        own = lane_ids(patches)
        zero = jnp.zeros_like(queries)
        marks = [own < HEAD_DIM, own >= HEAD_DIM]
        head_queries = [jnp.where(m, queries, zero) for m in marks]
        head_given = [jnp.where(m, given, zero) for m in marks]
        turned_keys = jnp.transpose(qkv_ref[:, key_at] * scale)
        query_parts = [None, None]
        for part in row_parts(patches, chunk):
            keys = qkv_ref[part, key_at]
            values = qkv_ref[part, value_at]
            value_out, key_out = [], []
            for head in range(2):
                log_row = logs_ref[2 * pair + head : 2 * pair + head + 1, :]
                center_row = logs_ref[16 + 2 * pair + head : 17 + 2 * pair + head, :]
                prob = jnp.exp(nt(keys, head_queries[head]) - log_row)
                value_out.append(nn(prob.astype(low), given))
                dscore = (prob * (nt(values, head_given[head]) - center_row)).astype(low)
                key_out.append(nn(dscore, queries))
                head_keys = turned_keys[HEAD_DIM * head : HEAD_DIM * (head + 1), part.start : part.start + part.size]
                piece = nn(head_keys, dscore)
                query_parts[head] = piece if query_parts[head] is None else query_parts[head] + piece
            side = lane_ids(chunk) < HEAD_DIM
            joined[part, LANES : 2 * LANES] = jnp.where(side, key_out[0], key_out[1]).astype(low)
            joined[part, 2 * LANES :] = jnp.where(side, value_out[0], value_out[1]).astype(low)
        turned_query[...] = jnp.concatenate(query_parts, axis=0)
        joined[:, :LANES] = jnp.transpose(turned_query[...]).astype(low)
        product = nn(normed_turned[...], joined[...]).reshape(chips, shard2, trio_width).astype(low)
        if pair < 2 * (coarse - 1):
            main.grads[pair // 2 + 1, pair % 2] = product
        else:
            chunk_of = pair - 2 * (coarse - 1)
            fine.grads[chunk_of, 0] = product[:, :, :thin]
            fine.grads[chunk_of, 1, :, :, :LANES] = product[:, :, thin:]

    def spread(pair):
        trio = pair * trio_width
        part = nt(joined[...], weights[:, pl.ds(trio, trio_width)])
        work[...] = part if pair == 0 else work[...] + part
        column_parts = nn(ones, joined[...])
        sums[16:17, pl.ds(pair * LANES, LANES)] = column_parts[0:1, :LANES]
        sums[24:25, pl.ds(pair * LANES, LANES)] = column_parts[0:1, 2 * LANES :]

    fine.grads[0, 1, :, :, LANES:] = jnp.zeros((chips, shard2, thin - LANES), low)
    main.step1(0)
    attend(0)
    spread(0)
    main.step2(0)
    attend(1)
    main.step0(1)
    spread(1)
    main.step3(0)
    attend(2)
    main.step1(1)
    spread(2)
    attend(3)
    main.step0(2)
    main.step4(0)
    spread(3)
    main.step2(1)
    attend(4)
    fine.step0(0)
    main.step1(2)
    main.step3(1)
    spread(4)
    attend(5)
    fine.step1(0)
    spread(5)
    main.step2(2)
    for part in row_parts(patches, chunk):
        unit, inverse = unit_ref[part, :], inverse_ref[part, 0:1]
        grad = work[part, :]
        column_sum(0, grad * unit)
        column_sum(1, grad)
        dmid[part, :] = dmid[part, :] + norm_back(grad, unit, inverse, vector(0))
    keep_input = pltpu.make_async_copy(dmid, input_any, store.at[1])
    keep_input.start()
    vec[...] = router_rows
    for i in range(7):
        vec[experts + i : experts + i + 1, :] = jnp.sum(sums[pl.ds(8 * i, 8), :], axis=0, keepdims=True)
    fine.grads[1, 1, :, :, LANES:] = jnp.transpose(vec[...]).reshape(chips, shard2, LANES).astype(low)
    fine.step0(1)
    fine.step2(0)
    main.step4(1)
    fine.step1(1)
    main.step3(2)
    fine.step3(0)
    fine.step2(1)
    main.step4(2)
    fine.step4(0)
    deep = shard2 // 2
    his = pl.ds(pl.multiple_of((1 - p.core) * deep, 8), deep)
    mine = pl.ds(pl.multiple_of(p.core * deep, 8), deep)
    rows_copy = [
        remote(main.total.at[:, his], row, row_send.at[0], row_recv.at[0], main.partner),
        remote(fine.total.at[0, his], row_fine.at[0], row_send.at[1], row_recv.at[1], main.partner),
        remote(fine.total.at[1, his], row_fine.at[1], row_send.at[2], row_recv.at[2], main.partner),
    ]
    rows_copy[0].start()
    rows_copy[1].start()
    fine.step3(1)

    def squares_of(values):
        folded = jnp.sum((values * values).reshape(-1, 8, values.shape[1]), axis=0)
        out = folded[:, :LANES]
        for j in range(1, values.shape[1] // LANES):
            out = out + folded[:, j * LANES : (j + 1) * LANES]
        return out

    square = part_ref[...]
    for c in range(coarse):
        square = square + squares_of(main.total[c])
    square = square + squares_of(fine.total[0])
    fine.step4(1)
    rows_copy[2].start()
    plane = (p.a * p.ys + p.y) * 2 + p.core
    plane_tiles[plane] = square + squares_of(fine.total[1])

    def mate_copy(f):
        block = plane_tiles.at[plane]
        return remote(block, block, tile_send.at[f], tile_recv.at[f], mates[f - 1])

    def peer_copy(dz):
        block = line_tiles.at[p.z]
        return remote(block, block, tile_send.at[7 + dz], tile_recv.at[7 + dz], peers[dz - 1])

    for f in range(1, 8):
        mate_copy(f).start()

    def put(core, values, fine_values):
        for c in range(coarse):
            dense_ref[:, pl.ds(pl.multiple_of(c * width + core * half, LANES), half)] = values(c)
        for c in range(2):
            at = coarse * width + 2 * c * thin + core * thin
            dense_ref[:, pl.ds(pl.multiple_of(at, LANES), thin)] = fine_values(c)

    put(p.core, lambda c: main.total[c, mine, :], lambda c: fine.total[c, mine, :])
    for f in range(1, 8):
        from_plane = (flip(p.a, f // 4) * p.ys + flip(p.y, (f // 2) % 2)) * 2 + flip(p.core, f % 2)
        block = plane_tiles.at[from_plane]
        remote(block, block, tile_send.at[f], tile_recv.at[f], main.partner).wait_recv()
    total = plane_tiles[0]
    for j in range(1, 8):
        total = total + plane_tiles[j]
    line_tiles[p.z] = total
    for dz in range(1, p.zs):
        peer_copy(dz).start()
    for copy in rows_copy:
        copy.wait_recv()
    put(1 - p.core, lambda c: row[c], lambda c: row_fine[c])
    for dz in range(1, p.zs):
        block = line_tiles.at[lax.rem(p.z + p.zs - dz, p.zs)]
        remote(block, block, tile_send.at[7 + dz], tile_recv.at[7 + dz], main.partner).wait_recv()
    total = line_tiles[0]
    for j in range(1, p.zs):
        total = total + line_tiles[j]
    total_ref[...] = total
    main.finish(coarse)
    fine.finish(2)
    for copy in rows_copy:
        copy.wait_send()
    for f in range(1, 8):
        mate_copy(f).wait_send()
    for dz in range(1, p.zs):
        peer_copy(dz).wait_send()
    keep_out.wait()
    keep_input.wait()


def backward(
    tokens,
    cotangent,
    ret,
    back,
    aux,
    probs,
    mid,
    second,
    ctx,
    stat,
    qkv,
    weights,
    part,
    dp,
    experts,
    capacity,
    cid,
    chunk=576,
):
    patches, width = tokens.shape
    low, full = jnp.bfloat16, jnp.float32
    world = dp * experts
    chips, rows = world // 2, 2 * width // world
    thin = 2 * LANES
    chunks = width // LANES // 2
    columns = 4 * width + 2 * LANES
    return pl.pallas_call(
        functools.partial(backward_kernel, dp, experts, capacity, chunk),
        out_shape=[
            jax.ShapeDtypeStruct((patches, width), low),
            jax.ShapeDtypeStruct((patches, width), full),
            jax.ShapeDtypeStruct((rows // 2, columns), full),
            jax.ShapeDtypeStruct((8, LANES), full),
        ],
        in_specs=[VMEM] * 7 + [ANY] * 6,
        out_specs=[ANY, ANY, VMEM, VMEM],
        scratch_shapes=[
            pltpu.VMEM((patches, width), low),
            pltpu.VMEM((patches, width), full),
            pltpu.VMEM((patches, LANES), full),
            pltpu.VMEM((32, patches), full),
            pltpu.VMEM(back.shape, low),
            pltpu.VMEM((patches, width), low),
            pltpu.VMEM((patches, width), low),
            pltpu.VMEM(stat.shape, full),
            pltpu.VMEM(qkv.shape, low),
            pltpu.VMEM(weights.shape, low),
            pltpu.VMEM((LANES, width), full),
            pltpu.VMEM((capacity // 8 * LANES, width), low),
            pltpu.VMEM((width, patches), low),
            pltpu.VMEM((patches, width), low),
            pltpu.VMEM((patches, width), low),
            pltpu.VMEM((patches, 3 * LANES), low),
            pltpu.VMEM((LANES, patches), full),
            pltpu.VMEM((patches, width), full),
            pltpu.VMEM((patches, width), full),
            pltpu.VMEM((56, width), full),
            pltpu.SemaphoreType.DMA((6,)),
            pltpu.VMEM((chunks, rows // 2, width // 2), full),
            pltpu.VMEM((2, rows // 2, thin), full),
            pltpu.VMEM((8, 8, LANES), full),
            pltpu.VMEM((experts // 4, 8, LANES), full),
            pltpu.SemaphoreType.DMA((3,)),
            pltpu.SemaphoreType.DMA((3,)),
            pltpu.SemaphoreType.DMA((7 + experts // 4,)),
            pltpu.SemaphoreType.DMA((7 + experts // 4,)),
            pltpu.SemaphoreType.DMA((2,)),
            *stage_scratch(chunks, chips, rows, width // 2),
            *stage_scratch(2, chips, rows, thin),
        ],
        compiler_params=pltpu.CompilerParams(
            collective_id=cid, has_side_effects=True, vmem_limit_bytes=60 * 1024 * 1024
        ),
        cost_estimate=pl.CostEstimate(flops=15 * 10**9, bytes_accessed=30 * 10**6, transcendentals=4 * 10**6),
        name="attend_backward",
    )(tokens, cotangent, ret, aux, probs, mid, part, back, second, ctx, stat, qkv, weights)


ORDER = 7


def moe_kernel(
    dp,
    experts,
    chunk,
    rows_any,
    dy_any,
    inner_any,
    hidden_ref,
    outer_any,
    return_ref,
    y_any,
    drows_any,
    dinner_any,
    dhidden_ref,
    douter_any,
    dreturn_ref,
    square_ref,
    rows_all,
    dy_all,
    y_pack,
    drows_pack,
    y_theirs,
    drows_theirs,
    rows,
    turned,
    dy,
    inner,
    outer,
    act,
    grad,
    dz,
    acc,
    inner_stage,
    outer_stage,
    dinner_stage,
    douter_stage,
    square,
    own_sem,
    in_send,
    in_recv,
    over_send,
    over_recv,
    part_send,
    part_recv,
    out_send,
    out_recv,
    stage_sem,
    store_sem,
):
    low, full32 = jnp.bfloat16, jnp.float32
    width = rows.shape[1]
    count = dp * experts * 8
    half = width // 2
    full = rows_all.shape[3] // width
    steps = inner.shape[1] // chunk
    each = -(-(experts - 1) // (steps - 1))
    a = lax.axis_index("dp")
    e = lax.axis_index("expert")
    across = (1 - a, e)
    ins, alls = (rows_any, dy_any), (rows_all, dy_all)
    packs, theirs, outs = (y_pack, drows_pack), (y_theirs, drows_theirs), (y_any, drows_any)

    def to(j):
        return lax.rem(e + j, experts)

    def source(j):
        return lax.rem(e + experts - j, experts)

    def stage(k, slot):
        columns = pl.ds(pl.multiple_of(k * chunk, chunk), chunk)
        return (
            pltpu.make_async_copy(inner_any.at[0, :, columns], inner_stage.at[slot], stage_sem.at[0, slot]),
            pltpu.make_async_copy(outer_any.at[0, columns, :], outer_stage.at[slot], stage_sem.at[1, slot]),
        )

    def own_block(i):
        return pltpu.make_async_copy(ins[i].at[e], alls[i].at[a, e], own_sem.at[i])

    for slot in range(2):
        for copy in stage(slot, slot):
            copy.start()
    for i in range(2):
        own_block(i).start()
    greet([(a, to(j)) for j in range(1, experts)] + [across])

    def first_send(i, j):
        return remote(ins[i].at[to(j)], alls[i].at[a, e], in_send.at[i, j], in_recv.at[i, j], (a, to(j)))

    def forward_own(i):
        return remote(ins[i].at[e], alls[i].at[a, e], over_send.at[i, 0], over_recv.at[i, 0], across)

    def pass_on(i, j):
        block = alls[i].at[a, source(j)]
        return remote(block, block, over_send.at[i, j], over_recv.at[i, j], across)

    def received(i, j):
        block = alls[i].at[a, source(j)]
        return remote(block, block, in_send.at[i, j], in_recv.at[i, j], across)

    def from_across(i, j):
        block = alls[i].at[1 - a, source(j)]
        return remote(block, block, over_send.at[i, j], over_recv.at[i, j], across)

    def part_copy(i, j):
        return remote(
            packs[i].at[1 - a, to(j)], theirs[i].at[j], part_send.at[i, j], part_recv.at[i, j], across
        )

    def result_copy(i, j):
        return remote(packs[i].at[a, to(j)], outs[i].at[e], out_send.at[i, j], out_recv.at[i, j], (a, to(j)))

    for i in range(2):
        forward_own(i).start()

        @pl.loop(1, experts)
        def _(j):
            first_send(i, lax.rem(ORDER * j, experts)).start()

    def take_in(i, k):
        @pl.when(k < steps - 1)
        def _():
            @pl.loop(0, each)
            def _(d):
                turn = 1 + k * each + d
                j = lax.rem(ORDER * turn, experts)

                @pl.when(turn < experts)
                def _():
                    received(i, j).wait_recv()
                    pass_on(i, j).start()

    def hand_out(i, begin, number):
        @pl.loop(0, number)
        def _(d):
            turn = begin + d
            j = lax.rem(ORDER * turn, experts)

            @pl.when(turn < experts)
            def _():
                part_copy(i, j).wait_recv()
                at = to(j)
                packs[i][a, at] = (packs[i][a, at].astype(full32) + theirs[i][j].astype(full32)).astype(low)
                result_copy(i, j).start()

    @pl.loop(0, steps)
    def _(k):
        slot = lax.rem(k, 2)
        columns = pl.ds(pl.multiple_of(k * chunk, chunk), chunk)
        for copy in stage(k, slot):
            copy.wait()
        inner[:, columns] = inner_stage[slot].astype(low)
        outer[columns, :] = outer_stage[slot].astype(low)

        @pl.when(k + 2 < steps)
        def _():
            for copy in stage(k + 2, slot):
                copy.start()

        take_in(0, k)

    def unpack(i, place):
        own_block(i).wait()

        @pl.loop(0, experts)
        def _(j):
            from_across(i, j).wait_recv()

        group = 8
        for plane in range(dp):
            for s in range(0, experts, group):
                base = (plane * experts + s) * 8
                for b in range(full):
                    piece = alls[i][plane, s : s + group, :, b * width : (b + 1) * width].astype(full32)
                    place[pl.ds(b * count + base, 8 * group), :] = piece.reshape(8 * group, width).astype(low)
        tails = [
            alls[i][plane, :, :, full * width :].astype(full32).reshape(experts * 8, half) for plane in range(dp)
        ]
        tail = jnp.concatenate(tails, axis=0).astype(low)
        for right in range(2):
            place[pl.ds(full * count, count // 2), pl.ds(right * half, half)] = nn(
                tail_picks(count, right), tail
            ).astype(low)

    def pack(i):
        group = 8
        for plane in range(dp):
            for s in range(0, experts, group):
                base = (plane * experts + s) * 8
                for b in range(full):
                    piece = acc[pl.ds(b * count + base, 8 * group), :].reshape(group, 8, width)
                    packs[i][plane, s : s + group, :, b * width : (b + 1) * width] = piece.astype(low)
        tail = acc[pl.ds(full * count, count // 2), :].astype(low)
        spread = None
        for right in range(2):
            piece = lax.dot_general(
                tail_picks(count, right),
                tail[:, right * half : (right + 1) * half],
                (((0,), (0,)), ((), ())),
                preferred_element_type=full32,
            )
            spread = piece if spread is None else spread + piece
        for plane in range(dp):
            piece = spread[plane * experts * 8 : (plane + 1) * experts * 8].reshape(experts, 8, half)
            packs[i][plane, :, :, full * width :] = piece.astype(low)

        @pl.loop(0, experts)
        def _(d):
            part_copy(i, lax.rem(ORDER * (d + 1), experts)).start()

    unpack(0, rows)
    turned[...] = jnp.transpose(rows[...])
    acc[...] = jnp.zeros_like(acc)

    @pl.loop(0, steps)
    def _(k):
        columns = pl.ds(pl.multiple_of(k * chunk, chunk), chunk)
        z = nn(rows[...], inner[:, columns]) + hidden_ref[:, columns].astype(low).astype(full32)
        value, slope = gelu_both(z)
        act[:, columns] = value.astype(low)
        grad[:, columns] = slope
        acc[...] += nn(act[:, columns], outer[columns, :])
        take_in(1, k)

    part = return_ref.shape[1]
    bias = return_ref[...].astype(low).astype(full32)
    for i in range(dp):
        columns = pl.ds(i * part, part)
        acc[:, columns] = acc[:, columns] + jnp.where(a == i, bias, 0.0)
    pack(0)
    unpack(1, dy)
    total = jnp.zeros((1, width), full32)
    for i in range(rows.shape[0] // LANES):
        total = total + jnp.sum(dy[pl.ds(i * LANES, LANES), :].astype(full32), axis=0, keepdims=True)
    picked = total[:, :part]
    for i in range(1, dp):
        picked = jnp.where(a == i, total[:, i * part : (i + 1) * part], picked)
    dreturn_ref[...] = picked
    square[...] = jnp.zeros_like(square)
    flat = picked * picked
    for i in range(part // LANES):
        square[0:1, :] = square[0:1, :] + flat[:, i * LANES : (i + 1) * LANES]
    acc[...] = jnp.zeros_like(acc)

    @pl.loop(0, steps)
    def _(k):
        columns = pl.ds(pl.multiple_of(k * chunk, chunk), chunk)
        dz[:, columns] = (nt(dy[...], outer[columns, :]) * grad[:, columns]).astype(low)
        acc[...] += nt(dz[:, columns], inner[:, columns])
        hand_out(0, 1 + k, 1)

    pack(1)

    def finish(i):
        part_copy(i, 0).wait_recv()
        packs[i][a, e] = (packs[i][a, e].astype(full32) + theirs[i][0].astype(full32)).astype(low)
        pltpu.make_async_copy(packs[i].at[a, e], outs[i].at[e], own_sem.at[i]).start()

    def store(k, slot):
        columns = pl.ds(pl.multiple_of(k * chunk, chunk), chunk)
        return (
            pltpu.make_async_copy(dinner_stage.at[slot], dinner_any.at[0, :, columns], store_sem.at[0, slot]),
            pltpu.make_async_copy(douter_stage.at[slot], douter_any.at[0, columns, :], store_sem.at[1, slot]),
        )

    later = -(-(experts - 1 - steps) // (steps - 1))

    @pl.loop(0, steps)
    def _(k):
        slot = lax.rem(k, 2)
        columns = pl.ds(pl.multiple_of(k * chunk, chunk), chunk)
        douter = nn(jnp.transpose(act[:, columns]), dy[...])
        dinner = nn(turned[...], dz[:, columns])
        dhidden = jnp.sum(dz[:, columns].astype(full32), axis=0, keepdims=True)

        @pl.when(k >= 2)
        def _():
            for copy in store(k - 2, slot):
                copy.wait()

        douter_stage[slot] = douter.astype(low)
        dinner_stage[slot] = dinner.astype(low)
        for copy in store(k, slot):
            copy.start()
        dhidden_ref[:, columns] = dhidden
        parts = jnp.zeros((8, LANES), full32)
        folded = jnp.sum((douter * douter).reshape(-1, 8, width), axis=0)
        for i in range(width // LANES):
            parts = parts + folded[:, i * LANES : (i + 1) * LANES]
        folded = jnp.sum((dinner * dinner).reshape(-1, 8, chunk), axis=0)
        hidden_square = dhidden * dhidden
        for i in range(chunk // LANES):
            parts = parts + folded[:, i * LANES : (i + 1) * LANES]
            square[0:1, :] = square[0:1, :] + hidden_square[:, i * LANES : (i + 1) * LANES]
        square[...] += parts
        hand_out(0, 1 + steps + k * later, later)

    finish(0)
    hand_out(1, 1, experts - 1)
    finish(1)
    square_ref[...] = square[...]
    for k in range(steps - 2, steps):
        for copy in store(k, k % 2):
            copy.wait()
    for i in range(2):

        @pl.loop(1, experts)
        def _(j):
            block = outs[i].at[source(j)]
            remote(block, block, out_send.at[i, j], out_recv.at[i, j], across).wait_recv()

    for i in range(2):
        pltpu.make_async_copy(packs[i].at[a, e], outs[i].at[e], own_sem.at[i]).wait()
        forward_own(i).wait_send()
        part_copy(i, 0).wait_send()

        @pl.loop(1, experts)
        def _(j):
            first_send(i, j).wait_send()
            pass_on(i, j).wait_send()
            part_copy(i, j).wait_send()
            result_copy(i, j).wait_send()


def mixture(rows, dy, inner, hidden, outer, back, dp, cid, chunk=256):
    experts, _, packed = rows.shape
    width, units = inner.shape[1:]
    count = dp * experts * 8
    total = count * packed // width
    low, full = jnp.bfloat16, jnp.float32
    both = (dp, experts, 8, packed)
    sems = [pltpu.SemaphoreType.DMA((2, experts)) for _ in range(8)]
    return pl.pallas_call(
        functools.partial(moe_kernel, dp, experts, chunk),
        out_shape=[
            jax.ShapeDtypeStruct(rows.shape, low),
            jax.ShapeDtypeStruct(rows.shape, low),
            jax.ShapeDtypeStruct(inner.shape, low),
            jax.ShapeDtypeStruct(hidden.shape, full),
            jax.ShapeDtypeStruct(outer.shape, low),
            jax.ShapeDtypeStruct(back.shape, full),
            jax.ShapeDtypeStruct((8, LANES), full),
        ],
        in_specs=[ANY, ANY, ANY, VMEM, ANY, VMEM],
        out_specs=[ANY, ANY, ANY, VMEM, ANY, VMEM, VMEM],
        scratch_shapes=[
            pltpu.VMEM(both, low),
            pltpu.VMEM(both, low),
            pltpu.VMEM(both, low),
            pltpu.VMEM(both, low),
            pltpu.VMEM(both[1:], low),
            pltpu.VMEM(both[1:], low),
            pltpu.VMEM((total, width), low),
            pltpu.VMEM((width, total), low),
            pltpu.VMEM((total, width), low),
            pltpu.VMEM((width, units), low),
            pltpu.VMEM((units, width), low),
            pltpu.VMEM((total, units), low),
            pltpu.VMEM((total, units), full),
            pltpu.VMEM((total, units), low),
            pltpu.VMEM((total, width), full),
            pltpu.VMEM((2, width, chunk), full),
            pltpu.VMEM((2, chunk, width), full),
            pltpu.VMEM((2, width, chunk), low),
            pltpu.VMEM((2, chunk, width), low),
            pltpu.VMEM((8, LANES), full),
            pltpu.SemaphoreType.DMA((2,)),
            *sems,
            pltpu.SemaphoreType.DMA((2, 2)),
            pltpu.SemaphoreType.DMA((2, 2)),
        ],
        compiler_params=pltpu.CompilerParams(
            collective_id=cid, has_side_effects=True, vmem_limit_bytes=60 * 1024 * 1024
        ),
        cost_estimate=pl.CostEstimate(flops=17 * 10**9, bytes_accessed=25 * 10**6, transcendentals=2 * 10**6),
        name="mixture",
    )(rows, dy, inner, hidden, outer, back)


def adam_values(weight, first, second, gradient, clip, rate, decay):
    scaled = gradient * clip
    first_new = BETA_ONE * first + (1.0 - BETA_ONE) * scaled
    second_new = BETA_TWO * second + (1.0 - BETA_TWO) * scaled * scaled
    first_hat = first_new * (1.0 / (1.0 - BETA_ONE**STEP))
    second_hat = second_new * (1.0 / (1.0 - BETA_TWO**STEP))
    weight_new = weight - rate * (first_hat / (jnp.sqrt(second_hat) + ADAM_EPS) + decay * weight)
    return weight_new, first_new, second_new


def adam_kernel(experts, norm_ref, dense_any, *refs):
    small = 6
    large_ins, rest = refs[:8], refs[8:]
    small_ins, rest = rest[: 3 * small + 2], rest[3 * small + 2 :]
    large_outs, rest = rest[:6], rest[6:]
    small_outs, norm_out, rest = rest[: 3 * small], rest[3 * small], rest[3 * small + 1 :]
    held, dense_ref, load, store = rest[: 3 * small + 2], rest[3 * small + 2], rest[-2], rest[-1]
    step, steps = pl.program_id(0), pl.num_programs(0)
    loads = [pltpu.make_async_copy(s, d, load.at[i]) for i, (s, d) in enumerate(zip(small_ins, held))]
    loads.append(pltpu.make_async_copy(dense_any, dense_ref, load.at[3 * small + 2]))
    stores = [pltpu.make_async_copy(s, d, store.at[i]) for i, (s, d) in enumerate(zip(held, small_outs))]

    @pl.when(step == 0)
    def _():
        for copy in loads:
            copy.start()

    total = jnp.sum(jnp.sum(norm_ref[...], axis=0, keepdims=True), axis=1, keepdims=True)
    norm = jnp.sqrt(total)
    clip = THRESHOLD / jnp.maximum(norm, THRESHOLD)
    for i, rate in enumerate((RATE_INNER, RATE_OUTER)):
        grad = large_ins[6 + i][...].astype(jnp.float32)
        state = [ref[...] for ref in large_ins[3 * i : 3 * i + 3]]
        for place, value in zip(large_outs[3 * i : 3 * i + 3], adam_values(*state, grad, clip, rate, DECAY)):
            place[...] = value

    def update(i, grad, rate, decay, columns=slice(None)):
        places = held[3 * i : 3 * i + 3]
        new = adam_values(*(ref[:, columns] for ref in places), grad, clip, rate, decay)
        for place, value in zip(places, new):
            place[:, columns] = value

    @pl.when(step == 1)
    def _():
        for copy in loads:
            copy.wait()
        norm_out[...] = norm
        width = held[3].shape[1]
        trio = 3 * LANES
        for pair in range(width // LANES):
            base = width + pair * trio + (LANES if pair == width // LANES - 1 else 0)
            for kind in range(3):
                update(
                    0,
                    dense_ref[:, base + kind * LANES : base + (kind + 1) * LANES],
                    RATE_PROJECTION,
                    DECAY,
                    slice(kind * width + pair * LANES, kind * width + (pair + 1) * LANES),
                )
        update(1, dense_ref[:, :width], RATE_OUTPUT, DECAY)
        turned = jnp.transpose(dense_ref[:, dense_ref.shape[1] - LANES :])
        update(2, turned[:experts], RATE_ROUTER, DECAY)
        update(3, turned[experts : experts + 7], RATE_VECTORS, 0.0)
        update(4, held[3 * small][...], RATE_HIDDEN, 0.0)
        update(5, held[3 * small + 1][...], RATE_RETURN, 0.0)
        for copy in stores:
            copy.start()

    @pl.when(step == steps - 1)
    def _():
        for copy in stores:
            copy.wait()


def adam_all(experts, squares, dense, states, grads, steps=8):
    full = jnp.float32

    def blocks(array):
        return pl.BlockSpec((array.shape[0] // steps, array.shape[1]), lambda i: (i, 0))

    large = [v for group in states[:2] for v in group]
    small = [v for group in states[2:] for v in group]
    spread = [blocks(v) for v in large]
    held = small + list(grads[2:])
    out = pl.pallas_call(
        functools.partial(adam_kernel, experts),
        grid=(steps,),
        out_shape=[jax.ShapeDtypeStruct(v.shape, full) for v in large + small] + [jax.ShapeDtypeStruct((1, 1), full)],
        in_specs=[pl.BlockSpec(squares.shape, lambda i: (0, 0)), ANY]
        + spread
        + [blocks(v) for v in grads[:2]]
        + [ANY] * len(held),
        out_specs=spread + [ANY] * len(small) + [pl.BlockSpec((1, 1), lambda i: (0, 0))],
        scratch_shapes=[pltpu.VMEM(v.shape, full) for v in held]
        + [
            pltpu.VMEM(dense.shape, full),
            pltpu.SemaphoreType.DMA((len(held) + 1,)),
            pltpu.SemaphoreType.DMA((len(small),)),
        ],
        compiler_params=pltpu.CompilerParams(
            vmem_limit_bytes=60 * 1024 * 1024, dimension_semantics=("arbitrary",)
        ),
        cost_estimate=pl.CostEstimate(flops=5 * 10**7, bytes_accessed=62 * 10**6, transcendentals=10**7),
        name="adam_all",
    )(squares, dense, *large, *grads[:2], *held)
    return [tuple(out[3 * i : 3 * i + 3]) for i in range(len(states))], out[-1].reshape(())


def fits(dp, experts):
    return dp == 2 and experts == 16


def fast_shards(
    dp,
    experts,
    tokens,
    cotangent,
    expert_choice,
    priority,
    projection,
    projection_first,
    projection_second,
    output_weight,
    output_first,
    output_second,
    router_weight,
    router_first,
    router_second,
    vectors,
    vectors_first,
    vectors_second,
    expert_inner,
    inner_first,
    inner_second,
    hidden_bias,
    hidden_first,
    hidden_second,
    expert_outer,
    outer_first,
    outer_second,
    return_bias,
    return_first,
    return_second,
):
    patches = tokens.shape[1]
    capacity = max(2, patches // experts)
    rows, dy, aux, probs, qkv, ctx, mid, second, stat, weights = forward(
        tokens[0],
        cotangent[0],
        expert_choice[0],
        priority[0],
        projection,
        output_weight,
        router_weight,
        vectors,
        dp,
        experts,
        capacity,
        1,
    )
    blocks = (experts, 8, rows.shape[1])
    returned, back_rows, inner_grad, hidden_grad, outer_grad, return_grad, expert_square = mixture(
        rows.reshape(blocks),
        dy.reshape(blocks),
        expert_inner,
        hidden_bias,
        expert_outer,
        return_bias,
        dp,
        2,
    )
    block_output, input_grad, dense, squares = backward(
        tokens[0],
        cotangent[0],
        returned.reshape(rows.shape),
        back_rows.reshape(rows.shape),
        aux,
        probs,
        mid,
        second,
        ctx,
        stat,
        qkv,
        weights,
        expert_square,
        dp,
        experts,
        capacity,
        4,
    )
    states, grad_norm = adam_all(
        experts,
        squares,
        dense,
        [
            (expert_inner[0], inner_first[0], inner_second[0]),
            (expert_outer[0], outer_first[0], outer_second[0]),
            (projection, projection_first, projection_second),
            (output_weight, output_first, output_second),
            (router_weight.T, router_first.T, router_second.T),
            (vectors, vectors_first, vectors_second),
            (hidden_bias, hidden_first, hidden_second),
            (return_bias, return_first, return_second),
        ],
        [inner_grad[0], outer_grad[0], hidden_grad, return_grad],
    )
    inner_new, outer_new, projection_new, output_new, router_new, vectors_new, hidden_new, return_new = states
    return (
        block_output[None],
        input_grad[None],
        grad_norm,
        *projection_new,
        *output_new,
        *(v.T for v in router_new),
        *vectors_new,
        *(v[None] for v in inner_new),
        *hidden_new,
        *(v[None] for v in outer_new),
        *return_new,
    )


def solution(mesh):
    dp, experts = mesh.shape["dp"], mesh.shape["expert"]
    body = functools.partial(fast_shards, dp, experts) if fits(dp, experts) else shards
    return jax.shard_map(
        body,
        mesh=mesh,
        in_specs=(
            P(("dp", "expert"), None, None),
            P(("dp", "expert"), None, None),
            P(("dp", "expert"), None, None),
            P(("dp", "expert"), None),
            P(("dp", "expert"), None),
            P(("dp", "expert"), None),
            P(("dp", "expert"), None),
            P(("dp", "expert"), None),
            P(("dp", "expert"), None),
            P(("dp", "expert"), None),
            P(("dp", "expert"), None),
            P(("dp", "expert"), None),
            P(("dp", "expert"), None),
            P(None, ("dp", "expert")),
            P(None, ("dp", "expert")),
            P(None, ("dp", "expert")),
            P("expert", None, "dp"),
            P("expert", None, "dp"),
            P("expert", None, "dp"),
            P("expert", "dp"),
            P("expert", "dp"),
            P("expert", "dp"),
            P("expert", "dp", None),
            P("expert", "dp", None),
            P("expert", "dp", None),
            P("expert", "dp"),
            P("expert", "dp"),
            P("expert", "dp"),
        ),
        out_specs=(
            P(("dp", "expert"), None, None),
            P(("dp", "expert"), None, None),
            P(),
            P(("dp", "expert"), None),
            P(("dp", "expert"), None),
            P(("dp", "expert"), None),
            P(("dp", "expert"), None),
            P(("dp", "expert"), None),
            P(("dp", "expert"), None),
            P(("dp", "expert"), None),
            P(("dp", "expert"), None),
            P(("dp", "expert"), None),
            P(None, ("dp", "expert")),
            P(None, ("dp", "expert")),
            P(None, ("dp", "expert")),
            P("expert", None, "dp"),
            P("expert", None, "dp"),
            P("expert", None, "dp"),
            P("expert", "dp"),
            P("expert", "dp"),
            P("expert", "dp"),
            P("expert", "dp", None),
            P("expert", "dp", None),
            P("expert", "dp", None),
            P("expert", "dp"),
            P("expert", "dp"),
            P("expert", "dp"),
        ),
        check_vma=False,
    )
```

```python
import functools

import jax
import jax.numpy as jnp
from jax import lax
from jax.experimental import pallas as pl
from jax.experimental.pallas import tpu as pltpu
from jax.sharding import PartitionSpec as P

HEADS = 12
HEAD_DIM = 64
STEP = 10


NORM_EPS = 1e-06
ADAM_EPS = 1e-08
BETA_ONE = 0.9
BETA_TWO = 0.999
DECAY = 0.1
THRESHOLD = 1.0
RATE_PROJECTION = 0.1
RATE_OUTPUT = 1.0
RATE_ROUTER = 0.05
RATE_VECTORS = 0.5
RATE_INNER = 0.1
RATE_HIDDEN = 0.25
RATE_OUTER = 1.5
RATE_RETURN = 2.0


def layer_norm(values, norm_gain, norm_bias):
    center = values - jnp.mean(values, axis=-1, keepdims=True)
    spread = jnp.mean(center * center, axis=-1, keepdims=True)
    return center * lax.rsqrt(spread + NORM_EPS) * norm_gain + norm_bias


def smooth_gate(values):
    return jax.nn.gelu(values, approximate=True)


def mixed_dot(left, right):
    return jnp.dot(left, right, preferred_element_type=jnp.float32)


def rows_product(left, right):
    return lax.dot_general(
        left, right, (((0,), (0,)), ((), ())), preferred_element_type=jnp.float32
    )


def columns_product(left, right):
    return lax.dot_general(
        left, right, (((1,), (1,)), ((), ())), preferred_element_type=jnp.float32
    )


def assign_slots(chosen, claim_order, expert_count, capacity):
    patches = chosen.shape[0]
    top_count = chosen.shape[1]
    claim_rank = (
        jnp.arange(top_count, dtype=jnp.int32)[None, :] * patches + claim_order[:, None]
    ).T.reshape(-1)
    flat_choice = chosen.T.reshape(-1)
    onehot = (flat_choice[:, None] == jnp.arange(expert_count, dtype=jnp.int32)[None, :]).astype(
        jnp.float32
    )
    earlier = (claim_rank[None, :] < claim_rank[:, None]).astype(jnp.float32)
    counts = jnp.dot(
        earlier, onehot, precision=lax.Precision.HIGHEST, preferred_element_type=jnp.float32
    )
    position = jnp.sum(counts * onehot, axis=1).astype(jnp.int32).reshape(top_count, patches).T
    kept_mask = position < capacity
    flat_slot = chosen * capacity + jnp.minimum(position, capacity - 1)
    return (flat_slot, kept_mask)


def slot_matches(flat_slot, kept_mask, slot_count):
    slot_ids = jnp.arange(slot_count, dtype=jnp.int32)
    return (flat_slot[None, :, :] == slot_ids[:, None, None]) & kept_mask[None, :, :]


def select_gates(logits, chosen, expert_count):
    router_probs = jax.nn.softmax(logits, axis=-1)
    onehot = chosen[:, :, None] == jnp.arange(expert_count, dtype=jnp.int32)[None, None, :]
    return jnp.sum(jnp.where(onehot, router_probs[:, None, :], 0.0), axis=2)


def adam_update(weight, first_state, second, gradient, clip_factor, step_rate, decay_rate):
    scaled = gradient * clip_factor
    first_new = BETA_ONE * first_state + (1.0 - BETA_ONE) * scaled
    second_new = BETA_TWO * second + (1.0 - BETA_TWO) * scaled * scaled
    first_hat = first_new / (1.0 - BETA_ONE**STEP)
    second_hat = second_new / (1.0 - BETA_TWO**STEP)
    weight_new = weight - step_rate * (
        first_hat / (jnp.sqrt(second_hat) + ADAM_EPS) + decay_rate * weight
    )
    return (weight_new, first_new, second_new)


def shards(
    tokens,
    cotangent,
    expert_choice,
    priority,
    projection,
    projection_first,
    projection_second,
    output_weight,
    output_first,
    output_second,
    router_weight,
    router_first,
    router_second,
    vectors,
    vectors_first,
    vectors_second,
    expert_inner,
    inner_first,
    inner_second,
    hidden_bias,
    hidden_first,
    hidden_second,
    expert_outer,
    outer_first,
    outer_second,
    return_bias,
    return_first,
    return_second,
):
    model_width = tokens.shape[2]
    patches = tokens.shape[1]
    experts = lax.axis_size("expert")
    capacity = max(2, patches // experts)
    slot_count = experts * capacity
    score_scale = HEAD_DIM ** (-0.5)
    dense_shards = (
        projection.astype(jnp.bfloat16),
        output_weight.astype(jnp.bfloat16),
        router_weight.astype(jnp.bfloat16),
        vectors.astype(jnp.bfloat16),
    )
    partial_shards = (
        lax.all_gather(dense_shards[0], "expert", axis=0, tiled=True),
        lax.all_gather(dense_shards[1], "expert", axis=0, tiled=True),
        lax.all_gather(dense_shards[2], "expert", axis=0, tiled=True),
        lax.all_gather(dense_shards[3], "expert", axis=1, tiled=True),
    )
    whole_projection, whole_output, whole_router, whole_vectors = (
        lax.all_gather(partial_shards[0], "dp", axis=0, tiled=True),
        lax.all_gather(partial_shards[1], "dp", axis=0, tiled=True),
        lax.all_gather(partial_shards[2], "dp", axis=0, tiled=True),
        lax.all_gather(partial_shards[3], "dp", axis=1, tiled=True),
    )
    inner_low = expert_inner.astype(jnp.bfloat16)
    hidden_low = hidden_bias.astype(jnp.bfloat16)
    outer_low = expert_outer.astype(jnp.bfloat16)
    return_low = return_bias.astype(jnp.bfloat16)
    inner_all, hidden_all, outer_all, return_all = (
        lax.all_gather(inner_low, "dp", axis=2, tiled=True),
        lax.all_gather(hidden_low, "dp", axis=1, tiled=True),
        lax.all_gather(outer_low, "dp", axis=1, tiled=True),
        lax.all_gather(return_low, "dp", axis=1, tiled=True),
    )
    vector_rows = whole_vectors.astype(jnp.float32)
    image_rows = tokens[0].astype(jnp.float32)
    normed_one, norm_back_one = jax.vjp(layer_norm, image_rows, vector_rows[0], vector_rows[1])
    normed_low = normed_one.astype(jnp.bfloat16)
    projected = mixed_dot(normed_low, whole_projection)
    queries = (
        (projected[:, :model_width] + vector_rows[2])
        .astype(jnp.bfloat16)
        .reshape(patches, HEADS, HEAD_DIM)
    )
    key_rows = (
        projected[:, model_width : 2 * model_width]
        .astype(jnp.bfloat16)
        .reshape(patches, HEADS, HEAD_DIM)
    )
    value_rows = (
        (projected[:, 2 * model_width :] + vector_rows[3])
        .astype(jnp.bfloat16)
        .reshape(patches, HEADS, HEAD_DIM)
    )
    scores = (
        jnp.einsum("qhd,khd->hqk", queries, key_rows, preferred_element_type=jnp.float32)
        * score_scale
    )
    score_top = jnp.max(scores, axis=-1, keepdims=True)
    raised = jnp.exp(scores - score_top)
    totals = jnp.sum(raised, axis=-1, keepdims=True)
    attention = raised / totals
    log_total = score_top + jnp.log(totals)
    context = (
        jnp.einsum(
            "hqk,khd->qhd",
            attention.astype(jnp.bfloat16),
            value_rows,
            preferred_element_type=jnp.float32,
        )
        .reshape(patches, model_width)
        .astype(jnp.bfloat16)
    )
    middle = image_rows + (mixed_dot(context, whole_output) + vector_rows[4])
    normed_two, norm_back_two = jax.vjp(layer_norm, middle, vector_rows[5], vector_rows[6])
    second_low = normed_two.astype(jnp.bfloat16)
    logits = mixed_dot(second_low, whole_router)
    chosen = expert_choice[0]

    def gate_choice(values):
        return select_gates(values, chosen, experts)

    gate_values, gate_back = jax.vjp(gate_choice, logits)
    flat_slot, kept_mask = assign_slots(chosen, priority[0], experts, capacity)
    matches = slot_matches(flat_slot, kept_mask, slot_count)
    slot_table = jnp.any(matches, axis=2).astype(jnp.bfloat16)
    dispatched = (
        mixed_dot(slot_table, second_low)
        .astype(jnp.bfloat16)
        .reshape(experts, capacity, model_width)
    )
    arrived = lax.all_to_all(dispatched, "expert", split_axis=0, concat_axis=0, tiled=True).reshape(
        slot_count, model_width
    )
    pre_act = mixed_dot(arrived, inner_all[0]) + hidden_all[0].astype(jnp.float32)
    activated, gelu_back = jax.vjp(smooth_gate, pre_act)
    active_low = activated.astype(jnp.bfloat16)
    expert_out = (mixed_dot(active_low, outer_all[0]) + return_all[0].astype(jnp.float32)).astype(
        jnp.bfloat16
    )
    returned = lax.all_to_all(
        expert_out.reshape(experts, capacity, model_width),
        "expert",
        split_axis=0,
        concat_axis=0,
        tiled=True,
    ).reshape(slot_count, model_width)
    picked = returned[flat_slot].astype(jnp.float32)
    weighted = jnp.where(kept_mask, gate_values, 0.0)
    final = middle + jnp.sum(weighted[:, :, None] * picked, axis=1)
    block_output = final.astype(jnp.bfloat16)[None]
    upstream = cotangent[0].astype(jnp.float32)
    gate_grad = jnp.where(kept_mask, jnp.sum(upstream[:, None, :] * picked, axis=2), 0.0)
    slot_gate = jnp.sum(jnp.where(matches, weighted[None, :, :], 0.0), axis=(1, 2))
    slot_grad = (mixed_dot(slot_table, cotangent[0]) * slot_gate[:, None]).astype(jnp.bfloat16)
    sent_grad = lax.all_to_all(
        slot_grad.reshape(experts, capacity, model_width),
        "expert",
        split_axis=0,
        concat_axis=0,
        tiled=True,
    ).reshape(slot_count, model_width)
    outer_grad = rows_product(active_low, sent_grad)
    return_grad = jnp.sum(sent_grad, axis=0, dtype=jnp.float32)
    active_grad = columns_product(sent_grad, outer_all[0])
    (pre_grad,) = gelu_back(active_grad)
    pre_low = pre_grad.astype(jnp.bfloat16)
    inner_grad = rows_product(arrived, pre_low)
    hidden_grad = jnp.sum(pre_low, axis=0, dtype=jnp.float32)
    row_grad = columns_product(pre_low, inner_all[0]).astype(jnp.bfloat16)
    expert_grads = (
        lax.psum_scatter(
            inner_grad[None].astype(jnp.bfloat16), "dp", scatter_dimension=2, tiled=True
        ).astype(jnp.float32),
        lax.psum_scatter(
            hidden_grad[None].astype(jnp.bfloat16), "dp", scatter_dimension=1, tiled=True
        ).astype(jnp.float32),
        lax.psum_scatter(
            outer_grad[None].astype(jnp.bfloat16), "dp", scatter_dimension=1, tiled=True
        ).astype(jnp.float32),
        lax.psum_scatter(
            return_grad[None].astype(jnp.bfloat16), "dp", scatter_dimension=1, tiled=True
        ).astype(jnp.float32),
    )
    back_rows = lax.all_to_all(
        row_grad.reshape(experts, capacity, model_width),
        "expert",
        split_axis=0,
        concat_axis=0,
        tiled=True,
    ).reshape(slot_count, model_width)
    (logit_grad,) = gate_back(gate_grad)
    logit_low = logit_grad.astype(jnp.bfloat16)
    router_grad = rows_product(second_low, logit_low)
    second_grad = rows_product(slot_table, back_rows) + columns_product(logit_low, whole_router)
    middle_part, gain_two_grad, bias_two_grad = norm_back_two(second_grad)
    middle_grad = upstream + middle_part
    branch_low = middle_grad.astype(jnp.bfloat16)
    output_grad = rows_product(context, branch_low)
    out_bias_grad = jnp.sum(branch_low, axis=0, dtype=jnp.float32)
    context_grad = (
        columns_product(branch_low, whole_output)
        .astype(jnp.bfloat16)
        .reshape(patches, HEADS, HEAD_DIM)
    )
    scores = (
        jnp.einsum("qhd,khd->hqk", queries, key_rows, preferred_element_type=jnp.float32)
        * score_scale
    )
    attention = jnp.exp(scores - log_total)
    attention_grad = jnp.einsum(
        "qhd,khd->hqk", context_grad, value_rows, preferred_element_type=jnp.float32
    )
    value_grad = jnp.einsum(
        "hqk,qhd->khd",
        attention.astype(jnp.bfloat16),
        context_grad,
        preferred_element_type=jnp.float32,
    ).astype(jnp.bfloat16)
    centered = jnp.sum(attention * attention_grad, axis=-1, keepdims=True)
    score_grad = (attention * (attention_grad - centered)).astype(jnp.bfloat16)
    query_grad = (
        (
            jnp.einsum("hqk,khd->qhd", score_grad, key_rows, preferred_element_type=jnp.float32)
            * score_scale
        )
        .astype(jnp.bfloat16)
        .reshape(patches, model_width)
    )
    key_grad = (
        (
            jnp.einsum("hqk,qhd->khd", score_grad, queries, preferred_element_type=jnp.float32)
            * score_scale
        )
        .astype(jnp.bfloat16)
        .reshape(patches, model_width)
    )
    value_flat = value_grad.reshape(patches, model_width)
    joined_grad = jnp.concatenate([query_grad, key_grad, value_flat], axis=1)
    projection_grad = rows_product(normed_low, joined_grad)
    normed_grad = columns_product(joined_grad, whole_projection)
    input_part, gain_one_grad, bias_one_grad = norm_back_one(normed_grad)
    input_grad = (middle_grad + input_part)[None]
    vector_grad = jnp.stack(
        [
            gain_one_grad,
            bias_one_grad,
            jnp.sum(query_grad, axis=0, dtype=jnp.float32),
            jnp.sum(value_flat, axis=0, dtype=jnp.float32),
            out_bias_grad,
            gain_two_grad,
            bias_two_grad,
        ]
    )
    local_grads = (projection_grad, output_grad, router_grad, vector_grad)
    partial_grads = (
        lax.psum_scatter(
            local_grads[0].astype(jnp.bfloat16), "dp", scatter_dimension=0, tiled=True
        ).astype(jnp.float32),
        lax.psum_scatter(
            local_grads[1].astype(jnp.bfloat16), "dp", scatter_dimension=0, tiled=True
        ).astype(jnp.float32),
        lax.psum_scatter(
            local_grads[2].astype(jnp.bfloat16), "dp", scatter_dimension=0, tiled=True
        ).astype(jnp.float32),
        lax.psum_scatter(
            local_grads[3].astype(jnp.bfloat16), "dp", scatter_dimension=1, tiled=True
        ).astype(jnp.float32),
    )
    dense_grads = (
        lax.psum_scatter(
            partial_grads[0].astype(jnp.bfloat16), "expert", scatter_dimension=0, tiled=True
        ).astype(jnp.float32),
        lax.psum_scatter(
            partial_grads[1].astype(jnp.bfloat16), "expert", scatter_dimension=0, tiled=True
        ).astype(jnp.float32),
        lax.psum_scatter(
            partial_grads[2].astype(jnp.bfloat16), "expert", scatter_dimension=0, tiled=True
        ).astype(jnp.float32),
        lax.psum_scatter(
            partial_grads[3].astype(jnp.bfloat16), "expert", scatter_dimension=1, tiled=True
        ).astype(jnp.float32),
    )
    all_grads = tuple(dense_grads) + tuple(expert_grads)
    local_square = jnp.sum(all_grads[0] * all_grads[0])
    for gradient in all_grads[1:]:
        local_square = local_square + jnp.sum(gradient * gradient)
    square_total = lax.psum(local_square, ("dp", "expert"))
    grad_norm = jnp.sqrt(square_total)
    clip_factor = THRESHOLD / jnp.maximum(grad_norm, THRESHOLD)
    projection_next, projection_moment, projection_square = adam_update(
        projection,
        projection_first,
        projection_second,
        all_grads[0],
        clip_factor,
        RATE_PROJECTION,
        DECAY,
    )
    output_next, output_moment, output_square = adam_update(
        output_weight, output_first, output_second, all_grads[1], clip_factor, RATE_OUTPUT, DECAY
    )
    router_next, router_moment, router_square = adam_update(
        router_weight, router_first, router_second, all_grads[2], clip_factor, RATE_ROUTER, DECAY
    )
    vectors_next, vectors_moment, vectors_square = adam_update(
        vectors, vectors_first, vectors_second, all_grads[3], clip_factor, RATE_VECTORS, 0.0
    )
    inner_next, inner_moment, inner_square = adam_update(
        expert_inner, inner_first, inner_second, all_grads[4], clip_factor, RATE_INNER, DECAY
    )
    hidden_next, hidden_moment, hidden_square = adam_update(
        hidden_bias, hidden_first, hidden_second, all_grads[5], clip_factor, RATE_HIDDEN, 0.0
    )
    outer_next, outer_moment, outer_square = adam_update(
        expert_outer, outer_first, outer_second, all_grads[6], clip_factor, RATE_OUTER, DECAY
    )
    return_next, return_moment, return_square = adam_update(
        return_bias, return_first, return_second, all_grads[7], clip_factor, RATE_RETURN, 0.0
    )
    return (
        block_output,
        input_grad,
        grad_norm,
        projection_next,
        projection_moment,
        projection_square,
        output_next,
        output_moment,
        output_square,
        router_next,
        router_moment,
        router_square,
        vectors_next,
        vectors_moment,
        vectors_square,
        inner_next,
        inner_moment,
        inner_square,
        hidden_next,
        hidden_moment,
        hidden_square,
        outer_next,
        outer_moment,
        outer_square,
        return_next,
        return_moment,
        return_square,
    )


MESH = pl.DeviceIdType.MESH
ANY = pl.BlockSpec(memory_space=pl.ANY)
VMEM = pl.BlockSpec(memory_space=pltpu.VMEM)


class Place:
    def __init__(self, dp, experts):
        self.dp, self.experts = dp, experts
        self.ys = 2
        self.zs = experts // 4
        self.a = lax.axis_index("dp")
        self.e = lax.axis_index("expert")
        self.core = lax.rem(self.e, 2)
        self.y = lax.rem(lax.div(self.e, 2), self.ys)
        self.z = lax.div(self.e, 2 * self.ys)

    def chip_of(self, core, dz, s2, s3):
        zz = lax.rem(self.z + dz, self.zs)
        if s2 == s3:
            fa = fy = s2
        elif s2:
            fa, fy = core, 1 - core
        else:
            fa, fy = 1 - core, core
        aa = lax.rem(self.a + fa, 2)
        yy = lax.rem(self.y + fy, 2)
        return aa, zz, yy

    def device(self, core, dz, s2, s3, own_core=None):
        aa, zz, yy = self.chip_of(core, dz, s2, s3)
        c = core if own_core is None else own_core
        return (aa, (zz * self.ys + yy) * 2 + c)

    def flat(self, dev):
        return dev[0] * self.experts + dev[1]

    def chip(self, core, dz, s2, s3):
        aa, zz, yy = self.chip_of(core, dz, s2, s3)
        return (aa * self.zs + zz) * self.ys + yy


def remote(src, dst, send, recv, dev):
    return pltpu.make_async_remote_copy(src_ref=src, dst_ref=dst, send_sem=send, recv_sem=recv, device_id=dev, device_id_type=MESH)


def greet(devices):
    barrier = pltpu.get_barrier_semaphore()
    for dev in devices:
        pl.semaphore_signal(barrier, inc=1, device_id=dev, device_id_type=MESH)
    pl.semaphore_wait(barrier, len(devices))


def split_index(k, zs):
    return k % zs, (k // zs) % 2, k // (2 * zs)


LANES = 128


def nn(left, right):
    return lax.dot_general(left, right, (((1,), (0,)), ((), ())), preferred_element_type=jnp.float32)


def nt(left, right):
    return lax.dot_general(left, right, (((1,), (1,)), ((), ())), preferred_element_type=jnp.float32)


def lane_ids(rows, start=0):
    return lax.broadcasted_iota(jnp.int32, (rows, LANES), 1) + start


def row_parts(count, size):
    return [pl.ds(i * size, size) for i in range(count // size)]


def norm_parts(values):
    center = values - jnp.mean(values, axis=-1, keepdims=True)
    inverse = lax.rsqrt(jnp.mean(center * center, axis=-1, keepdims=True) + NORM_EPS)
    return center * inverse, inverse


def vector_table(weights, width):
    return jnp.transpose(weights[:, 4 * width :].astype(jnp.float32))


def forward_kernel(
    dp,
    experts,
    capacity,
    chunk,
    tok_ref,
    cot_ref,
    choice_ref,
    rank_row,
    projection_ref,
    output_ref,
    router_ref,
    vectors_ref,
    rows_ref,
    dy_ref,
    aux_ref,
    probs_ref,
    qkv_any,
    ctx_any,
    mid_any,
    second_any,
    stat_any,
    weights_any,
    qkv_ref,
    ctx_ref,
    mid_ref,
    second_ref,
    stat_ref,
    weights,
    vec,
    normed,
    mine,
    theirs,
    land_first,
    land,
    pre_send,
    pre_recv,
    line_send,
    line_recv,
    second_send,
    second_recv,
    third_send,
    third_recv,
    core_send,
    core_recv,
    store,
):
    low, full32 = jnp.bfloat16, jnp.float32
    patches, width = tok_ref.shape
    half = width // 2
    trio_width = 3 * LANES
    p = Place(dp, experts)
    c, zs = p.core, p.zs
    deep = projection_ref.shape[0]
    partner = (p.a, p.e + 1 - 2 * c)
    second, third = p.device(c, 0, 1, 0), p.device(c, 0, 0, 1)
    peers = [p.device(c, dz, 0, 0) for dz in range(1, zs)]
    narrow = jnp.concatenate(
        [router_ref[...], vectors_ref[...], jnp.zeros((LANES - experts - vectors_ref.shape[0], deep), full32)], axis=0
    )
    for h in range(2):
        mine[h, :, :LANES] = jnp.transpose(narrow) if h == 0 else jnp.zeros((deep, LANES), full32)
        for i in range(width // LANES // 2):
            for kind in range(3):
                at = kind * width + (2 * i + h) * LANES
                mine[h, :, LANES + i * trio_width + kind * LANES : LANES + i * trio_width + (kind + 1) * LANES] = (
                    projection_ref[:, at : at + LANES]
                )
        mine[h, :, LANES + 3 * half :] = output_ref[:, h * half : (h + 1) * half]
    greet(peers + [second, third, partner])
    before_all = remote(mine.at[1 - c], theirs, pre_send, pre_recv, partner)
    before_all.start()
    lanes = lane_ids(patches)
    named = jnp.concatenate([choice_ref[...], rank_row[...]], axis=0).astype(full32)
    named = jnp.transpose(jnp.concatenate([named, jnp.zeros((LANES - 3, patches), full32)], axis=0))
    first, other = named[:, 0:1].astype(jnp.int32), named[:, 1:2].astype(jnp.int32)
    is_first, is_other = lanes == first, lanes == other
    chunks = width // LANES // 2 + 1
    lands = [land_first] + [land.at[i] for i in range(chunks - 1)]
    my_line = p.a * p.ys + p.y
    second_line = jnp.where(c == 0, p.a * p.ys + 1 - p.y, (1 - p.a) * p.ys + p.y)
    third_lines = [
        jnp.where(c == 0, (1 - p.a) * p.ys + p.y, p.a * p.ys + 1 - p.y),
        (1 - p.a) * p.ys + 1 - p.y,
    ]

    def line_copy(i, dz):
        block = lands[i].at[c, my_line, p.z]
        return remote(block, block, line_send.at[i, dz], line_recv.at[i, dz], peers[dz - 1])

    def second_copy(i):
        block = lands[i].at[c, my_line]
        return remote(block, block, second_send.at[i], second_recv.at[i], second)

    def third_copy(i, which):
        block = lands[i].at[c, my_line if which == 0 else second_line]
        return remote(block, block, third_send.at[i, which], third_recv.at[i, which], third)

    def core_copy(i, which):
        block = lands[i].at[c, (my_line, second_line, *third_lines)[which]]
        return remote(block, block, core_send.at[i, which], core_recv.at[i, which], partner)

    def step0(i):
        for dz in range(1, zs):
            line_copy(i, dz).start()

    def step1(i):
        for dz in range(1, zs):
            block = lands[i].at[c, my_line, lax.rem(p.z + zs - dz, zs)]
            remote(block, block, line_send.at[i, dz], line_recv.at[i, dz], partner).wait_recv()
        third_copy(i, 0).start()
        second_copy(i).start()
        core_copy(i, 0).start()

    def step2(i):
        second_copy(i).wait_recv()
        third_copy(i, 1).start()
        core_copy(i, 1).start()

    def step3(i):
        for which in range(2):
            third_copy(i, which).wait_recv()
            core_copy(i, 2 + which).start()

    def unpack(i):
        for which in range(4):
            core_copy(i, which).wait_recv()
        for line in range(2 * p.ys):
            for z in range(zs):
                at = (line // p.ys * zs + z) * p.ys + line % p.ys
                rows = pl.ds(2 * deep * at, 2 * deep)
                for h in range(2):
                    if i == 0:
                        weights[rows, h * trio_width : (h + 1) * trio_width] = land_first[h, line, z, :, LANES:]
                    else:
                        columns = pl.ds((2 * i + h) * half, half)
                        weights[rows, columns] = land[i - 1, h, line, z]
                if i == 0:
                    weights[rows, 4 * width :] = land_first[0, line, z, :, :LANES]

    before_all.wait_recv()
    own, their = mine[c], theirs[...]
    top, bottom = jnp.where(c == 0, own, their), jnp.where(c == 0, their, own)
    block = jnp.concatenate([top, bottom], axis=0).astype(low)
    land_first[c, my_line, p.z] = block[:, : LANES + half]
    for i in range(1, chunks):
        land[i - 1, c, my_line, p.z] = block[:, LANES + i * half : LANES + (i + 1) * half]
    for i in range(chunks):
        step0(i)
    earlier = (rank_row[...].astype(full32) < named[:, 2:3]).astype(full32).astype(low)
    hot = (is_first | (lanes == other + experts)).astype(full32)
    counts = nn(earlier, hot.astype(low))
    totals = jnp.sum(hot, axis=0, keepdims=True)
    place_first = jnp.sum(jnp.where(is_first, counts, 0.0), axis=1, keepdims=True)
    place_other = jnp.sum(
        jnp.where(lanes == other + experts, counts, 0.0) + jnp.where(is_other, totals, 0.0), axis=1, keepdims=True
    )
    aux_ref[...] = jnp.where(lanes == 0, place_first, jnp.where(lanes == 1, place_other, 0.0))

    def row(i):
        return vec[experts + i : experts + i + 1, :]

    def attend(pair):
        at = pair * LANES
        trio = pair * trio_width
        product = nn(normed[...], weights[:, trio : trio + trio_width])
        queries_all = (product[:, :LANES] + vec[experts + 2 : experts + 3, at : at + LANES]).astype(low)
        keys = product[:, LANES : 2 * LANES].astype(low)
        values = (product[:, 2 * LANES :] + vec[experts + 3 : experts + 4, at : at + LANES]).astype(low)
        qkv_ref[:, trio : trio + LANES] = queries_all
        qkv_ref[:, trio + LANES : trio + 2 * LANES] = keys
        qkv_ref[:, trio + 2 * LANES : trio + 3 * LANES] = values
        key_lanes = lane_ids(patches)
        values_two = [
            jnp.where(key_lanes < HEAD_DIM, values, (key_lanes == HEAD_DIM).astype(full32).astype(low)),
            jnp.where(key_lanes >= HEAD_DIM, values, (key_lanes == 0).astype(full32).astype(low)),
        ]
        for part in row_parts(patches, chunk):
            own_lanes = lane_ids(chunk)
            queries = qkv_ref[part, trio : trio + LANES] * jnp.asarray(HEAD_DIM**-0.5, low)
            outs = []
            stat = stat_ref[part, :]
            for head in range(2):
                side = (own_lanes < HEAD_DIM) if head == 0 else (own_lanes >= HEAD_DIM)
                scores = nt(jnp.where(side, queries, jnp.zeros_like(queries)), keys)
                peak = jnp.max(scores, axis=1, keepdims=True)
                raised = jnp.exp(scores - peak)
                mixed = nn(raised.astype(low), values_two[head])
                spare = HEAD_DIM if head == 0 else 0
                total = mixed[:, spare : spare + 1]
                outs.append(mixed / total)
                stat = jnp.where(own_lanes == 2 * pair + head, peak + jnp.log(total), stat)
            stat_ref[part, :] = stat
            ctx_ref[part, at : at + LANES] = jnp.where(own_lanes < HEAD_DIM, outs[0], outs[1]).astype(low)

    stat_ref[...] = jnp.zeros_like(stat_ref)
    step1(0)
    step1(1)
    step2(0)
    step1(2)
    step2(1)
    step3(0)
    step1(3)
    unpack(0)
    vec[...] = vector_table(weights, width)
    for part in row_parts(patches, chunk):
        unit, _ = norm_parts(tok_ref[part, :].astype(full32))
        normed[part, :] = (unit * row(0) + row(1)).astype(low)
    step2(2)
    step3(1)
    attend(0)
    step2(3)
    attend(1)
    step3(2)
    unpack(1)
    attend(2)
    step3(3)
    attend(3)
    unpack(2)
    attend(4)
    attend(5)
    unpack(3)
    kept = [(weights, weights_any), (qkv_ref, qkv_any), (ctx_ref, ctx_any), (stat_ref, stat_any)]
    kept += [(mid_ref, mid_any), (second_ref, second_any)]
    keep = [pltpu.make_async_copy(s, d, store.at[i]) for i, (s, d) in enumerate(kept)]
    for copy in keep[:4]:
        copy.start()
    third_columns = 256
    for j in range(width // third_columns):
        columns = pl.ds(j * third_columns, third_columns)
        product = nn(ctx_ref[...], weights[:, pl.ds(3 * width + j * third_columns, third_columns)])
        mid_ref[:, columns] = tok_ref[:, columns].astype(full32) + (product + vec[experts + 4 : experts + 5, columns])
    for part in row_parts(patches, chunk):
        unit, _ = norm_parts(mid_ref[part, :])
        second_ref[part, :] = (unit * row(5) + row(6)).astype(low)
    keep[4].start()
    keep[5].start()
    logits = jnp.where(lanes < experts, nn(second_ref[...], weights[:, 4 * width :]), -1e30)
    raised = jnp.exp(logits - jnp.max(logits, axis=1, keepdims=True))
    probs = raised / jnp.sum(raised, axis=1, keepdims=True)
    probs_ref[...] = probs
    place_first, place_other = aux_ref[:, 0:1], aux_ref[:, 1:2]

    def slot_of(place, expert):
        place = place.astype(jnp.int32)
        kept = place < capacity
        slot = (place // 8) * LANES + expert * 8 + place % 8
        tail = kept & (place >= capacity - 4)
        return kept, jnp.where(kept, slot, -1), jnp.where(tail, slot + 4, -1)

    aux = jnp.zeros((patches, LANES), jnp.float32)
    for j, (place, expert, hit) in enumerate(((place_first, first, is_first), (place_other, other, is_other))):
        kept, slot, twin = slot_of(place, expert)
        gate = jnp.where(kept, jnp.sum(jnp.where(hit, probs, 0.0), axis=1, keepdims=True), 0.0)
        for lane, column in ((j, slot.astype(jnp.float32)), (2 + j, twin.astype(jnp.float32)), (4 + j, gate), (6 + j, expert.astype(jnp.float32))):
            aux = jnp.where(lanes == lane, column, aux)
    aux_ref[...] = aux
    turned = jnp.transpose(aux)
    slots = [turned[i : i + 1, :] for i in range(4)]
    gates = [turned[4 + i : 5 + i, :] for i in range(2)]
    full = capacity // 8
    for i in range(full + 1):
        ids = (lax.broadcasted_iota(jnp.int32, (LANES, patches), 0) + i * LANES).astype(jnp.float32)
        hits = [ids == slots[0], ids == slots[1]]
        if i == full:
            hits = [hits[0] | (ids == slots[2]), hits[1] | (ids == slots[3])]
        table = (hits[0] | hits[1]).astype(jnp.float32).astype(low)
        gate = jnp.sum(
            jnp.where(hits[0], gates[0], 0.0) + jnp.where(hits[1], gates[1], 0.0), axis=1, keepdims=True
        )
        sent = nn(table, second_ref[...])
        back = nn(table, cot_ref[...]) * gate
        columns = pl.ds(i * width, width)
        if i == full:
            columns = pl.ds(i * width, width // 2)
            left = lax.broadcasted_iota(jnp.int32, (LANES, width // 2), 0) % 8 < 4
            sent = jnp.where(left, sent[:, : width // 2], sent[:, width // 2 :])
            back = jnp.where(left, back[:, : width // 2], back[:, width // 2 :])
        rows_ref[:, columns] = sent.astype(low)
        dy_ref[:, columns] = back.astype(low)
    for copy in keep:
        copy.wait()
    before_all.wait_send()
    for i in range(chunks):
        for dz in range(1, zs):
            line_copy(i, dz).wait_send()
        second_copy(i).wait_send()
        for which in range(2):
            third_copy(i, which).wait_send()
        for which in range(4):
            core_copy(i, which).wait_send()


def forward(
    tokens,
    cotangent,
    choice,
    priority,
    projection,
    output_weight,
    router_weight,
    vectors,
    dp,
    experts,
    capacity,
    cid,
    chunk=576,
):
    patches, width = tokens.shape
    low, full = jnp.bfloat16, jnp.float32
    packed = (8 * experts, capacity * width // 8)
    shapes = [
        (packed, low),
        (packed, low),
        ((patches, LANES), full),
        ((patches, LANES), full),
        ((patches, 3 * width), low),
        ((patches, width), low),
        ((patches, width), full),
        ((patches, width), low),
        ((patches, LANES), full),
        ((width, 4 * width + LANES), low),
    ]
    deep, half = projection.shape[0], width // 2
    chunks = width // LANES // 2 + 1
    zs = experts // 4
    lines = dp * experts // 2 // zs
    dma = pltpu.SemaphoreType.DMA
    return pl.pallas_call(
        functools.partial(forward_kernel, dp, experts, capacity, chunk),
        out_shape=[jax.ShapeDtypeStruct(*s) for s in shapes],
        in_specs=[VMEM] * 8,
        out_specs=[VMEM] * 4 + [ANY] * 6,
        scratch_shapes=[
            *(pltpu.VMEM(*shape) for shape in shapes[4:]),
            pltpu.VMEM((LANES, width), full),
            pltpu.VMEM((patches, width), low),
            pltpu.VMEM((2, deep, LANES + 4 * half), full),
            pltpu.VMEM((deep, LANES + 4 * half), full),
            pltpu.VMEM((2, lines, zs, 2 * deep, LANES + half), low),
            pltpu.VMEM((chunks - 1, 2, lines, zs, 2 * deep, half), low),
            dma,
            dma,
            dma((chunks, zs)),
            dma((chunks, zs)),
            dma((chunks,)),
            dma((chunks,)),
            dma((chunks, 2)),
            dma((chunks, 2)),
            dma((chunks, 4)),
            dma((chunks, 4)),
            dma((6,)),
        ],
        compiler_params=pltpu.CompilerParams(
            collective_id=cid, has_side_effects=True, vmem_limit_bytes=60 * 1024 * 1024
        ),
        cost_estimate=pl.CostEstimate(flops=6 * 10**9, bytes_accessed=20 * 10**6, transcendentals=4 * 10**6),
        name="attend_forward",
    )(
        tokens,
        cotangent,
        choice.T,
        priority.reshape(1, patches),
        projection,
        output_weight,
        router_weight.T,
        vectors,
    )


def gelu_both(z):
    root = 0.7978845608028654
    square = z * z
    slope = jnp.tanh(root * z * (1.0 + 0.044715 * square))
    half = 0.5 * (1.0 + slope)
    act = z * half
    grad = half + 0.5 * z * (1.0 - slope * slope) * (root * (1.0 + 3 * 0.044715 * square))
    return act, grad


def tail_picks(count, right):
    rows = lax.broadcasted_iota(jnp.int32, (count // 2, count), 0)
    ids = lax.broadcasted_iota(jnp.int32, (count // 2, count), 1)
    hit = ids == (rows // 4) * 8 + rows % 4 + (4 if right else 0)
    return hit.astype(jnp.float32).astype(jnp.bfloat16)


class Stages:
    def __init__(self, place, refs):
        (self.grads, self.other, self.give3, self.take3, self.give2, self.take2, self.givez, self.takez, self.total) = refs[:9]
        (self.cs, self.cr, self.s3, self.r3, self.s2, self.r2, self.sz, self.rz) = refs[9:]
        self.p, self.zs, self.core = place, place.zs, place.core
        self.partner = (place.a, place.e + 1 - 2 * place.core)

    def to_partner(self, c):
        return remote(
            self.grads.at[c, 1 - self.core], self.other.at[c], self.cs.at[c], self.cr.at[c], self.partner
        )

    def to_third(self, c):
        return remote(
            self.give3.at[c], self.take3.at[c], self.s3.at[c], self.r3.at[c], self.p.device(self.core, 0, 0, 1)
        )

    def to_second(self, c):
        return remote(
            self.give2.at[c], self.take2.at[c], self.s2.at[c], self.r2.at[c], self.p.device(self.core, 0, 1, 0)
        )

    def along(self, c, dz):
        return remote(
            self.givez.at[c, dz - 1],
            self.takez.at[c, dz - 1],
            self.sz.at[c, dz],
            self.rz.at[c, dz],
            self.p.device(self.core, dz, 0, 0),
        )

    def sum_of(self, c, k, *more):
        at = self.p.chip(self.core, *split_index(k, self.zs))
        total = self.grads[c, self.core, at].astype(jnp.float32) + self.other[c, at].astype(jnp.float32)
        for ref in more:
            total = total + ref[c, k].astype(jnp.float32)
        return total

    def step0(self, c):
        self.to_partner(c).start()

    def step1(self, c):
        self.to_partner(c).wait_recv()
        zs = self.zs
        for k in range(2 * zs, 4 * zs):
            self.give3[c, k - 2 * zs] = self.sum_of(c, k).astype(self.give3.dtype)
        self.to_third(c).start()

    def step2(self, c):
        self.to_third(c).wait_recv()
        zs = self.zs
        for k in range(zs, 2 * zs):
            self.give2[c, k - zs] = self.sum_of(c, k, self.take3).astype(self.give2.dtype)
        self.to_second(c).start()

    def step3(self, c):
        self.to_second(c).wait_recv()
        for dz in range(1, self.zs):
            self.givez[c, dz - 1] = self.sum_of(c, dz, self.take3, self.take2).astype(self.givez.dtype)
            self.along(c, dz).start()

    def step4(self, c):
        total = self.sum_of(c, 0, self.take3, self.take2)
        for dz in range(1, self.zs):
            self.along(c, dz).wait_recv()
            total = total + self.takez[c, dz - 1].astype(jnp.float32)
        self.total[c] = total

    def finish(self, count):
        for c in range(count):
            self.to_partner(c).wait_send()
            self.to_third(c).wait_send()
            self.to_second(c).wait_send()
            for dz in range(1, self.zs):
                self.along(c, dz).wait_send()


def stage_scratch(chunks, chips, rows, columns):
    low = jnp.bfloat16
    zs = chips // 4
    shapes = [
        (chunks, 2, chips, rows, columns),
        (chunks, chips, rows, columns),
        (chunks, 2 * zs, rows, columns),
        (chunks, 2 * zs, rows, columns),
        (chunks, zs, rows, columns),
        (chunks, zs, rows, columns),
        (chunks, zs - 1, rows, columns),
        (chunks, zs - 1, rows, columns),
    ]
    sems = [pltpu.SemaphoreType.DMA((chunks,)) for _ in range(6)]
    sems += [pltpu.SemaphoreType.DMA((chunks, zs)) for _ in range(2)]
    return [pltpu.VMEM(s, low) for s in shapes] + [pltpu.VMEM((chunks, rows, columns), jnp.float32)] + sems


STAGE_REFS = 17


def backward_kernel(
    dp,
    experts,
    capacity,
    chunk,
    tok_ref,
    cot_ref,
    ret_ref,
    aux_ref,
    probs_ref,
    mid_ref,
    part_ref,
    back_any,
    second_any,
    ctx_any,
    stat_any,
    qkv_any,
    weights_any,
    out_any,
    input_any,
    dense_ref,
    total_ref,
    out_ref,
    unit_ref,
    inverse_ref,
    logs_ref,
    back_ref,
    second_ref,
    ctx_ref,
    stat_ref,
    qkv_ref,
    weights,
    vec,
    stacked,
    normed_turned,
    branch,
    dctx,
    joined,
    turned_query,
    dmid,
    work,
    sums,
    load,
    row,
    row_fine,
    plane_tiles,
    line_tiles,
    row_send,
    row_recv,
    tile_send,
    tile_recv,
    store,
    *stage_refs,
):
    low, full32 = jnp.bfloat16, jnp.float32
    patches, width = tok_ref.shape
    trio_width = 3 * LANES
    p = Place(dp, experts)
    main, fine = Stages(p, stage_refs[:STAGE_REFS]), Stages(p, stage_refs[STAGE_REFS:])
    coarse, chips, shard2 = main.grads.shape[0], *main.grads.shape[2:4]
    thin = fine.grads.shape[4]
    pieces = [
        (back_any, back_ref),
        (weights_any, weights),
        (ctx_any, ctx_ref),
        (second_any, second_ref),
        (stat_any, stat_ref),
        (qkv_any, qkv_ref),
    ]
    fetch = [pltpu.make_async_copy(s, d, load.at[i]) for i, (s, d) in enumerate(pieces)]
    for copy in fetch:
        copy.start()
    barrier = pltpu.get_barrier_semaphore()

    def flip(value, bit):
        return value + bit - 2 * bit * value

    mates = []
    for f in range(1, 8):
        chip_y = p.z * p.ys + flip(p.y, (f // 2) % 2)
        mates.append((flip(p.a, f // 4), chip_y * 2 + flip(p.core, f % 2)))
    peers = [p.device(p.core, dz, 0, 0) for dz in range(1, p.zs)]
    for device in mates + peers:
        pl.semaphore_signal(barrier, inc=1, device_id=device, device_id_type=MESH)

    full = capacity // 8
    half = width // 2
    lanes = lane_ids(patches)
    aux = aux_ref[...]
    slots = [aux[:, i : i + 1] for i in range(4)]
    gates = [aux[:, 4 + i : 5 + i] for i in range(2)]
    ids = lax.broadcasted_iota(jnp.int32, (patches, full * LANES), 1).astype(full32)
    tail_ids = lane_ids(patches, full * LANES).astype(full32)
    hits = [ids == slots[0], ids == slots[1]]
    lefts = [tail_ids == slots[0], tail_ids == slots[1]]
    rights = [tail_ids == slots[2], tail_ids == slots[3]]

    def mix(marks):
        return (jnp.where(marks[0], gates[0], 0.0) + jnp.where(marks[1], gates[1], 0.0)).astype(low)

    def pick(marks):
        return (marks[0] | marks[1]).astype(full32).astype(low)

    for i in range(full):
        stacked[pl.ds(i * LANES, LANES), :] = ret_ref[:, pl.ds(i * width, width)]
    tail = ret_ref[:, pl.ds(full * width, half)]
    left_mix, right_mix = nn(mix(lefts), tail), nn(mix(rights), tail)
    final = nn(mix(hits), stacked[...])
    out_ref[:, :half] = (mid_ref[:, :half] + (final[:, :half] + left_mix)).astype(low)
    out_ref[:, half:] = (mid_ref[:, half:] + (final[:, half:] + right_mix)).astype(low)
    keep_out = pltpu.make_async_copy(out_ref, out_any, store.at[0])
    keep_out.start()
    along = nt(cot_ref[...], stacked[...])
    along_left, along_right = nt(cot_ref[:, :half], tail), nt(cot_ref[:, half:], tail)
    dprobs = jnp.zeros((patches, LANES), full32)
    for j in range(2):
        dgate = jnp.sum(jnp.where(hits[j], along, 0.0), axis=1, keepdims=True) + jnp.sum(
            jnp.where(lefts[j], along_left, 0.0) + jnp.where(rights[j], along_right, 0.0), axis=1, keepdims=True
        )
        dprobs = dprobs + jnp.where(lanes == aux[:, 6 + j : 7 + j].astype(jnp.int32), dgate, 0.0)
    probs = probs_ref[...]
    dlogits = (probs * (dprobs - jnp.sum(probs * dprobs, axis=1, keepdims=True))).astype(low)
    fetch[0].wait()
    for i in range(full):
        stacked[pl.ds(i * LANES, LANES), :] = back_ref[:, pl.ds(i * width, width)]
    tail = back_ref[:, pl.ds(full * width, half)]
    fetch[1].wait()
    vec[...] = vector_table(weights, width)

    def vector(i):
        return vec[experts + i : experts + i + 1, :]

    routed = weights[:, 4 * width :]
    work[...] = nn(pick(hits), stacked[...]) + nt(dlogits, routed)
    work[:, :half] = work[:, :half] + nn(pick(lefts), tail)
    work[:, half:] = work[:, half:] + nn(pick(rights), tail)
    sums[...] = jnp.zeros_like(sums)

    def column_sum(slot, values):
        sums[pl.ds(8 * slot, 8), :] = sums[pl.ds(8 * slot, 8), :] + jnp.sum(
            values.reshape(-1, 8, values.shape[-1]), axis=0
        )

    def norm_back(grad, unit, inverse, gain):
        weighted = grad * gain
        return inverse * (
            weighted
            - jnp.mean(weighted, axis=-1, keepdims=True)
            - unit * jnp.mean(weighted * unit, axis=-1, keepdims=True)
        )

    for part in row_parts(patches, chunk):
        unit, inverse = norm_parts(mid_ref[part, :])
        grad = work[part, :]
        column_sum(5, grad * unit)
        column_sum(6, grad)
        total = cot_ref[part, :].astype(full32) + norm_back(grad, unit, inverse, vector(5))
        dmid[part, :] = total
        rounded = total.astype(low)
        branch[part, :] = rounded
        column_sum(4, rounded.astype(full32))
    fetch[2].wait()
    ctx_turned = jnp.transpose(ctx_ref[...])
    for core in range(2):
        columns = pl.ds(core * half, half)
        product = nn(ctx_turned, branch[:, columns])
        main.grads[0, core] = product.reshape(chips, shard2, half).astype(low)
    pl.semaphore_wait(barrier, len(mates) + len(peers))
    main.step0(0)
    third = 256
    for j in range(width // third):
        rows = pl.ds(j * third, third)
        dctx[:, rows] = nt(branch[...], weights[rows, pl.ds(3 * width, width)]).astype(low)
    fetch[3].wait()
    router_rows = nn(jnp.transpose(dlogits.astype(full32)).astype(low), second_ref[...])
    for part in row_parts(patches, chunk):
        unit, inverse = norm_parts(tok_ref[part, :].astype(full32))
        second_ref[part, :] = (unit * vector(0) + vector(1)).astype(low)
        unit_ref[part, :] = unit
        inverse_ref[part, :] = jnp.broadcast_to(inverse, (chunk, LANES))
    normed_turned[...] = jnp.transpose(second_ref[...])
    heads = (
        lax.broadcasted_iota(jnp.int32, (16, width), 1) // HEAD_DIM == lax.broadcasted_iota(jnp.int32, (16, width), 0)
    ).astype(full32).astype(low)
    product = dctx[...].astype(full32) * ctx_ref[...].astype(full32)
    upper = product.astype(low)
    center = nt(heads, upper) + nt(heads, (product - upper.astype(full32)).astype(low))
    fetch[4].wait()
    logs = jnp.transpose(stat_ref[...])
    logs_ref[...] = jnp.concatenate([logs[:16], center], axis=0)
    fetch[5].wait()

    ones = jnp.ones((8, patches), low)
    scale = jnp.asarray(HEAD_DIM**-0.5, low)

    def attend(pair):
        at, trio = pair * LANES, pair * trio_width
        key_at, value_at = pl.ds(trio + LANES, LANES), pl.ds(trio + 2 * LANES, LANES)
        queries = qkv_ref[:, pl.ds(trio, LANES)] * scale
        given = dctx[:, pl.ds(at, LANES)]
        own = lane_ids(patches)
        zero = jnp.zeros_like(queries)
        marks = [own < HEAD_DIM, own >= HEAD_DIM]
        head_queries = [jnp.where(m, queries, zero) for m in marks]
        head_given = [jnp.where(m, given, zero) for m in marks]
        turned_keys = jnp.transpose(qkv_ref[:, key_at] * scale)
        query_parts = [None, None]
        for part in row_parts(patches, chunk):
            keys = qkv_ref[part, key_at]
            values = qkv_ref[part, value_at]
            value_out, key_out = [], []
            for head in range(2):
                log_row = logs_ref[2 * pair + head : 2 * pair + head + 1, :]
                center_row = logs_ref[16 + 2 * pair + head : 17 + 2 * pair + head, :]
                prob = jnp.exp(nt(keys, head_queries[head]) - log_row)
                value_out.append(nn(prob.astype(low), given))
                dscore = (prob * (nt(values, head_given[head]) - center_row)).astype(low)
                key_out.append(nn(dscore, queries))
                head_keys = turned_keys[HEAD_DIM * head : HEAD_DIM * (head + 1), part.start : part.start + part.size]
                piece = nn(head_keys, dscore)
                query_parts[head] = piece if query_parts[head] is None else query_parts[head] + piece
            side = lane_ids(chunk) < HEAD_DIM
            joined[part, LANES : 2 * LANES] = jnp.where(side, key_out[0], key_out[1]).astype(low)
            joined[part, 2 * LANES :] = jnp.where(side, value_out[0], value_out[1]).astype(low)
        turned_query[...] = jnp.concatenate(query_parts, axis=0)
        joined[:, :LANES] = jnp.transpose(turned_query[...]).astype(low)
        product = nn(normed_turned[...], joined[...]).reshape(chips, shard2, trio_width).astype(low)
        if pair < 2 * (coarse - 1):
            main.grads[pair // 2 + 1, pair % 2] = product
        else:
            chunk_of = pair - 2 * (coarse - 1)
            fine.grads[chunk_of, 0] = product[:, :, :thin]
            fine.grads[chunk_of, 1, :, :, :LANES] = product[:, :, thin:]

    def spread(pair):
        trio = pair * trio_width
        part = nt(joined[...], weights[:, pl.ds(trio, trio_width)])
        work[...] = part if pair == 0 else work[...] + part
        column_parts = nn(ones, joined[...])
        sums[16:17, pl.ds(pair * LANES, LANES)] = column_parts[0:1, :LANES]
        sums[24:25, pl.ds(pair * LANES, LANES)] = column_parts[0:1, 2 * LANES :]

    fine.grads[0, 1, :, :, LANES:] = jnp.zeros((chips, shard2, thin - LANES), low)
    main.step1(0)
    attend(0)
    spread(0)
    main.step2(0)
    attend(1)
    main.step0(1)
    spread(1)
    main.step3(0)
    attend(2)
    main.step1(1)
    spread(2)
    attend(3)
    main.step0(2)
    main.step4(0)
    spread(3)
    main.step2(1)
    attend(4)
    fine.step0(0)
    main.step1(2)
    main.step3(1)
    spread(4)
    attend(5)
    fine.step1(0)
    spread(5)
    main.step2(2)
    for part in row_parts(patches, chunk):
        unit, inverse = unit_ref[part, :], inverse_ref[part, 0:1]
        grad = work[part, :]
        column_sum(0, grad * unit)
        column_sum(1, grad)
        dmid[part, :] = dmid[part, :] + norm_back(grad, unit, inverse, vector(0))
    keep_input = pltpu.make_async_copy(dmid, input_any, store.at[1])
    keep_input.start()
    vec[...] = router_rows
    for i in range(7):
        vec[experts + i : experts + i + 1, :] = jnp.sum(sums[pl.ds(8 * i, 8), :], axis=0, keepdims=True)
    fine.grads[1, 1, :, :, LANES:] = jnp.transpose(vec[...]).reshape(chips, shard2, LANES).astype(low)
    fine.step0(1)
    fine.step2(0)
    main.step4(1)
    fine.step1(1)
    main.step3(2)
    fine.step3(0)
    fine.step2(1)
    main.step4(2)
    fine.step4(0)
    deep = shard2 // 2
    his = pl.ds(pl.multiple_of((1 - p.core) * deep, 8), deep)
    mine = pl.ds(pl.multiple_of(p.core * deep, 8), deep)
    rows_copy = [
        remote(main.total.at[:, his], row, row_send.at[0], row_recv.at[0], main.partner),
        remote(fine.total.at[0, his], row_fine.at[0], row_send.at[1], row_recv.at[1], main.partner),
        remote(fine.total.at[1, his], row_fine.at[1], row_send.at[2], row_recv.at[2], main.partner),
    ]
    rows_copy[0].start()
    rows_copy[1].start()
    fine.step3(1)

    def squares_of(values):
        folded = jnp.sum((values * values).reshape(-1, 8, values.shape[1]), axis=0)
        out = folded[:, :LANES]
        for j in range(1, values.shape[1] // LANES):
            out = out + folded[:, j * LANES : (j + 1) * LANES]
        return out

    square = part_ref[...]
    for c in range(coarse):
        square = square + squares_of(main.total[c])
    square = square + squares_of(fine.total[0])
    fine.step4(1)
    rows_copy[2].start()
    plane = (p.a * p.ys + p.y) * 2 + p.core
    plane_tiles[plane] = square + squares_of(fine.total[1])

    def mate_copy(f):
        block = plane_tiles.at[plane]
        return remote(block, block, tile_send.at[f], tile_recv.at[f], mates[f - 1])

    def peer_copy(dz):
        block = line_tiles.at[p.z]
        return remote(block, block, tile_send.at[7 + dz], tile_recv.at[7 + dz], peers[dz - 1])

    for f in range(1, 8):
        mate_copy(f).start()

    def put(core, values, fine_values):
        for c in range(coarse):
            dense_ref[:, pl.ds(pl.multiple_of(c * width + core * half, LANES), half)] = values(c)
        for c in range(2):
            at = coarse * width + 2 * c * thin + core * thin
            dense_ref[:, pl.ds(pl.multiple_of(at, LANES), thin)] = fine_values(c)

    put(p.core, lambda c: main.total[c, mine, :], lambda c: fine.total[c, mine, :])
    for f in range(1, 8):
        from_plane = (flip(p.a, f // 4) * p.ys + flip(p.y, (f // 2) % 2)) * 2 + flip(p.core, f % 2)
        block = plane_tiles.at[from_plane]
        remote(block, block, tile_send.at[f], tile_recv.at[f], main.partner).wait_recv()
    total = plane_tiles[0]
    for j in range(1, 8):
        total = total + plane_tiles[j]
    line_tiles[p.z] = total
    for dz in range(1, p.zs):
        peer_copy(dz).start()
    for copy in rows_copy:
        copy.wait_recv()
    put(1 - p.core, lambda c: row[c], lambda c: row_fine[c])
    for dz in range(1, p.zs):
        block = line_tiles.at[lax.rem(p.z + p.zs - dz, p.zs)]
        remote(block, block, tile_send.at[7 + dz], tile_recv.at[7 + dz], main.partner).wait_recv()
    total = line_tiles[0]
    for j in range(1, p.zs):
        total = total + line_tiles[j]
    total_ref[...] = total
    main.finish(coarse)
    fine.finish(2)
    for copy in rows_copy:
        copy.wait_send()
    for f in range(1, 8):
        mate_copy(f).wait_send()
    for dz in range(1, p.zs):
        peer_copy(dz).wait_send()
    keep_out.wait()
    keep_input.wait()


def backward(
    tokens,
    cotangent,
    ret,
    back,
    aux,
    probs,
    mid,
    second,
    ctx,
    stat,
    qkv,
    weights,
    part,
    dp,
    experts,
    capacity,
    cid,
    chunk=576,
):
    patches, width = tokens.shape
    low, full = jnp.bfloat16, jnp.float32
    world = dp * experts
    chips, rows = world // 2, 2 * width // world
    thin = 2 * LANES
    chunks = width // LANES // 2
    columns = 4 * width + 2 * LANES
    return pl.pallas_call(
        functools.partial(backward_kernel, dp, experts, capacity, chunk),
        out_shape=[
            jax.ShapeDtypeStruct((patches, width), low),
            jax.ShapeDtypeStruct((patches, width), full),
            jax.ShapeDtypeStruct((rows // 2, columns), full),
            jax.ShapeDtypeStruct((8, LANES), full),
        ],
        in_specs=[VMEM] * 7 + [ANY] * 6,
        out_specs=[ANY, ANY, VMEM, VMEM],
        scratch_shapes=[
            pltpu.VMEM((patches, width), low),
            pltpu.VMEM((patches, width), full),
            pltpu.VMEM((patches, LANES), full),
            pltpu.VMEM((32, patches), full),
            pltpu.VMEM(back.shape, low),
            pltpu.VMEM((patches, width), low),
            pltpu.VMEM((patches, width), low),
            pltpu.VMEM(stat.shape, full),
            pltpu.VMEM(qkv.shape, low),
            pltpu.VMEM(weights.shape, low),
            pltpu.VMEM((LANES, width), full),
            pltpu.VMEM((capacity // 8 * LANES, width), low),
            pltpu.VMEM((width, patches), low),
            pltpu.VMEM((patches, width), low),
            pltpu.VMEM((patches, width), low),
            pltpu.VMEM((patches, 3 * LANES), low),
            pltpu.VMEM((LANES, patches), full),
            pltpu.VMEM((patches, width), full),
            pltpu.VMEM((patches, width), full),
            pltpu.VMEM((56, width), full),
            pltpu.SemaphoreType.DMA((6,)),
            pltpu.VMEM((chunks, rows // 2, width // 2), full),
            pltpu.VMEM((2, rows // 2, thin), full),
            pltpu.VMEM((8, 8, LANES), full),
            pltpu.VMEM((experts // 4, 8, LANES), full),
            pltpu.SemaphoreType.DMA((3,)),
            pltpu.SemaphoreType.DMA((3,)),
            pltpu.SemaphoreType.DMA((7 + experts // 4,)),
            pltpu.SemaphoreType.DMA((7 + experts // 4,)),
            pltpu.SemaphoreType.DMA((2,)),
            *stage_scratch(chunks, chips, rows, width // 2),
            *stage_scratch(2, chips, rows, thin),
        ],
        compiler_params=pltpu.CompilerParams(
            collective_id=cid, has_side_effects=True, vmem_limit_bytes=60 * 1024 * 1024
        ),
        cost_estimate=pl.CostEstimate(flops=15 * 10**9, bytes_accessed=30 * 10**6, transcendentals=4 * 10**6),
        name="attend_backward",
    )(tokens, cotangent, ret, aux, probs, mid, part, back, second, ctx, stat, qkv, weights)


ORDER = 7
WINDOW = 6
PARTS = 15


def moe_kernel(
    dp,
    experts,
    chunk,
    rows_any,
    dy_any,
    inner_any,
    hidden_ref,
    outer_any,
    return_ref,
    y_any,
    drows_any,
    dinner_any,
    dhidden_ref,
    douter_any,
    dreturn_ref,
    square_ref,
    rows_all,
    dy_all,
    y_pack,
    drows_pack,
    y_theirs,
    drows_theirs,
    rows,
    turned,
    dy,
    inner,
    outer,
    act,
    grad,
    dz,
    acc,
    inner_stage,
    outer_stage,
    dinner_stage,
    douter_stage,
    square,
    own_sem,
    in_send,
    in_recv,
    over_send,
    over_recv,
    part_send,
    part_recv,
    out_send,
    out_recv,
    stage_sem,
    store_sem,
):
    low, full32 = jnp.bfloat16, jnp.float32
    width = rows.shape[1]
    half = width // 2
    full = rows_all.shape[3] // width
    steps = inner.shape[1] // chunk
    groups = 2
    group = experts // groups
    block_rows = dp * group * 8
    deep = rows.shape[0] // groups
    a = lax.axis_index("dp")
    e = lax.axis_index("expert")
    across = (1 - a, e)
    ins, alls = (rows_any, dy_any), (rows_all, dy_all)
    packs, theirs, outs = (y_pack, drows_pack), (y_theirs, drows_theirs), (y_any, drows_any)

    def to(turn):
        return lax.rem(e + lax.rem(ORDER * turn, experts), experts)

    def source(turn):
        return lax.rem(e + experts - lax.rem(ORDER * turn, experts), experts)

    def columns_of(k):
        return pl.ds(pl.multiple_of(k * chunk, chunk), chunk)

    def stage(k, slot):
        return (
            pltpu.make_async_copy(inner_any.at[0, :, columns_of(k)], inner_stage.at[slot], stage_sem.at[0, slot]),
            pltpu.make_async_copy(outer_any.at[0, columns_of(k), :], outer_stage.at[slot], stage_sem.at[1, slot]),
        )

    def own_block(i):
        return pltpu.make_async_copy(ins[i].at[e], alls[i].at[a, 0], own_sem.at[i])

    for slot in range(2):
        for copy in stage(slot, slot):
            copy.start()
    for i in range(2):
        own_block(i).start()
    greet([(a, to(j)) for j in range(1, experts)] + [across])

    def first_send(i, turn):
        return remote(
            ins[i].at[to(turn)], alls[i].at[a, turn], in_send.at[i, turn], in_recv.at[i, turn], (a, to(turn))
        )

    def forward_own(i):
        return remote(ins[i].at[e], alls[i].at[a, 0], over_send.at[i, 0], over_recv.at[i, 0], across)

    def pass_on(i, turn):
        block = alls[i].at[a, turn]
        return remote(block, block, over_send.at[i, turn], over_recv.at[i, turn], across)

    def received(i, turn):
        block = alls[i].at[a, turn]
        return remote(block, block, in_send.at[i, turn], in_recv.at[i, turn], across)

    def from_across(i, turn):
        block = alls[i].at[1 - a, turn]
        return remote(block, block, over_send.at[i, turn], over_recv.at[i, turn], across)

    def part_copy(i, turn):
        return remote(
            packs[i].at[1 - a, turn], theirs[i].at[turn], part_send.at[i, turn], part_recv.at[i, turn], across
        )

    def result_copy(i, turn):
        return remote(
            packs[i].at[a, turn], outs[i].at[e], out_send.at[i, turn], out_recv.at[i, turn], (a, source(turn))
        )

    forward_own(0).start()

    @pl.loop(1, 1 + WINDOW)
    def _(turn):
        first_send(0, turn).start()

    def take_in(i, begin, number):
        @pl.loop(0, number)
        def _(d):
            turn = begin + d

            @pl.when(turn < experts)
            def _():
                received(i, turn).wait_recv()
                pass_on(i, turn).start()

                @pl.when(turn + WINDOW < experts)
                def _():
                    first_send(i, turn + WINDOW).start()

                if i == 0:

                    @pl.when(turn + WINDOW >= experts)
                    def _():
                        first_send(1, turn + WINDOW - experts + 1).start()

    def hand_out(i, begin, number):
        @pl.loop(0, number)
        def _(d):
            turn = begin + d

            @pl.when(turn < experts)
            def _():
                part_copy(i, turn).wait_recv()

                @pl.when(turn + PARTS <= experts)
                def _():
                    part_copy(i, lax.rem(turn + PARTS, experts)).start()

                packs[i][a, turn] = (packs[i][a, turn].astype(full32) + theirs[i][turn].astype(full32)).astype(low)
                result_copy(i, turn).start()

    def finish(i):
        part_copy(i, 0).wait_recv()
        packs[i][a, 0] = (packs[i][a, 0].astype(full32) + theirs[i][0].astype(full32)).astype(low)
        pltpu.make_async_copy(packs[i].at[a, 0], outs[i].at[e], own_sem.at[i]).start()

    def unpack(i, g, place):
        if g == 0:
            own_block(i).wait()

        @pl.loop(g * group, (g + 1) * group)
        def _(turn):
            from_across(i, turn).wait_recv()

        tails = []
        for plane in range(dp):
            for b in range(full):
                piece = alls[i][plane, g * group : (g + 1) * group, :, b * width : (b + 1) * width].astype(full32)
                at = g * deep + b * block_rows + plane * group * 8
                place[pl.ds(at, group * 8), :] = piece.reshape(group * 8, width).astype(low)
            piece = alls[i][plane, g * group : (g + 1) * group, :, full * width :].astype(full32)
            tails.append(piece.reshape(group * 8, half))
        tail = jnp.concatenate(tails, axis=0).astype(low)
        for right in range(2):
            place[pl.ds(g * deep + full * block_rows, block_rows // 2), pl.ds(right * half, half)] = nn(
                tail_picks(block_rows, right), tail
            ).astype(low)

    def pack(i, g):
        tail = acc[pl.ds(g * deep + full * block_rows, block_rows // 2), :].astype(low)
        spread = None
        for right in range(2):
            piece = lax.dot_general(
                tail_picks(block_rows, right),
                tail[:, right * half : (right + 1) * half],
                (((0,), (0,)), ((), ())),
                preferred_element_type=full32,
            )
            spread = piece if spread is None else spread + piece
        for plane in range(dp):
            turns = slice(g * group, (g + 1) * group)
            for b in range(full):
                at = g * deep + b * block_rows + plane * group * 8
                piece = acc[pl.ds(at, group * 8), :].reshape(group, 8, width)
                packs[i][plane, turns, :, b * width : (b + 1) * width] = piece.astype(low)
            piece = spread[plane * group * 8 : (plane + 1) * group * 8].reshape(group, 8, half)
            packs[i][plane, turns, :, full * width :] = piece.astype(low)

    def send_parts(i):
        @pl.loop(1, 1 + PARTS)
        def _(turn):
            part_copy(i, turn).start()

    @pl.loop(0, steps)
    def _(k):
        slot = lax.rem(k, 2)
        for copy in stage(k, slot):
            copy.wait()
        inner[:, columns_of(k)] = inner_stage[slot].astype(low)
        outer[columns_of(k), :] = outer_stage[slot].astype(low)

        @pl.when(k + 2 < steps)
        def _():
            for copy in stage(k + 2, slot):
                copy.start()

        take_in(0, 1 + k, 1)

    part = return_ref.shape[1]
    bias = return_ref[...].astype(low).astype(full32)
    for i in range(dp):
        acc[:, pl.ds(i * part, part)] = jnp.broadcast_to(jnp.where(a == i, bias, 0.0), (rows.shape[0], part))

    def onward(g):
        mine = pl.ds(g * deep, deep)

        def run(k):
            columns = columns_of(k)
            z = nn(rows[mine, :], inner[:, columns]) + hidden_ref[:, columns].astype(low).astype(full32)
            value, slope = gelu_both(z)
            act[mine, columns] = value.astype(low)
            grad[mine, columns] = slope
            acc[mine, :] += nn(act[mine, columns], outer[columns, :])

        return run

    def backward_of(g):
        mine = pl.ds(g * deep, deep)

        def run(k):
            columns = columns_of(k)
            dz[mine, columns] = (nt(dy[mine, :], outer[columns, :]) * grad[mine, columns]).astype(low)
            acc[mine, :] += nt(dz[mine, columns], inner[:, columns])

        return run

    forward_own(1).start()
    early = 1 + steps
    take_in(0, early, 4)
    early += 4
    unpack(0, 0, rows)
    forward_of = onward(0)
    left = experts - early

    @pl.loop(0, steps)
    def _(k):
        forward_of(k)
        take_in(0, early + k, 1)

        @pl.when(k >= left)
        def _():
            take_in(1, 1 + k - left, 1)

    taken = 1 + max(steps - left, 0)
    unpack(0, 1, rows)
    forward_late = onward(1)

    @pl.loop(0, steps)
    def _(k):
        forward_late(k)
        take_in(1, taken + k, 1)

    taken += steps
    for g in range(groups):
        pack(0, g)
    turned[...] = jnp.transpose(rows[...])
    take_in(1, taken, 2)
    taken += 2
    acc[...] = jnp.zeros_like(acc)
    unpack(1, 0, dy)
    back_first = backward_of(0)

    @pl.loop(0, steps)
    def _(k):
        back_first(k)
        take_in(1, taken + k, 1)

    taken += steps
    take_in(1, taken, max(experts - taken, 0))
    send_parts(0)
    pack(1, 0)
    unpack(1, 1, dy)
    back_last = backward_of(1)

    @pl.loop(0, steps)
    def _(k):
        back_last(k)
        hand_out(0, 1 + k, 1)

    pack(1, 1)
    send_parts(1)
    total = jnp.zeros((1, width), full32)
    for i in range(rows.shape[0] // LANES):
        total = total + jnp.sum(dy[pl.ds(i * LANES, LANES), :].astype(full32), axis=0, keepdims=True)
    picked = total[:, :part]
    for i in range(1, dp):
        picked = jnp.where(a == i, total[:, i * part : (i + 1) * part], picked)
    dreturn_ref[...] = picked
    square[...] = jnp.zeros_like(square)
    flat = picked * picked
    for i in range(part // LANES):
        square[0:1, :] = square[0:1, :] + flat[:, i * LANES : (i + 1) * LANES]

    def store(k, slot):
        return (
            pltpu.make_async_copy(dinner_stage.at[slot], dinner_any.at[0, :, columns_of(k)], store_sem.at[0, slot]),
            pltpu.make_async_copy(douter_stage.at[slot], douter_any.at[0, columns_of(k), :], store_sem.at[1, slot]),
        )

    later = -(-(experts - 1 - steps) // (steps - 1))

    @pl.loop(0, steps)
    def _(k):
        slot = lax.rem(k, 2)
        columns = columns_of(k)
        douter = nn(jnp.transpose(act[:, columns]), dy[...])
        dinner = nn(turned[...], dz[:, columns])
        dhidden = jnp.sum(dz[:, columns].astype(full32), axis=0, keepdims=True)

        @pl.when(k >= 2)
        def _():
            for copy in store(k - 2, slot):
                copy.wait()

        douter_stage[slot] = douter.astype(low)
        dinner_stage[slot] = dinner.astype(low)
        for copy in store(k, slot):
            copy.start()
        dhidden_ref[:, columns] = dhidden
        parts = jnp.zeros((8, LANES), full32)
        folded = jnp.sum((douter * douter).reshape(-1, 8, width), axis=0)
        for i in range(width // LANES):
            parts = parts + folded[:, i * LANES : (i + 1) * LANES]
        folded = jnp.sum((dinner * dinner).reshape(-1, 8, chunk), axis=0)
        hidden_square = dhidden * dhidden
        for i in range(chunk // LANES):
            parts = parts + folded[:, i * LANES : (i + 1) * LANES]
            square[0:1, :] = square[0:1, :] + hidden_square[:, i * LANES : (i + 1) * LANES]
        square[...] += parts
        hand_out(0, 1 + steps + k * later, later)

    finish(0)
    hand_out(1, 1, experts - 1)
    finish(1)
    square_ref[...] = square[...]
    for k in range(steps - 2, steps):
        for copy in store(k, k % 2):
            copy.wait()
    for i in range(2):

        @pl.loop(1, experts)
        def _(turn):
            block = outs[i].at[to(turn)]
            remote(block, block, out_send.at[i, turn], out_recv.at[i, turn], across).wait_recv()

    for i in range(2):
        pltpu.make_async_copy(packs[i].at[a, 0], outs[i].at[e], own_sem.at[i]).wait()
        forward_own(i).wait_send()
        part_copy(i, 0).wait_send()

        @pl.loop(1, experts)
        def _(turn):
            first_send(i, turn).wait_send()
            pass_on(i, turn).wait_send()
            part_copy(i, turn).wait_send()
            result_copy(i, turn).wait_send()


def mixture(rows, dy, inner, hidden, outer, back, dp, cid, chunk=256):
    experts, _, packed = rows.shape
    width, units = inner.shape[1:]
    count = dp * experts * 8
    total = count * packed // width
    low, full = jnp.bfloat16, jnp.float32
    both = (dp, experts, 8, packed)
    sems = [pltpu.SemaphoreType.DMA((2, experts)) for _ in range(8)]
    return pl.pallas_call(
        functools.partial(moe_kernel, dp, experts, chunk),
        out_shape=[
            jax.ShapeDtypeStruct(rows.shape, low),
            jax.ShapeDtypeStruct(rows.shape, low),
            jax.ShapeDtypeStruct(inner.shape, low),
            jax.ShapeDtypeStruct(hidden.shape, full),
            jax.ShapeDtypeStruct(outer.shape, low),
            jax.ShapeDtypeStruct(back.shape, full),
            jax.ShapeDtypeStruct((8, LANES), full),
        ],
        in_specs=[ANY, ANY, ANY, VMEM, ANY, VMEM],
        out_specs=[ANY, ANY, ANY, VMEM, ANY, VMEM, VMEM],
        scratch_shapes=[
            pltpu.VMEM(both, low),
            pltpu.VMEM(both, low),
            pltpu.VMEM(both, low),
            pltpu.VMEM(both, low),
            pltpu.VMEM(both[1:], low),
            pltpu.VMEM(both[1:], low),
            pltpu.VMEM((total, width), low),
            pltpu.VMEM((width, total), low),
            pltpu.VMEM((total, width), low),
            pltpu.VMEM((width, units), low),
            pltpu.VMEM((units, width), low),
            pltpu.VMEM((total, units), low),
            pltpu.VMEM((total, units), full),
            pltpu.VMEM((total, units), low),
            pltpu.VMEM((total, width), full),
            pltpu.VMEM((2, width, chunk), full),
            pltpu.VMEM((2, chunk, width), full),
            pltpu.VMEM((2, width, chunk), low),
            pltpu.VMEM((2, chunk, width), low),
            pltpu.VMEM((8, LANES), full),
            pltpu.SemaphoreType.DMA((2,)),
            *sems,
            pltpu.SemaphoreType.DMA((2, 2)),
            pltpu.SemaphoreType.DMA((2, 2)),
        ],
        compiler_params=pltpu.CompilerParams(
            collective_id=cid, has_side_effects=True, vmem_limit_bytes=60 * 1024 * 1024
        ),
        cost_estimate=pl.CostEstimate(flops=17 * 10**9, bytes_accessed=25 * 10**6, transcendentals=2 * 10**6),
        name="mixture",
    )(rows, dy, inner, hidden, outer, back)


def adam_values(weight, first, second, gradient, clip, rate, decay):
    scaled = gradient * clip
    first_new = BETA_ONE * first + (1.0 - BETA_ONE) * scaled
    second_new = BETA_TWO * second + (1.0 - BETA_TWO) * scaled * scaled
    first_hat = first_new * (1.0 / (1.0 - BETA_ONE**STEP))
    second_hat = second_new * (1.0 / (1.0 - BETA_TWO**STEP))
    weight_new = weight - rate * (first_hat / (jnp.sqrt(second_hat) + ADAM_EPS) + decay * weight)
    return weight_new, first_new, second_new


def adam_kernel(experts, norm_ref, dense_any, *refs):
    small = 6
    large_ins, rest = refs[:8], refs[8:]
    small_ins, rest = rest[: 3 * small + 2], rest[3 * small + 2 :]
    large_outs, rest = rest[:6], rest[6:]
    small_outs, norm_out, rest = rest[: 3 * small], rest[3 * small], rest[3 * small + 1 :]
    held, dense_ref, load, store = rest[: 3 * small + 2], rest[3 * small + 2], rest[-2], rest[-1]
    step, steps = pl.program_id(0), pl.num_programs(0)
    loads = [pltpu.make_async_copy(s, d, load.at[i]) for i, (s, d) in enumerate(zip(small_ins, held))]
    loads.append(pltpu.make_async_copy(dense_any, dense_ref, load.at[3 * small + 2]))
    stores = [pltpu.make_async_copy(s, d, store.at[i]) for i, (s, d) in enumerate(zip(held, small_outs))]

    @pl.when(step == 0)
    def _():
        for copy in loads:
            copy.start()

    total = jnp.sum(jnp.sum(norm_ref[...], axis=0, keepdims=True), axis=1, keepdims=True)
    norm = jnp.sqrt(total)
    clip = THRESHOLD / jnp.maximum(norm, THRESHOLD)
    for i, rate in enumerate((RATE_INNER, RATE_OUTER)):
        grad = large_ins[6 + i][...].astype(jnp.float32)
        state = [ref[...] for ref in large_ins[3 * i : 3 * i + 3]]
        for place, value in zip(large_outs[3 * i : 3 * i + 3], adam_values(*state, grad, clip, rate, DECAY)):
            place[...] = value

    def update(i, grad, rate, decay, columns=slice(None)):
        places = held[3 * i : 3 * i + 3]
        new = adam_values(*(ref[:, columns] for ref in places), grad, clip, rate, decay)
        for place, value in zip(places, new):
            place[:, columns] = value

    @pl.when(step == 1)
    def _():
        for copy in loads:
            copy.wait()
        norm_out[...] = norm
        width = held[3].shape[1]
        trio = 3 * LANES
        for pair in range(width // LANES):
            base = width + pair * trio + (LANES if pair == width // LANES - 1 else 0)
            for kind in range(3):
                update(
                    0,
                    dense_ref[:, base + kind * LANES : base + (kind + 1) * LANES],
                    RATE_PROJECTION,
                    DECAY,
                    slice(kind * width + pair * LANES, kind * width + (pair + 1) * LANES),
                )
        update(1, dense_ref[:, :width], RATE_OUTPUT, DECAY)
        turned = jnp.transpose(dense_ref[:, dense_ref.shape[1] - LANES :])
        update(2, turned[:experts], RATE_ROUTER, DECAY)
        update(3, turned[experts : experts + 7], RATE_VECTORS, 0.0)
        update(4, held[3 * small][...], RATE_HIDDEN, 0.0)
        update(5, held[3 * small + 1][...], RATE_RETURN, 0.0)
        for copy in stores:
            copy.start()

    @pl.when(step == steps - 1)
    def _():
        for copy in stores:
            copy.wait()


def adam_all(experts, squares, dense, states, grads, steps=8):
    full = jnp.float32

    def blocks(array):
        return pl.BlockSpec((array.shape[0] // steps, array.shape[1]), lambda i: (i, 0))

    large = [v for group in states[:2] for v in group]
    small = [v for group in states[2:] for v in group]
    spread = [blocks(v) for v in large]
    held = small + list(grads[2:])
    out = pl.pallas_call(
        functools.partial(adam_kernel, experts),
        grid=(steps,),
        out_shape=[jax.ShapeDtypeStruct(v.shape, full) for v in large + small] + [jax.ShapeDtypeStruct((1, 1), full)],
        in_specs=[pl.BlockSpec(squares.shape, lambda i: (0, 0)), ANY]
        + spread
        + [blocks(v) for v in grads[:2]]
        + [ANY] * len(held),
        out_specs=spread + [ANY] * len(small) + [pl.BlockSpec((1, 1), lambda i: (0, 0))],
        scratch_shapes=[pltpu.VMEM(v.shape, full) for v in held]
        + [
            pltpu.VMEM(dense.shape, full),
            pltpu.SemaphoreType.DMA((len(held) + 1,)),
            pltpu.SemaphoreType.DMA((len(small),)),
        ],
        compiler_params=pltpu.CompilerParams(
            vmem_limit_bytes=60 * 1024 * 1024, dimension_semantics=("arbitrary",)
        ),
        cost_estimate=pl.CostEstimate(flops=5 * 10**7, bytes_accessed=62 * 10**6, transcendentals=10**7),
        name="adam_all",
    )(squares, dense, *large, *grads[:2], *held)
    return [tuple(out[3 * i : 3 * i + 3]) for i in range(len(states))], out[-1].reshape(())


def fits(dp, experts):
    return dp == 2 and experts == 16


def fast_shards(
    dp,
    experts,
    tokens,
    cotangent,
    expert_choice,
    priority,
    projection,
    projection_first,
    projection_second,
    output_weight,
    output_first,
    output_second,
    router_weight,
    router_first,
    router_second,
    vectors,
    vectors_first,
    vectors_second,
    expert_inner,
    inner_first,
    inner_second,
    hidden_bias,
    hidden_first,
    hidden_second,
    expert_outer,
    outer_first,
    outer_second,
    return_bias,
    return_first,
    return_second,
):
    patches = tokens.shape[1]
    capacity = max(2, patches // experts)
    rows, dy, aux, probs, qkv, ctx, mid, second, stat, weights = forward(
        tokens[0],
        cotangent[0],
        expert_choice[0],
        priority[0],
        projection,
        output_weight,
        router_weight,
        vectors,
        dp,
        experts,
        capacity,
        1,
    )
    blocks = (experts, 8, rows.shape[1])
    returned, back_rows, inner_grad, hidden_grad, outer_grad, return_grad, expert_square = mixture(
        rows.reshape(blocks),
        dy.reshape(blocks),
        expert_inner,
        hidden_bias,
        expert_outer,
        return_bias,
        dp,
        2,
    )
    block_output, input_grad, dense, squares = backward(
        tokens[0],
        cotangent[0],
        returned.reshape(rows.shape),
        back_rows.reshape(rows.shape),
        aux,
        probs,
        mid,
        second,
        ctx,
        stat,
        qkv,
        weights,
        expert_square,
        dp,
        experts,
        capacity,
        4,
    )
    states, grad_norm = adam_all(
        experts,
        squares,
        dense,
        [
            (expert_inner[0], inner_first[0], inner_second[0]),
            (expert_outer[0], outer_first[0], outer_second[0]),
            (projection, projection_first, projection_second),
            (output_weight, output_first, output_second),
            (router_weight.T, router_first.T, router_second.T),
            (vectors, vectors_first, vectors_second),
            (hidden_bias, hidden_first, hidden_second),
            (return_bias, return_first, return_second),
        ],
        [inner_grad[0], outer_grad[0], hidden_grad, return_grad],
    )
    inner_new, outer_new, projection_new, output_new, router_new, vectors_new, hidden_new, return_new = states
    return (
        block_output[None],
        input_grad[None],
        grad_norm,
        *projection_new,
        *output_new,
        *(v.T for v in router_new),
        *vectors_new,
        *(v[None] for v in inner_new),
        *hidden_new,
        *(v[None] for v in outer_new),
        *return_new,
    )


def solution(mesh):
    dp, experts = mesh.shape["dp"], mesh.shape["expert"]
    body = functools.partial(fast_shards, dp, experts) if fits(dp, experts) else shards
    return jax.shard_map(
        body,
        mesh=mesh,
        in_specs=(
            P(("dp", "expert"), None, None),
            P(("dp", "expert"), None, None),
            P(("dp", "expert"), None, None),
            P(("dp", "expert"), None),
            P(("dp", "expert"), None),
            P(("dp", "expert"), None),
            P(("dp", "expert"), None),
            P(("dp", "expert"), None),
            P(("dp", "expert"), None),
            P(("dp", "expert"), None),
            P(("dp", "expert"), None),
            P(("dp", "expert"), None),
            P(("dp", "expert"), None),
            P(None, ("dp", "expert")),
            P(None, ("dp", "expert")),
            P(None, ("dp", "expert")),
            P("expert", None, "dp"),
            P("expert", None, "dp"),
            P("expert", None, "dp"),
            P("expert", "dp"),
            P("expert", "dp"),
            P("expert", "dp"),
            P("expert", "dp", None),
            P("expert", "dp", None),
            P("expert", "dp", None),
            P("expert", "dp"),
            P("expert", "dp"),
            P("expert", "dp"),
        ),
        out_specs=(
            P(("dp", "expert"), None, None),
            P(("dp", "expert"), None, None),
            P(),
            P(("dp", "expert"), None),
            P(("dp", "expert"), None),
            P(("dp", "expert"), None),
            P(("dp", "expert"), None),
            P(("dp", "expert"), None),
            P(("dp", "expert"), None),
            P(("dp", "expert"), None),
            P(("dp", "expert"), None),
            P(("dp", "expert"), None),
            P(None, ("dp", "expert")),
            P(None, ("dp", "expert")),
            P(None, ("dp", "expert")),
            P("expert", None, "dp"),
            P("expert", None, "dp"),
            P("expert", None, "dp"),
            P("expert", "dp"),
            P("expert", "dp"),
            P("expert", "dp"),
            P("expert", "dp", None),
            P("expert", "dp", None),
            P("expert", "dp", None),
            P("expert", "dp"),
            P("expert", "dp"),
            P("expert", "dp"),
        ),
        check_vma=False,
    )
```

```python
import functools

import jax
import jax.numpy as jnp
from jax import lax
from jax.experimental import pallas as pl
from jax.experimental.pallas import tpu as pltpu
from jax.sharding import PartitionSpec as P

HEADS = 12
HEAD_DIM = 64
STEP = 10


NORM_EPS = 1e-06
ADAM_EPS = 1e-08
BETA_ONE = 0.9
BETA_TWO = 0.999
DECAY = 0.1
THRESHOLD = 1.0
RATE_PROJECTION = 0.1
RATE_OUTPUT = 1.0
RATE_ROUTER = 0.05
RATE_VECTORS = 0.5
RATE_INNER = 0.1
RATE_HIDDEN = 0.25
RATE_OUTER = 1.5
RATE_RETURN = 2.0


def layer_norm(values, norm_gain, norm_bias):
    center = values - jnp.mean(values, axis=-1, keepdims=True)
    spread = jnp.mean(center * center, axis=-1, keepdims=True)
    return center * lax.rsqrt(spread + NORM_EPS) * norm_gain + norm_bias


def smooth_gate(values):
    return jax.nn.gelu(values, approximate=True)


def mixed_dot(left, right):
    return jnp.dot(left, right, preferred_element_type=jnp.float32)


def rows_product(left, right):
    return lax.dot_general(
        left, right, (((0,), (0,)), ((), ())), preferred_element_type=jnp.float32
    )


def columns_product(left, right):
    return lax.dot_general(
        left, right, (((1,), (1,)), ((), ())), preferred_element_type=jnp.float32
    )


def assign_slots(chosen, claim_order, expert_count, capacity):
    patches = chosen.shape[0]
    top_count = chosen.shape[1]
    claim_rank = (
        jnp.arange(top_count, dtype=jnp.int32)[None, :] * patches + claim_order[:, None]
    ).T.reshape(-1)
    flat_choice = chosen.T.reshape(-1)
    onehot = (flat_choice[:, None] == jnp.arange(expert_count, dtype=jnp.int32)[None, :]).astype(
        jnp.float32
    )
    earlier = (claim_rank[None, :] < claim_rank[:, None]).astype(jnp.float32)
    counts = jnp.dot(
        earlier, onehot, precision=lax.Precision.HIGHEST, preferred_element_type=jnp.float32
    )
    position = jnp.sum(counts * onehot, axis=1).astype(jnp.int32).reshape(top_count, patches).T
    kept_mask = position < capacity
    flat_slot = chosen * capacity + jnp.minimum(position, capacity - 1)
    return (flat_slot, kept_mask)


def slot_matches(flat_slot, kept_mask, slot_count):
    slot_ids = jnp.arange(slot_count, dtype=jnp.int32)
    return (flat_slot[None, :, :] == slot_ids[:, None, None]) & kept_mask[None, :, :]


def select_gates(logits, chosen, expert_count):
    router_probs = jax.nn.softmax(logits, axis=-1)
    onehot = chosen[:, :, None] == jnp.arange(expert_count, dtype=jnp.int32)[None, None, :]
    return jnp.sum(jnp.where(onehot, router_probs[:, None, :], 0.0), axis=2)


def adam_update(weight, first_state, second, gradient, clip_factor, step_rate, decay_rate):
    scaled = gradient * clip_factor
    first_new = BETA_ONE * first_state + (1.0 - BETA_ONE) * scaled
    second_new = BETA_TWO * second + (1.0 - BETA_TWO) * scaled * scaled
    first_hat = first_new / (1.0 - BETA_ONE**STEP)
    second_hat = second_new / (1.0 - BETA_TWO**STEP)
    weight_new = weight - step_rate * (
        first_hat / (jnp.sqrt(second_hat) + ADAM_EPS) + decay_rate * weight
    )
    return (weight_new, first_new, second_new)


def shards(
    tokens,
    cotangent,
    expert_choice,
    priority,
    projection,
    projection_first,
    projection_second,
    output_weight,
    output_first,
    output_second,
    router_weight,
    router_first,
    router_second,
    vectors,
    vectors_first,
    vectors_second,
    expert_inner,
    inner_first,
    inner_second,
    hidden_bias,
    hidden_first,
    hidden_second,
    expert_outer,
    outer_first,
    outer_second,
    return_bias,
    return_first,
    return_second,
):
    model_width = tokens.shape[2]
    patches = tokens.shape[1]
    experts = lax.axis_size("expert")
    capacity = max(2, patches // experts)
    slot_count = experts * capacity
    score_scale = HEAD_DIM ** (-0.5)
    dense_shards = (
        projection.astype(jnp.bfloat16),
        output_weight.astype(jnp.bfloat16),
        router_weight.astype(jnp.bfloat16),
        vectors.astype(jnp.bfloat16),
    )
    partial_shards = (
        lax.all_gather(dense_shards[0], "expert", axis=0, tiled=True),
        lax.all_gather(dense_shards[1], "expert", axis=0, tiled=True),
        lax.all_gather(dense_shards[2], "expert", axis=0, tiled=True),
        lax.all_gather(dense_shards[3], "expert", axis=1, tiled=True),
    )
    whole_projection, whole_output, whole_router, whole_vectors = (
        lax.all_gather(partial_shards[0], "dp", axis=0, tiled=True),
        lax.all_gather(partial_shards[1], "dp", axis=0, tiled=True),
        lax.all_gather(partial_shards[2], "dp", axis=0, tiled=True),
        lax.all_gather(partial_shards[3], "dp", axis=1, tiled=True),
    )
    inner_low = expert_inner.astype(jnp.bfloat16)
    hidden_low = hidden_bias.astype(jnp.bfloat16)
    outer_low = expert_outer.astype(jnp.bfloat16)
    return_low = return_bias.astype(jnp.bfloat16)
    inner_all, hidden_all, outer_all, return_all = (
        lax.all_gather(inner_low, "dp", axis=2, tiled=True),
        lax.all_gather(hidden_low, "dp", axis=1, tiled=True),
        lax.all_gather(outer_low, "dp", axis=1, tiled=True),
        lax.all_gather(return_low, "dp", axis=1, tiled=True),
    )
    vector_rows = whole_vectors.astype(jnp.float32)
    image_rows = tokens[0].astype(jnp.float32)
    normed_one, norm_back_one = jax.vjp(layer_norm, image_rows, vector_rows[0], vector_rows[1])
    normed_low = normed_one.astype(jnp.bfloat16)
    projected = mixed_dot(normed_low, whole_projection)
    queries = (
        (projected[:, :model_width] + vector_rows[2])
        .astype(jnp.bfloat16)
        .reshape(patches, HEADS, HEAD_DIM)
    )
    key_rows = (
        projected[:, model_width : 2 * model_width]
        .astype(jnp.bfloat16)
        .reshape(patches, HEADS, HEAD_DIM)
    )
    value_rows = (
        (projected[:, 2 * model_width :] + vector_rows[3])
        .astype(jnp.bfloat16)
        .reshape(patches, HEADS, HEAD_DIM)
    )
    scores = (
        jnp.einsum("qhd,khd->hqk", queries, key_rows, preferred_element_type=jnp.float32)
        * score_scale
    )
    score_top = jnp.max(scores, axis=-1, keepdims=True)
    raised = jnp.exp(scores - score_top)
    totals = jnp.sum(raised, axis=-1, keepdims=True)
    attention = raised / totals
    log_total = score_top + jnp.log(totals)
    context = (
        jnp.einsum(
            "hqk,khd->qhd",
            attention.astype(jnp.bfloat16),
            value_rows,
            preferred_element_type=jnp.float32,
        )
        .reshape(patches, model_width)
        .astype(jnp.bfloat16)
    )
    middle = image_rows + (mixed_dot(context, whole_output) + vector_rows[4])
    normed_two, norm_back_two = jax.vjp(layer_norm, middle, vector_rows[5], vector_rows[6])
    second_low = normed_two.astype(jnp.bfloat16)
    logits = mixed_dot(second_low, whole_router)
    chosen = expert_choice[0]

    def gate_choice(values):
        return select_gates(values, chosen, experts)

    gate_values, gate_back = jax.vjp(gate_choice, logits)
    flat_slot, kept_mask = assign_slots(chosen, priority[0], experts, capacity)
    matches = slot_matches(flat_slot, kept_mask, slot_count)
    slot_table = jnp.any(matches, axis=2).astype(jnp.bfloat16)
    dispatched = (
        mixed_dot(slot_table, second_low)
        .astype(jnp.bfloat16)
        .reshape(experts, capacity, model_width)
    )
    arrived = lax.all_to_all(dispatched, "expert", split_axis=0, concat_axis=0, tiled=True).reshape(
        slot_count, model_width
    )
    pre_act = mixed_dot(arrived, inner_all[0]) + hidden_all[0].astype(jnp.float32)
    activated, gelu_back = jax.vjp(smooth_gate, pre_act)
    active_low = activated.astype(jnp.bfloat16)
    expert_out = (mixed_dot(active_low, outer_all[0]) + return_all[0].astype(jnp.float32)).astype(
        jnp.bfloat16
    )
    returned = lax.all_to_all(
        expert_out.reshape(experts, capacity, model_width),
        "expert",
        split_axis=0,
        concat_axis=0,
        tiled=True,
    ).reshape(slot_count, model_width)
    picked = returned[flat_slot].astype(jnp.float32)
    weighted = jnp.where(kept_mask, gate_values, 0.0)
    final = middle + jnp.sum(weighted[:, :, None] * picked, axis=1)
    block_output = final.astype(jnp.bfloat16)[None]
    upstream = cotangent[0].astype(jnp.float32)
    gate_grad = jnp.where(kept_mask, jnp.sum(upstream[:, None, :] * picked, axis=2), 0.0)
    slot_gate = jnp.sum(jnp.where(matches, weighted[None, :, :], 0.0), axis=(1, 2))
    slot_grad = (mixed_dot(slot_table, cotangent[0]) * slot_gate[:, None]).astype(jnp.bfloat16)
    sent_grad = lax.all_to_all(
        slot_grad.reshape(experts, capacity, model_width),
        "expert",
        split_axis=0,
        concat_axis=0,
        tiled=True,
    ).reshape(slot_count, model_width)
    outer_grad = rows_product(active_low, sent_grad)
    return_grad = jnp.sum(sent_grad, axis=0, dtype=jnp.float32)
    active_grad = columns_product(sent_grad, outer_all[0])
    (pre_grad,) = gelu_back(active_grad)
    pre_low = pre_grad.astype(jnp.bfloat16)
    inner_grad = rows_product(arrived, pre_low)
    hidden_grad = jnp.sum(pre_low, axis=0, dtype=jnp.float32)
    row_grad = columns_product(pre_low, inner_all[0]).astype(jnp.bfloat16)
    expert_grads = (
        lax.psum_scatter(
            inner_grad[None].astype(jnp.bfloat16), "dp", scatter_dimension=2, tiled=True
        ).astype(jnp.float32),
        lax.psum_scatter(
            hidden_grad[None].astype(jnp.bfloat16), "dp", scatter_dimension=1, tiled=True
        ).astype(jnp.float32),
        lax.psum_scatter(
            outer_grad[None].astype(jnp.bfloat16), "dp", scatter_dimension=1, tiled=True
        ).astype(jnp.float32),
        lax.psum_scatter(
            return_grad[None].astype(jnp.bfloat16), "dp", scatter_dimension=1, tiled=True
        ).astype(jnp.float32),
    )
    back_rows = lax.all_to_all(
        row_grad.reshape(experts, capacity, model_width),
        "expert",
        split_axis=0,
        concat_axis=0,
        tiled=True,
    ).reshape(slot_count, model_width)
    (logit_grad,) = gate_back(gate_grad)
    logit_low = logit_grad.astype(jnp.bfloat16)
    router_grad = rows_product(second_low, logit_low)
    second_grad = rows_product(slot_table, back_rows) + columns_product(logit_low, whole_router)
    middle_part, gain_two_grad, bias_two_grad = norm_back_two(second_grad)
    middle_grad = upstream + middle_part
    branch_low = middle_grad.astype(jnp.bfloat16)
    output_grad = rows_product(context, branch_low)
    out_bias_grad = jnp.sum(branch_low, axis=0, dtype=jnp.float32)
    context_grad = (
        columns_product(branch_low, whole_output)
        .astype(jnp.bfloat16)
        .reshape(patches, HEADS, HEAD_DIM)
    )
    scores = (
        jnp.einsum("qhd,khd->hqk", queries, key_rows, preferred_element_type=jnp.float32)
        * score_scale
    )
    attention = jnp.exp(scores - log_total)
    attention_grad = jnp.einsum(
        "qhd,khd->hqk", context_grad, value_rows, preferred_element_type=jnp.float32
    )
    value_grad = jnp.einsum(
        "hqk,qhd->khd",
        attention.astype(jnp.bfloat16),
        context_grad,
        preferred_element_type=jnp.float32,
    ).astype(jnp.bfloat16)
    centered = jnp.sum(attention * attention_grad, axis=-1, keepdims=True)
    score_grad = (attention * (attention_grad - centered)).astype(jnp.bfloat16)
    query_grad = (
        (
            jnp.einsum("hqk,khd->qhd", score_grad, key_rows, preferred_element_type=jnp.float32)
            * score_scale
        )
        .astype(jnp.bfloat16)
        .reshape(patches, model_width)
    )
    key_grad = (
        (
            jnp.einsum("hqk,qhd->khd", score_grad, queries, preferred_element_type=jnp.float32)
            * score_scale
        )
        .astype(jnp.bfloat16)
        .reshape(patches, model_width)
    )
    value_flat = value_grad.reshape(patches, model_width)
    joined_grad = jnp.concatenate([query_grad, key_grad, value_flat], axis=1)
    projection_grad = rows_product(normed_low, joined_grad)
    normed_grad = columns_product(joined_grad, whole_projection)
    input_part, gain_one_grad, bias_one_grad = norm_back_one(normed_grad)
    input_grad = (middle_grad + input_part)[None]
    vector_grad = jnp.stack(
        [
            gain_one_grad,
            bias_one_grad,
            jnp.sum(query_grad, axis=0, dtype=jnp.float32),
            jnp.sum(value_flat, axis=0, dtype=jnp.float32),
            out_bias_grad,
            gain_two_grad,
            bias_two_grad,
        ]
    )
    local_grads = (projection_grad, output_grad, router_grad, vector_grad)
    partial_grads = (
        lax.psum_scatter(
            local_grads[0].astype(jnp.bfloat16), "dp", scatter_dimension=0, tiled=True
        ).astype(jnp.float32),
        lax.psum_scatter(
            local_grads[1].astype(jnp.bfloat16), "dp", scatter_dimension=0, tiled=True
        ).astype(jnp.float32),
        lax.psum_scatter(
            local_grads[2].astype(jnp.bfloat16), "dp", scatter_dimension=0, tiled=True
        ).astype(jnp.float32),
        lax.psum_scatter(
            local_grads[3].astype(jnp.bfloat16), "dp", scatter_dimension=1, tiled=True
        ).astype(jnp.float32),
    )
    dense_grads = (
        lax.psum_scatter(
            partial_grads[0].astype(jnp.bfloat16), "expert", scatter_dimension=0, tiled=True
        ).astype(jnp.float32),
        lax.psum_scatter(
            partial_grads[1].astype(jnp.bfloat16), "expert", scatter_dimension=0, tiled=True
        ).astype(jnp.float32),
        lax.psum_scatter(
            partial_grads[2].astype(jnp.bfloat16), "expert", scatter_dimension=0, tiled=True
        ).astype(jnp.float32),
        lax.psum_scatter(
            partial_grads[3].astype(jnp.bfloat16), "expert", scatter_dimension=1, tiled=True
        ).astype(jnp.float32),
    )
    all_grads = tuple(dense_grads) + tuple(expert_grads)
    local_square = jnp.sum(all_grads[0] * all_grads[0])
    for gradient in all_grads[1:]:
        local_square = local_square + jnp.sum(gradient * gradient)
    square_total = lax.psum(local_square, ("dp", "expert"))
    grad_norm = jnp.sqrt(square_total)
    clip_factor = THRESHOLD / jnp.maximum(grad_norm, THRESHOLD)
    projection_next, projection_moment, projection_square = adam_update(
        projection,
        projection_first,
        projection_second,
        all_grads[0],
        clip_factor,
        RATE_PROJECTION,
        DECAY,
    )
    output_next, output_moment, output_square = adam_update(
        output_weight, output_first, output_second, all_grads[1], clip_factor, RATE_OUTPUT, DECAY
    )
    router_next, router_moment, router_square = adam_update(
        router_weight, router_first, router_second, all_grads[2], clip_factor, RATE_ROUTER, DECAY
    )
    vectors_next, vectors_moment, vectors_square = adam_update(
        vectors, vectors_first, vectors_second, all_grads[3], clip_factor, RATE_VECTORS, 0.0
    )
    inner_next, inner_moment, inner_square = adam_update(
        expert_inner, inner_first, inner_second, all_grads[4], clip_factor, RATE_INNER, DECAY
    )
    hidden_next, hidden_moment, hidden_square = adam_update(
        hidden_bias, hidden_first, hidden_second, all_grads[5], clip_factor, RATE_HIDDEN, 0.0
    )
    outer_next, outer_moment, outer_square = adam_update(
        expert_outer, outer_first, outer_second, all_grads[6], clip_factor, RATE_OUTER, DECAY
    )
    return_next, return_moment, return_square = adam_update(
        return_bias, return_first, return_second, all_grads[7], clip_factor, RATE_RETURN, 0.0
    )
    return (
        block_output,
        input_grad,
        grad_norm,
        projection_next,
        projection_moment,
        projection_square,
        output_next,
        output_moment,
        output_square,
        router_next,
        router_moment,
        router_square,
        vectors_next,
        vectors_moment,
        vectors_square,
        inner_next,
        inner_moment,
        inner_square,
        hidden_next,
        hidden_moment,
        hidden_square,
        outer_next,
        outer_moment,
        outer_square,
        return_next,
        return_moment,
        return_square,
    )


MESH = pl.DeviceIdType.MESH
ANY = pl.BlockSpec(memory_space=pl.ANY)
VMEM = pl.BlockSpec(memory_space=pltpu.VMEM)


class Place:
    def __init__(self, dp, experts):
        self.dp, self.experts = dp, experts
        self.ys = 2
        self.zs = experts // 4
        self.a = lax.axis_index("dp")
        self.e = lax.axis_index("expert")
        self.core = lax.rem(self.e, 2)
        self.y = lax.rem(lax.div(self.e, 2), self.ys)
        self.z = lax.div(self.e, 2 * self.ys)

    def chip_of(self, core, dz, s2, s3):
        zz = lax.rem(self.z + dz, self.zs)
        if s2 == s3:
            fa = fy = s2
        elif s2:
            fa, fy = core, 1 - core
        else:
            fa, fy = 1 - core, core
        aa = lax.rem(self.a + fa, 2)
        yy = lax.rem(self.y + fy, 2)
        return aa, zz, yy

    def device(self, core, dz, s2, s3, own_core=None):
        aa, zz, yy = self.chip_of(core, dz, s2, s3)
        c = core if own_core is None else own_core
        return (aa, (zz * self.ys + yy) * 2 + c)

    def flat(self, dev):
        return dev[0] * self.experts + dev[1]

    def chip(self, core, dz, s2, s3):
        aa, zz, yy = self.chip_of(core, dz, s2, s3)
        return (aa * self.zs + zz) * self.ys + yy


def remote(src, dst, send, recv, dev):
    return pltpu.make_async_remote_copy(src_ref=src, dst_ref=dst, send_sem=send, recv_sem=recv, device_id=dev, device_id_type=MESH)


def greet(devices):
    barrier = pltpu.get_barrier_semaphore()
    for dev in devices:
        pl.semaphore_signal(barrier, inc=1, device_id=dev, device_id_type=MESH)
    pl.semaphore_wait(barrier, len(devices))


def split_index(k, zs):
    return k % zs, (k // zs) % 2, k // (2 * zs)


LANES = 128


def nn(left, right):
    return lax.dot_general(left, right, (((1,), (0,)), ((), ())), preferred_element_type=jnp.float32)


def nt(left, right):
    return lax.dot_general(left, right, (((1,), (1,)), ((), ())), preferred_element_type=jnp.float32)


def lane_ids(rows, start=0):
    return lax.broadcasted_iota(jnp.int32, (rows, LANES), 1) + start


def row_parts(count, size):
    return [pl.ds(i * size, size) for i in range(count // size)]


def norm_parts(values):
    center = values - jnp.mean(values, axis=-1, keepdims=True)
    inverse = lax.rsqrt(jnp.mean(center * center, axis=-1, keepdims=True) + NORM_EPS)
    return center * inverse, inverse


def vector_table(weights, width):
    return jnp.transpose(weights[:, 4 * width :].astype(jnp.float32))


def forward_kernel(
    dp,
    experts,
    capacity,
    chunk,
    tok_ref,
    cot_ref,
    choice_ref,
    rank_row,
    projection_ref,
    output_ref,
    router_ref,
    vectors_ref,
    rows_ref,
    dy_ref,
    aux_ref,
    probs_ref,
    qkv_any,
    ctx_any,
    mid_any,
    second_any,
    stat_any,
    weights_any,
    qkv_ref,
    ctx_ref,
    mid_ref,
    second_ref,
    stat_ref,
    weights,
    vec,
    normed,
    mine,
    theirs,
    tables,
    given,
    land_first,
    land,
    pre_send,
    pre_recv,
    line_send,
    line_recv,
    second_send,
    second_recv,
    third_send,
    third_recv,
    core_send,
    core_recv,
    store,
):
    low, full32 = jnp.bfloat16, jnp.float32
    patches, width = tok_ref.shape
    half = width // 2
    trio_width = 3 * LANES
    p = Place(dp, experts)
    c, zs = p.core, p.zs
    deep = projection_ref.shape[0]
    partner = (p.a, p.e + 1 - 2 * c)
    second, third = p.device(c, 0, 1, 0), p.device(c, 0, 0, 1)
    peers = [p.device(c, dz, 0, 0) for dz in range(1, zs)]
    narrow = jnp.concatenate(
        [router_ref[...], vectors_ref[...], jnp.zeros((LANES - experts - vectors_ref.shape[0], deep), full32)], axis=0
    )
    for h in range(2):
        mine[h, :, :LANES] = jnp.transpose(narrow) if h == 0 else jnp.zeros((deep, LANES), full32)
        for i in range(width // LANES // 2):
            for kind in range(3):
                at = kind * width + (2 * i + h) * LANES
                mine[h, :, LANES + i * trio_width + kind * LANES : LANES + i * trio_width + (kind + 1) * LANES] = (
                    projection_ref[:, at : at + LANES]
                )
        mine[h, :, LANES + 3 * half :] = output_ref[:, h * half : (h + 1) * half]
    greet(peers + [second, third, partner])
    before_all = remote(mine.at[1 - c], theirs, pre_send, pre_recv, partner)
    before_all.start()
    lanes = lane_ids(patches)
    named = jnp.concatenate([choice_ref[...], rank_row[...]], axis=0).astype(full32)
    named = jnp.transpose(jnp.concatenate([named, jnp.zeros((LANES - 3, patches), full32)], axis=0))
    first, other = named[:, 0:1].astype(jnp.int32), named[:, 1:2].astype(jnp.int32)
    is_first, is_other = lanes == first, lanes == other
    chunks = width // LANES // 2 + 1
    lands = [land_first] + [land.at[i] for i in range(chunks - 1)]
    my_line = p.a * p.ys + p.y
    second_line = jnp.where(c == 0, p.a * p.ys + 1 - p.y, (1 - p.a) * p.ys + p.y)
    third_lines = [
        jnp.where(c == 0, (1 - p.a) * p.ys + p.y, p.a * p.ys + 1 - p.y),
        (1 - p.a) * p.ys + 1 - p.y,
    ]

    def line_copy(i, dz):
        block = lands[i].at[c, my_line, p.z]
        return remote(block, block, line_send.at[i, dz], line_recv.at[i, dz], peers[dz - 1])

    def second_copy(i):
        block = lands[i].at[c, my_line]
        return remote(block, block, second_send.at[i], second_recv.at[i], second)

    def third_copy(i, which):
        block = lands[i].at[c, my_line if which == 0 else second_line]
        return remote(block, block, third_send.at[i, which], third_recv.at[i, which], third)

    def core_copy(i, which):
        block = lands[i].at[c, (my_line, second_line, *third_lines)[which]]
        return remote(block, block, core_send.at[i, which], core_recv.at[i, which], partner)

    def step0(i):
        for dz in range(1, zs):
            line_copy(i, dz).start()

    def step1(i):
        for dz in range(1, zs):
            block = lands[i].at[c, my_line, lax.rem(p.z + zs - dz, zs)]
            remote(block, block, line_send.at[i, dz], line_recv.at[i, dz], partner).wait_recv()
        third_copy(i, 0).start()
        second_copy(i).start()
        core_copy(i, 0).start()

    def step2(i):
        second_copy(i).wait_recv()
        third_copy(i, 1).start()
        core_copy(i, 1).start()

    def step3(i):
        for which in range(2):
            third_copy(i, which).wait_recv()
            core_copy(i, 2 + which).start()

    def unpack(i):
        for which in range(4):
            core_copy(i, which).wait_recv()
        for line in range(2 * p.ys):
            for z in range(zs):
                at = (line // p.ys * zs + z) * p.ys + line % p.ys
                rows = pl.ds(2 * deep * at, 2 * deep)
                for h in range(2):
                    if i == 0:
                        weights[rows, h * trio_width : (h + 1) * trio_width] = land_first[h, line, z, :, LANES:]
                    else:
                        columns = pl.ds((2 * i + h) * half, half)
                        weights[rows, columns] = land[i - 1, h, line, z]
                if i == 0:
                    weights[rows, 4 * width :] = land_first[0, line, z, :, :LANES]

    before_all.wait_recv()
    own, their = mine[c], theirs[...]
    top, bottom = jnp.where(c == 0, own, their), jnp.where(c == 0, their, own)
    block = jnp.concatenate([top, bottom], axis=0).astype(low)
    land_first[c, my_line, p.z] = block[:, : LANES + half]
    for i in range(1, chunks):
        land[i - 1, c, my_line, p.z] = block[:, LANES + i * half : LANES + (i + 1) * half]
    for i in range(chunks):
        step0(i)
    earlier = (rank_row[...].astype(full32) < named[:, 2:3]).astype(full32).astype(low)
    hot = (is_first | (lanes == other + experts)).astype(full32)
    counts = nn(earlier, hot.astype(low))
    totals = jnp.sum(hot, axis=0, keepdims=True)
    place_first = jnp.sum(jnp.where(is_first, counts, 0.0), axis=1, keepdims=True)
    place_other = jnp.sum(
        jnp.where(lanes == other + experts, counts, 0.0) + jnp.where(is_other, totals, 0.0), axis=1, keepdims=True
    )

    def slot_of(place, expert):
        place = place.astype(jnp.int32)
        kept = place < capacity
        slot = (place // 8) * LANES + expert * 8 + place % 8
        tail = kept & (place >= capacity - 4)
        return kept, jnp.where(kept, slot, -1), jnp.where(tail, slot + 4, -1)

    aux = jnp.zeros((patches, LANES), full32)
    for j, (place, expert) in enumerate(((place_first, first), (place_other, other))):
        kept, slot, twin = slot_of(place, expert)
        for lane, column in ((j, slot), (2 + j, twin), (4 + j, kept), (6 + j, expert)):
            aux = jnp.where(lanes == lane, column.astype(full32), aux)
    aux_ref[...] = aux
    turned = jnp.transpose(aux)
    slots = [turned[i : i + 1, :] for i in range(4)]
    full = capacity // 8
    for i in range(full + 1):
        ids = (lax.broadcasted_iota(jnp.int32, (LANES, patches), 0) + i * LANES).astype(full32)
        hit = (ids == slots[0]) | (ids == slots[1])
        if i == full:
            hit = hit | (ids == slots[2]) | (ids == slots[3])
        tables[i] = hit.astype(full32).astype(low)
        given[i] = nn(tables[i], cot_ref[...]).astype(low)

    def row(i):
        return vec[experts + i : experts + i + 1, :]

    def attend(pair):
        at = pair * LANES
        trio = pair * trio_width
        product = nn(normed[...], weights[:, trio : trio + trio_width])
        queries_all = (product[:, :LANES] + vec[experts + 2 : experts + 3, at : at + LANES]).astype(low)
        keys = product[:, LANES : 2 * LANES].astype(low)
        values = (product[:, 2 * LANES :] + vec[experts + 3 : experts + 4, at : at + LANES]).astype(low)
        qkv_ref[:, trio : trio + LANES] = queries_all
        qkv_ref[:, trio + LANES : trio + 2 * LANES] = keys
        qkv_ref[:, trio + 2 * LANES : trio + 3 * LANES] = values
        key_lanes = lane_ids(patches)
        values_two = [
            jnp.where(key_lanes < HEAD_DIM, values, (key_lanes == HEAD_DIM).astype(full32).astype(low)),
            jnp.where(key_lanes >= HEAD_DIM, values, (key_lanes == 0).astype(full32).astype(low)),
        ]
        for part in row_parts(patches, chunk):
            own_lanes = lane_ids(chunk)
            queries = qkv_ref[part, trio : trio + LANES] * jnp.asarray(HEAD_DIM**-0.5, low)
            outs = []
            stat = stat_ref[part, :]
            for head in range(2):
                side = (own_lanes < HEAD_DIM) if head == 0 else (own_lanes >= HEAD_DIM)
                scores = nt(jnp.where(side, queries, jnp.zeros_like(queries)), keys)
                peak = jnp.max(scores, axis=1, keepdims=True)
                raised = jnp.exp(scores - peak)
                mixed = nn(raised.astype(low), values_two[head])
                spare = HEAD_DIM if head == 0 else 0
                total = mixed[:, spare : spare + 1]
                outs.append(mixed / total)
                stat = jnp.where(own_lanes == 2 * pair + head, peak + jnp.log(total), stat)
            stat_ref[part, :] = stat
            ctx_ref[part, at : at + LANES] = jnp.where(own_lanes < HEAD_DIM, outs[0], outs[1]).astype(low)

    stat_ref[...] = jnp.zeros_like(stat_ref)
    step1(0)
    step1(1)
    step2(0)
    step1(2)
    step2(1)
    step3(0)
    step1(3)
    unpack(0)
    vec[...] = vector_table(weights, width)
    for part in row_parts(patches, chunk):
        unit, _ = norm_parts(tok_ref[part, :].astype(full32))
        normed[part, :] = (unit * row(0) + row(1)).astype(low)
    step2(2)
    step3(1)
    attend(0)
    step2(3)
    attend(1)
    step3(2)
    unpack(1)
    attend(2)
    step3(3)
    attend(3)
    unpack(2)
    attend(4)
    attend(5)
    unpack(3)
    kept = [(weights, weights_any), (qkv_ref, qkv_any), (ctx_ref, ctx_any), (stat_ref, stat_any)]
    kept += [(mid_ref, mid_any), (second_ref, second_any)]
    keep = [pltpu.make_async_copy(s, d, store.at[i]) for i, (s, d) in enumerate(kept)]
    for copy in keep[:4]:
        copy.start()
    third_columns = 256
    for j in range(width // third_columns):
        columns = pl.ds(j * third_columns, third_columns)
        product = nn(ctx_ref[...], weights[:, pl.ds(3 * width + j * third_columns, third_columns)])
        mid_ref[:, columns] = tok_ref[:, columns].astype(full32) + (product + vec[experts + 4 : experts + 5, columns])
    for part in row_parts(patches, chunk):
        unit, _ = norm_parts(mid_ref[part, :])
        second_ref[part, :] = (unit * row(5) + row(6)).astype(low)
    keep[4].start()
    keep[5].start()
    logits = jnp.where(lanes < experts, nn(second_ref[...], weights[:, 4 * width :]), -1e30)
    raised = jnp.exp(logits - jnp.max(logits, axis=1, keepdims=True))
    probs = raised / jnp.sum(raised, axis=1, keepdims=True)
    probs_ref[...] = probs
    for j, hit in enumerate((is_first, is_other)):
        gate = jnp.sum(jnp.where(hit, probs, 0.0), axis=1, keepdims=True)
        aux_ref[...] = jnp.where(lanes == 4 + j, aux_ref[...] * gate, aux_ref[...])
    parts = []
    rest = probs
    for _ in range(3):
        parts.append(rest.astype(low))
        rest = rest - parts[-1].astype(full32)
    slot_expert = lax.broadcasted_iota(jnp.int32, (LANES, LANES), 0) // 8
    for i in range(full + 1):
        chances = nn(tables[i], parts[0])
        chances = chances + nn(tables[i], parts[1])
        chances = chances + nn(tables[i], parts[2])
        gate = jnp.sum(jnp.where(lane_ids(LANES) == slot_expert, chances, 0.0), axis=1, keepdims=True)
        sent = nn(tables[i], second_ref[...])
        back = given[i].astype(full32) * gate
        columns = pl.ds(i * width, width)
        if i == full:
            columns = pl.ds(i * width, width // 2)
            left = lax.broadcasted_iota(jnp.int32, (LANES, width // 2), 0) % 8 < 4
            sent = jnp.where(left, sent[:, : width // 2], sent[:, width // 2 :])
            back = jnp.where(left, back[:, : width // 2], back[:, width // 2 :])
        rows_ref[:, columns] = sent.astype(low)
        dy_ref[:, columns] = back.astype(low)

    for copy in keep:
        copy.wait()
    before_all.wait_send()
    for i in range(chunks):
        for dz in range(1, zs):
            line_copy(i, dz).wait_send()
        second_copy(i).wait_send()
        for which in range(2):
            third_copy(i, which).wait_send()
        for which in range(4):
            core_copy(i, which).wait_send()


def forward(
    tokens,
    cotangent,
    choice,
    priority,
    projection,
    output_weight,
    router_weight,
    vectors,
    dp,
    experts,
    capacity,
    cid,
    chunk=576,
):
    patches, width = tokens.shape
    low, full = jnp.bfloat16, jnp.float32
    packed = (8 * experts, capacity * width // 8)
    shapes = [
        (packed, low),
        (packed, low),
        ((patches, LANES), full),
        ((patches, LANES), full),
        ((patches, 3 * width), low),
        ((patches, width), low),
        ((patches, width), full),
        ((patches, width), low),
        ((patches, LANES), full),
        ((width, 4 * width + LANES), low),
    ]
    deep, half = projection.shape[0], width // 2
    chunks = width // LANES // 2 + 1
    zs = experts // 4
    lines = dp * experts // 2 // zs
    dma = pltpu.SemaphoreType.DMA
    return pl.pallas_call(
        functools.partial(forward_kernel, dp, experts, capacity, chunk),
        out_shape=[jax.ShapeDtypeStruct(*s) for s in shapes],
        in_specs=[VMEM] * 8,
        out_specs=[VMEM] * 4 + [ANY] * 6,
        scratch_shapes=[
            *(pltpu.VMEM(*shape) for shape in shapes[4:]),
            pltpu.VMEM((LANES, width), full),
            pltpu.VMEM((patches, width), low),
            pltpu.VMEM((2, deep, LANES + 4 * half), full),
            pltpu.VMEM((deep, LANES + 4 * half), full),
            pltpu.VMEM((capacity // 8 + 1, LANES, patches), low),
            pltpu.VMEM((capacity // 8 + 1, LANES, width), low),
            pltpu.VMEM((2, lines, zs, 2 * deep, LANES + half), low),
            pltpu.VMEM((chunks - 1, 2, lines, zs, 2 * deep, half), low),
            dma,
            dma,
            dma((chunks, zs)),
            dma((chunks, zs)),
            dma((chunks,)),
            dma((chunks,)),
            dma((chunks, 2)),
            dma((chunks, 2)),
            dma((chunks, 4)),
            dma((chunks, 4)),
            dma((6,)),
        ],
        compiler_params=pltpu.CompilerParams(
            collective_id=cid, has_side_effects=True, vmem_limit_bytes=60 * 1024 * 1024
        ),
        cost_estimate=pl.CostEstimate(flops=6 * 10**9, bytes_accessed=20 * 10**6, transcendentals=4 * 10**6),
        name="attend_forward",
    )(
        tokens,
        cotangent,
        choice.T,
        priority.reshape(1, patches),
        projection,
        output_weight,
        router_weight.T,
        vectors,
    )


def gelu_both(z):
    root = 0.7978845608028654
    square = z * z
    slope = jnp.tanh(root * z * (1.0 + 0.044715 * square))
    half = 0.5 * (1.0 + slope)
    act = z * half
    grad = half + 0.5 * z * (1.0 - slope * slope) * (root * (1.0 + 3 * 0.044715 * square))
    return act, grad


def tail_picks(count, right):
    rows = lax.broadcasted_iota(jnp.int32, (count // 2, count), 0)
    ids = lax.broadcasted_iota(jnp.int32, (count // 2, count), 1)
    hit = ids == (rows // 4) * 8 + rows % 4 + (4 if right else 0)
    return hit.astype(jnp.float32).astype(jnp.bfloat16)


class Stages:
    def __init__(self, place, refs):
        (self.grads, self.other, self.give3, self.take3, self.give2, self.take2, self.givez, self.takez, self.total) = refs[:9]
        (self.cs, self.cr, self.s3, self.r3, self.s2, self.r2, self.sz, self.rz) = refs[9:]
        self.p, self.zs, self.core = place, place.zs, place.core
        self.partner = (place.a, place.e + 1 - 2 * place.core)

    def to_partner(self, c):
        return remote(
            self.grads.at[c, 1 - self.core], self.other.at[c], self.cs.at[c], self.cr.at[c], self.partner
        )

    def to_third(self, c):
        return remote(
            self.give3.at[c], self.take3.at[c], self.s3.at[c], self.r3.at[c], self.p.device(self.core, 0, 0, 1)
        )

    def to_second(self, c):
        return remote(
            self.give2.at[c], self.take2.at[c], self.s2.at[c], self.r2.at[c], self.p.device(self.core, 0, 1, 0)
        )

    def along(self, c, dz):
        return remote(
            self.givez.at[c, dz - 1],
            self.takez.at[c, dz - 1],
            self.sz.at[c, dz],
            self.rz.at[c, dz],
            self.p.device(self.core, dz, 0, 0),
        )

    def sum_of(self, c, k, *more):
        at = self.p.chip(self.core, *split_index(k, self.zs))
        total = self.grads[c, self.core, at].astype(jnp.float32) + self.other[c, at].astype(jnp.float32)
        for ref in more:
            total = total + ref[c, k].astype(jnp.float32)
        return total

    def step0(self, c):
        self.to_partner(c).start()

    def step1(self, c):
        self.to_partner(c).wait_recv()
        zs = self.zs
        for k in range(2 * zs, 4 * zs):
            self.give3[c, k - 2 * zs] = self.sum_of(c, k).astype(self.give3.dtype)
        self.to_third(c).start()

    def step2(self, c):
        self.to_third(c).wait_recv()
        zs = self.zs
        for k in range(zs, 2 * zs):
            self.give2[c, k - zs] = self.sum_of(c, k, self.take3).astype(self.give2.dtype)
        self.to_second(c).start()

    def step3(self, c):
        self.to_second(c).wait_recv()
        for dz in range(1, self.zs):
            self.givez[c, dz - 1] = self.sum_of(c, dz, self.take3, self.take2).astype(self.givez.dtype)
            self.along(c, dz).start()

    def step4(self, c):
        total = self.sum_of(c, 0, self.take3, self.take2)
        for dz in range(1, self.zs):
            self.along(c, dz).wait_recv()
            total = total + self.takez[c, dz - 1].astype(jnp.float32)
        self.total[c] = total

    def finish(self, count):
        for c in range(count):
            self.to_partner(c).wait_send()
            self.to_third(c).wait_send()
            self.to_second(c).wait_send()
            for dz in range(1, self.zs):
                self.along(c, dz).wait_send()


def stage_scratch(chunks, chips, rows, columns):
    low = jnp.bfloat16
    zs = chips // 4
    shapes = [
        (chunks, 2, chips, rows, columns),
        (chunks, chips, rows, columns),
        (chunks, 2 * zs, rows, columns),
        (chunks, 2 * zs, rows, columns),
        (chunks, zs, rows, columns),
        (chunks, zs, rows, columns),
        (chunks, zs - 1, rows, columns),
        (chunks, zs - 1, rows, columns),
    ]
    sems = [pltpu.SemaphoreType.DMA((chunks,)) for _ in range(6)]
    sems += [pltpu.SemaphoreType.DMA((chunks, zs)) for _ in range(2)]
    return [pltpu.VMEM(s, low) for s in shapes] + [pltpu.VMEM((chunks, rows, columns), jnp.float32)] + sems


STAGE_REFS = 17


def backward_kernel(
    dp,
    experts,
    capacity,
    chunk,
    tok_ref,
    cot_ref,
    ret_ref,
    aux_ref,
    probs_ref,
    mid_ref,
    part_ref,
    back_any,
    second_any,
    ctx_any,
    stat_any,
    qkv_any,
    weights_any,
    out_any,
    input_any,
    dense_ref,
    total_ref,
    out_ref,
    unit_ref,
    inverse_ref,
    logs_ref,
    back_ref,
    second_ref,
    ctx_ref,
    stat_ref,
    qkv_ref,
    weights,
    vec,
    stacked,
    normed_turned,
    branch,
    dctx,
    joined,
    turned_query,
    dmid,
    work,
    sums,
    load,
    row,
    row_fine,
    plane_tiles,
    line_tiles,
    row_send,
    row_recv,
    tile_send,
    tile_recv,
    store,
    *stage_refs,
):
    low, full32 = jnp.bfloat16, jnp.float32
    patches, width = tok_ref.shape
    trio_width = 3 * LANES
    p = Place(dp, experts)
    main, fine = Stages(p, stage_refs[:STAGE_REFS]), Stages(p, stage_refs[STAGE_REFS:])
    coarse, chips, shard2 = main.grads.shape[0], *main.grads.shape[2:4]
    thin = fine.grads.shape[4]
    pieces = [
        (back_any, back_ref),
        (weights_any, weights),
        (ctx_any, ctx_ref),
        (second_any, second_ref),
        (stat_any, stat_ref),
        (qkv_any, qkv_ref),
    ]
    fetch = [pltpu.make_async_copy(s, d, load.at[i]) for i, (s, d) in enumerate(pieces)]
    for copy in fetch:
        copy.start()
    barrier = pltpu.get_barrier_semaphore()

    def flip(value, bit):
        return value + bit - 2 * bit * value

    mates = []
    for f in range(1, 8):
        chip_y = p.z * p.ys + flip(p.y, (f // 2) % 2)
        mates.append((flip(p.a, f // 4), chip_y * 2 + flip(p.core, f % 2)))
    peers = [p.device(p.core, dz, 0, 0) for dz in range(1, p.zs)]
    for device in mates + peers:
        pl.semaphore_signal(barrier, inc=1, device_id=device, device_id_type=MESH)

    full = capacity // 8
    half = width // 2
    lanes = lane_ids(patches)
    aux = aux_ref[...]
    slots = [aux[:, i : i + 1] for i in range(4)]
    gates = [aux[:, 4 + i : 5 + i] for i in range(2)]
    ids = lax.broadcasted_iota(jnp.int32, (patches, full * LANES), 1).astype(full32)
    tail_ids = lane_ids(patches, full * LANES).astype(full32)
    hits = [ids == slots[0], ids == slots[1]]
    lefts = [tail_ids == slots[0], tail_ids == slots[1]]
    rights = [tail_ids == slots[2], tail_ids == slots[3]]

    def mix(marks):
        return (jnp.where(marks[0], gates[0], 0.0) + jnp.where(marks[1], gates[1], 0.0)).astype(low)

    def pick(marks):
        return (marks[0] | marks[1]).astype(full32).astype(low)

    for i in range(full):
        stacked[pl.ds(i * LANES, LANES), :] = ret_ref[:, pl.ds(i * width, width)]
    tail = ret_ref[:, pl.ds(full * width, half)]
    along = nt(cot_ref[...], stacked[...])
    along_left, along_right = nt(cot_ref[:, :half], tail), nt(cot_ref[:, half:], tail)
    dprobs = jnp.zeros((patches, LANES), full32)
    for j in range(2):
        dgate = jnp.sum(jnp.where(hits[j], along, 0.0), axis=1, keepdims=True) + jnp.sum(
            jnp.where(lefts[j], along_left, 0.0) + jnp.where(rights[j], along_right, 0.0), axis=1, keepdims=True
        )
        dprobs = dprobs + jnp.where(lanes == aux[:, 6 + j : 7 + j].astype(jnp.int32), dgate, 0.0)
    probs = probs_ref[...]
    dlogits = (probs * (dprobs - jnp.sum(probs * dprobs, axis=1, keepdims=True))).astype(low)
    fetch[0].wait()
    for i in range(full):
        stacked[pl.ds(i * LANES, LANES), :] = back_ref[:, pl.ds(i * width, width)]
    tail = back_ref[:, pl.ds(full * width, half)]
    fetch[1].wait()
    vec[...] = vector_table(weights, width)

    def vector(i):
        return vec[experts + i : experts + i + 1, :]

    routed = weights[:, 4 * width :]
    work[...] = nn(pick(hits), stacked[...]) + nt(dlogits, routed)
    work[:, :half] = work[:, :half] + nn(pick(lefts), tail)
    work[:, half:] = work[:, half:] + nn(pick(rights), tail)
    sums[...] = jnp.zeros_like(sums)

    def column_sum(slot, values):
        sums[pl.ds(8 * slot, 8), :] = sums[pl.ds(8 * slot, 8), :] + jnp.sum(
            values.reshape(-1, 8, values.shape[-1]), axis=0
        )

    def norm_back(grad, unit, inverse, gain):
        weighted = grad * gain
        return inverse * (
            weighted
            - jnp.mean(weighted, axis=-1, keepdims=True)
            - unit * jnp.mean(weighted * unit, axis=-1, keepdims=True)
        )

    for part in row_parts(patches, chunk):
        unit, inverse = norm_parts(mid_ref[part, :])
        grad = work[part, :]
        column_sum(5, grad * unit)
        column_sum(6, grad)
        total = cot_ref[part, :].astype(full32) + norm_back(grad, unit, inverse, vector(5))
        dmid[part, :] = total
        rounded = total.astype(low)
        branch[part, :] = rounded
        column_sum(4, rounded.astype(full32))
    fetch[2].wait()
    ctx_turned = jnp.transpose(ctx_ref[...])
    for core in range(2):
        columns = pl.ds(core * half, half)
        product = nn(ctx_turned, branch[:, columns])
        main.grads[0, core] = product.reshape(chips, shard2, half).astype(low)
    pl.semaphore_wait(barrier, len(mates) + len(peers))
    main.step0(0)
    third = 256
    for j in range(width // third):
        rows = pl.ds(j * third, third)
        dctx[:, rows] = nt(branch[...], weights[rows, pl.ds(3 * width, width)]).astype(low)
    fetch[3].wait()
    router_rows = nn(jnp.transpose(dlogits.astype(full32)).astype(low), second_ref[...])
    for part in row_parts(patches, chunk):
        unit, inverse = norm_parts(tok_ref[part, :].astype(full32))
        second_ref[part, :] = (unit * vector(0) + vector(1)).astype(low)
        unit_ref[part, :] = unit
        inverse_ref[part, :] = jnp.broadcast_to(inverse, (chunk, LANES))
    normed_turned[...] = jnp.transpose(second_ref[...])
    heads = (
        lax.broadcasted_iota(jnp.int32, (16, width), 1) // HEAD_DIM == lax.broadcasted_iota(jnp.int32, (16, width), 0)
    ).astype(full32).astype(low)
    product = dctx[...].astype(full32) * ctx_ref[...].astype(full32)
    upper = product.astype(low)
    center = nt(heads, upper) + nt(heads, (product - upper.astype(full32)).astype(low))
    fetch[4].wait()
    logs = jnp.transpose(stat_ref[...])
    logs_ref[...] = jnp.concatenate([logs[:16], center], axis=0)
    fetch[5].wait()

    ones = jnp.ones((8, patches), low)
    scale = jnp.asarray(HEAD_DIM**-0.5, low)

    def attend(pair):
        at, trio = pair * LANES, pair * trio_width
        key_at, value_at = pl.ds(trio + LANES, LANES), pl.ds(trio + 2 * LANES, LANES)
        queries = qkv_ref[:, pl.ds(trio, LANES)] * scale
        given = dctx[:, pl.ds(at, LANES)]
        own = lane_ids(patches)
        zero = jnp.zeros_like(queries)
        marks = [own < HEAD_DIM, own >= HEAD_DIM]
        head_queries = [jnp.where(m, queries, zero) for m in marks]
        head_given = [jnp.where(m, given, zero) for m in marks]
        turned_keys = jnp.transpose(qkv_ref[:, key_at] * scale)
        query_parts = [None, None]
        for part in row_parts(patches, chunk):
            keys = qkv_ref[part, key_at]
            values = qkv_ref[part, value_at]
            value_out, key_out = [], []
            for head in range(2):
                log_row = logs_ref[2 * pair + head : 2 * pair + head + 1, :]
                center_row = logs_ref[16 + 2 * pair + head : 17 + 2 * pair + head, :]
                prob = jnp.exp(nt(keys, head_queries[head]) - log_row)
                value_out.append(nn(prob.astype(low), given))
                dscore = (prob * (nt(values, head_given[head]) - center_row)).astype(low)
                key_out.append(nn(dscore, queries))
                head_keys = turned_keys[HEAD_DIM * head : HEAD_DIM * (head + 1), part.start : part.start + part.size]
                piece = nn(head_keys, dscore)
                query_parts[head] = piece if query_parts[head] is None else query_parts[head] + piece
            side = lane_ids(chunk) < HEAD_DIM
            joined[part, LANES : 2 * LANES] = jnp.where(side, key_out[0], key_out[1]).astype(low)
            joined[part, 2 * LANES :] = jnp.where(side, value_out[0], value_out[1]).astype(low)
        turned_query[...] = jnp.concatenate(query_parts, axis=0)
        joined[:, :LANES] = jnp.transpose(turned_query[...]).astype(low)
        product = nn(normed_turned[...], joined[...]).reshape(chips, shard2, trio_width).astype(low)
        if pair < 2 * (coarse - 1):
            main.grads[pair // 2 + 1, pair % 2] = product
        else:
            chunk_of = pair - 2 * (coarse - 1)
            fine.grads[chunk_of, 0] = product[:, :, :thin]
            fine.grads[chunk_of, 1, :, :, :LANES] = product[:, :, thin:]

    def spread(pair):
        trio = pair * trio_width
        part = nt(joined[...], weights[:, pl.ds(trio, trio_width)])
        work[...] = part if pair == 0 else work[...] + part
        column_parts = nn(ones, joined[...])
        sums[16:17, pl.ds(pair * LANES, LANES)] = column_parts[0:1, :LANES]
        sums[24:25, pl.ds(pair * LANES, LANES)] = column_parts[0:1, 2 * LANES :]

    fine.grads[0, 1, :, :, LANES:] = jnp.zeros((chips, shard2, thin - LANES), low)
    main.step1(0)
    attend(0)
    spread(0)
    main.step2(0)
    attend(1)
    main.step0(1)
    spread(1)
    main.step3(0)
    attend(2)
    main.step1(1)
    spread(2)
    attend(3)
    main.step0(2)
    spread(3)
    main.step2(1)
    main.step1(2)
    attend(4)
    fine.step0(0)
    main.step3(1)
    spread(4)
    main.step2(2)
    fine.step1(0)
    attend(5)
    spread(5)
    fine.step2(0)
    for part in row_parts(patches, chunk):
        unit = unit_ref[part, :]
        grad = work[part, :]
        column_sum(0, grad * unit)
        column_sum(1, grad)
    gain = vector(0)
    vec[...] = router_rows
    for i in range(7):
        vec[experts + i : experts + i + 1, :] = jnp.sum(sums[pl.ds(8 * i, 8), :], axis=0, keepdims=True)
    fine.grads[1, 1, :, :, LANES:] = jnp.transpose(vec[...]).reshape(chips, shard2, LANES).astype(low)
    def combine():
        for i in range(full):
            stacked[pl.ds(i * LANES, LANES), :] = ret_ref[:, pl.ds(i * width, width)]
        pieces_of = ret_ref[:, pl.ds(full * width, half)]
        final = nn(mix(hits), stacked[...])
        out_ref[:, :half] = (mid_ref[:, :half] + (final[:, :half] + nn(mix(lefts), pieces_of))).astype(low)
        out_ref[:, half:] = (mid_ref[:, half:] + (final[:, half:] + nn(mix(rights), pieces_of))).astype(low)

    keep_out = pltpu.make_async_copy(out_ref, out_any, store.at[0])
    fine.step0(1)
    main.step3(2)
    fine.step1(1)
    fine.step3(0)
    for part in row_parts(patches, chunk):
        part_grad = norm_back(work[part, :], unit_ref[part, :], inverse_ref[part, 0:1], gain)
        dmid[part, :] = dmid[part, :] + part_grad
    keep_input = pltpu.make_async_copy(dmid, input_any, store.at[1])
    keep_input.start()
    main.step4(0)
    main.step4(1)
    fine.step2(1)
    main.step4(2)
    fine.step4(0)
    combine()
    keep_out.start()
    deep = shard2 // 2
    his = pl.ds(pl.multiple_of((1 - p.core) * deep, 8), deep)
    mine = pl.ds(pl.multiple_of(p.core * deep, 8), deep)
    rows_copy = [
        remote(main.total.at[:, his], row, row_send.at[0], row_recv.at[0], main.partner),
        remote(fine.total.at[0, his], row_fine.at[0], row_send.at[1], row_recv.at[1], main.partner),
        remote(fine.total.at[1, his], row_fine.at[1], row_send.at[2], row_recv.at[2], main.partner),
    ]
    rows_copy[0].start()
    rows_copy[1].start()
    fine.step3(1)

    def squares_of(values):
        folded = jnp.sum((values * values).reshape(-1, 8, values.shape[1]), axis=0)
        out = folded[:, :LANES]
        for j in range(1, values.shape[1] // LANES):
            out = out + folded[:, j * LANES : (j + 1) * LANES]
        return out

    square = part_ref[...]
    for c in range(coarse):
        square = square + squares_of(main.total[c])
    square = square + squares_of(fine.total[0])
    fine.step4(1)
    rows_copy[2].start()
    plane = (p.a * p.ys + p.y) * 2 + p.core
    plane_tiles[plane] = square + squares_of(fine.total[1])

    def mate_copy(f):
        block = plane_tiles.at[plane]
        return remote(block, block, tile_send.at[f], tile_recv.at[f], mates[f - 1])

    def peer_copy(dz):
        block = line_tiles.at[p.z]
        return remote(block, block, tile_send.at[7 + dz], tile_recv.at[7 + dz], peers[dz - 1])

    for f in range(1, 8):
        mate_copy(f).start()

    def put(core, values, fine_values):
        for c in range(coarse):
            dense_ref[:, pl.ds(pl.multiple_of(c * width + core * half, LANES), half)] = values(c)
        for c in range(2):
            at = coarse * width + 2 * c * thin + core * thin
            dense_ref[:, pl.ds(pl.multiple_of(at, LANES), thin)] = fine_values(c)

    put(p.core, lambda c: main.total[c, mine, :], lambda c: fine.total[c, mine, :])
    for f in range(1, 8):
        from_plane = (flip(p.a, f // 4) * p.ys + flip(p.y, (f // 2) % 2)) * 2 + flip(p.core, f % 2)
        block = plane_tiles.at[from_plane]
        remote(block, block, tile_send.at[f], tile_recv.at[f], main.partner).wait_recv()
    total = plane_tiles[0]
    for j in range(1, 8):
        total = total + plane_tiles[j]
    line_tiles[p.z] = total
    for dz in range(1, p.zs):
        peer_copy(dz).start()
    for copy in rows_copy:
        copy.wait_recv()
    put(1 - p.core, lambda c: row[c], lambda c: row_fine[c])
    for dz in range(1, p.zs):
        block = line_tiles.at[lax.rem(p.z + p.zs - dz, p.zs)]
        remote(block, block, tile_send.at[7 + dz], tile_recv.at[7 + dz], main.partner).wait_recv()
    total = line_tiles[0]
    for j in range(1, p.zs):
        total = total + line_tiles[j]
    total_ref[...] = total
    main.finish(coarse)
    fine.finish(2)
    for copy in rows_copy:
        copy.wait_send()
    for f in range(1, 8):
        mate_copy(f).wait_send()
    for dz in range(1, p.zs):
        peer_copy(dz).wait_send()
    keep_out.wait()
    keep_input.wait()


def backward(
    tokens,
    cotangent,
    ret,
    back,
    aux,
    probs,
    mid,
    second,
    ctx,
    stat,
    qkv,
    weights,
    part,
    dp,
    experts,
    capacity,
    cid,
    chunk=576,
):
    patches, width = tokens.shape
    low, full = jnp.bfloat16, jnp.float32
    world = dp * experts
    chips, rows = world // 2, 2 * width // world
    thin = 2 * LANES
    chunks = width // LANES // 2
    columns = 4 * width + 2 * LANES
    return pl.pallas_call(
        functools.partial(backward_kernel, dp, experts, capacity, chunk),
        out_shape=[
            jax.ShapeDtypeStruct((patches, width), low),
            jax.ShapeDtypeStruct((patches, width), full),
            jax.ShapeDtypeStruct((rows // 2, columns), full),
            jax.ShapeDtypeStruct((8, LANES), full),
        ],
        in_specs=[VMEM] * 7 + [ANY] * 6,
        out_specs=[ANY, ANY, VMEM, VMEM],
        scratch_shapes=[
            pltpu.VMEM((patches, width), low),
            pltpu.VMEM((patches, width), full),
            pltpu.VMEM((patches, LANES), full),
            pltpu.VMEM((32, patches), full),
            pltpu.VMEM(back.shape, low),
            pltpu.VMEM((patches, width), low),
            pltpu.VMEM((patches, width), low),
            pltpu.VMEM(stat.shape, full),
            pltpu.VMEM(qkv.shape, low),
            pltpu.VMEM(weights.shape, low),
            pltpu.VMEM((LANES, width), full),
            pltpu.VMEM((capacity // 8 * LANES, width), low),
            pltpu.VMEM((width, patches), low),
            pltpu.VMEM((patches, width), low),
            pltpu.VMEM((patches, width), low),
            pltpu.VMEM((patches, 3 * LANES), low),
            pltpu.VMEM((LANES, patches), full),
            pltpu.VMEM((patches, width), full),
            pltpu.VMEM((patches, width), full),
            pltpu.VMEM((56, width), full),
            pltpu.SemaphoreType.DMA((6,)),
            pltpu.VMEM((chunks, rows // 2, width // 2), full),
            pltpu.VMEM((2, rows // 2, thin), full),
            pltpu.VMEM((8, 8, LANES), full),
            pltpu.VMEM((experts // 4, 8, LANES), full),
            pltpu.SemaphoreType.DMA((3,)),
            pltpu.SemaphoreType.DMA((3,)),
            pltpu.SemaphoreType.DMA((7 + experts // 4,)),
            pltpu.SemaphoreType.DMA((7 + experts // 4,)),
            pltpu.SemaphoreType.DMA((2,)),
            *stage_scratch(chunks, chips, rows, width // 2),
            *stage_scratch(2, chips, rows, thin),
        ],
        compiler_params=pltpu.CompilerParams(
            collective_id=cid, has_side_effects=True, vmem_limit_bytes=60 * 1024 * 1024
        ),
        cost_estimate=pl.CostEstimate(flops=15 * 10**9, bytes_accessed=30 * 10**6, transcendentals=4 * 10**6),
        name="attend_backward",
    )(tokens, cotangent, ret, aux, probs, mid, part, back, second, ctx, stat, qkv, weights)


ORDER = 7
WINDOW = 5
PARTS = 15


def moe_kernel(
    dp,
    experts,
    chunk,
    rows_any,
    dy_any,
    inner_any,
    hidden_ref,
    outer_any,
    return_ref,
    y_any,
    drows_any,
    dinner_any,
    dhidden_ref,
    douter_any,
    dreturn_ref,
    square_ref,
    rows_all,
    dy_all,
    y_pack,
    drows_pack,
    y_theirs,
    drows_theirs,
    rows,
    turned,
    dy,
    inner,
    outer,
    act,
    grad,
    dz,
    acc,
    inner_stage,
    outer_stage,
    dinner_stage,
    douter_stage,
    square,
    own_sem,
    in_send,
    in_recv,
    over_send,
    over_recv,
    part_send,
    part_recv,
    out_send,
    out_recv,
    stage_sem,
    store_sem,
):
    low, full32 = jnp.bfloat16, jnp.float32
    width = rows.shape[1]
    half = width // 2
    full = rows_all.shape[3] // width
    steps = inner.shape[1] // chunk
    groups = 2
    group = experts // groups
    block_rows = dp * group * 8
    deep = rows.shape[0] // groups
    a = lax.axis_index("dp")
    e = lax.axis_index("expert")
    across = (1 - a, e)
    ins, alls = (rows_any, dy_any), (rows_all, dy_all)
    packs, theirs, outs = (y_pack, drows_pack), (y_theirs, drows_theirs), (y_any, drows_any)

    def to(turn):
        return lax.rem(e + lax.rem(ORDER * turn, experts), experts)

    def source(turn):
        return lax.rem(e + experts - lax.rem(ORDER * turn, experts), experts)

    def columns_of(k):
        return pl.ds(pl.multiple_of(k * chunk, chunk), chunk)

    def stage(k, slot):
        return (
            pltpu.make_async_copy(inner_any.at[0, :, columns_of(k)], inner_stage.at[slot], stage_sem.at[0, slot]),
            pltpu.make_async_copy(outer_any.at[0, columns_of(k), :], outer_stage.at[slot], stage_sem.at[1, slot]),
        )

    def own_block(i):
        return pltpu.make_async_copy(ins[i].at[e], alls[i].at[a, 0], own_sem.at[i])

    for slot in range(2):
        for copy in stage(slot, slot):
            copy.start()
    for i in range(2):
        own_block(i).start()
    greet([(a, to(j)) for j in range(1, experts)] + [across])

    def first_send(i, turn):
        return remote(
            ins[i].at[to(turn)], alls[i].at[a, turn], in_send.at[i, turn], in_recv.at[i, turn], (a, to(turn))
        )

    def forward_own(i):
        return remote(ins[i].at[e], alls[i].at[a, 0], over_send.at[i, 0], over_recv.at[i, 0], across)

    def pass_on(i, turn):
        block = alls[i].at[a, turn]
        return remote(block, block, over_send.at[i, turn], over_recv.at[i, turn], across)

    def received(i, turn):
        block = alls[i].at[a, turn]
        return remote(block, block, in_send.at[i, turn], in_recv.at[i, turn], across)

    def from_across(i, turn):
        block = alls[i].at[1 - a, turn]
        return remote(block, block, over_send.at[i, turn], over_recv.at[i, turn], across)

    def part_copy(i, turn):
        return remote(
            packs[i].at[1 - a, turn], theirs[i].at[turn], part_send.at[i, turn], part_recv.at[i, turn], across
        )

    def result_copy(i, turn):
        return remote(
            packs[i].at[a, turn], outs[i].at[e], out_send.at[i, turn], out_recv.at[i, turn], (a, source(turn))
        )

    forward_own(0).start()

    @pl.loop(1, 1 + WINDOW)
    def _(turn):
        first_send(0, turn).start()

    def take_in(i, begin, number):
        @pl.loop(0, number)
        def _(d):
            turn = begin + d

            @pl.when(turn < experts)
            def _():
                received(i, turn).wait_recv()
                pass_on(i, turn).start()

                @pl.when(turn + WINDOW < experts)
                def _():
                    first_send(i, turn + WINDOW).start()

                if i == 0:

                    @pl.when(turn + WINDOW >= experts)
                    def _():
                        first_send(1, turn + WINDOW - experts + 1).start()

    def hand_out(i, begin, number):
        @pl.loop(0, number)
        def _(d):
            turn = begin + d

            @pl.when(turn < experts)
            def _():
                part_copy(i, turn).wait_recv()

                @pl.when(turn + PARTS <= experts)
                def _():
                    part_copy(i, lax.rem(turn + PARTS, experts)).start()

                packs[i][a, turn] = (packs[i][a, turn].astype(full32) + theirs[i][turn].astype(full32)).astype(low)
                result_copy(i, turn).start()

    def finish(i):
        part_copy(i, 0).wait_recv()
        packs[i][a, 0] = (packs[i][a, 0].astype(full32) + theirs[i][0].astype(full32)).astype(low)
        pltpu.make_async_copy(packs[i].at[a, 0], outs[i].at[e], own_sem.at[i]).start()

    def unpack(i, g, place):
        if g == 0:
            own_block(i).wait()

        @pl.loop(g * group, (g + 1) * group)
        def _(turn):
            from_across(i, turn).wait_recv()

        tails = []
        for plane in range(dp):
            for b in range(full):
                piece = alls[i][plane, g * group : (g + 1) * group, :, b * width : (b + 1) * width].astype(full32)
                at = g * deep + b * block_rows + plane * group * 8
                place[pl.ds(at, group * 8), :] = piece.reshape(group * 8, width).astype(low)
            piece = alls[i][plane, g * group : (g + 1) * group, :, full * width :].astype(full32)
            tails.append(piece.reshape(group * 8, half))
        tail = jnp.concatenate(tails, axis=0).astype(low)
        for right in range(2):
            place[pl.ds(g * deep + full * block_rows, block_rows // 2), pl.ds(right * half, half)] = nn(
                tail_picks(block_rows, right), tail
            ).astype(low)

    def pack(i, g):
        tail = acc[pl.ds(g * deep + full * block_rows, block_rows // 2), :].astype(low)
        spread = None
        for right in range(2):
            piece = lax.dot_general(
                tail_picks(block_rows, right),
                tail[:, right * half : (right + 1) * half],
                (((0,), (0,)), ((), ())),
                preferred_element_type=full32,
            )
            spread = piece if spread is None else spread + piece
        for plane in range(dp):
            turns = slice(g * group, (g + 1) * group)
            for b in range(full):
                at = g * deep + b * block_rows + plane * group * 8
                piece = acc[pl.ds(at, group * 8), :].reshape(group, 8, width)
                packs[i][plane, turns, :, b * width : (b + 1) * width] = piece.astype(low)
            piece = spread[plane * group * 8 : (plane + 1) * group * 8].reshape(group, 8, half)
            packs[i][plane, turns, :, full * width :] = piece.astype(low)

    def send_parts(i):
        @pl.loop(1, 1 + PARTS)
        def _(turn):
            part_copy(i, turn).start()

    @pl.loop(0, steps)
    def _(k):
        slot = lax.rem(k, 2)
        for copy in stage(k, slot):
            copy.wait()
        inner[:, columns_of(k)] = inner_stage[slot].astype(low)
        outer[columns_of(k), :] = outer_stage[slot].astype(low)

        @pl.when(k + 2 < steps)
        def _():
            for copy in stage(k + 2, slot):
                copy.start()

        take_in(0, 1 + k, 1)

    part = return_ref.shape[1]
    bias = return_ref[...].astype(low).astype(full32)
    for i in range(dp):
        acc[:, pl.ds(i * part, part)] = jnp.broadcast_to(jnp.where(a == i, bias, 0.0), (rows.shape[0], part))

    def onward(g):
        mine = pl.ds(g * deep, deep)

        def run(k):
            columns = columns_of(k)
            z = nn(rows[mine, :], inner[:, columns]) + hidden_ref[:, columns].astype(low).astype(full32)
            value, slope = gelu_both(z)
            act[mine, columns] = value.astype(low)
            grad[mine, columns] = slope
            acc[mine, :] += nn(act[mine, columns], outer[columns, :])

        return run

    def backward_of(g):
        mine = pl.ds(g * deep, deep)

        def run(k):
            columns = columns_of(k)
            dz[mine, columns] = (nt(dy[mine, :], outer[columns, :]) * grad[mine, columns]).astype(low)
            acc[mine, :] += nt(dz[mine, columns], inner[:, columns])

        return run

    forward_own(1).start()
    early = 1 + steps
    take_in(0, early, 4)
    early += 4
    unpack(0, 0, rows)
    forward_of = onward(0)
    left = experts - early

    @pl.loop(0, steps)
    def _(k):
        forward_of(k)
        take_in(0, early + k, 1)

        @pl.when(k >= left)
        def _():
            take_in(1, 1 + k - left, 1)

    taken = 1 + max(steps - left, 0)
    unpack(0, 1, rows)
    forward_late = onward(1)

    @pl.loop(0, steps)
    def _(k):
        forward_late(k)
        take_in(1, taken + k, 1)

    taken += steps
    for g in range(groups):
        pack(0, g)
    turned[...] = jnp.transpose(rows[...])
    take_in(1, taken, 2)
    taken += 2
    acc[...] = jnp.zeros_like(acc)
    unpack(1, 0, dy)
    back_first = backward_of(0)

    @pl.loop(0, steps)
    def _(k):
        back_first(k)
        take_in(1, taken + k, 1)

    taken += steps
    take_in(1, taken, max(experts - taken, 0))
    send_parts(0)
    pack(1, 0)
    unpack(1, 1, dy)
    back_last = backward_of(1)

    @pl.loop(0, steps)
    def _(k):
        back_last(k)
        hand_out(0, 1 + k, 1)

    pack(1, 1)
    send_parts(1)
    total = jnp.zeros((1, width), full32)
    for i in range(rows.shape[0] // LANES):
        total = total + jnp.sum(dy[pl.ds(i * LANES, LANES), :].astype(full32), axis=0, keepdims=True)
    picked = total[:, :part]
    for i in range(1, dp):
        picked = jnp.where(a == i, total[:, i * part : (i + 1) * part], picked)
    dreturn_ref[...] = picked
    square[...] = jnp.zeros_like(square)
    flat = picked * picked
    for i in range(part // LANES):
        square[0:1, :] = square[0:1, :] + flat[:, i * LANES : (i + 1) * LANES]

    def store(k, slot):
        return (
            pltpu.make_async_copy(dinner_stage.at[slot], dinner_any.at[0, :, columns_of(k)], store_sem.at[0, slot]),
            pltpu.make_async_copy(douter_stage.at[slot], douter_any.at[0, columns_of(k), :], store_sem.at[1, slot]),
        )

    later = -(-(experts - 1 - steps) // (steps - 1))

    @pl.loop(0, steps)
    def _(k):
        slot = lax.rem(k, 2)
        columns = columns_of(k)
        douter = nn(jnp.transpose(act[:, columns]), dy[...])
        dinner = nn(turned[...], dz[:, columns])
        dhidden = jnp.sum(dz[:, columns].astype(full32), axis=0, keepdims=True)

        @pl.when(k >= 2)
        def _():
            for copy in store(k - 2, slot):
                copy.wait()

        douter_stage[slot] = douter.astype(low)
        dinner_stage[slot] = dinner.astype(low)
        for copy in store(k, slot):
            copy.start()
        dhidden_ref[:, columns] = dhidden
        parts = jnp.zeros((8, LANES), full32)
        folded = jnp.sum((douter * douter).reshape(-1, 8, width), axis=0)
        for i in range(width // LANES):
            parts = parts + folded[:, i * LANES : (i + 1) * LANES]
        folded = jnp.sum((dinner * dinner).reshape(-1, 8, chunk), axis=0)
        hidden_square = dhidden * dhidden
        for i in range(chunk // LANES):
            parts = parts + folded[:, i * LANES : (i + 1) * LANES]
            square[0:1, :] = square[0:1, :] + hidden_square[:, i * LANES : (i + 1) * LANES]
        square[...] += parts
        hand_out(0, 1 + steps + k * later, later)

    finish(0)
    hand_out(1, 1, experts - 1)
    finish(1)
    square_ref[...] = square[...]
    for k in range(steps - 2, steps):
        for copy in store(k, k % 2):
            copy.wait()
    for i in range(2):

        @pl.loop(1, experts)
        def _(turn):
            block = outs[i].at[to(turn)]
            remote(block, block, out_send.at[i, turn], out_recv.at[i, turn], across).wait_recv()

    for i in range(2):
        pltpu.make_async_copy(packs[i].at[a, 0], outs[i].at[e], own_sem.at[i]).wait()
        forward_own(i).wait_send()
        part_copy(i, 0).wait_send()

        @pl.loop(1, experts)
        def _(turn):
            first_send(i, turn).wait_send()
            pass_on(i, turn).wait_send()
            part_copy(i, turn).wait_send()
            result_copy(i, turn).wait_send()


def mixture(rows, dy, inner, hidden, outer, back, dp, cid, chunk=256):
    experts, _, packed = rows.shape
    width, units = inner.shape[1:]
    count = dp * experts * 8
    total = count * packed // width
    low, full = jnp.bfloat16, jnp.float32
    both = (dp, experts, 8, packed)
    sems = [pltpu.SemaphoreType.DMA((2, experts)) for _ in range(8)]
    return pl.pallas_call(
        functools.partial(moe_kernel, dp, experts, chunk),
        out_shape=[
            jax.ShapeDtypeStruct(rows.shape, low),
            jax.ShapeDtypeStruct(rows.shape, low),
            jax.ShapeDtypeStruct(inner.shape, low),
            jax.ShapeDtypeStruct(hidden.shape, full),
            jax.ShapeDtypeStruct(outer.shape, low),
            jax.ShapeDtypeStruct(back.shape, full),
            jax.ShapeDtypeStruct((8, LANES), full),
        ],
        in_specs=[ANY, ANY, ANY, VMEM, ANY, VMEM],
        out_specs=[ANY, ANY, ANY, VMEM, ANY, VMEM, VMEM],
        scratch_shapes=[
            pltpu.VMEM(both, low),
            pltpu.VMEM(both, low),
            pltpu.VMEM(both, low),
            pltpu.VMEM(both, low),
            pltpu.VMEM(both[1:], low),
            pltpu.VMEM(both[1:], low),
            pltpu.VMEM((total, width), low),
            pltpu.VMEM((width, total), low),
            pltpu.VMEM((total, width), low),
            pltpu.VMEM((width, units), low),
            pltpu.VMEM((units, width), low),
            pltpu.VMEM((total, units), low),
            pltpu.VMEM((total, units), full),
            pltpu.VMEM((total, units), low),
            pltpu.VMEM((total, width), full),
            pltpu.VMEM((2, width, chunk), full),
            pltpu.VMEM((2, chunk, width), full),
            pltpu.VMEM((2, width, chunk), low),
            pltpu.VMEM((2, chunk, width), low),
            pltpu.VMEM((8, LANES), full),
            pltpu.SemaphoreType.DMA((2,)),
            *sems,
            pltpu.SemaphoreType.DMA((2, 2)),
            pltpu.SemaphoreType.DMA((2, 2)),
        ],
        compiler_params=pltpu.CompilerParams(
            collective_id=cid, has_side_effects=True, vmem_limit_bytes=60 * 1024 * 1024
        ),
        cost_estimate=pl.CostEstimate(flops=17 * 10**9, bytes_accessed=25 * 10**6, transcendentals=2 * 10**6),
        name="mixture",
    )(rows, dy, inner, hidden, outer, back)


def adam_values(weight, first, second, gradient, clip, rate, decay):
    scaled = gradient * clip
    first_new = BETA_ONE * first + (1.0 - BETA_ONE) * scaled
    second_new = BETA_TWO * second + (1.0 - BETA_TWO) * scaled * scaled
    first_hat = first_new * (1.0 / (1.0 - BETA_ONE**STEP))
    second_hat = second_new * (1.0 / (1.0 - BETA_TWO**STEP))
    weight_new = weight - rate * (first_hat / (jnp.sqrt(second_hat) + ADAM_EPS) + decay * weight)
    return weight_new, first_new, second_new


def adam_kernel(experts, norm_ref, dense_any, *refs):
    small = 6
    large_ins, rest = refs[:8], refs[8:]
    small_ins, rest = rest[: 3 * small + 2], rest[3 * small + 2 :]
    large_outs, rest = rest[:6], rest[6:]
    small_outs, norm_out, rest = rest[: 3 * small], rest[3 * small], rest[3 * small + 1 :]
    held, dense_ref, load, store = rest[: 3 * small + 2], rest[3 * small + 2], rest[-2], rest[-1]
    step, steps = pl.program_id(0), pl.num_programs(0)
    loads = [pltpu.make_async_copy(s, d, load.at[i]) for i, (s, d) in enumerate(zip(small_ins, held))]
    loads.append(pltpu.make_async_copy(dense_any, dense_ref, load.at[3 * small + 2]))
    stores = [pltpu.make_async_copy(s, d, store.at[i]) for i, (s, d) in enumerate(zip(held, small_outs))]

    @pl.when(step == 0)
    def _():
        for copy in loads:
            copy.start()

    total = jnp.sum(jnp.sum(norm_ref[...], axis=0, keepdims=True), axis=1, keepdims=True)
    norm = jnp.sqrt(total)
    clip = THRESHOLD / jnp.maximum(norm, THRESHOLD)
    for i, rate in enumerate((RATE_INNER, RATE_OUTER)):
        grad = large_ins[6 + i][...].astype(jnp.float32)
        state = [ref[...] for ref in large_ins[3 * i : 3 * i + 3]]
        for place, value in zip(large_outs[3 * i : 3 * i + 3], adam_values(*state, grad, clip, rate, DECAY)):
            place[...] = value

    def update(i, grad, rate, decay, columns=slice(None)):
        places = held[3 * i : 3 * i + 3]
        new = adam_values(*(ref[:, columns] for ref in places), grad, clip, rate, decay)
        for place, value in zip(places, new):
            place[:, columns] = value

    @pl.when(step == 1)
    def _():
        for copy in loads:
            copy.wait()
        norm_out[...] = norm
        width = held[3].shape[1]
        trio = 3 * LANES
        for pair in range(width // LANES):
            base = width + pair * trio + (LANES if pair == width // LANES - 1 else 0)
            for kind in range(3):
                update(
                    0,
                    dense_ref[:, base + kind * LANES : base + (kind + 1) * LANES],
                    RATE_PROJECTION,
                    DECAY,
                    slice(kind * width + pair * LANES, kind * width + (pair + 1) * LANES),
                )
        update(1, dense_ref[:, :width], RATE_OUTPUT, DECAY)
        turned = jnp.transpose(dense_ref[:, dense_ref.shape[1] - LANES :])
        update(2, turned[:experts], RATE_ROUTER, DECAY)
        update(3, turned[experts : experts + 7], RATE_VECTORS, 0.0)
        update(4, held[3 * small][...], RATE_HIDDEN, 0.0)
        update(5, held[3 * small + 1][...], RATE_RETURN, 0.0)
        for copy in stores:
            copy.start()

    @pl.when(step == steps - 1)
    def _():
        for copy in stores:
            copy.wait()


def adam_all(experts, squares, dense, states, grads, steps=8):
    full = jnp.float32

    def blocks(array):
        return pl.BlockSpec((array.shape[0] // steps, array.shape[1]), lambda i: (i, 0))

    large = [v for group in states[:2] for v in group]
    small = [v for group in states[2:] for v in group]
    spread = [blocks(v) for v in large]
    held = small + list(grads[2:])
    out = pl.pallas_call(
        functools.partial(adam_kernel, experts),
        grid=(steps,),
        out_shape=[jax.ShapeDtypeStruct(v.shape, full) for v in large + small] + [jax.ShapeDtypeStruct((1, 1), full)],
        in_specs=[pl.BlockSpec(squares.shape, lambda i: (0, 0)), ANY]
        + spread
        + [blocks(v) for v in grads[:2]]
        + [ANY] * len(held),
        out_specs=spread + [ANY] * len(small) + [pl.BlockSpec((1, 1), lambda i: (0, 0))],
        scratch_shapes=[pltpu.VMEM(v.shape, full) for v in held]
        + [
            pltpu.VMEM(dense.shape, full),
            pltpu.SemaphoreType.DMA((len(held) + 1,)),
            pltpu.SemaphoreType.DMA((len(small),)),
        ],
        compiler_params=pltpu.CompilerParams(
            vmem_limit_bytes=60 * 1024 * 1024, dimension_semantics=("arbitrary",)
        ),
        cost_estimate=pl.CostEstimate(flops=5 * 10**7, bytes_accessed=62 * 10**6, transcendentals=10**7),
        name="adam_all",
    )(squares, dense, *large, *grads[:2], *held)
    return [tuple(out[3 * i : 3 * i + 3]) for i in range(len(states))], out[-1].reshape(())


def fits(dp, experts):
    return dp == 2 and experts == 16


def fast_shards(
    dp,
    experts,
    tokens,
    cotangent,
    expert_choice,
    priority,
    projection,
    projection_first,
    projection_second,
    output_weight,
    output_first,
    output_second,
    router_weight,
    router_first,
    router_second,
    vectors,
    vectors_first,
    vectors_second,
    expert_inner,
    inner_first,
    inner_second,
    hidden_bias,
    hidden_first,
    hidden_second,
    expert_outer,
    outer_first,
    outer_second,
    return_bias,
    return_first,
    return_second,
):
    patches = tokens.shape[1]
    capacity = max(2, patches // experts)
    rows, dy, aux, probs, qkv, ctx, mid, second, stat, weights = forward(
        tokens[0],
        cotangent[0],
        expert_choice[0],
        priority[0],
        projection,
        output_weight,
        router_weight,
        vectors,
        dp,
        experts,
        capacity,
        1,
    )
    blocks = (experts, 8, rows.shape[1])
    returned, back_rows, inner_grad, hidden_grad, outer_grad, return_grad, expert_square = mixture(
        rows.reshape(blocks),
        dy.reshape(blocks),
        expert_inner,
        hidden_bias,
        expert_outer,
        return_bias,
        dp,
        2,
    )
    block_output, input_grad, dense, squares = backward(
        tokens[0],
        cotangent[0],
        returned.reshape(rows.shape),
        back_rows.reshape(rows.shape),
        aux,
        probs,
        mid,
        second,
        ctx,
        stat,
        qkv,
        weights,
        expert_square,
        dp,
        experts,
        capacity,
        4,
    )
    states, grad_norm = adam_all(
        experts,
        squares,
        dense,
        [
            (expert_inner[0], inner_first[0], inner_second[0]),
            (expert_outer[0], outer_first[0], outer_second[0]),
            (projection, projection_first, projection_second),
            (output_weight, output_first, output_second),
            (router_weight.T, router_first.T, router_second.T),
            (vectors, vectors_first, vectors_second),
            (hidden_bias, hidden_first, hidden_second),
            (return_bias, return_first, return_second),
        ],
        [inner_grad[0], outer_grad[0], hidden_grad, return_grad],
    )
    inner_new, outer_new, projection_new, output_new, router_new, vectors_new, hidden_new, return_new = states
    return (
        block_output[None],
        input_grad[None],
        grad_norm,
        *projection_new,
        *output_new,
        *(v.T for v in router_new),
        *vectors_new,
        *(v[None] for v in inner_new),
        *hidden_new,
        *(v[None] for v in outer_new),
        *return_new,
    )


def solution(mesh):
    dp, experts = mesh.shape["dp"], mesh.shape["expert"]
    body = functools.partial(fast_shards, dp, experts) if fits(dp, experts) else shards
    return jax.shard_map(
        body,
        mesh=mesh,
        in_specs=(
            P(("dp", "expert"), None, None),
            P(("dp", "expert"), None, None),
            P(("dp", "expert"), None, None),
            P(("dp", "expert"), None),
            P(("dp", "expert"), None),
            P(("dp", "expert"), None),
            P(("dp", "expert"), None),
            P(("dp", "expert"), None),
            P(("dp", "expert"), None),
            P(("dp", "expert"), None),
            P(("dp", "expert"), None),
            P(("dp", "expert"), None),
            P(("dp", "expert"), None),
            P(None, ("dp", "expert")),
            P(None, ("dp", "expert")),
            P(None, ("dp", "expert")),
            P("expert", None, "dp"),
            P("expert", None, "dp"),
            P("expert", None, "dp"),
            P("expert", "dp"),
            P("expert", "dp"),
            P("expert", "dp"),
            P("expert", "dp", None),
            P("expert", "dp", None),
            P("expert", "dp", None),
            P("expert", "dp"),
            P("expert", "dp"),
            P("expert", "dp"),
        ),
        out_specs=(
            P(("dp", "expert"), None, None),
            P(("dp", "expert"), None, None),
            P(),
            P(("dp", "expert"), None),
            P(("dp", "expert"), None),
            P(("dp", "expert"), None),
            P(("dp", "expert"), None),
            P(("dp", "expert"), None),
            P(("dp", "expert"), None),
            P(("dp", "expert"), None),
            P(("dp", "expert"), None),
            P(("dp", "expert"), None),
            P(None, ("dp", "expert")),
            P(None, ("dp", "expert")),
            P(None, ("dp", "expert")),
            P("expert", None, "dp"),
            P("expert", None, "dp"),
            P("expert", None, "dp"),
            P("expert", "dp"),
            P("expert", "dp"),
            P("expert", "dp"),
            P("expert", "dp", None),
            P("expert", "dp", None),
            P("expert", "dp", None),
            P("expert", "dp"),
            P("expert", "dp"),
            P("expert", "dp"),
        ),
        check_vma=False,
    )
```

```python
import functools

import jax
import jax.numpy as jnp
from jax import lax
from jax.experimental import pallas as pl
from jax.experimental.pallas import tpu as pltpu
from jax.sharding import PartitionSpec as P

HEADS = 12
HEAD_DIM = 64
STEP = 10


NORM_EPS = 1e-06
ADAM_EPS = 1e-08
BETA_ONE = 0.9
BETA_TWO = 0.999
DECAY = 0.1
THRESHOLD = 1.0
RATE_PROJECTION = 0.1
RATE_OUTPUT = 1.0
RATE_ROUTER = 0.05
RATE_VECTORS = 0.5
RATE_INNER = 0.1
RATE_HIDDEN = 0.25
RATE_OUTER = 1.5
RATE_RETURN = 2.0


def layer_norm(values, norm_gain, norm_bias):
    center = values - jnp.mean(values, axis=-1, keepdims=True)
    spread = jnp.mean(center * center, axis=-1, keepdims=True)
    return center * lax.rsqrt(spread + NORM_EPS) * norm_gain + norm_bias


def smooth_gate(values):
    return jax.nn.gelu(values, approximate=True)


def mixed_dot(left, right):
    return jnp.dot(left, right, preferred_element_type=jnp.float32)


def rows_product(left, right):
    return lax.dot_general(
        left, right, (((0,), (0,)), ((), ())), preferred_element_type=jnp.float32
    )


def columns_product(left, right):
    return lax.dot_general(
        left, right, (((1,), (1,)), ((), ())), preferred_element_type=jnp.float32
    )


def assign_slots(chosen, claim_order, expert_count, capacity):
    patches = chosen.shape[0]
    top_count = chosen.shape[1]
    claim_rank = (
        jnp.arange(top_count, dtype=jnp.int32)[None, :] * patches + claim_order[:, None]
    ).T.reshape(-1)
    flat_choice = chosen.T.reshape(-1)
    onehot = (flat_choice[:, None] == jnp.arange(expert_count, dtype=jnp.int32)[None, :]).astype(
        jnp.float32
    )
    earlier = (claim_rank[None, :] < claim_rank[:, None]).astype(jnp.float32)
    counts = jnp.dot(
        earlier, onehot, precision=lax.Precision.HIGHEST, preferred_element_type=jnp.float32
    )
    position = jnp.sum(counts * onehot, axis=1).astype(jnp.int32).reshape(top_count, patches).T
    kept_mask = position < capacity
    flat_slot = chosen * capacity + jnp.minimum(position, capacity - 1)
    return (flat_slot, kept_mask)


def slot_matches(flat_slot, kept_mask, slot_count):
    slot_ids = jnp.arange(slot_count, dtype=jnp.int32)
    return (flat_slot[None, :, :] == slot_ids[:, None, None]) & kept_mask[None, :, :]


def select_gates(logits, chosen, expert_count):
    router_probs = jax.nn.softmax(logits, axis=-1)
    onehot = chosen[:, :, None] == jnp.arange(expert_count, dtype=jnp.int32)[None, None, :]
    return jnp.sum(jnp.where(onehot, router_probs[:, None, :], 0.0), axis=2)


def adam_update(weight, first_state, second, gradient, clip_factor, step_rate, decay_rate):
    scaled = gradient * clip_factor
    first_new = BETA_ONE * first_state + (1.0 - BETA_ONE) * scaled
    second_new = BETA_TWO * second + (1.0 - BETA_TWO) * scaled * scaled
    first_hat = first_new / (1.0 - BETA_ONE**STEP)
    second_hat = second_new / (1.0 - BETA_TWO**STEP)
    weight_new = weight - step_rate * (
        first_hat / (jnp.sqrt(second_hat) + ADAM_EPS) + decay_rate * weight
    )
    return (weight_new, first_new, second_new)


def shards(
    tokens,
    cotangent,
    expert_choice,
    priority,
    projection,
    projection_first,
    projection_second,
    output_weight,
    output_first,
    output_second,
    router_weight,
    router_first,
    router_second,
    vectors,
    vectors_first,
    vectors_second,
    expert_inner,
    inner_first,
    inner_second,
    hidden_bias,
    hidden_first,
    hidden_second,
    expert_outer,
    outer_first,
    outer_second,
    return_bias,
    return_first,
    return_second,
):
    model_width = tokens.shape[2]
    patches = tokens.shape[1]
    experts = lax.axis_size("expert")
    capacity = max(2, patches // experts)
    slot_count = experts * capacity
    score_scale = HEAD_DIM ** (-0.5)
    dense_shards = (
        projection.astype(jnp.bfloat16),
        output_weight.astype(jnp.bfloat16),
        router_weight.astype(jnp.bfloat16),
        vectors.astype(jnp.bfloat16),
    )
    partial_shards = (
        lax.all_gather(dense_shards[0], "expert", axis=0, tiled=True),
        lax.all_gather(dense_shards[1], "expert", axis=0, tiled=True),
        lax.all_gather(dense_shards[2], "expert", axis=0, tiled=True),
        lax.all_gather(dense_shards[3], "expert", axis=1, tiled=True),
    )
    whole_projection, whole_output, whole_router, whole_vectors = (
        lax.all_gather(partial_shards[0], "dp", axis=0, tiled=True),
        lax.all_gather(partial_shards[1], "dp", axis=0, tiled=True),
        lax.all_gather(partial_shards[2], "dp", axis=0, tiled=True),
        lax.all_gather(partial_shards[3], "dp", axis=1, tiled=True),
    )
    inner_low = expert_inner.astype(jnp.bfloat16)
    hidden_low = hidden_bias.astype(jnp.bfloat16)
    outer_low = expert_outer.astype(jnp.bfloat16)
    return_low = return_bias.astype(jnp.bfloat16)
    inner_all, hidden_all, outer_all, return_all = (
        lax.all_gather(inner_low, "dp", axis=2, tiled=True),
        lax.all_gather(hidden_low, "dp", axis=1, tiled=True),
        lax.all_gather(outer_low, "dp", axis=1, tiled=True),
        lax.all_gather(return_low, "dp", axis=1, tiled=True),
    )
    vector_rows = whole_vectors.astype(jnp.float32)
    image_rows = tokens[0].astype(jnp.float32)
    normed_one, norm_back_one = jax.vjp(layer_norm, image_rows, vector_rows[0], vector_rows[1])
    normed_low = normed_one.astype(jnp.bfloat16)
    projected = mixed_dot(normed_low, whole_projection)
    queries = (
        (projected[:, :model_width] + vector_rows[2])
        .astype(jnp.bfloat16)
        .reshape(patches, HEADS, HEAD_DIM)
    )
    key_rows = (
        projected[:, model_width : 2 * model_width]
        .astype(jnp.bfloat16)
        .reshape(patches, HEADS, HEAD_DIM)
    )
    value_rows = (
        (projected[:, 2 * model_width :] + vector_rows[3])
        .astype(jnp.bfloat16)
        .reshape(patches, HEADS, HEAD_DIM)
    )
    scores = (
        jnp.einsum("qhd,khd->hqk", queries, key_rows, preferred_element_type=jnp.float32)
        * score_scale
    )
    score_top = jnp.max(scores, axis=-1, keepdims=True)
    raised = jnp.exp(scores - score_top)
    totals = jnp.sum(raised, axis=-1, keepdims=True)
    attention = raised / totals
    log_total = score_top + jnp.log(totals)
    context = (
        jnp.einsum(
            "hqk,khd->qhd",
            attention.astype(jnp.bfloat16),
            value_rows,
            preferred_element_type=jnp.float32,
        )
        .reshape(patches, model_width)
        .astype(jnp.bfloat16)
    )
    middle = image_rows + (mixed_dot(context, whole_output) + vector_rows[4])
    normed_two, norm_back_two = jax.vjp(layer_norm, middle, vector_rows[5], vector_rows[6])
    second_low = normed_two.astype(jnp.bfloat16)
    logits = mixed_dot(second_low, whole_router)
    chosen = expert_choice[0]

    def gate_choice(values):
        return select_gates(values, chosen, experts)

    gate_values, gate_back = jax.vjp(gate_choice, logits)
    flat_slot, kept_mask = assign_slots(chosen, priority[0], experts, capacity)
    matches = slot_matches(flat_slot, kept_mask, slot_count)
    slot_table = jnp.any(matches, axis=2).astype(jnp.bfloat16)
    dispatched = (
        mixed_dot(slot_table, second_low)
        .astype(jnp.bfloat16)
        .reshape(experts, capacity, model_width)
    )
    arrived = lax.all_to_all(dispatched, "expert", split_axis=0, concat_axis=0, tiled=True).reshape(
        slot_count, model_width
    )
    pre_act = mixed_dot(arrived, inner_all[0]) + hidden_all[0].astype(jnp.float32)
    activated, gelu_back = jax.vjp(smooth_gate, pre_act)
    active_low = activated.astype(jnp.bfloat16)
    expert_out = (mixed_dot(active_low, outer_all[0]) + return_all[0].astype(jnp.float32)).astype(
        jnp.bfloat16
    )
    returned = lax.all_to_all(
        expert_out.reshape(experts, capacity, model_width),
        "expert",
        split_axis=0,
        concat_axis=0,
        tiled=True,
    ).reshape(slot_count, model_width)
    picked = returned[flat_slot].astype(jnp.float32)
    weighted = jnp.where(kept_mask, gate_values, 0.0)
    final = middle + jnp.sum(weighted[:, :, None] * picked, axis=1)
    block_output = final.astype(jnp.bfloat16)[None]
    upstream = cotangent[0].astype(jnp.float32)
    gate_grad = jnp.where(kept_mask, jnp.sum(upstream[:, None, :] * picked, axis=2), 0.0)
    slot_gate = jnp.sum(jnp.where(matches, weighted[None, :, :], 0.0), axis=(1, 2))
    slot_grad = (mixed_dot(slot_table, cotangent[0]) * slot_gate[:, None]).astype(jnp.bfloat16)
    sent_grad = lax.all_to_all(
        slot_grad.reshape(experts, capacity, model_width),
        "expert",
        split_axis=0,
        concat_axis=0,
        tiled=True,
    ).reshape(slot_count, model_width)
    outer_grad = rows_product(active_low, sent_grad)
    return_grad = jnp.sum(sent_grad, axis=0, dtype=jnp.float32)
    active_grad = columns_product(sent_grad, outer_all[0])
    (pre_grad,) = gelu_back(active_grad)
    pre_low = pre_grad.astype(jnp.bfloat16)
    inner_grad = rows_product(arrived, pre_low)
    hidden_grad = jnp.sum(pre_low, axis=0, dtype=jnp.float32)
    row_grad = columns_product(pre_low, inner_all[0]).astype(jnp.bfloat16)
    expert_grads = (
        lax.psum_scatter(
            inner_grad[None].astype(jnp.bfloat16), "dp", scatter_dimension=2, tiled=True
        ).astype(jnp.float32),
        lax.psum_scatter(
            hidden_grad[None].astype(jnp.bfloat16), "dp", scatter_dimension=1, tiled=True
        ).astype(jnp.float32),
        lax.psum_scatter(
            outer_grad[None].astype(jnp.bfloat16), "dp", scatter_dimension=1, tiled=True
        ).astype(jnp.float32),
        lax.psum_scatter(
            return_grad[None].astype(jnp.bfloat16), "dp", scatter_dimension=1, tiled=True
        ).astype(jnp.float32),
    )
    back_rows = lax.all_to_all(
        row_grad.reshape(experts, capacity, model_width),
        "expert",
        split_axis=0,
        concat_axis=0,
        tiled=True,
    ).reshape(slot_count, model_width)
    (logit_grad,) = gate_back(gate_grad)
    logit_low = logit_grad.astype(jnp.bfloat16)
    router_grad = rows_product(second_low, logit_low)
    second_grad = rows_product(slot_table, back_rows) + columns_product(logit_low, whole_router)
    middle_part, gain_two_grad, bias_two_grad = norm_back_two(second_grad)
    middle_grad = upstream + middle_part
    branch_low = middle_grad.astype(jnp.bfloat16)
    output_grad = rows_product(context, branch_low)
    out_bias_grad = jnp.sum(branch_low, axis=0, dtype=jnp.float32)
    context_grad = (
        columns_product(branch_low, whole_output)
        .astype(jnp.bfloat16)
        .reshape(patches, HEADS, HEAD_DIM)
    )
    scores = (
        jnp.einsum("qhd,khd->hqk", queries, key_rows, preferred_element_type=jnp.float32)
        * score_scale
    )
    attention = jnp.exp(scores - log_total)
    attention_grad = jnp.einsum(
        "qhd,khd->hqk", context_grad, value_rows, preferred_element_type=jnp.float32
    )
    value_grad = jnp.einsum(
        "hqk,qhd->khd",
        attention.astype(jnp.bfloat16),
        context_grad,
        preferred_element_type=jnp.float32,
    ).astype(jnp.bfloat16)
    centered = jnp.sum(attention * attention_grad, axis=-1, keepdims=True)
    score_grad = (attention * (attention_grad - centered)).astype(jnp.bfloat16)
    query_grad = (
        (
            jnp.einsum("hqk,khd->qhd", score_grad, key_rows, preferred_element_type=jnp.float32)
            * score_scale
        )
        .astype(jnp.bfloat16)
        .reshape(patches, model_width)
    )
    key_grad = (
        (
            jnp.einsum("hqk,qhd->khd", score_grad, queries, preferred_element_type=jnp.float32)
            * score_scale
        )
        .astype(jnp.bfloat16)
        .reshape(patches, model_width)
    )
    value_flat = value_grad.reshape(patches, model_width)
    joined_grad = jnp.concatenate([query_grad, key_grad, value_flat], axis=1)
    projection_grad = rows_product(normed_low, joined_grad)
    normed_grad = columns_product(joined_grad, whole_projection)
    input_part, gain_one_grad, bias_one_grad = norm_back_one(normed_grad)
    input_grad = (middle_grad + input_part)[None]
    vector_grad = jnp.stack(
        [
            gain_one_grad,
            bias_one_grad,
            jnp.sum(query_grad, axis=0, dtype=jnp.float32),
            jnp.sum(value_flat, axis=0, dtype=jnp.float32),
            out_bias_grad,
            gain_two_grad,
            bias_two_grad,
        ]
    )
    local_grads = (projection_grad, output_grad, router_grad, vector_grad)
    partial_grads = (
        lax.psum_scatter(
            local_grads[0].astype(jnp.bfloat16), "dp", scatter_dimension=0, tiled=True
        ).astype(jnp.float32),
        lax.psum_scatter(
            local_grads[1].astype(jnp.bfloat16), "dp", scatter_dimension=0, tiled=True
        ).astype(jnp.float32),
        lax.psum_scatter(
            local_grads[2].astype(jnp.bfloat16), "dp", scatter_dimension=0, tiled=True
        ).astype(jnp.float32),
        lax.psum_scatter(
            local_grads[3].astype(jnp.bfloat16), "dp", scatter_dimension=1, tiled=True
        ).astype(jnp.float32),
    )
    dense_grads = (
        lax.psum_scatter(
            partial_grads[0].astype(jnp.bfloat16), "expert", scatter_dimension=0, tiled=True
        ).astype(jnp.float32),
        lax.psum_scatter(
            partial_grads[1].astype(jnp.bfloat16), "expert", scatter_dimension=0, tiled=True
        ).astype(jnp.float32),
        lax.psum_scatter(
            partial_grads[2].astype(jnp.bfloat16), "expert", scatter_dimension=0, tiled=True
        ).astype(jnp.float32),
        lax.psum_scatter(
            partial_grads[3].astype(jnp.bfloat16), "expert", scatter_dimension=1, tiled=True
        ).astype(jnp.float32),
    )
    all_grads = tuple(dense_grads) + tuple(expert_grads)
    local_square = jnp.sum(all_grads[0] * all_grads[0])
    for gradient in all_grads[1:]:
        local_square = local_square + jnp.sum(gradient * gradient)
    square_total = lax.psum(local_square, ("dp", "expert"))
    grad_norm = jnp.sqrt(square_total)
    clip_factor = THRESHOLD / jnp.maximum(grad_norm, THRESHOLD)
    projection_next, projection_moment, projection_square = adam_update(
        projection,
        projection_first,
        projection_second,
        all_grads[0],
        clip_factor,
        RATE_PROJECTION,
        DECAY,
    )
    output_next, output_moment, output_square = adam_update(
        output_weight, output_first, output_second, all_grads[1], clip_factor, RATE_OUTPUT, DECAY
    )
    router_next, router_moment, router_square = adam_update(
        router_weight, router_first, router_second, all_grads[2], clip_factor, RATE_ROUTER, DECAY
    )
    vectors_next, vectors_moment, vectors_square = adam_update(
        vectors, vectors_first, vectors_second, all_grads[3], clip_factor, RATE_VECTORS, 0.0
    )
    inner_next, inner_moment, inner_square = adam_update(
        expert_inner, inner_first, inner_second, all_grads[4], clip_factor, RATE_INNER, DECAY
    )
    hidden_next, hidden_moment, hidden_square = adam_update(
        hidden_bias, hidden_first, hidden_second, all_grads[5], clip_factor, RATE_HIDDEN, 0.0
    )
    outer_next, outer_moment, outer_square = adam_update(
        expert_outer, outer_first, outer_second, all_grads[6], clip_factor, RATE_OUTER, DECAY
    )
    return_next, return_moment, return_square = adam_update(
        return_bias, return_first, return_second, all_grads[7], clip_factor, RATE_RETURN, 0.0
    )
    return (
        block_output,
        input_grad,
        grad_norm,
        projection_next,
        projection_moment,
        projection_square,
        output_next,
        output_moment,
        output_square,
        router_next,
        router_moment,
        router_square,
        vectors_next,
        vectors_moment,
        vectors_square,
        inner_next,
        inner_moment,
        inner_square,
        hidden_next,
        hidden_moment,
        hidden_square,
        outer_next,
        outer_moment,
        outer_square,
        return_next,
        return_moment,
        return_square,
    )


MESH = pl.DeviceIdType.MESH
ANY = pl.BlockSpec(memory_space=pl.ANY)
VMEM = pl.BlockSpec(memory_space=pltpu.VMEM)


class Place:
    def __init__(self, dp, experts):
        self.dp, self.experts = dp, experts
        self.ys = 2
        self.zs = experts // 4
        self.a = lax.axis_index("dp")
        self.e = lax.axis_index("expert")
        self.core = lax.rem(self.e, 2)
        self.y = lax.rem(lax.div(self.e, 2), self.ys)
        self.z = lax.div(self.e, 2 * self.ys)

    def chip_of(self, core, dz, s2, s3):
        zz = lax.rem(self.z + dz, self.zs)
        if s2 == s3:
            fa = fy = s2
        elif s2:
            fa, fy = core, 1 - core
        else:
            fa, fy = 1 - core, core
        aa = lax.rem(self.a + fa, 2)
        yy = lax.rem(self.y + fy, 2)
        return aa, zz, yy

    def device(self, core, dz, s2, s3, own_core=None):
        aa, zz, yy = self.chip_of(core, dz, s2, s3)
        c = core if own_core is None else own_core
        return (aa, (zz * self.ys + yy) * 2 + c)

    def flat(self, dev):
        return dev[0] * self.experts + dev[1]

    def chip(self, core, dz, s2, s3):
        aa, zz, yy = self.chip_of(core, dz, s2, s3)
        return (aa * self.zs + zz) * self.ys + yy


def remote(src, dst, send, recv, dev):
    return pltpu.make_async_remote_copy(src_ref=src, dst_ref=dst, send_sem=send, recv_sem=recv, device_id=dev, device_id_type=MESH)


def greet(devices):
    barrier = pltpu.get_barrier_semaphore()
    for dev in devices:
        pl.semaphore_signal(barrier, inc=1, device_id=dev, device_id_type=MESH)
    pl.semaphore_wait(barrier, len(devices))


def split_index(k, zs):
    return k % zs, (k // zs) % 2, k // (2 * zs)


LANES = 128


def nn(left, right):
    return lax.dot_general(left, right, (((1,), (0,)), ((), ())), preferred_element_type=jnp.float32)


def nt(left, right):
    return lax.dot_general(left, right, (((1,), (1,)), ((), ())), preferred_element_type=jnp.float32)


def lane_ids(rows, start=0):
    return lax.broadcasted_iota(jnp.int32, (rows, LANES), 1) + start


def row_parts(count, size):
    return [pl.ds(i * size, size) for i in range(count // size)]


def norm_parts(values):
    center = values - jnp.mean(values, axis=-1, keepdims=True)
    inverse = lax.rsqrt(jnp.mean(center * center, axis=-1, keepdims=True) + NORM_EPS)
    return center * inverse, inverse


def vector_table(weights, width):
    return jnp.transpose(weights[:, 4 * width :].astype(jnp.float32))


def forward_kernel(
    dp,
    experts,
    capacity,
    chunk,
    tok_ref,
    cot_ref,
    choice_ref,
    rank_row,
    projection_ref,
    output_ref,
    router_ref,
    vectors_ref,
    rows_ref,
    dy_ref,
    aux_ref,
    probs_ref,
    qkv_any,
    ctx_any,
    mid_any,
    second_any,
    stat_any,
    weights_any,
    qkv_ref,
    ctx_ref,
    mid_ref,
    second_ref,
    stat_ref,
    weights,
    vec,
    normed,
    mine,
    theirs,
    tables,
    given,
    land_first,
    land,
    pre_send,
    pre_recv,
    line_send,
    line_recv,
    second_send,
    second_recv,
    third_send,
    third_recv,
    core_send,
    core_recv,
    store,
):
    low, full32 = jnp.bfloat16, jnp.float32
    patches, width = tok_ref.shape
    half = width // 2
    trio_width = 3 * LANES
    p = Place(dp, experts)
    c, zs = p.core, p.zs
    deep = projection_ref.shape[0]
    partner = (p.a, p.e + 1 - 2 * c)
    second, third = p.device(c, 0, 1, 0), p.device(c, 0, 0, 1)
    peers = [p.device(c, dz, 0, 0) for dz in range(1, zs)]
    narrow = jnp.concatenate(
        [router_ref[...], vectors_ref[...], jnp.zeros((LANES - experts - vectors_ref.shape[0], deep), full32)], axis=0
    )
    for h in range(2):
        mine[h, :, :LANES] = jnp.transpose(narrow) if h == 0 else jnp.zeros((deep, LANES), full32)
        for i in range(width // LANES // 2):
            for kind in range(3):
                at = kind * width + (2 * i + h) * LANES
                mine[h, :, LANES + i * trio_width + kind * LANES : LANES + i * trio_width + (kind + 1) * LANES] = (
                    projection_ref[:, at : at + LANES]
                )
        mine[h, :, LANES + 3 * half :] = output_ref[:, h * half : (h + 1) * half]
    greet(peers + [second, third, partner])
    before_all = remote(mine.at[1 - c], theirs, pre_send, pre_recv, partner)
    before_all.start()
    lanes = lane_ids(patches)
    named = jnp.concatenate([choice_ref[...], rank_row[...]], axis=0).astype(full32)
    named = jnp.transpose(jnp.concatenate([named, jnp.zeros((LANES - 3, patches), full32)], axis=0))
    first, other = named[:, 0:1].astype(jnp.int32), named[:, 1:2].astype(jnp.int32)
    is_first, is_other = lanes == first, lanes == other
    chunks = width // LANES // 2 + 1
    lands = [land_first] + [land.at[i] for i in range(chunks - 1)]
    my_line = p.a * p.ys + p.y
    second_line = jnp.where(c == 0, p.a * p.ys + 1 - p.y, (1 - p.a) * p.ys + p.y)
    third_lines = [
        jnp.where(c == 0, (1 - p.a) * p.ys + p.y, p.a * p.ys + 1 - p.y),
        (1 - p.a) * p.ys + 1 - p.y,
    ]

    def line_copy(i, dz):
        block = lands[i].at[c, my_line, p.z]
        return remote(block, block, line_send.at[i, dz], line_recv.at[i, dz], peers[dz - 1])

    def second_copy(i):
        block = lands[i].at[c, my_line]
        return remote(block, block, second_send.at[i], second_recv.at[i], second)

    def third_copy(i, which):
        block = lands[i].at[c, my_line if which == 0 else second_line]
        return remote(block, block, third_send.at[i, which], third_recv.at[i, which], third)

    def core_copy(i, which):
        block = lands[i].at[c, (my_line, second_line, *third_lines)[which]]
        return remote(block, block, core_send.at[i, which], core_recv.at[i, which], partner)

    def step0(i):
        for dz in range(1, zs):
            line_copy(i, dz).start()

    def step1(i):
        for dz in range(1, zs):
            block = lands[i].at[c, my_line, lax.rem(p.z + zs - dz, zs)]
            remote(block, block, line_send.at[i, dz], line_recv.at[i, dz], partner).wait_recv()
        third_copy(i, 0).start()
        second_copy(i).start()
        core_copy(i, 0).start()

    def step2(i):
        second_copy(i).wait_recv()
        third_copy(i, 1).start()
        core_copy(i, 1).start()

    def step3(i):
        for which in range(2):
            third_copy(i, which).wait_recv()
            core_copy(i, 2 + which).start()

    def unpack(i):
        for which in range(4):
            core_copy(i, which).wait_recv()
        for line in range(2 * p.ys):
            for z in range(zs):
                at = (line // p.ys * zs + z) * p.ys + line % p.ys
                rows = pl.ds(2 * deep * at, 2 * deep)
                for h in range(2):
                    if i == 0:
                        weights[rows, h * trio_width : (h + 1) * trio_width] = land_first[h, line, z, :, LANES:]
                    else:
                        columns = pl.ds((2 * i + h) * half, half)
                        weights[rows, columns] = land[i - 1, h, line, z]
                if i == 0:
                    weights[rows, 4 * width :] = land_first[0, line, z, :, :LANES]

    before_all.wait_recv()
    own, their = mine[c], theirs[...]
    top, bottom = jnp.where(c == 0, own, their), jnp.where(c == 0, their, own)
    block = jnp.concatenate([top, bottom], axis=0).astype(low)
    land_first[c, my_line, p.z] = block[:, : LANES + half]
    for i in range(1, chunks):
        land[i - 1, c, my_line, p.z] = block[:, LANES + i * half : LANES + (i + 1) * half]
    for i in range(chunks):
        step0(i)
    earlier = (rank_row[...].astype(full32) < named[:, 2:3]).astype(full32).astype(low)
    hot = (is_first | (lanes == other + experts)).astype(full32)
    counts = nn(earlier, hot.astype(low))
    totals = jnp.sum(hot, axis=0, keepdims=True)
    place_first = jnp.sum(jnp.where(is_first, counts, 0.0), axis=1, keepdims=True)
    place_other = jnp.sum(
        jnp.where(lanes == other + experts, counts, 0.0) + jnp.where(is_other, totals, 0.0), axis=1, keepdims=True
    )

    def slot_of(place, expert):
        place = place.astype(jnp.int32)
        kept = place < capacity
        slot = (place // 8) * LANES + expert * 8 + place % 8
        tail = kept & (place >= capacity - 4)
        return kept, jnp.where(kept, slot, -1), jnp.where(tail, slot + 4, -1)

    aux = jnp.zeros((patches, LANES), full32)
    for j, (place, expert) in enumerate(((place_first, first), (place_other, other))):
        kept, slot, twin = slot_of(place, expert)
        for lane, column in ((j, slot), (2 + j, twin), (4 + j, kept), (6 + j, expert)):
            aux = jnp.where(lanes == lane, column.astype(full32), aux)
    aux_ref[...] = aux
    turned = jnp.transpose(aux)
    slots = [turned[i : i + 1, :] for i in range(4)]
    full = capacity // 8
    for i in range(full + 1):
        ids = (lax.broadcasted_iota(jnp.int32, (LANES, patches), 0) + i * LANES).astype(full32)
        hit = (ids == slots[0]) | (ids == slots[1])
        if i == full:
            hit = hit | (ids == slots[2]) | (ids == slots[3])
        tables[i] = hit.astype(full32).astype(low)
        given[i] = nn(tables[i], cot_ref[...]).astype(low)

    def row(i):
        return vec[experts + i : experts + i + 1, :]

    def attend(pair):
        at = pair * LANES
        trio = pair * trio_width
        product = nn(normed[...], weights[:, trio : trio + trio_width])
        queries_all = (product[:, :LANES] + vec[experts + 2 : experts + 3, at : at + LANES]).astype(low)
        keys = product[:, LANES : 2 * LANES].astype(low)
        values = (product[:, 2 * LANES :] + vec[experts + 3 : experts + 4, at : at + LANES]).astype(low)
        qkv_ref[:, trio : trio + LANES] = queries_all
        qkv_ref[:, trio + LANES : trio + 2 * LANES] = keys
        qkv_ref[:, trio + 2 * LANES : trio + 3 * LANES] = values
        key_lanes = lane_ids(patches)
        values_two = [
            jnp.where(key_lanes < HEAD_DIM, values, (key_lanes == HEAD_DIM).astype(full32).astype(low)),
            jnp.where(key_lanes >= HEAD_DIM, values, (key_lanes == 0).astype(full32).astype(low)),
        ]
        for part in row_parts(patches, chunk):
            own_lanes = lane_ids(chunk)
            queries = qkv_ref[part, trio : trio + LANES] * jnp.asarray(HEAD_DIM**-0.5, low)
            outs = []
            stat = stat_ref[part, :]
            for head in range(2):
                side = (own_lanes < HEAD_DIM) if head == 0 else (own_lanes >= HEAD_DIM)
                scores = nt(jnp.where(side, queries, jnp.zeros_like(queries)), keys)
                peak = jnp.max(scores, axis=1, keepdims=True)
                raised = jnp.exp(scores - peak)
                mixed = nn(raised.astype(low), values_two[head])
                spare = HEAD_DIM if head == 0 else 0
                total = mixed[:, spare : spare + 1]
                outs.append(mixed / total)
                stat = jnp.where(own_lanes == 2 * pair + head, peak + jnp.log(total), stat)
            stat_ref[part, :] = stat
            ctx_ref[part, at : at + LANES] = jnp.where(own_lanes < HEAD_DIM, outs[0], outs[1]).astype(low)

    stat_ref[...] = jnp.zeros_like(stat_ref)
    step1(0)
    step1(1)
    step2(0)
    step1(2)
    step2(1)
    step3(0)
    step1(3)
    unpack(0)
    vec[...] = vector_table(weights, width)
    for part in row_parts(patches, chunk):
        unit, _ = norm_parts(tok_ref[part, :].astype(full32))
        normed[part, :] = (unit * row(0) + row(1)).astype(low)
    step2(2)
    step3(1)
    attend(0)
    step2(3)
    attend(1)
    step3(2)
    unpack(1)
    attend(2)
    step3(3)
    attend(3)
    unpack(2)
    attend(4)
    attend(5)
    unpack(3)
    kept = [(weights, weights_any), (qkv_ref, qkv_any), (ctx_ref, ctx_any), (stat_ref, stat_any)]
    kept += [(mid_ref, mid_any), (second_ref, second_any)]
    keep = [pltpu.make_async_copy(s, d, store.at[i]) for i, (s, d) in enumerate(kept)]
    for copy in keep[:4]:
        copy.start()
    third_columns = 256
    for j in range(width // third_columns):
        columns = pl.ds(j * third_columns, third_columns)
        product = nn(ctx_ref[...], weights[:, pl.ds(3 * width + j * third_columns, third_columns)])
        mid_ref[:, columns] = tok_ref[:, columns].astype(full32) + (product + vec[experts + 4 : experts + 5, columns])
    for part in row_parts(patches, chunk):
        unit, _ = norm_parts(mid_ref[part, :])
        second_ref[part, :] = (unit * row(5) + row(6)).astype(low)
    keep[4].start()
    keep[5].start()
    logits = jnp.where(lanes < experts, nn(second_ref[...], weights[:, 4 * width :]), -1e30)
    raised = jnp.exp(logits - jnp.max(logits, axis=1, keepdims=True))
    probs = raised / jnp.sum(raised, axis=1, keepdims=True)
    probs_ref[...] = probs
    for j, hit in enumerate((is_first, is_other)):
        gate = jnp.sum(jnp.where(hit, probs, 0.0), axis=1, keepdims=True)
        aux_ref[...] = jnp.where(lanes == 4 + j, aux_ref[...] * gate, aux_ref[...])
    parts = []
    rest = probs
    for _ in range(3):
        parts.append(rest.astype(low))
        rest = rest - parts[-1].astype(full32)
    slot_expert = lax.broadcasted_iota(jnp.int32, (LANES, LANES), 0) // 8
    for i in range(full + 1):
        chances = nn(tables[i], parts[0])
        chances = chances + nn(tables[i], parts[1])
        chances = chances + nn(tables[i], parts[2])
        gate = jnp.sum(jnp.where(lane_ids(LANES) == slot_expert, chances, 0.0), axis=1, keepdims=True)
        sent = nn(tables[i], second_ref[...])
        back = given[i].astype(full32) * gate
        columns = pl.ds(i * width, width)
        if i == full:
            columns = pl.ds(i * width, width // 2)
            left = lax.broadcasted_iota(jnp.int32, (LANES, width // 2), 0) % 8 < 4
            sent = jnp.where(left, sent[:, : width // 2], sent[:, width // 2 :])
            back = jnp.where(left, back[:, : width // 2], back[:, width // 2 :])
        rows_ref[:, columns] = sent.astype(low)
        dy_ref[:, columns] = back.astype(low)

    for copy in keep:
        copy.wait()
    before_all.wait_send()
    for i in range(chunks):
        for dz in range(1, zs):
            line_copy(i, dz).wait_send()
        second_copy(i).wait_send()
        for which in range(2):
            third_copy(i, which).wait_send()
        for which in range(4):
            core_copy(i, which).wait_send()


def forward(
    tokens,
    cotangent,
    choice,
    priority,
    projection,
    output_weight,
    router_weight,
    vectors,
    dp,
    experts,
    capacity,
    cid,
    chunk=576,
):
    patches, width = tokens.shape
    low, full = jnp.bfloat16, jnp.float32
    packed = (8 * experts, capacity * width // 8)
    shapes = [
        (packed, low),
        (packed, low),
        ((patches, LANES), full),
        ((patches, LANES), full),
        ((patches, 3 * width), low),
        ((patches, width), low),
        ((patches, width), full),
        ((patches, width), low),
        ((patches, LANES), full),
        ((width, 4 * width + LANES), low),
    ]
    deep, half = projection.shape[0], width // 2
    chunks = width // LANES // 2 + 1
    zs = experts // 4
    lines = dp * experts // 2 // zs
    dma = pltpu.SemaphoreType.DMA
    return pl.pallas_call(
        functools.partial(forward_kernel, dp, experts, capacity, chunk),
        out_shape=[jax.ShapeDtypeStruct(*s) for s in shapes],
        in_specs=[VMEM] * 8,
        out_specs=[VMEM] * 4 + [ANY] * 6,
        scratch_shapes=[
            *(pltpu.VMEM(*shape) for shape in shapes[4:]),
            pltpu.VMEM((LANES, width), full),
            pltpu.VMEM((patches, width), low),
            pltpu.VMEM((2, deep, LANES + 4 * half), full),
            pltpu.VMEM((deep, LANES + 4 * half), full),
            pltpu.VMEM((capacity // 8 + 1, LANES, patches), low),
            pltpu.VMEM((capacity // 8 + 1, LANES, width), low),
            pltpu.VMEM((2, lines, zs, 2 * deep, LANES + half), low),
            pltpu.VMEM((chunks - 1, 2, lines, zs, 2 * deep, half), low),
            dma,
            dma,
            dma((chunks, zs)),
            dma((chunks, zs)),
            dma((chunks,)),
            dma((chunks,)),
            dma((chunks, 2)),
            dma((chunks, 2)),
            dma((chunks, 4)),
            dma((chunks, 4)),
            dma((6,)),
        ],
        compiler_params=pltpu.CompilerParams(
            collective_id=cid, has_side_effects=True, vmem_limit_bytes=60 * 1024 * 1024
        ),
        cost_estimate=pl.CostEstimate(flops=6 * 10**9, bytes_accessed=20 * 10**6, transcendentals=4 * 10**6),
        name="attend_forward",
    )(
        tokens,
        cotangent,
        choice.T,
        priority.reshape(1, patches),
        projection,
        output_weight,
        router_weight.T,
        vectors,
    )


def gelu_both(z):
    root = 0.7978845608028654
    square = z * z
    slope = jnp.tanh(root * z * (1.0 + 0.044715 * square))
    half = 0.5 * (1.0 + slope)
    act = z * half
    grad = half + 0.5 * z * (1.0 - slope * slope) * (root * (1.0 + 3 * 0.044715 * square))
    return act, grad


def tail_picks(count, right):
    rows = lax.broadcasted_iota(jnp.int32, (count // 2, count), 0)
    ids = lax.broadcasted_iota(jnp.int32, (count // 2, count), 1)
    hit = ids == (rows // 4) * 8 + rows % 4 + (4 if right else 0)
    return hit.astype(jnp.float32).astype(jnp.bfloat16)


class Stages:
    def __init__(self, place, refs):
        (self.grads, self.other, self.give3, self.take3, self.give2, self.take2, self.givez, self.takez, self.total) = refs[:9]
        (self.cs, self.cr, self.s3, self.r3, self.s2, self.r2, self.sz, self.rz) = refs[9:]
        self.p, self.zs, self.core = place, place.zs, place.core
        self.partner = (place.a, place.e + 1 - 2 * place.core)

    def to_partner(self, c):
        return remote(
            self.grads.at[c, 1 - self.core], self.other.at[c], self.cs.at[c], self.cr.at[c], self.partner
        )

    def to_third(self, c):
        return remote(
            self.give3.at[c], self.take3.at[c], self.s3.at[c], self.r3.at[c], self.p.device(self.core, 0, 0, 1)
        )

    def to_second(self, c):
        return remote(
            self.give2.at[c], self.take2.at[c], self.s2.at[c], self.r2.at[c], self.p.device(self.core, 0, 1, 0)
        )

    def along(self, c, dz):
        return remote(
            self.givez.at[c, dz - 1],
            self.takez.at[c, dz - 1],
            self.sz.at[c, dz],
            self.rz.at[c, dz],
            self.p.device(self.core, dz, 0, 0),
        )

    def sum_of(self, c, k, *more):
        at = self.p.chip(self.core, *split_index(k, self.zs))
        total = self.grads[c, self.core, at].astype(jnp.float32) + self.other[c, at].astype(jnp.float32)
        for ref in more:
            total = total + ref[c, k].astype(jnp.float32)
        return total

    def step0(self, c):
        self.to_partner(c).start()

    def step1(self, c):
        self.to_partner(c).wait_recv()
        zs = self.zs
        for k in range(2 * zs, 4 * zs):
            self.give3[c, k - 2 * zs] = self.sum_of(c, k).astype(self.give3.dtype)
        self.to_third(c).start()

    def step2(self, c):
        self.to_third(c).wait_recv()
        zs = self.zs
        for k in range(zs, 2 * zs):
            self.give2[c, k - zs] = self.sum_of(c, k, self.take3).astype(self.give2.dtype)
        self.to_second(c).start()

    def step3(self, c):
        self.to_second(c).wait_recv()
        for dz in range(1, self.zs):
            self.givez[c, dz - 1] = self.sum_of(c, dz, self.take3, self.take2).astype(self.givez.dtype)
            self.along(c, dz).start()

    def step4(self, c):
        total = self.sum_of(c, 0, self.take3, self.take2)
        for dz in range(1, self.zs):
            self.along(c, dz).wait_recv()
            total = total + self.takez[c, dz - 1].astype(jnp.float32)
        self.total[c] = total

    def finish(self, count):
        for c in range(count):
            self.to_partner(c).wait_send()
            self.to_third(c).wait_send()
            self.to_second(c).wait_send()
            for dz in range(1, self.zs):
                self.along(c, dz).wait_send()


def stage_scratch(chunks, chips, rows, columns):
    low = jnp.bfloat16
    zs = chips // 4
    shapes = [
        (chunks, 2, chips, rows, columns),
        (chunks, chips, rows, columns),
        (chunks, 2 * zs, rows, columns),
        (chunks, 2 * zs, rows, columns),
        (chunks, zs, rows, columns),
        (chunks, zs, rows, columns),
        (chunks, zs - 1, rows, columns),
        (chunks, zs - 1, rows, columns),
    ]
    sems = [pltpu.SemaphoreType.DMA((chunks,)) for _ in range(6)]
    sems += [pltpu.SemaphoreType.DMA((chunks, zs)) for _ in range(2)]
    return [pltpu.VMEM(s, low) for s in shapes] + [pltpu.VMEM((chunks, rows, columns), jnp.float32)] + sems


STAGE_REFS = 17


def backward_kernel(
    dp,
    experts,
    capacity,
    chunk,
    tok_ref,
    cot_ref,
    ret_ref,
    aux_ref,
    probs_ref,
    mid_ref,
    part_ref,
    back_any,
    second_any,
    ctx_any,
    stat_any,
    qkv_any,
    weights_any,
    out_any,
    input_any,
    dense_ref,
    total_ref,
    out_ref,
    unit_ref,
    inverse_ref,
    logs_ref,
    back_ref,
    second_ref,
    ctx_ref,
    stat_ref,
    qkv_ref,
    weights,
    vec,
    stacked,
    normed_turned,
    branch,
    dctx,
    joined,
    turned_query,
    dmid,
    work,
    sums,
    load,
    row,
    row_fine,
    plane_tiles,
    line_tiles,
    row_send,
    row_recv,
    tile_send,
    tile_recv,
    store,
    *stage_refs,
):
    low, full32 = jnp.bfloat16, jnp.float32
    patches, width = tok_ref.shape
    trio_width = 3 * LANES
    p = Place(dp, experts)
    main, fine = Stages(p, stage_refs[:STAGE_REFS]), Stages(p, stage_refs[STAGE_REFS:])
    coarse, chips, shard2 = main.grads.shape[0], *main.grads.shape[2:4]
    thin = fine.grads.shape[4]
    pieces = [
        (back_any, back_ref),
        (weights_any, weights),
        (ctx_any, ctx_ref),
        (second_any, second_ref),
        (stat_any, stat_ref),
        (qkv_any, qkv_ref),
    ]
    fetch = [pltpu.make_async_copy(s, d, load.at[i]) for i, (s, d) in enumerate(pieces)]
    for copy in fetch:
        copy.start()
    barrier = pltpu.get_barrier_semaphore()

    def flip(value, bit):
        return value + bit - 2 * bit * value

    mates = []
    for f in range(1, 8):
        chip_y = p.z * p.ys + flip(p.y, (f // 2) % 2)
        mates.append((flip(p.a, f // 4), chip_y * 2 + flip(p.core, f % 2)))
    peers = [p.device(p.core, dz, 0, 0) for dz in range(1, p.zs)]
    for device in mates + peers:
        pl.semaphore_signal(barrier, inc=1, device_id=device, device_id_type=MESH)

    full = capacity // 8
    half = width // 2
    lanes = lane_ids(patches)
    aux = aux_ref[...]
    slots = [aux[:, i : i + 1] for i in range(4)]
    gates = [aux[:, 4 + i : 5 + i] for i in range(2)]
    ids = lax.broadcasted_iota(jnp.int32, (patches, full * LANES), 1).astype(full32)
    tail_ids = lane_ids(patches, full * LANES).astype(full32)
    hits = [ids == slots[0], ids == slots[1]]
    lefts = [tail_ids == slots[0], tail_ids == slots[1]]
    rights = [tail_ids == slots[2], tail_ids == slots[3]]

    def mix(marks):
        return (jnp.where(marks[0], gates[0], 0.0) + jnp.where(marks[1], gates[1], 0.0)).astype(low)

    def pick(marks):
        return (marks[0] | marks[1]).astype(full32).astype(low)

    for i in range(full):
        stacked[pl.ds(i * LANES, LANES), :] = ret_ref[:, pl.ds(i * width, width)]
    tail = ret_ref[:, pl.ds(full * width, half)]
    along = nt(cot_ref[...], stacked[...])
    along_left, along_right = nt(cot_ref[:, :half], tail), nt(cot_ref[:, half:], tail)
    dprobs = jnp.zeros((patches, LANES), full32)
    for j in range(2):
        dgate = jnp.sum(jnp.where(hits[j], along, 0.0), axis=1, keepdims=True) + jnp.sum(
            jnp.where(lefts[j], along_left, 0.0) + jnp.where(rights[j], along_right, 0.0), axis=1, keepdims=True
        )
        dprobs = dprobs + jnp.where(lanes == aux[:, 6 + j : 7 + j].astype(jnp.int32), dgate, 0.0)
    probs = probs_ref[...]
    dlogits = (probs * (dprobs - jnp.sum(probs * dprobs, axis=1, keepdims=True))).astype(low)
    fetch[0].wait()
    for i in range(full):
        stacked[pl.ds(i * LANES, LANES), :] = back_ref[:, pl.ds(i * width, width)]
    tail = back_ref[:, pl.ds(full * width, half)]
    fetch[1].wait()
    vec[...] = vector_table(weights, width)

    def vector(i):
        return vec[experts + i : experts + i + 1, :]

    routed = weights[:, 4 * width :]
    work[...] = nn(pick(hits), stacked[...]) + nt(dlogits, routed)
    work[:, :half] = work[:, :half] + nn(pick(lefts), tail)
    work[:, half:] = work[:, half:] + nn(pick(rights), tail)
    sums[...] = jnp.zeros_like(sums)

    def column_sum(slot, values):
        sums[pl.ds(8 * slot, 8), :] = sums[pl.ds(8 * slot, 8), :] + jnp.sum(
            values.reshape(-1, 8, values.shape[-1]), axis=0
        )

    def norm_back(grad, unit, inverse, gain):
        weighted = grad * gain
        return inverse * (
            weighted
            - jnp.mean(weighted, axis=-1, keepdims=True)
            - unit * jnp.mean(weighted * unit, axis=-1, keepdims=True)
        )

    for part in row_parts(patches, chunk):
        unit, inverse = norm_parts(mid_ref[part, :])
        grad = work[part, :]
        column_sum(5, grad * unit)
        column_sum(6, grad)
        total = cot_ref[part, :].astype(full32) + norm_back(grad, unit, inverse, vector(5))
        dmid[part, :] = total
        rounded = total.astype(low)
        branch[part, :] = rounded
        column_sum(4, rounded.astype(full32))
    fetch[2].wait()
    ctx_turned = jnp.transpose(ctx_ref[...])
    for core in range(2):
        columns = pl.ds(core * half, half)
        product = nn(ctx_turned, branch[:, columns])
        main.grads[0, core] = product.reshape(chips, shard2, half).astype(low)
    pl.semaphore_wait(barrier, len(mates) + len(peers))
    main.step0(0)
    third = 256
    for j in range(width // third):
        rows = pl.ds(j * third, third)
        dctx[:, rows] = nt(branch[...], weights[rows, pl.ds(3 * width, width)]).astype(low)
    fetch[3].wait()
    router_rows = nn(jnp.transpose(dlogits.astype(full32)).astype(low), second_ref[...])
    for part in row_parts(patches, chunk):
        unit, inverse = norm_parts(tok_ref[part, :].astype(full32))
        second_ref[part, :] = (unit * vector(0) + vector(1)).astype(low)
        unit_ref[part, :] = unit
        inverse_ref[part, :] = jnp.broadcast_to(inverse, (chunk, LANES))
    normed_turned[...] = jnp.transpose(second_ref[...])
    heads = (
        lax.broadcasted_iota(jnp.int32, (16, width), 1) // HEAD_DIM == lax.broadcasted_iota(jnp.int32, (16, width), 0)
    ).astype(full32).astype(low)
    product = dctx[...].astype(full32) * ctx_ref[...].astype(full32)
    upper = product.astype(low)
    center = nt(heads, upper) + nt(heads, (product - upper.astype(full32)).astype(low))
    fetch[4].wait()
    logs = jnp.transpose(stat_ref[...])
    logs_ref[...] = jnp.concatenate([logs[:16], center], axis=0)
    fetch[5].wait()

    ones = jnp.ones((8, patches), low)
    scale = jnp.asarray(HEAD_DIM**-0.5, low)

    def attend(pair):
        at, trio = pair * LANES, pair * trio_width
        key_at, value_at = pl.ds(trio + LANES, LANES), pl.ds(trio + 2 * LANES, LANES)
        queries = qkv_ref[:, pl.ds(trio, LANES)] * scale
        given = dctx[:, pl.ds(at, LANES)]
        own = lane_ids(patches)
        zero = jnp.zeros_like(queries)
        marks = [own < HEAD_DIM, own >= HEAD_DIM]
        head_queries = [jnp.where(m, queries, zero) for m in marks]
        head_given = [jnp.where(m, given, zero) for m in marks]
        turned_keys = jnp.transpose(qkv_ref[:, key_at] * scale)
        query_parts = [None, None]
        for part in row_parts(patches, chunk):
            keys = qkv_ref[part, key_at]
            values = qkv_ref[part, value_at]
            value_out, key_out = [], []
            for head in range(2):
                log_row = logs_ref[2 * pair + head : 2 * pair + head + 1, :]
                center_row = logs_ref[16 + 2 * pair + head : 17 + 2 * pair + head, :]
                prob = jnp.exp(nt(keys, head_queries[head]) - log_row)
                value_out.append(nn(prob.astype(low), given))
                dscore = (prob * (nt(values, head_given[head]) - center_row)).astype(low)
                key_out.append(nn(dscore, queries))
                head_keys = turned_keys[HEAD_DIM * head : HEAD_DIM * (head + 1), part.start : part.start + part.size]
                piece = nn(head_keys, dscore)
                query_parts[head] = piece if query_parts[head] is None else query_parts[head] + piece
            side = lane_ids(chunk) < HEAD_DIM
            joined[part, LANES : 2 * LANES] = jnp.where(side, key_out[0], key_out[1]).astype(low)
            joined[part, 2 * LANES :] = jnp.where(side, value_out[0], value_out[1]).astype(low)
        turned_query[...] = jnp.concatenate(query_parts, axis=0)
        joined[:, :LANES] = jnp.transpose(turned_query[...]).astype(low)
        product = nn(normed_turned[...], joined[...]).reshape(chips, shard2, trio_width).astype(low)
        if pair < 2 * (coarse - 1):
            main.grads[pair // 2 + 1, pair % 2] = product
        else:
            chunk_of = pair - 2 * (coarse - 1)
            fine.grads[chunk_of, 0] = product[:, :, :thin]
            fine.grads[chunk_of, 1, :, :, :LANES] = product[:, :, thin:]

    def spread(pair):
        trio = pair * trio_width
        part = nt(joined[...], weights[:, pl.ds(trio, trio_width)])
        work[...] = part if pair == 0 else work[...] + part
        column_parts = nn(ones, joined[...])
        sums[16:17, pl.ds(pair * LANES, LANES)] = column_parts[0:1, :LANES]
        sums[24:25, pl.ds(pair * LANES, LANES)] = column_parts[0:1, 2 * LANES :]

    fine.grads[0, 1, :, :, LANES:] = jnp.zeros((chips, shard2, thin - LANES), low)
    main.step1(0)
    attend(0)
    spread(0)
    main.step2(0)
    attend(1)
    main.step0(1)
    spread(1)
    attend(2)
    main.step1(1)
    main.step3(0)
    spread(2)
    attend(3)
    main.step0(2)
    main.step2(1)
    spread(3)
    main.step1(2)
    attend(4)
    fine.step0(0)
    spread(4)
    fine.step1(0)
    main.step3(1)
    main.step2(2)
    attend(5)
    fine.step2(0)
    spread(5)
    for part in row_parts(patches, chunk):
        unit = unit_ref[part, :]
        grad = work[part, :]
        column_sum(0, grad * unit)
        column_sum(1, grad)
    gain = vector(0)
    vec[...] = router_rows
    for i in range(7):
        vec[experts + i : experts + i + 1, :] = jnp.sum(sums[pl.ds(8 * i, 8), :], axis=0, keepdims=True)
    fine.grads[1, 1, :, :, LANES:] = jnp.transpose(vec[...]).reshape(chips, shard2, LANES).astype(low)
    def combine():
        for i in range(full):
            stacked[pl.ds(i * LANES, LANES), :] = ret_ref[:, pl.ds(i * width, width)]
        pieces_of = ret_ref[:, pl.ds(full * width, half)]
        final = nn(mix(hits), stacked[...])
        out_ref[:, :half] = (mid_ref[:, :half] + (final[:, :half] + nn(mix(lefts), pieces_of))).astype(low)
        out_ref[:, half:] = (mid_ref[:, half:] + (final[:, half:] + nn(mix(rights), pieces_of))).astype(low)

    keep_out = pltpu.make_async_copy(out_ref, out_any, store.at[0])
    fine.step0(1)
    main.step3(2)
    fine.step1(1)
    fine.step3(0)
    for part in row_parts(patches, chunk):
        part_grad = norm_back(work[part, :], unit_ref[part, :], inverse_ref[part, 0:1], gain)
        dmid[part, :] = dmid[part, :] + part_grad
    keep_input = pltpu.make_async_copy(dmid, input_any, store.at[1])
    keep_input.start()
    main.step4(0)
    main.step4(1)
    fine.step2(1)
    main.step4(2)
    fine.step4(0)
    combine()
    keep_out.start()
    deep = shard2 // 2
    his = pl.ds(pl.multiple_of((1 - p.core) * deep, 8), deep)
    mine = pl.ds(pl.multiple_of(p.core * deep, 8), deep)
    rows_copy = [
        remote(main.total.at[:, his], row, row_send.at[0], row_recv.at[0], main.partner),
        remote(fine.total.at[0, his], row_fine.at[0], row_send.at[1], row_recv.at[1], main.partner),
        remote(fine.total.at[1, his], row_fine.at[1], row_send.at[2], row_recv.at[2], main.partner),
    ]
    rows_copy[0].start()
    rows_copy[1].start()
    fine.step3(1)

    def squares_of(values):
        folded = jnp.sum((values * values).reshape(-1, 8, values.shape[1]), axis=0)
        out = folded[:, :LANES]
        for j in range(1, values.shape[1] // LANES):
            out = out + folded[:, j * LANES : (j + 1) * LANES]
        return out

    square = part_ref[...]
    for c in range(coarse):
        square = square + squares_of(main.total[c])
    square = square + squares_of(fine.total[0])
    fine.step4(1)
    rows_copy[2].start()
    plane = (p.a * p.ys + p.y) * 2 + p.core
    plane_tiles[plane] = square + squares_of(fine.total[1])

    def mate_copy(f):
        block = plane_tiles.at[plane]
        return remote(block, block, tile_send.at[f], tile_recv.at[f], mates[f - 1])

    def peer_copy(dz):
        block = line_tiles.at[p.z]
        return remote(block, block, tile_send.at[7 + dz], tile_recv.at[7 + dz], peers[dz - 1])

    for f in range(1, 8):
        mate_copy(f).start()

    def put(core, values, fine_values):
        for c in range(coarse):
            dense_ref[:, pl.ds(pl.multiple_of(c * width + core * half, LANES), half)] = values(c)
        for c in range(2):
            at = coarse * width + 2 * c * thin + core * thin
            dense_ref[:, pl.ds(pl.multiple_of(at, LANES), thin)] = fine_values(c)

    put(p.core, lambda c: main.total[c, mine, :], lambda c: fine.total[c, mine, :])
    for f in range(1, 8):
        from_plane = (flip(p.a, f // 4) * p.ys + flip(p.y, (f // 2) % 2)) * 2 + flip(p.core, f % 2)
        block = plane_tiles.at[from_plane]
        remote(block, block, tile_send.at[f], tile_recv.at[f], main.partner).wait_recv()
    total = plane_tiles[0]
    for j in range(1, 8):
        total = total + plane_tiles[j]
    line_tiles[p.z] = total
    for dz in range(1, p.zs):
        peer_copy(dz).start()
    for copy in rows_copy:
        copy.wait_recv()
    put(1 - p.core, lambda c: row[c], lambda c: row_fine[c])
    for dz in range(1, p.zs):
        block = line_tiles.at[lax.rem(p.z + p.zs - dz, p.zs)]
        remote(block, block, tile_send.at[7 + dz], tile_recv.at[7 + dz], main.partner).wait_recv()
    total = line_tiles[0]
    for j in range(1, p.zs):
        total = total + line_tiles[j]
    total_ref[...] = total
    main.finish(coarse)
    fine.finish(2)
    for copy in rows_copy:
        copy.wait_send()
    for f in range(1, 8):
        mate_copy(f).wait_send()
    for dz in range(1, p.zs):
        peer_copy(dz).wait_send()
    keep_out.wait()
    keep_input.wait()


def backward(
    tokens,
    cotangent,
    ret,
    back,
    aux,
    probs,
    mid,
    second,
    ctx,
    stat,
    qkv,
    weights,
    part,
    dp,
    experts,
    capacity,
    cid,
    chunk=576,
):
    patches, width = tokens.shape
    low, full = jnp.bfloat16, jnp.float32
    world = dp * experts
    chips, rows = world // 2, 2 * width // world
    thin = 2 * LANES
    chunks = width // LANES // 2
    columns = 4 * width + 2 * LANES
    return pl.pallas_call(
        functools.partial(backward_kernel, dp, experts, capacity, chunk),
        out_shape=[
            jax.ShapeDtypeStruct((patches, width), low),
            jax.ShapeDtypeStruct((patches, width), full),
            jax.ShapeDtypeStruct((rows // 2, columns), full),
            jax.ShapeDtypeStruct((8, LANES), full),
        ],
        in_specs=[VMEM] * 7 + [ANY] * 6,
        out_specs=[ANY, ANY, VMEM, VMEM],
        scratch_shapes=[
            pltpu.VMEM((patches, width), low),
            pltpu.VMEM((patches, width), full),
            pltpu.VMEM((patches, LANES), full),
            pltpu.VMEM((32, patches), full),
            pltpu.VMEM(back.shape, low),
            pltpu.VMEM((patches, width), low),
            pltpu.VMEM((patches, width), low),
            pltpu.VMEM(stat.shape, full),
            pltpu.VMEM(qkv.shape, low),
            pltpu.VMEM(weights.shape, low),
            pltpu.VMEM((LANES, width), full),
            pltpu.VMEM((capacity // 8 * LANES, width), low),
            pltpu.VMEM((width, patches), low),
            pltpu.VMEM((patches, width), low),
            pltpu.VMEM((patches, width), low),
            pltpu.VMEM((patches, 3 * LANES), low),
            pltpu.VMEM((LANES, patches), full),
            pltpu.VMEM((patches, width), full),
            pltpu.VMEM((patches, width), full),
            pltpu.VMEM((56, width), full),
            pltpu.SemaphoreType.DMA((6,)),
            pltpu.VMEM((chunks, rows // 2, width // 2), full),
            pltpu.VMEM((2, rows // 2, thin), full),
            pltpu.VMEM((8, 8, LANES), full),
            pltpu.VMEM((experts // 4, 8, LANES), full),
            pltpu.SemaphoreType.DMA((3,)),
            pltpu.SemaphoreType.DMA((3,)),
            pltpu.SemaphoreType.DMA((7 + experts // 4,)),
            pltpu.SemaphoreType.DMA((7 + experts // 4,)),
            pltpu.SemaphoreType.DMA((2,)),
            *stage_scratch(chunks, chips, rows, width // 2),
            *stage_scratch(2, chips, rows, thin),
        ],
        compiler_params=pltpu.CompilerParams(
            collective_id=cid, has_side_effects=True, vmem_limit_bytes=60 * 1024 * 1024
        ),
        cost_estimate=pl.CostEstimate(flops=15 * 10**9, bytes_accessed=30 * 10**6, transcendentals=4 * 10**6),
        name="attend_backward",
    )(tokens, cotangent, ret, aux, probs, mid, part, back, second, ctx, stat, qkv, weights)


ORDER = 7
WINDOW = 5
PARTS = 15


def moe_kernel(
    dp,
    experts,
    chunk,
    rows_any,
    dy_any,
    inner_any,
    hidden_ref,
    outer_any,
    return_ref,
    y_any,
    drows_any,
    dinner_any,
    dhidden_ref,
    douter_any,
    dreturn_ref,
    square_ref,
    rows_all,
    dy_all,
    y_pack,
    drows_pack,
    y_theirs,
    drows_theirs,
    rows,
    turned,
    dy,
    inner,
    outer,
    act,
    grad,
    dz,
    acc,
    inner_stage,
    outer_stage,
    dinner_stage,
    douter_stage,
    square,
    own_sem,
    in_send,
    in_recv,
    over_send,
    over_recv,
    part_send,
    part_recv,
    out_send,
    out_recv,
    stage_sem,
    store_sem,
):
    low, full32 = jnp.bfloat16, jnp.float32
    width = rows.shape[1]
    half = width // 2
    full = rows_all.shape[3] // width
    steps = inner.shape[1] // chunk
    groups = 2
    group = experts // groups
    block_rows = dp * group * 8
    deep = rows.shape[0] // groups
    a = lax.axis_index("dp")
    e = lax.axis_index("expert")
    across = (1 - a, e)
    ins, alls = (rows_any, dy_any), (rows_all, dy_all)
    packs, theirs, outs = (y_pack, drows_pack), (y_theirs, drows_theirs), (y_any, drows_any)

    def to(turn):
        return lax.rem(e + lax.rem(ORDER * turn, experts), experts)

    def source(turn):
        return lax.rem(e + experts - lax.rem(ORDER * turn, experts), experts)

    def columns_of(k):
        return pl.ds(pl.multiple_of(k * chunk, chunk), chunk)

    def stage(k, slot):
        return (
            pltpu.make_async_copy(inner_any.at[0, :, columns_of(k)], inner_stage.at[slot], stage_sem.at[0, slot]),
            pltpu.make_async_copy(outer_any.at[0, columns_of(k), :], outer_stage.at[slot], stage_sem.at[1, slot]),
        )

    def own_block(i):
        return pltpu.make_async_copy(ins[i].at[e], alls[i].at[a, 0], own_sem.at[i])

    for slot in range(2):
        for copy in stage(slot, slot):
            copy.start()
    for i in range(2):
        own_block(i).start()
    greet([(a, to(j)) for j in range(1, experts)] + [across])

    def first_send(i, turn):
        return remote(
            ins[i].at[to(turn)], alls[i].at[a, turn], in_send.at[i, turn], in_recv.at[i, turn], (a, to(turn))
        )

    def forward_own(i):
        return remote(ins[i].at[e], alls[i].at[a, 0], over_send.at[i, 0], over_recv.at[i, 0], across)

    def pass_on(i, turn):
        block = alls[i].at[a, turn]
        return remote(block, block, over_send.at[i, turn], over_recv.at[i, turn], across)

    def received(i, turn):
        block = alls[i].at[a, turn]
        return remote(block, block, in_send.at[i, turn], in_recv.at[i, turn], across)

    def from_across(i, turn):
        block = alls[i].at[1 - a, turn]
        return remote(block, block, over_send.at[i, turn], over_recv.at[i, turn], across)

    def part_copy(i, turn):
        return remote(
            packs[i].at[1 - a, turn], theirs[i].at[turn], part_send.at[i, turn], part_recv.at[i, turn], across
        )

    def result_copy(i, turn):
        return remote(
            packs[i].at[a, turn], outs[i].at[e], out_send.at[i, turn], out_recv.at[i, turn], (a, source(turn))
        )

    forward_own(0).start()

    @pl.loop(1, 1 + WINDOW)
    def _(turn):
        first_send(0, turn).start()

    def take_in(i, begin, number):
        @pl.loop(0, number)
        def _(d):
            turn = begin + d

            @pl.when(turn < experts)
            def _():
                received(i, turn).wait_recv()
                pass_on(i, turn).start()

                @pl.when(turn + WINDOW < experts)
                def _():
                    first_send(i, turn + WINDOW).start()

                if i == 0:

                    @pl.when(turn + WINDOW >= experts)
                    def _():
                        first_send(1, turn + WINDOW - experts + 1).start()

    def hand_out(i, begin, number):
        @pl.loop(0, number)
        def _(d):
            turn = begin + d

            @pl.when(turn < experts)
            def _():
                part_copy(i, turn).wait_recv()

                @pl.when(turn + PARTS <= experts)
                def _():
                    part_copy(i, lax.rem(turn + PARTS, experts)).start()

                packs[i][a, turn] = (packs[i][a, turn].astype(full32) + theirs[i][turn].astype(full32)).astype(low)
                result_copy(i, turn).start()

    def finish(i):
        part_copy(i, 0).wait_recv()
        packs[i][a, 0] = (packs[i][a, 0].astype(full32) + theirs[i][0].astype(full32)).astype(low)
        pltpu.make_async_copy(packs[i].at[a, 0], outs[i].at[e], own_sem.at[i]).start()

    def unpack(i, g, place):
        if g == 0:
            own_block(i).wait()

        @pl.loop(g * group, (g + 1) * group)
        def _(turn):
            from_across(i, turn).wait_recv()

        tails = []
        for plane in range(dp):
            for b in range(full):
                piece = alls[i][plane, g * group : (g + 1) * group, :, b * width : (b + 1) * width].astype(full32)
                at = g * deep + b * block_rows + plane * group * 8
                place[pl.ds(at, group * 8), :] = piece.reshape(group * 8, width).astype(low)
            piece = alls[i][plane, g * group : (g + 1) * group, :, full * width :].astype(full32)
            tails.append(piece.reshape(group * 8, half))
        tail = jnp.concatenate(tails, axis=0).astype(low)
        for right in range(2):
            place[pl.ds(g * deep + full * block_rows, block_rows // 2), pl.ds(right * half, half)] = nn(
                tail_picks(block_rows, right), tail
            ).astype(low)

    def pack(i, g):
        tail = acc[pl.ds(g * deep + full * block_rows, block_rows // 2), :].astype(low)
        spread = None
        for right in range(2):
            piece = lax.dot_general(
                tail_picks(block_rows, right),
                tail[:, right * half : (right + 1) * half],
                (((0,), (0,)), ((), ())),
                preferred_element_type=full32,
            )
            spread = piece if spread is None else spread + piece
        for plane in range(dp):
            turns = slice(g * group, (g + 1) * group)
            for b in range(full):
                at = g * deep + b * block_rows + plane * group * 8
                piece = acc[pl.ds(at, group * 8), :].reshape(group, 8, width)
                packs[i][plane, turns, :, b * width : (b + 1) * width] = piece.astype(low)
            piece = spread[plane * group * 8 : (plane + 1) * group * 8].reshape(group, 8, half)
            packs[i][plane, turns, :, full * width :] = piece.astype(low)

    def send_parts(i):
        @pl.loop(1, 1 + PARTS)
        def _(turn):
            part_copy(i, turn).start()

    @pl.loop(0, steps)
    def _(k):
        slot = lax.rem(k, 2)
        for copy in stage(k, slot):
            copy.wait()
        inner[:, columns_of(k)] = inner_stage[slot].astype(low)
        outer[columns_of(k), :] = outer_stage[slot].astype(low)

        @pl.when(k + 2 < steps)
        def _():
            for copy in stage(k + 2, slot):
                copy.start()

        take_in(0, 1 + k, 1)

    part = return_ref.shape[1]
    bias = return_ref[...].astype(low).astype(full32)
    for i in range(dp):
        acc[:, pl.ds(i * part, part)] = jnp.broadcast_to(jnp.where(a == i, bias, 0.0), (rows.shape[0], part))

    def onward(g):
        mine = pl.ds(g * deep, deep)

        def run(k):
            columns = columns_of(k)
            z = nn(rows[mine, :], inner[:, columns]) + hidden_ref[:, columns].astype(low).astype(full32)
            value, slope = gelu_both(z)
            act[mine, columns] = value.astype(low)
            grad[mine, columns] = slope
            acc[mine, :] += nn(act[mine, columns], outer[columns, :])

        return run

    def backward_of(g):
        mine = pl.ds(g * deep, deep)

        def run(k):
            columns = columns_of(k)
            dz[mine, columns] = (nt(dy[mine, :], outer[columns, :]) * grad[mine, columns]).astype(low)
            acc[mine, :] += nt(dz[mine, columns], inner[:, columns])

        return run

    forward_own(1).start()
    early = 1 + steps
    take_in(0, early, 4)
    early += 4
    unpack(0, 0, rows)
    forward_of = onward(0)
    left = experts - early

    @pl.loop(0, steps)
    def _(k):
        forward_of(k)
        take_in(0, early + k, 1)

        @pl.when(k >= left)
        def _():
            take_in(1, 1 + k - left, 1)

    taken = 1 + max(steps - left, 0)
    unpack(0, 1, rows)
    forward_late = onward(1)

    @pl.loop(0, steps)
    def _(k):
        forward_late(k)
        take_in(1, taken + k, 1)

    taken += steps
    for g in range(groups):
        pack(0, g)
    turned[...] = jnp.transpose(rows[...])
    take_in(1, taken, 2)
    taken += 2
    acc[...] = jnp.zeros_like(acc)
    unpack(1, 0, dy)
    back_first = backward_of(0)

    @pl.loop(0, steps)
    def _(k):
        back_first(k)
        take_in(1, taken + k, 1)

    taken += steps
    take_in(1, taken, max(experts - taken, 0))
    send_parts(0)
    pack(1, 0)
    unpack(1, 1, dy)
    back_last = backward_of(1)

    @pl.loop(0, steps)
    def _(k):
        back_last(k)
        hand_out(0, 1 + k, 1)

    pack(1, 1)
    send_parts(1)
    total = jnp.zeros((1, width), full32)
    for i in range(rows.shape[0] // LANES):
        total = total + jnp.sum(dy[pl.ds(i * LANES, LANES), :].astype(full32), axis=0, keepdims=True)
    picked = total[:, :part]
    for i in range(1, dp):
        picked = jnp.where(a == i, total[:, i * part : (i + 1) * part], picked)
    dreturn_ref[...] = picked
    square[...] = jnp.zeros_like(square)
    flat = picked * picked
    for i in range(part // LANES):
        square[0:1, :] = square[0:1, :] + flat[:, i * LANES : (i + 1) * LANES]

    def store(k, slot):
        return (
            pltpu.make_async_copy(dinner_stage.at[slot], dinner_any.at[0, :, columns_of(k)], store_sem.at[0, slot]),
            pltpu.make_async_copy(douter_stage.at[slot], douter_any.at[0, columns_of(k), :], store_sem.at[1, slot]),
        )

    later = -(-(experts - 1 - steps) // (steps - 1))

    @pl.loop(0, steps)
    def _(k):
        slot = lax.rem(k, 2)
        columns = columns_of(k)
        douter = nn(jnp.transpose(act[:, columns]), dy[...])
        dinner = nn(turned[...], dz[:, columns])
        dhidden = jnp.sum(dz[:, columns].astype(full32), axis=0, keepdims=True)

        @pl.when(k >= 2)
        def _():
            for copy in store(k - 2, slot):
                copy.wait()

        douter_stage[slot] = douter.astype(low)
        dinner_stage[slot] = dinner.astype(low)
        for copy in store(k, slot):
            copy.start()
        dhidden_ref[:, columns] = dhidden
        parts = jnp.zeros((8, LANES), full32)
        folded = jnp.sum((douter * douter).reshape(-1, 8, width), axis=0)
        for i in range(width // LANES):
            parts = parts + folded[:, i * LANES : (i + 1) * LANES]
        folded = jnp.sum((dinner * dinner).reshape(-1, 8, chunk), axis=0)
        hidden_square = dhidden * dhidden
        for i in range(chunk // LANES):
            parts = parts + folded[:, i * LANES : (i + 1) * LANES]
            square[0:1, :] = square[0:1, :] + hidden_square[:, i * LANES : (i + 1) * LANES]
        square[...] += parts
        hand_out(0, 1 + steps + k * later, later)

    finish(0)
    hand_out(1, 1, experts - 1)
    finish(1)
    square_ref[...] = square[...]
    for k in range(steps - 2, steps):
        for copy in store(k, k % 2):
            copy.wait()
    for i in range(2):

        @pl.loop(1, experts)
        def _(turn):
            block = outs[i].at[to(turn)]
            remote(block, block, out_send.at[i, turn], out_recv.at[i, turn], across).wait_recv()

    for i in range(2):
        pltpu.make_async_copy(packs[i].at[a, 0], outs[i].at[e], own_sem.at[i]).wait()
        forward_own(i).wait_send()
        part_copy(i, 0).wait_send()

        @pl.loop(1, experts)
        def _(turn):
            first_send(i, turn).wait_send()
            pass_on(i, turn).wait_send()
            part_copy(i, turn).wait_send()
            result_copy(i, turn).wait_send()


def mixture(rows, dy, inner, hidden, outer, back, dp, cid, chunk=256):
    experts, _, packed = rows.shape
    width, units = inner.shape[1:]
    count = dp * experts * 8
    total = count * packed // width
    low, full = jnp.bfloat16, jnp.float32
    both = (dp, experts, 8, packed)
    sems = [pltpu.SemaphoreType.DMA((2, experts)) for _ in range(8)]
    return pl.pallas_call(
        functools.partial(moe_kernel, dp, experts, chunk),
        out_shape=[
            jax.ShapeDtypeStruct(rows.shape, low),
            jax.ShapeDtypeStruct(rows.shape, low),
            jax.ShapeDtypeStruct(inner.shape, low),
            jax.ShapeDtypeStruct(hidden.shape, full),
            jax.ShapeDtypeStruct(outer.shape, low),
            jax.ShapeDtypeStruct(back.shape, full),
            jax.ShapeDtypeStruct((8, LANES), full),
        ],
        in_specs=[ANY, ANY, ANY, VMEM, ANY, VMEM],
        out_specs=[ANY, ANY, ANY, VMEM, ANY, VMEM, VMEM],
        scratch_shapes=[
            pltpu.VMEM(both, low),
            pltpu.VMEM(both, low),
            pltpu.VMEM(both, low),
            pltpu.VMEM(both, low),
            pltpu.VMEM(both[1:], low),
            pltpu.VMEM(both[1:], low),
            pltpu.VMEM((total, width), low),
            pltpu.VMEM((width, total), low),
            pltpu.VMEM((total, width), low),
            pltpu.VMEM((width, units), low),
            pltpu.VMEM((units, width), low),
            pltpu.VMEM((total, units), low),
            pltpu.VMEM((total, units), full),
            pltpu.VMEM((total, units), low),
            pltpu.VMEM((total, width), full),
            pltpu.VMEM((2, width, chunk), full),
            pltpu.VMEM((2, chunk, width), full),
            pltpu.VMEM((2, width, chunk), low),
            pltpu.VMEM((2, chunk, width), low),
            pltpu.VMEM((8, LANES), full),
            pltpu.SemaphoreType.DMA((2,)),
            *sems,
            pltpu.SemaphoreType.DMA((2, 2)),
            pltpu.SemaphoreType.DMA((2, 2)),
        ],
        compiler_params=pltpu.CompilerParams(
            collective_id=cid, has_side_effects=True, vmem_limit_bytes=60 * 1024 * 1024
        ),
        cost_estimate=pl.CostEstimate(flops=17 * 10**9, bytes_accessed=25 * 10**6, transcendentals=2 * 10**6),
        name="mixture",
    )(rows, dy, inner, hidden, outer, back)


def adam_values(weight, first, second, gradient, clip, rate, decay):
    scaled = gradient * clip
    first_new = BETA_ONE * first + (1.0 - BETA_ONE) * scaled
    second_new = BETA_TWO * second + (1.0 - BETA_TWO) * scaled * scaled
    first_hat = first_new * (1.0 / (1.0 - BETA_ONE**STEP))
    second_hat = second_new * (1.0 / (1.0 - BETA_TWO**STEP))
    weight_new = weight - rate * (first_hat / (jnp.sqrt(second_hat) + ADAM_EPS) + decay * weight)
    return weight_new, first_new, second_new


def adam_kernel(experts, norm_ref, dense_any, *refs):
    small = 6
    large_ins, rest = refs[:8], refs[8:]
    small_ins, rest = rest[: 3 * small + 2], rest[3 * small + 2 :]
    large_outs, rest = rest[:6], rest[6:]
    small_outs, norm_out, rest = rest[: 3 * small], rest[3 * small], rest[3 * small + 1 :]
    held, dense_ref, load, store = rest[: 3 * small + 2], rest[3 * small + 2], rest[-2], rest[-1]
    step, steps = pl.program_id(0), pl.num_programs(0)
    loads = [pltpu.make_async_copy(s, d, load.at[i]) for i, (s, d) in enumerate(zip(small_ins, held))]
    loads.append(pltpu.make_async_copy(dense_any, dense_ref, load.at[3 * small + 2]))
    stores = [pltpu.make_async_copy(s, d, store.at[i]) for i, (s, d) in enumerate(zip(held, small_outs))]

    @pl.when(step == 0)
    def _():
        for copy in loads:
            copy.start()

    total = jnp.sum(jnp.sum(norm_ref[...], axis=0, keepdims=True), axis=1, keepdims=True)
    norm = jnp.sqrt(total)
    clip = THRESHOLD / jnp.maximum(norm, THRESHOLD)
    for i, rate in enumerate((RATE_INNER, RATE_OUTER)):
        grad = large_ins[6 + i][...].astype(jnp.float32)
        state = [ref[...] for ref in large_ins[3 * i : 3 * i + 3]]
        for place, value in zip(large_outs[3 * i : 3 * i + 3], adam_values(*state, grad, clip, rate, DECAY)):
            place[...] = value

    def update(i, grad, rate, decay, columns=slice(None)):
        places = held[3 * i : 3 * i + 3]
        new = adam_values(*(ref[:, columns] for ref in places), grad, clip, rate, decay)
        for place, value in zip(places, new):
            place[:, columns] = value

    @pl.when(step == 1)
    def _():
        for copy in loads:
            copy.wait()
        norm_out[...] = norm
        width = held[3].shape[1]
        trio = 3 * LANES
        for pair in range(width // LANES):
            base = width + pair * trio + (LANES if pair == width // LANES - 1 else 0)
            for kind in range(3):
                update(
                    0,
                    dense_ref[:, base + kind * LANES : base + (kind + 1) * LANES],
                    RATE_PROJECTION,
                    DECAY,
                    slice(kind * width + pair * LANES, kind * width + (pair + 1) * LANES),
                )
        update(1, dense_ref[:, :width], RATE_OUTPUT, DECAY)
        turned = jnp.transpose(dense_ref[:, dense_ref.shape[1] - LANES :])
        update(2, turned[:experts], RATE_ROUTER, DECAY)
        update(3, turned[experts : experts + 7], RATE_VECTORS, 0.0)
        update(4, held[3 * small][...], RATE_HIDDEN, 0.0)
        update(5, held[3 * small + 1][...], RATE_RETURN, 0.0)
        for copy in stores:
            copy.start()

    @pl.when(step == steps - 1)
    def _():
        for copy in stores:
            copy.wait()


def adam_all(experts, squares, dense, states, grads, steps=8):
    full = jnp.float32

    def blocks(array):
        return pl.BlockSpec((array.shape[0] // steps, array.shape[1]), lambda i: (i, 0))

    large = [v for group in states[:2] for v in group]
    small = [v for group in states[2:] for v in group]
    spread = [blocks(v) for v in large]
    held = small + list(grads[2:])
    out = pl.pallas_call(
        functools.partial(adam_kernel, experts),
        grid=(steps,),
        out_shape=[jax.ShapeDtypeStruct(v.shape, full) for v in large + small] + [jax.ShapeDtypeStruct((1, 1), full)],
        in_specs=[pl.BlockSpec(squares.shape, lambda i: (0, 0)), ANY]
        + spread
        + [blocks(v) for v in grads[:2]]
        + [ANY] * len(held),
        out_specs=spread + [ANY] * len(small) + [pl.BlockSpec((1, 1), lambda i: (0, 0))],
        scratch_shapes=[pltpu.VMEM(v.shape, full) for v in held]
        + [
            pltpu.VMEM(dense.shape, full),
            pltpu.SemaphoreType.DMA((len(held) + 1,)),
            pltpu.SemaphoreType.DMA((len(small),)),
        ],
        compiler_params=pltpu.CompilerParams(
            vmem_limit_bytes=60 * 1024 * 1024, dimension_semantics=("arbitrary",)
        ),
        cost_estimate=pl.CostEstimate(flops=5 * 10**7, bytes_accessed=62 * 10**6, transcendentals=10**7),
        name="adam_all",
    )(squares, dense, *large, *grads[:2], *held)
    return [tuple(out[3 * i : 3 * i + 3]) for i in range(len(states))], out[-1].reshape(())


def fits(dp, experts):
    return dp == 2 and experts == 16


def fast_shards(
    dp,
    experts,
    tokens,
    cotangent,
    expert_choice,
    priority,
    projection,
    projection_first,
    projection_second,
    output_weight,
    output_first,
    output_second,
    router_weight,
    router_first,
    router_second,
    vectors,
    vectors_first,
    vectors_second,
    expert_inner,
    inner_first,
    inner_second,
    hidden_bias,
    hidden_first,
    hidden_second,
    expert_outer,
    outer_first,
    outer_second,
    return_bias,
    return_first,
    return_second,
):
    patches = tokens.shape[1]
    capacity = max(2, patches // experts)
    rows, dy, aux, probs, qkv, ctx, mid, second, stat, weights = forward(
        tokens[0],
        cotangent[0],
        expert_choice[0],
        priority[0],
        projection,
        output_weight,
        router_weight,
        vectors,
        dp,
        experts,
        capacity,
        1,
    )
    blocks = (experts, 8, rows.shape[1])
    returned, back_rows, inner_grad, hidden_grad, outer_grad, return_grad, expert_square = mixture(
        rows.reshape(blocks),
        dy.reshape(blocks),
        expert_inner,
        hidden_bias,
        expert_outer,
        return_bias,
        dp,
        2,
    )
    block_output, input_grad, dense, squares = backward(
        tokens[0],
        cotangent[0],
        returned.reshape(rows.shape),
        back_rows.reshape(rows.shape),
        aux,
        probs,
        mid,
        second,
        ctx,
        stat,
        qkv,
        weights,
        expert_square,
        dp,
        experts,
        capacity,
        4,
    )
    states, grad_norm = adam_all(
        experts,
        squares,
        dense,
        [
            (expert_inner[0], inner_first[0], inner_second[0]),
            (expert_outer[0], outer_first[0], outer_second[0]),
            (projection, projection_first, projection_second),
            (output_weight, output_first, output_second),
            (router_weight.T, router_first.T, router_second.T),
            (vectors, vectors_first, vectors_second),
            (hidden_bias, hidden_first, hidden_second),
            (return_bias, return_first, return_second),
        ],
        [inner_grad[0], outer_grad[0], hidden_grad, return_grad],
    )
    inner_new, outer_new, projection_new, output_new, router_new, vectors_new, hidden_new, return_new = states
    return (
        block_output[None],
        input_grad[None],
        grad_norm,
        *projection_new,
        *output_new,
        *(v.T for v in router_new),
        *vectors_new,
        *(v[None] for v in inner_new),
        *hidden_new,
        *(v[None] for v in outer_new),
        *return_new,
    )


def solution(mesh):
    dp, experts = mesh.shape["dp"], mesh.shape["expert"]
    body = functools.partial(fast_shards, dp, experts) if fits(dp, experts) else shards
    return jax.shard_map(
        body,
        mesh=mesh,
        in_specs=(
            P(("dp", "expert"), None, None),
            P(("dp", "expert"), None, None),
            P(("dp", "expert"), None, None),
            P(("dp", "expert"), None),
            P(("dp", "expert"), None),
            P(("dp", "expert"), None),
            P(("dp", "expert"), None),
            P(("dp", "expert"), None),
            P(("dp", "expert"), None),
            P(("dp", "expert"), None),
            P(("dp", "expert"), None),
            P(("dp", "expert"), None),
            P(("dp", "expert"), None),
            P(None, ("dp", "expert")),
            P(None, ("dp", "expert")),
            P(None, ("dp", "expert")),
            P("expert", None, "dp"),
            P("expert", None, "dp"),
            P("expert", None, "dp"),
            P("expert", "dp"),
            P("expert", "dp"),
            P("expert", "dp"),
            P("expert", "dp", None),
            P("expert", "dp", None),
            P("expert", "dp", None),
            P("expert", "dp"),
            P("expert", "dp"),
            P("expert", "dp"),
        ),
        out_specs=(
            P(("dp", "expert"), None, None),
            P(("dp", "expert"), None, None),
            P(),
            P(("dp", "expert"), None),
            P(("dp", "expert"), None),
            P(("dp", "expert"), None),
            P(("dp", "expert"), None),
            P(("dp", "expert"), None),
            P(("dp", "expert"), None),
            P(("dp", "expert"), None),
            P(("dp", "expert"), None),
            P(("dp", "expert"), None),
            P(None, ("dp", "expert")),
            P(None, ("dp", "expert")),
            P(None, ("dp", "expert")),
            P("expert", None, "dp"),
            P("expert", None, "dp"),
            P("expert", None, "dp"),
            P("expert", "dp"),
            P("expert", "dp"),
            P("expert", "dp"),
            P("expert", "dp", None),
            P("expert", "dp", None),
            P("expert", "dp", None),
            P("expert", "dp"),
            P("expert", "dp"),
            P("expert", "dp"),
        ),
        check_vma=False,
    )
```
